32 devices in a mesh: field: 2 (over y), sky: 4 (over z), epoch: 2 (over x), vel: 2 (over core).
Axes of the slice: x: 2, y: 2, z: 4, core: 2. Of those that a mesh axis runs over, the one named last changes fastest.
Arguments:
- images: bfloat16 [64, 8, 128, 128], P(('epoch', 'vel'), ('field', 'sky')), parts along dimension 1, may hold values from -6 to 6
- variances: bfloat16 [64, 8, 128, 128], P(('epoch', 'vel'), ('field', 'sky')), parts along dimension 1, may hold values from 0.5 to 2
- valid: int32 [64, 8], P(('epoch', 'vel'), ('field', 'sky')), parts along dimension 1, may hold values from 0 to 1, as said below
- psf_sigma: float32 [128], P(('field', 'epoch', 'vel')), parts along dimension 0, may hold values from 0.8 to 2.5
- offsets: int32 [2, 16, 64], P(None, None, 'epoch'), may hold values from -12 to 12, as said below
Outputs:
- likelihood: float32 [16, 8, 128, 128], P(('epoch', 'vel'), ('field', 'sky')), parts along dimension 1
- flux: float32 [16, 8, 128, 128], P(('epoch', 'vel'), ('field', 'sky')), parts along dimension 1
The draws below stay inside these ranges and needn't reach their ends.
There are 2 independent parts, one for each index of `field`. The reference program is written for one: setup_inputs(seed, part) draws one part's arguments, and reference() takes and returns one part's arrays. A program takes and returns all parts, laid end to end along the dimension named above; an argument that names none is the same for every part. Nothing has to cross between parts.
Inputs may be any that keep to these rules, and one draw needn't show every extreme that they name: Each hypothesis moves linearly: offsets[c, k, e] = floor(s[c, k] * e / 63) for integer speeds s within the range; both ends of the range are reached. `valid`: in one tile of the field, drawn from the seed, exactly one epoch is usable; in every other tile each frame is usable with probability 3/4, independently.
All inputs are finite; a program needn't handle non-finite values.
Results may differ from the reference program's by a relative error of at most 0.0058.
Values may be sent and summed in bfloat16 or wider, within the bound.
No kernel may reach another device: no remote copies, remote signals or barrier semaphores. Data moves between devices by JAX's collectives and lax.ppermute only.
A program may use at most 64 MiB of HBM per device.

```python
import math
import jax
import jax.numpy as jnp
from jax import lax

TILE = 128
VELS = 16
REACH = 12
PSFR = 7
GRID_X = 4
EPOCHS = 64
N_SKY = 4


def draw_offsets(key, part):
    speeds = jax.random.randint(key, (2, VELS), -REACH, REACH + 1).astype(jnp.int32)
    speeds = speeds.at[1, 0].set(REACH).at[0, 1].set(-REACH)
    epoch_ids = jnp.arange(EPOCHS, dtype=jnp.int32)
    return (speeds[:, :, None] * epoch_ids[None, None, :] // (EPOCHS - 1)).astype(jnp.int32)


def draw_valid(key, part):
    levels = jax.random.randint(jax.random.fold_in(key, 11), (EPOCHS, N_SKY), 0, 4)
    usable = (levels < 3).astype(jnp.int32)
    sparse_tile = jax.random.randint(jax.random.fold_in(key, 12), (), 0, N_SKY)
    kept_epoch = jax.random.randint(jax.random.fold_in(key, 13), (), 0, EPOCHS)
    tile_ids = jnp.arange(N_SKY, dtype=jnp.int32)
    epoch_ids = jnp.arange(EPOCHS, dtype=jnp.int32)
    single = (epoch_ids[:, None] == kept_epoch).astype(jnp.int32) * jnp.ones((1, N_SKY), jnp.int32)
    return jnp.where(tile_ids[None, :] == sparse_tile, single, usable).astype(jnp.int32)


def shard_levels(own_key, shape, split, least, top_value):
    def one(axis_at, blocks):
        draws = jax.random.uniform(jax.random.fold_in(jax.random.fold_in(own_key, 6), axis_at), (blocks,), jnp.float32, least / len(split), top_value / len(split))
        return jnp.repeat(jnp.exp(draws), shape[axis_at] // blocks).reshape((-1,) + (1,) * (len(shape) - axis_at - 1))

    loudness = one(*split[0])
    for cut in split[1:]:
        loudness = loudness * one(*cut)
    return loudness


def scatter_about(stream_key, dims, scale, reach, shards=(), held_as=jnp.bfloat16):
    array = scale * jax.random.normal(stream_key, dims, jnp.float32)
    if shards:
        array = array * shard_levels(stream_key, dims, shards, -0.22, 0.18)
    return jnp.clip(array, -reach, reach).astype(held_as)


def setup_inputs(seed: int = 0, part: int = 0) -> dict:
    streams_of = jax.random.split(jax.random.key(seed), 6)
    own_keys = jax.random.split(jax.random.fold_in(streams_of[5], part), 6)
    images = scatter_about(own_keys[0], (EPOCHS, N_SKY, TILE, TILE), 1.0, 6.0, ((0, 4), (1, 4)))
    variances = jnp.clip(jnp.exp(math.log(2.0) - 1.3862944 * jax.random.uniform(own_keys[1], (EPOCHS, N_SKY, TILE, TILE), jnp.float32) ** shard_levels(own_keys[1], (EPOCHS, N_SKY, TILE, TILE), ((0, 4), (1, 4)), -0.2, 0.2)), 0.5, 2.0).astype(jnp.bfloat16)
    valid = draw_valid(jax.random.fold_in(jax.random.fold_in(streams_of[5], part), 71), part)
    psf_sigma = jnp.clip(jnp.exp(math.log(2.5) - 1.13943427 * jax.random.uniform(own_keys[3], (EPOCHS,), jnp.float32) ** shard_levels(own_keys[3], (EPOCHS,), ((0, 4),), -0.2, 0.2)), 0.8, 2.5)
    offsets = draw_offsets(jax.random.fold_in(streams_of[5], 71), part)
    return dict(images=images, variances=variances, valid=valid, psf_sigma=psf_sigma, offsets=offsets)


phi_floor = 0.25

def round_keep(values):
    rounded = values.astype(jnp.bfloat16)
    rounded = lax.optimization_barrier(rounded)
    return rounded.astype(jnp.float32)

def kernel_taps(psf_sigma):
    spread = jnp.arange(-PSFR, PSFR + 1).astype(jnp.float32)
    profile = jnp.exp(-0.5 * (spread[None, :] / psf_sigma[:, None]) ** 2)
    profile = profile / lax.optimization_barrier(jnp.sum(profile, axis=1, keepdims=True))
    return (round_keep(profile), round_keep(profile * profile))

def whole_field(tiles):
    epoch_count = tiles.shape[0]
    grid_rows = N_SKY // GRID_X
    placed = jnp.roll(tiles, GRID_X // 2, axis=1)
    shaped = placed.reshape(epoch_count, grid_rows, GRID_X, TILE, TILE)
    return shaped.transpose(0, 1, 3, 2, 4).reshape(epoch_count, grid_rows * TILE, GRID_X * TILE)

def back_to_tiles(field):
    leading = field.shape[0]
    grid_rows = N_SKY // GRID_X
    shaped = field.reshape(leading, grid_rows, TILE, GRID_X, TILE)
    placed = shaped.transpose(0, 1, 3, 2, 4).reshape(leading, N_SKY, TILE, TILE)
    return jnp.roll(placed, -(GRID_X // 2), axis=1)

def correlate(field, kernel, axis):
    widths = [(0, 0), (0, 0), (0, 0)]
    widths[axis] = (PSFR, PSFR)
    padded = jnp.pad(field, widths)
    length = field.shape[axis]
    summed = jnp.zeros(field.shape, jnp.float32)
    for tap_index in range(2 * PSFR + 1):
        window = lax.slice_in_dim(padded, tap_index, tap_index + length, axis=axis)
        summed = summed + kernel[:, tap_index][:, None, None] * window
    return summed

def reference(images, variances, valid, psf_sigma, offsets):
    usable = valid.astype(jnp.float32)[:, :, None, None]
    scaled = images.astype(jnp.float32) / variances.astype(jnp.float32) * usable
    inverse = usable / variances.astype(jnp.float32)
    scaled = whole_field(round_keep(scaled))
    inverse = whole_field(round_keep(inverse))
    edges = ((0, 0), (REACH, REACH), (REACH, REACH))
    scaled = jnp.pad(scaled, edges)
    inverse = jnp.pad(inverse, edges)
    first_taps, second_taps = kernel_taps(psf_sigma)
    psi = correlate(round_keep(correlate(scaled, first_taps, 1)), first_taps, 2)
    phi = correlate(round_keep(correlate(inverse, second_taps, 1)), second_taps, 2)
    paired = jnp.stack([psi, phi], axis=1)
    height = paired.shape[2] - 2 * REACH
    breadth = paired.shape[3] - 2 * REACH

    def stack_one(motion):

        def accumulate(epoch_id, summed):
            epoch_map = lax.dynamic_index_in_dim(paired, epoch_id, 0, keepdims=False)
            start_y = (REACH + motion[0, epoch_id]).astype(jnp.int32)
            start_x = (REACH + motion[1, epoch_id]).astype(jnp.int32)
            window = lax.dynamic_slice(epoch_map, (jnp.zeros((), jnp.int32), start_y, start_x), (2, height, breadth))
            return summed + window
        return lax.fori_loop(0, EPOCHS, accumulate, jnp.zeros((2, height, breadth), jnp.float32))
    sums = lax.map(stack_one, jnp.transpose(offsets, (1, 0, 2)))
    psi_sum = sums[:, 0]
    phi_sum = jnp.maximum(sums[:, 1], phi_floor)
    likelihood = psi_sum / jnp.sqrt(phi_sum)
    flux = psi_sum / phi_sum
    return (back_to_tiles(likelihood), back_to_tiles(flux))
```

```python
import functools

import jax
import jax.numpy as jnp
from jax import lax
from jax.experimental import pallas as pl
from jax.experimental.pallas import tpu as pltpu
from jax.sharding import PartitionSpec as P

VELS = 16
REACH = 12
PSFR = 7
GRID_X = 4

phi_floor = 0.25

F32 = jnp.float32
BF16 = jnp.bfloat16
EDGE = REACH + PSFR
PAD = 16
HALO = 32
SIDE = 48
HALF = 64


def iota(shape, axis):
    return lax.broadcasted_iota(jnp.int32, shape, axis)


def by_distance(distance, taps_ref, first, count):
    value = jnp.full(distance.shape, taps_ref[first], F32)
    for a in range(1, count):
        value = jnp.where(distance == a, taps_ref[first + a], value)
    return value


def pick_edges(tile):
    row, lane = iota((2 * SIDE, tile), 0), iota((2 * SIDE, tile), 1)
    within = row % SIDE
    left = row >= SIDE
    wanted = jnp.where(
        within < EDGE,
        jnp.where(left, tile - EDGE, 0) + within,
        jnp.where(left, HALF - EDGE, HALF) + within - EDGE,
    )
    return jnp.where((within < 2 * EDGE) & (lane == wanted), 1.0, 0.0).astype(BF16)


def stack_kernel(
    epochs, tile, block, n_epoch, n_vel, prepared,
    place_ref, dy_ref, dx_ref, next_ref, taps_ref, valid_ref, first_ref, second_ref,
    send_ref, keep_ref, maps_ref, sum_ref,
):
    taps = PSFR + 1
    height = tile + 2 * PAD
    row, lane = iota((tile, tile), 0), iota((tile, tile), 1)
    gap = jnp.abs(row - lane)
    ring = jnp.minimum(gap, tile - gap)
    near = gap <= PSFR
    far = gap >= tile - PSFR
    if prepared:
        depth = tile + 2 * HALO
        drop = jnp.abs(iota((height, depth), 1) - HALO - iota((height, depth), 0) + PAD)

    maps_ref[0] = jnp.zeros(maps_ref.shape[1:], F32)

    def correlate(e, carry):
        if prepared:
            scaled, inverse = first_ref[e], second_ref[e]
        else:
            usable = valid_ref[e].astype(F32)
            variance = second_ref[e].astype(F32)
            scaled = (first_ref[e].astype(F32) / variance * usable).astype(BF16)
            inverse = (usable / variance).astype(BF16)
        rows, inner, outer = [], [], []
        for m, data in ((0, scaled), (1, inverse)):
            at = (2 * e + m) * taps
            turned = by_distance(ring, taps_ref, at, taps)
            inside = jnp.where(near, turned, 0.0).astype(BF16)
            beyond_f32 = jnp.where(far, turned, 0.0)
            beyond = beyond_f32.astype(BF16)
            if prepared:
                band = jnp.where(
                    drop <= PSFR, by_distance(drop, taps_ref, at, taps), 0.0
                ).astype(BF16)
            else:
                band = jnp.concatenate([beyond[tile - PAD :], inside, beyond[:PAD]], axis=0)
            rows.append(jnp.dot(band, data, preferred_element_type=F32).astype(BF16))
            inner.append(inside)
            outer.append(beyond if m == 0 else pltpu.roll(beyond_f32, HALF, 1).astype(BF16))
        maps_ref[e + 1, 0] = maps_ref[e, 0] + jnp.dot(rows[0], inner[0], preferred_element_type=F32)
        maps_ref[e + 1, 1] = maps_ref[e, 1] + jnp.dot(rows[1], inner[1], preferred_element_type=F32)
        maps_ref[e + 1, 2] = maps_ref[e, 2] + jnp.dot(
            jnp.concatenate(rows, axis=1),
            jnp.concatenate(outer, axis=0),
            preferred_element_type=F32,
        )
        return carry

    lax.fori_loop(0, epochs, correlate, 0)

    selector = pick_edges(tile)
    lane_turned = (lane + HALF) % tile

    def segment(k, e):
        at = k * epochs + e
        e_end = next_ref[at]
        start, dx = PAD + dy_ref[at], dx_ref[at]
        shift = jnp.where(dx > 0, tile - dx, -dx)

        def part(m):
            window = pl.ds(start, tile)
            return pltpu.roll(maps_ref[e_end, m, window, :] - maps_ref[e, m, window, :], shift, 1)

        psi, phi, side = part(0), part(1), part(2)
        source = lane + dx
        out = (source < 0) | (source >= tile)
        source = lane_turned + dx
        out_turned = (source < 0) | (source >= tile)
        return e_end, (
            jnp.where(out, side, psi),
            jnp.where(out, 0.0, phi),
            jnp.where(out, psi, jnp.where(out_turned, 0.0, side)),
            jnp.where(out, phi, jnp.where(out_turned, side, 0.0)),
        )

    def stack(k):
        e, parts = segment(k, 0)
        for i, value in enumerate(parts):
            sum_ref[i] = value

        def more(e):
            e, parts = segment(k, e)
            for i, value in enumerate(parts):
                sum_ref[i] += value
            return e

        lax.while_loop(lambda e: e < epochs, more, e)
        crossed = pltpu.roll(sum_ref[3], HALF, 1)
        middle = (lane >= HALF // 2) & (lane < tile - HALF // 2)
        phi = sum_ref[1] + jnp.where(middle, 0.0, crossed)
        side = sum_ref[2] + jnp.where(middle, crossed, 0.0)
        packed = lax.dot_general(
            selector, side.astype(BF16), (((1,), (1,)), ((), ())), preferred_element_type=F32
        )
        return sum_ref[0], phi, packed

    def run(target_ref, member_shift):
        def one(j, carry):
            owner = lax.rem(place_ref[0] + 1 + j // block, n_epoch)
            member = lax.rem(place_ref[1] + member_shift + j // (block * n_epoch), n_vel)
            k = (owner * n_vel + member) * block + lax.rem(j, block)
            psi, phi, packed = stack(k)
            target_ref[j, :tile] = psi.astype(target_ref.dtype)
            target_ref[j, tile : 2 * tile] = phi.astype(target_ref.dtype)
            target_ref[j, 2 * tile :] = packed.astype(target_ref.dtype)
            return carry

        lax.fori_loop(0, target_ref.shape[0], one, 0)

    if n_vel > 1:
        run(send_ref, 1)
    run(keep_ref, 0)


def finish_kernel(tile, keep_ref, own_ref, main_ref, right_ref, left_ref, like_ref, flux_ref):
    row, lane = iota((SIDE, tile), 0), iota((SIDE, tile), 1)
    for i in range(keep_ref.shape[0]):
        sums = []
        for m in range(2):
            rows = slice(m * tile, (m + 1) * tile)
            total = keep_ref[i, rows] + own_ref[i, rows] + main_ref[i, rows]
            at = row - m * EDGE
            used = (at >= 0) & (at < EDGE)
            for side_ref, first in ((right_ref, 0), (left_ref, tile - EDGE)):
                placed = jnp.where(used & (lane == at + first), 1.0, 0.0).astype(BF16)
                total = total + lax.dot_general(
                    side_ref[i], placed, (((0,), (0,)), ((), ())), preferred_element_type=F32
                )
            sums.append(total)
        phi = jnp.maximum(sums[1], phi_floor)
        like_ref[i] = sums[0] / jnp.sqrt(phi)
        flux_ref[i] = sums[0] / phi


def kernel_taps(psf_sigma):
    spread = jnp.arange(-PSFR, PSFR + 1).astype(F32)
    profile = jnp.exp(-0.5 * (spread[None, :] / psf_sigma[:, None]) ** 2)
    profile = profile / jnp.sum(profile, axis=1, keepdims=True)
    half = profile[:, PSFR:]
    both = jnp.stack([half.astype(BF16), (half * half).astype(BF16)], axis=1)
    return both.astype(F32)


def move(block, axis, distance):
    count = lax.axis_size(axis)
    return lax.ppermute(block, axis, [(i, (i + distance) % count) for i in range(count)])


def beside(block, step, keep):
    count = lax.axis_size("sky")
    device = [(q - GRID_X // 2) % count for q in range(count)]
    route = [(device[q], device[q + step]) for q in range(count) if keep(q)]
    return lax.ppermute(block, "sky", route)


def on_device(images, variances, valid, psf_sigma, offsets):
    epochs, tile = images.shape[0], images.shape[-1]
    n_epoch, n_vel = lax.axis_size("epoch"), lax.axis_size("vel")
    n_sky = lax.axis_size("sky")
    block = VELS // (n_epoch * n_vel)
    first, second = images[:, 0], variances[:, 0]
    prepared = n_sky > GRID_X
    if prepared:
        usable = valid[:, 0].astype(F32)[:, None, None]
        scaled = (first.astype(F32) / second.astype(F32) * usable).astype(BF16)
        inverse = (usable / second.astype(F32)).astype(BF16)
        pair = jnp.stack([scaled, inverse])
        above = beside(pair[:, :, tile - HALO :], GRID_X, lambda q: q + GRID_X < n_sky)
        below = beside(pair[:, :, :HALO], -GRID_X, lambda q: q >= GRID_X)
        first, second = jnp.concatenate([above, pair, below], axis=2)
    start = lax.axis_index("vel") * epochs
    motion = lax.dynamic_slice_in_dim(offsets, start, epochs, axis=2)
    step = jnp.arange(epochs, dtype=jnp.int32)
    changed = jnp.any(motion[:, :, 1:] != motion[:, :, :-1], axis=0)
    bounds = jnp.where(changed, step[None, 1:], epochs)
    following = jnp.min(
        jnp.where(step[1:][None, None, :] > step[None, :, None], bounds[:, None, :], epochs), axis=2
    )
    place = jnp.stack([lax.axis_index("epoch"), lax.axis_index("vel")]).astype(jnp.int32)
    taps = kernel_taps(psf_sigma)

    held = n_epoch * block
    length = 2 * tile + 2 * SIDE
    smem = pl.BlockSpec(memory_space=pltpu.SMEM)
    vmem = pl.BlockSpec(memory_space=pltpu.VMEM)
    send, keep = pl.pallas_call(
        functools.partial(stack_kernel, epochs, tile, block, n_epoch, n_vel, prepared),
        out_shape=(
            jax.ShapeDtypeStruct((held * max(n_vel - 1, 1), length, tile), BF16),
            jax.ShapeDtypeStruct((held, length, tile), F32),
        ),
        in_specs=[smem] * 6 + [vmem] * 2,
        out_specs=(vmem, vmem),
        scratch_shapes=[
            pltpu.VMEM((epochs + 1, 3, tile + 2 * PAD, tile), F32),
            pltpu.VMEM((4, tile, tile), F32),
        ],
        compiler_params=pltpu.CompilerParams(vmem_limit_bytes=32 * 1024 * 1024),
    )(
        place, motion[0].reshape(-1), motion[1].reshape(-1), following.reshape(-1),
        taps.reshape(-1), valid[:, 0], first, second,
    )

    arrived = jnp.zeros((held, length, tile), F32)
    for d in range(1, n_vel):
        arrived = arrived + move(send[(d - 1) * held : d * held], "vel", d).astype(F32)
    joined = keep + arrived
    own = held - block
    edges = joined[own:, 2 * tile :]
    main = jnp.zeros((block, 2 * tile, tile), F32)
    outgoing = []
    for d in range(1, n_epoch):
        away = joined[(d - 1) * block : d * block].astype(BF16)
        outgoing.append((d, away[:, 2 * tile :], away[:, : 2 * tile]))
    for d, away_edges, away_main in outgoing:
        edges = edges + move(away_edges, "epoch", d).astype(F32)
    for d, away_edges, away_main in outgoing:
        main = main + move(away_main, "epoch", d).astype(F32)
    edges = edges.astype(BF16)
    from_left = beside(edges[:, :SIDE], 1, lambda q: q % GRID_X < GRID_X - 1)
    from_right = beside(edges[:, SIDE:], -1, lambda q: q % GRID_X > 0)

    likelihood, flux = pl.pallas_call(
        functools.partial(finish_kernel, tile),
        out_shape=(jax.ShapeDtypeStruct((block, tile, tile), F32),) * 2,
        in_specs=[vmem] * 5,
        out_specs=(vmem, vmem),
        compiler_params=pltpu.CompilerParams(vmem_limit_bytes=32 * 1024 * 1024),
    )(keep[own:, : 2 * tile], arrived[own:, : 2 * tile], main, from_left, from_right)
    return likelihood[:, None], flux[:, None]


def solution(mesh):
    placed = (
        P(("epoch", "vel"), ("field", "sky"), None, None),
        P(("epoch", "vel"), ("field", "sky"), None, None),
        P(("epoch", "vel"), ("field", "sky")),
        P(("field", "epoch", "vel")),
        P(None, None, "epoch"),
    )
    return jax.shard_map(
        on_device,
        mesh=mesh,
        in_specs=placed,
        out_specs=(
            P(("epoch", "vel"), ("field", "sky"), None, None),
            P(("epoch", "vel"), ("field", "sky"), None, None),
        ),
        check_vma=False,
    )
```

```python
import functools

import jax
import jax.numpy as jnp
from jax import lax
from jax.experimental import pallas as pl
from jax.experimental.pallas import tpu as pltpu
from jax.sharding import PartitionSpec as P

VELS = 16
REACH = 12
PSFR = 7
GRID_X = 4

phi_floor = 0.25

F32 = jnp.float32
BF16 = jnp.bfloat16
EDGE = REACH + PSFR
PAD = 16
HALO = 32
SIDE = 48
HALF = 64
CHUNK = 4


def iota(shape, axis):
    return lax.broadcasted_iota(jnp.int32, shape, axis)


def pick_edges(tile, first_left):
    row, lane = iota((2 * SIDE, tile), 0), iota((2 * SIDE, tile), 1)
    within = row % SIDE
    left = (row >= SIDE) != first_left
    wanted = jnp.where(
        within < EDGE,
        jnp.where(left, tile - EDGE, 0) + within,
        jnp.where(left, HALF - EDGE, HALF) + within - EDGE,
    )
    return jnp.where((within < 2 * EDGE) & (lane == wanted), 1.0, 0.0).astype(BF16)


def segment_table(motion, epochs, first):
    code = (motion[0] + REACH) * 32 + motion[1] + REACH
    total = code.shape[1]
    lane = iota(code.shape, 1)
    later = jnp.roll(code, -1, axis=1) if total < 128 else pltpu.roll(code, total - 1, 1)
    stop = first + epochs
    end = jnp.where((later != code) | (lane == stop - 1), lane + 1, total)
    reach = 1
    while reach < epochs:
        end = jnp.minimum(end, jnp.where(lane + reach < total, jnp.roll(end, -reach, axis=1), total))
        reach *= 2
    return jnp.clip(end - first, 0, epochs) * 1024 + code


def stack_kernel(
    epochs, tile, block, n_epoch, n_vel, prepared,
    sigma_hbm, valid_hbm, motion_hbm, first_hbm, second_hbm,
    send_ref, keep_ref,
    sigma_ref, valid_ref, motion_ref, coded_ref, table_ref, first_ref, second_ref,
    maps_ref, sum_ref, side_ref, small_sems, data_sems, table_sem,
):
    height = tile + 2 * PAD
    chunks = epochs // CHUNK
    column = lax.axis_index("epoch")
    member = lax.axis_index("vel")

    small = [
        pltpu.make_async_copy(motion_hbm, motion_ref, small_sems.at[0]),
        pltpu.make_async_copy(sigma_hbm, sigma_ref, small_sems.at[1]),
        pltpu.make_async_copy(valid_hbm, valid_ref, small_sems.at[2]),
    ]
    for copy in small:
        copy.start()
    data = []
    for c in range(chunks):
        at = pl.ds(c * CHUNK, CHUNK)
        for i, (source, target) in enumerate(((first_hbm, first_ref), (second_hbm, second_ref))):
            data.append(pltpu.make_async_copy(source.at[at], target.at[at], data_sems.at[2 * c + i]))
            data[-1].start()

    row, lane = iota((tile, tile), 0), iota((tile, tile), 1)
    gap = jnp.abs(row - lane)
    ring = jnp.minimum(gap, tile - gap)
    outside = ring > PSFR
    far = gap >= tile // 2
    ring = ring.astype(F32)
    if prepared:
        depth = tile + 2 * HALO
        drop = jnp.abs(iota((height, depth), 1) - HALO - iota((height, depth), 0) + PAD)
        dropped = drop > PSFR
        drop = drop.astype(F32)

    maps_ref[0] = jnp.zeros(maps_ref.shape[1:], F32)
    for copy in small:
        copy.wait()
    coded_ref[...] = segment_table(motion_ref[...], epochs, member * epochs)
    table = pltpu.make_async_copy(coded_ref, table_ref, table_sem)
    table.start()

    def weights(e):
        def profile(distance, beyond):
            scaled = distance * (1.0 / jnp.full((1, distance.shape[1]), sigma_ref[e], F32))
            return jnp.where(beyond, 0.0, jnp.exp(-0.5 * (scaled * scaled)))

        turned = profile(ring, outside)
        scale = 1.0 / jnp.sum(turned[:8], axis=1, keepdims=True)[:1]
        turned = turned * scale
        bands = profile(drop, dropped) * scale if prepared else None
        result = []
        for m in range(2):
            value = turned if m == 0 else turned * turned
            inside = jnp.where(far, 0.0, value).astype(BF16)
            beyond = jnp.where(far, value, 0.0)
            top, bottom = beyond[:PAD], beyond[tile - PAD :]
            if prepared:
                band = (bands if m == 0 else bands * bands).astype(BF16)
            else:
                band = jnp.concatenate([bottom.astype(BF16), inside, top.astype(BF16)], axis=0)
            if m == 1:
                top, bottom = pltpu.roll(top, HALF, 1), pltpu.roll(bottom, HALF, 1)
            blank = jnp.zeros((tile - 2 * PAD, tile), BF16)
            outer = jnp.concatenate([top.astype(BF16), blank, bottom.astype(BF16)], axis=0)
            result.append((band, inside, outer))
        return result

    def correlate(e):
        if prepared:
            pair = first_ref[e], second_ref[e]
        else:
            usable = valid_ref[e].astype(F32)
            variance = second_ref[e].astype(F32)
            pair = (
                (first_ref[e].astype(F32) / variance * usable).astype(BF16),
                (usable / variance).astype(BF16),
            )
        built = weights(e)
        rows = [
            jnp.dot(built[m][0], pair[m], preferred_element_type=F32).astype(BF16) for m in range(2)
        ]
        return (
            jnp.dot(rows[0], built[0][1], preferred_element_type=F32),
            jnp.dot(rows[1], built[1][1], preferred_element_type=F32),
            jnp.dot(
                jnp.concatenate(rows, axis=1),
                jnp.concatenate([built[0][2], built[1][2]], axis=0),
                preferred_element_type=F32,
            ),
        )

    def correlate_chunk(c, carry):
        for i in range(2):
            at = pl.ds(c * CHUNK, CHUNK)
            source, target = ((first_hbm, first_ref), (second_hbm, second_ref))[i]
            pltpu.make_async_copy(source.at[at], target.at[at], data_sems.at[2 * c + i]).wait()
        made = [correlate(c * CHUNK + u) for u in range(CHUNK)]
        for i in range(3):
            total = maps_ref[c * CHUNK, i]
            for u in range(CHUNK):
                total = total + made[u][i]
                maps_ref[c * CHUNK + u + 1, i] = total
        return carry

    lax.fori_loop(0, chunks, correlate_chunk, 0)
    table.wait()

    turned_lane = (lane + HALF) % tile

    def segment(k, e):
        word = table_ref[k, member * epochs + jnp.minimum(e, epochs - 1)]
        e_end = jnp.where(e < epochs, word >> 10, epochs)
        start = PAD - REACH + ((word >> 5) & 31)
        dx = (word & 31) - REACH
        shift = jnp.where(dx > 0, tile - dx, -dx)
        window = pl.ds(start, tile)

        def part(m):
            return pltpu.roll(maps_ref[e_end, m, window, :] - maps_ref[e, m, window, :], shift, 1)

        psi, phi, side = part(0), part(1), part(2)
        source = lane + dx
        out = (source < 0) | (source >= tile)
        source = turned_lane + dx
        out_turned = (source < 0) | (source >= tile)
        return e_end, (
            jnp.where(out, side, psi),
            jnp.where(out, 0.0, phi),
            jnp.where(out, psi, jnp.where(out_turned, 0.0, side)),
            jnp.where(out, phi, jnp.where(out_turned, side, 0.0)),
        )

    def two_segments(k, e):
        e, one = segment(k, e)
        e, two = segment(k, e)
        return e, [a + b for a, b in zip(one, two)]

    middle = (lane >= HALF // 2) & (lane < tile - HALF // 2)

    def stack(k, at, target_ref, target_at):
        e, parts = two_segments(k, 0)
        for i, value in enumerate(parts):
            sum_ref[i] = value

        def more(e):
            e, parts = two_segments(k, e)
            for i, value in enumerate(parts):
                sum_ref[i] += value
            return e

        lax.while_loop(lambda e: e < epochs, more, e)
        crossed = pltpu.roll(sum_ref[3], HALF, 1)
        phi = sum_ref[1] + jnp.where(middle, 0.0, crossed)
        side = sum_ref[2] + jnp.where(middle, crossed, 0.0)
        target_ref[pl.ds(target_at, tile)] = sum_ref[0].astype(target_ref.dtype)
        target_ref[pl.ds(target_at + tile, tile)] = phi.astype(target_ref.dtype)
        side_ref[at] = side.astype(BF16)

    def run(target_ref, whose):
        def one(j, carry):
            rank, i = j // block, lax.rem(j, block)
            owner = lax.rem(column + 1 + rank, n_epoch)
            k = (owner * n_vel + whose) * block + i
            stack(k, (rank * n_vel + whose) * block + i, target_ref, j * 2 * tile)
            return carry

        lax.fori_loop(0, n_epoch * block, one, 0)

    run(send_ref, 1 - member)
    run(keep_ref, member)

    selector = pick_edges(tile, member == 1)
    edge_rows = 2 * tile * n_epoch * block

    def pack(c, carry):
        for u in range(CHUNK):
            at = c * CHUNK + u
            packed = lax.dot_general(
                selector, side_ref[at], (((1,), (1,)), ((), ())), preferred_element_type=F32
            )
            rows = pl.ds(edge_rows + at * SIDE, SIDE)
            keep_ref[rows] = packed[:SIDE]
            send_ref[rows] = packed[SIDE:].astype(BF16)
        return carry

    lax.fori_loop(0, VELS // CHUNK, pack, 0)


def finish_kernel(
    tile, keep_ref, own_ref, main_ref, near_ref, other_ref, like_ref, flux_ref
):
    row, lane = iota((SIDE, tile), 0), iota((SIDE, tile), 1)
    member = lax.axis_index("vel")
    i = pl.program_id(0)
    sums = []
    for m in range(2):
        rows = pl.ds(i * 2 * tile + m * tile, tile)
        total = keep_ref[rows] + own_ref[rows].astype(F32) + main_ref[rows].astype(F32)
        at = row - m * EDGE
        used = (at >= 0) & (at < EDGE)
        for side_ref, right in ((near_ref, 1 - member), (other_ref, member)):
            wanted = at + jnp.where(right == 1, 0, tile - EDGE)
            placed = jnp.where(used & (lane == wanted), 1.0, 0.0).astype(BF16)
            total = total + lax.dot_general(
                side_ref[pl.ds(i * SIDE, SIDE)], placed, (((0,), (0,)), ((), ())),
                preferred_element_type=F32,
            )
        sums.append(total)
    root = lax.rsqrt(jnp.maximum(sums[1], phi_floor))
    like = sums[0] * root
    like_ref[0] = like
    flux_ref[0] = like * root


def move(block, axis, distance):
    count = lax.axis_size(axis)
    return lax.ppermute(block, axis, [(i, (i + distance) % count) for i in range(count)])


def beside(block, step, keep):
    count = lax.axis_size("sky")
    device = [(q - GRID_X // 2) % count for q in range(count)]
    route = [(device[q], device[q + step]) for q in range(count) if keep(q)]
    return lax.ppermute(block, "sky", route)


def beside_by_member(block, distance):
    n_sky, n_epoch = lax.axis_size("sky"), lax.axis_size("epoch")
    device = [(q - GRID_X // 2) % n_sky for q in range(n_sky)]
    route = []
    for q in range(n_sky):
        for p in range(n_epoch):
            for v, step in ((0, 1), (1, -1)):
                if 0 <= q % GRID_X + step < GRID_X:
                    away = (p + distance) % n_epoch
                    route.append(
                        (
                            (device[q] * n_epoch + p) * 2 + v,
                            (device[q + step] * n_epoch + away) * 2 + v,
                        )
                    )
    return lax.ppermute(block, ("sky", "epoch", "vel"), route)


def on_device(images, variances, valid, psf_sigma, offsets):
    epochs, tile = images.shape[0], images.shape[-1]
    n_epoch, n_vel = lax.axis_size("epoch"), lax.axis_size("vel")
    n_sky = lax.axis_size("sky")
    assert n_vel == 2 and epochs % CHUNK == 0
    block = VELS // (n_epoch * n_vel)
    first, second = images[:, 0], variances[:, 0]
    prepared = n_sky > GRID_X
    if prepared:
        usable = valid[:, 0].astype(F32)[:, None, None]
        scaled = (first.astype(F32) / second.astype(F32) * usable).astype(BF16)
        inverse = (usable / second.astype(F32)).astype(BF16)
        pair = jnp.stack([scaled, inverse])
        above = beside(pair[:, :, tile - HALO :], GRID_X, lambda q: q + GRID_X < n_sky)
        below = beside(pair[:, :, :HALO], -GRID_X, lambda q: q >= GRID_X)
        first, second = jnp.concatenate([above, pair, below], axis=2)

    main_rows = block * 2 * tile
    edge_rows = block * SIDE
    length = n_epoch * (main_rows + n_vel * edge_rows)
    anywhere = pl.BlockSpec(memory_space=pl.ANY)
    vmem = pl.BlockSpec(memory_space=pltpu.VMEM)
    params = pltpu.CompilerParams(vmem_limit_bytes=32 * 1024 * 1024)
    send, keep = pl.pallas_call(
        functools.partial(stack_kernel, epochs, tile, block, n_epoch, n_vel, prepared),
        out_shape=(
            jax.ShapeDtypeStruct((length, tile), BF16),
            jax.ShapeDtypeStruct((length, tile), F32),
        ),
        in_specs=[anywhere] * 5,
        out_specs=(vmem, vmem),
        scratch_shapes=[
            pltpu.SMEM((epochs,), F32),
            pltpu.SMEM((epochs,), jnp.int32),
            pltpu.VMEM(offsets.shape, jnp.int32),
            pltpu.VMEM(offsets.shape[1:], jnp.int32),
            pltpu.SMEM(offsets.shape[1:], jnp.int32),
            pltpu.VMEM(first.shape, BF16),
            pltpu.VMEM(second.shape, BF16),
            pltpu.VMEM((epochs + 1, 3, tile + 2 * PAD, tile), F32),
            pltpu.VMEM((4, tile, tile), F32),
            pltpu.VMEM((VELS, tile, tile), BF16),
            pltpu.SemaphoreType.DMA((3,)),
            pltpu.SemaphoreType.DMA((2 * (epochs // CHUNK),)),
            pltpu.SemaphoreType.DMA,
        ],
        compiler_params=params,
    )(psf_sigma, valid[:, 0], offsets, first, second)

    arrived = move(send, "vel", 1)
    joined = keep + arrived.astype(F32)
    edges_at = n_epoch * main_rows
    far = joined.astype(BF16)
    mains, sides = [], []
    for d in range(1, n_epoch):
        mains.append(move(far[(d - 1) * main_rows : d * main_rows], "epoch", d))
    for d in range(1, n_epoch + 1):
        at = edges_at + (d - 1) * n_vel * edge_rows
        sides.append(beside_by_member(far[at : at + n_vel * edge_rows], d % n_epoch))
    side = sum(s.astype(F32) for s in sides)
    member = lax.axis_index("vel")
    halves = side.astype(BF16).reshape(n_vel, edge_rows, tile)
    near = jnp.where(member == 0, halves[0], halves[1])
    other = move(jnp.where(member == 0, halves[1], halves[0]), "vel", 1)
    main = sum(m.astype(F32) for m in mains) if len(mains) > 1 else mains[0]

    own_at = edges_at - main_rows
    shape = jax.ShapeDtypeStruct((block, tile, tile), F32)
    out = pl.BlockSpec((1, tile, tile), lambda i: (i, 0, 0))
    likelihood, flux = pl.pallas_call(
        functools.partial(finish_kernel, tile),
        grid=(block,),
        out_shape=(shape, shape),
        in_specs=[vmem] * 5,
        out_specs=(out, out),
        compiler_params=params,
    )(keep[own_at:edges_at], arrived[own_at:edges_at], main, near, other)
    return likelihood[:, None], flux[:, None]


def solution(mesh):
    placed = (
        P(("epoch", "vel"), ("field", "sky"), None, None),
        P(("epoch", "vel"), ("field", "sky"), None, None),
        P(("epoch", "vel"), ("field", "sky")),
        P(("field", "epoch", "vel")),
        P(None, None, "epoch"),
    )
    return jax.shard_map(
        on_device,
        mesh=mesh,
        in_specs=placed,
        out_specs=(
            P(("epoch", "vel"), ("field", "sky"), None, None),
            P(("epoch", "vel"), ("field", "sky"), None, None),
        ),
        check_vma=False,
    )
```

```python
import functools

import jax
import jax.numpy as jnp
from jax import lax
from jax.experimental import pallas as pl
from jax.experimental.pallas import tpu as pltpu
from jax.sharding import PartitionSpec as P

VELS = 16
REACH = 12
PSFR = 7
GRID_X = 4

phi_floor = 0.25

F32 = jnp.float32
BF16 = jnp.bfloat16
EDGE = REACH + PSFR
PAD = 16
HALO = 32
SIDE = 48
HALF = 64
CHUNK = 4


def iota(shape, axis):
    return lax.broadcasted_iota(jnp.int32, shape, axis)


def pick_edges(tile, first_left):
    row, lane = iota((2 * SIDE, tile), 0), iota((2 * SIDE, tile), 1)
    within = row % SIDE
    left = (row >= SIDE) != first_left
    wanted = jnp.where(
        within < EDGE,
        jnp.where(left, tile - EDGE, 0) + within,
        jnp.where(left, HALF - EDGE, HALF) + within - EDGE,
    )
    return jnp.where((within < 2 * EDGE) & (lane == wanted), 1.0, 0.0).astype(BF16)


def segment_table(motion, epochs, first):
    code = (motion[0] + REACH) * 32 + motion[1] + REACH
    total = code.shape[1]
    lane = iota(code.shape, 1)
    later = jnp.roll(code, -1, axis=1) if total < 128 else pltpu.roll(code, total - 1, 1)
    stop = first + epochs
    end = jnp.where((later != code) | (lane == stop - 1), lane + 1, total)
    reach = 1
    while reach < epochs:
        end = jnp.minimum(end, jnp.where(lane + reach < total, jnp.roll(end, -reach, axis=1), total))
        reach *= 2
    return jnp.clip(end - first, 0, epochs) * 1024 + code


def segment_sums(table_ref, maps_ref, sum_ref, epochs, tile, member, k):
    lane = iota((8, tile), 1)
    turned = (lane + HALF) % tile

    def segment(e):
        word = table_ref[k, member * epochs + jnp.minimum(e, epochs - 1)]
        e_end = jnp.where(e < epochs, word >> 10, epochs)
        start = PAD - REACH + ((word >> 5) & 31)
        dx = (word & 31) - REACH
        shift = jnp.where(dx > 0, tile - dx, -dx)
        out = (lane + dx < 0) | (lane + dx >= tile)
        out_turned = (turned + dx < 0) | (turned + dx >= tile)

        def at(r):
            window = pl.ds(start + r, 8)
            psi, phi, side = (
                pltpu.roll(maps_ref[e_end, m, window] - maps_ref[e, m, window], shift, 1)
                for m in range(3)
            )
            return (
                jnp.where(out, side, psi),
                jnp.where(out_turned, side, phi),
                jnp.where(out, psi, jnp.where(out_turned, phi, side)),
            )

        return e_end, at

    def two_segments(e, first):
        e, one = segment(e)
        e, two = segment(e)
        for r in range(0, tile, 8):
            for m, (a, b) in enumerate(zip(one(r), two(r))):
                value = a + b
                sum_ref[m, r : r + 8] = value if first else sum_ref[m, r : r + 8] + value
        return e

    e = two_segments(0, True)
    lax.while_loop(lambda e: e < epochs, lambda e: two_segments(e, False), e)


def stack_kernel(
    epochs, tile, block, n_epoch, n_vel, prepared,
    sigma_hbm, valid_hbm, motion_hbm, first_hbm, second_hbm,
    send_ref, keep_ref, maps_ref, side_ref, coded_ref,
    sigma_ref, valid_ref, motion_ref, table_ref, first_ref, second_ref, sum_ref,
    small_sems, data_sems, table_sem,
):
    height = tile + 2 * PAD
    chunks = epochs // CHUNK
    column = lax.axis_index("epoch")
    member = lax.axis_index("vel")

    small = [
        pltpu.make_async_copy(motion_hbm, motion_ref, small_sems.at[0]),
        pltpu.make_async_copy(sigma_hbm, sigma_ref, small_sems.at[1]),
        pltpu.make_async_copy(valid_hbm, valid_ref, small_sems.at[2]),
    ]
    for copy in small:
        copy.start()

    def data_copy(c, i):
        at = pl.ds(c * CHUNK, CHUNK)
        source, target = ((first_hbm, first_ref), (second_hbm, second_ref))[i]
        return pltpu.make_async_copy(source.at[at], target.at[at], data_sems.at[2 * c + i])

    for c in range(chunks):
        for i in range(2):
            data_copy(c, i).start()

    row, lane = iota((tile, tile), 0), iota((tile, tile), 1)
    gap = jnp.abs(row - lane)
    ring = jnp.minimum(gap, tile - gap)
    outside = ring > PSFR
    far = gap >= tile // 2
    ring = ring.astype(F32)
    if prepared:
        depth = tile + 2 * HALO
        drop = jnp.abs(iota((height, depth), 1) - HALO - iota((height, depth), 0) + PAD)
        dropped = drop > PSFR
        drop = drop.astype(F32)

    maps_ref[0] = jnp.zeros(maps_ref.shape[1:], F32)
    for copy in small:
        copy.wait()
    coded_ref[...] = segment_table(motion_ref[...], epochs, member * epochs)
    table = pltpu.make_async_copy(coded_ref, table_ref, table_sem)
    table.start()

    def weights(e):
        def profile(distance, beyond):
            scaled = distance * (1.0 / jnp.full((1, distance.shape[1]), sigma_ref[e], F32))
            return jnp.where(beyond, 0.0, jnp.exp(-0.5 * (scaled * scaled)))

        turned = profile(ring, outside)
        scale = 1.0 / jnp.sum(turned[:8], axis=1, keepdims=True)[:1]
        turned = turned * scale
        bands = profile(drop, dropped) * scale if prepared else None
        result = []
        for m in range(2):
            value = turned if m == 0 else turned * turned
            inside = jnp.where(far, 0.0, value)
            beyond = jnp.where(far, value, 0.0)
            top, bottom = beyond[:PAD], beyond[tile - PAD :]
            if prepared:
                band = (bands if m == 0 else bands * bands).astype(BF16)
            else:
                band = jnp.concatenate([bottom, inside, top], axis=0).astype(BF16)
            if m == 1:
                inside, top, bottom = (pltpu.roll(v, HALF, 1) for v in (inside, top, bottom))
            blank = jnp.zeros((tile - 2 * PAD, tile), F32)
            outer = jnp.concatenate([top, blank, bottom], axis=0)
            result.append((band, inside.astype(BF16), outer.astype(BF16)))
        return result

    def correlate(e):
        if prepared:
            pair = first_ref[e], second_ref[e]
        else:
            inverse = valid_ref[e].astype(F32) / second_ref[e].astype(F32)
            pair = (first_ref[e].astype(F32) * inverse).astype(BF16), inverse.astype(BF16)
        built = weights(e)
        rows = [
            jnp.dot(built[m][0], pair[m], preferred_element_type=F32).astype(BF16) for m in range(2)
        ]
        return (
            jnp.dot(rows[0], built[0][1], preferred_element_type=F32),
            jnp.dot(rows[1], built[1][1], preferred_element_type=F32),
            jnp.dot(
                jnp.concatenate(rows, axis=1),
                jnp.concatenate([built[0][2], built[1][2]], axis=0),
                preferred_element_type=F32,
            ),
        )

    def correlate_chunk(c, carry):
        for i in range(2):
            data_copy(c, i).wait()
        made = [correlate(c * CHUNK + u) for u in range(CHUNK)]
        for i in range(3):
            total = maps_ref[c * CHUNK, i]
            for u in range(CHUNK):
                total = total + made[u][i]
                maps_ref[c * CHUNK + u + 1, i] = total
        return carry

    lax.fori_loop(0, chunks, correlate_chunk, 0)
    table.wait()

    def run(count, target_ref, whose):
        def one(j, carry):
            rank, i = j // block, lax.rem(j, block)
            owner = lax.rem(column + 1 + rank, n_epoch)
            k = (owner * n_vel + whose) * block + i
            segment_sums(table_ref, maps_ref, sum_ref, epochs, tile, member, k)
            target_ref[pl.ds(j * 2 * tile, 2 * tile)] = (
                sum_ref[:2].reshape(2 * tile, tile).astype(target_ref.dtype)
            )
            side_ref[(rank * n_vel + whose) * block + i] = sum_ref[2].astype(BF16)
            return carry

        lax.fori_loop(0, count, one, 0)

    run(n_epoch * block, send_ref, 1 - member)
    run((n_epoch - 1) * block, keep_ref, member)


def own_kernel(
    epochs, tile, block, n_epoch, n_vel,
    table_ref, maps_ref, side_ref, keep_ref, send_edge_ref, keep_edge_ref, sum_ref,
):
    column = lax.axis_index("epoch")
    member = lax.axis_index("vel")
    selector = pick_edges(tile, member == 1)

    def pack(at, side):
        packed = lax.dot_general(
            selector, side, (((1,), (1,)), ((), ())), preferred_element_type=F32
        )
        rows = pl.ds(at * SIDE, SIDE)
        keep_edge_ref[rows] = packed[:SIDE]
        send_edge_ref[rows] = packed[SIDE:].astype(BF16)

    def own(i, carry):
        k = (column * n_vel + member) * block + i
        segment_sums(table_ref, maps_ref, sum_ref, epochs, tile, member, k)
        keep_ref[pl.ds(i * 2 * tile, 2 * tile)] = sum_ref[:2].reshape(2 * tile, tile)
        pack(((n_epoch - 1) * n_vel + member) * block + i, sum_ref[2].astype(BF16))
        return carry

    lax.fori_loop(0, block, own, 0)

    def others(c, carry):
        for u in range(block):
            rank = jnp.where(c < (n_epoch - 1) * n_vel, c // n_vel, n_epoch - 1)
            whose = jnp.where(c < (n_epoch - 1) * n_vel, lax.rem(c, n_vel), 1 - member)
            at = (rank * n_vel + whose) * block + u
            pack(at, side_ref[at])
        return carry

    lax.fori_loop(0, n_epoch * n_vel - 1, others, 0)


def finish_kernel(
    tile, block, keep_ref, own_ref, main_ref, near_ref, other_ref, like_ref, flux_ref
):
    row, lane = iota((SIDE, tile), 0), iota((SIDE, tile), 1)
    member = lax.axis_index("vel")
    placed = []
    for m in range(2):
        at = row - m * EDGE
        used = (at >= 0) & (at < EDGE)
        for right in (1 - member, member):
            wanted = at + jnp.where(right == 1, 0, tile - EDGE) + m * HALF
            placed.append(jnp.where(used & (lane == wanted % tile), 1.0, 0.0).astype(BF16))
    for i in range(block):
        sums = []
        for m in range(2):
            rows = slice((2 * i + m) * tile, (2 * i + m + 1) * tile)
            total = keep_ref[rows] + own_ref[rows].astype(F32) + main_ref[rows].astype(F32)
            for side_ref, put in zip((near_ref, other_ref), placed[2 * m : 2 * m + 2]):
                total = total + lax.dot_general(
                    side_ref[i * SIDE : (i + 1) * SIDE], put, (((0,), (0,)), ((), ())),
                    preferred_element_type=F32,
                )
            sums.append(total)
        root = lax.rsqrt(jnp.maximum(pltpu.roll(sums[1], HALF, 1), phi_floor))
        like = sums[0] * root
        like_ref[i] = like
        flux_ref[i] = like * root


def move(block, axis, distance):
    count = lax.axis_size(axis)
    return lax.ppermute(block, axis, [(i, (i + distance) % count) for i in range(count)])


def beside(block, step, keep):
    count = lax.axis_size("sky")
    device = [(q - GRID_X // 2) % count for q in range(count)]
    route = [(device[q], device[q + step]) for q in range(count) if keep(q)]
    return lax.ppermute(block, "sky", route)


def beside_by_member(block, distance):
    n_sky, n_epoch = lax.axis_size("sky"), lax.axis_size("epoch")
    device = [(q - GRID_X // 2) % n_sky for q in range(n_sky)]
    route = []
    for q in range(n_sky):
        for p in range(n_epoch):
            for v, step in ((0, 1), (1, -1)):
                if 0 <= q % GRID_X + step < GRID_X:
                    away = (p + distance) % n_epoch
                    route.append(
                        (
                            (device[q] * n_epoch + p) * 2 + v,
                            (device[q + step] * n_epoch + away) * 2 + v,
                        )
                    )
    return lax.ppermute(block, ("sky", "epoch", "vel"), route)


def on_device(images, variances, valid, psf_sigma, offsets):
    epochs, tile = images.shape[0], images.shape[-1]
    n_epoch, n_vel = lax.axis_size("epoch"), lax.axis_size("vel")
    n_sky = lax.axis_size("sky")
    assert n_vel == 2 and epochs % CHUNK == 0
    block = VELS // (n_epoch * n_vel)
    first, second = images[:, 0], variances[:, 0]
    prepared = n_sky > GRID_X
    if prepared:
        usable = valid[:, 0].astype(F32)[:, None, None]
        scaled = (first.astype(F32) / second.astype(F32) * usable).astype(BF16)
        inverse = (usable / second.astype(F32)).astype(BF16)
        pair = jnp.stack([scaled, inverse])
        above = beside(pair[:, :, tile - HALO :], GRID_X, lambda q: q + GRID_X < n_sky)
        below = beside(pair[:, :, :HALO], -GRID_X, lambda q: q >= GRID_X)
        first, second = jnp.concatenate([above, pair, below], axis=2)

    main_rows = block * 2 * tile
    edge_rows = block * SIDE
    hbm = pl.BlockSpec(memory_space=pltpu.HBM)
    smem = pl.BlockSpec(memory_space=pltpu.SMEM)
    vmem = pl.BlockSpec(memory_space=pltpu.VMEM)
    params = pltpu.CompilerParams(vmem_limit_bytes=32 * 1024 * 1024)
    plane = pltpu.VMEM((3, tile, tile), F32)
    send, keep_far, maps, side, table = pl.pallas_call(
        functools.partial(stack_kernel, epochs, tile, block, n_epoch, n_vel, prepared),
        out_shape=(
            jax.ShapeDtypeStruct((n_epoch * main_rows, tile), BF16),
            jax.ShapeDtypeStruct(((n_epoch - 1) * main_rows, tile), F32),
            jax.ShapeDtypeStruct((epochs + 1, 3, tile + 2 * PAD, tile), F32),
            jax.ShapeDtypeStruct((VELS, tile, tile), BF16),
            jax.ShapeDtypeStruct(offsets.shape[1:], jnp.int32),
        ),
        in_specs=[hbm] * 5,
        out_specs=(vmem,) * 5,
        scratch_shapes=[
            pltpu.SMEM((epochs,), F32),
            pltpu.SMEM((epochs,), jnp.int32),
            pltpu.VMEM(offsets.shape, jnp.int32),
            pltpu.SMEM(offsets.shape[1:], jnp.int32),
            pltpu.VMEM(first.shape, BF16),
            pltpu.VMEM(second.shape, BF16),
            plane,
            pltpu.SemaphoreType.DMA((3,)),
            pltpu.SemaphoreType.DMA((2 * (epochs // CHUNK),)),
            pltpu.SemaphoreType.DMA,
        ],
        compiler_params=params,
    )(psf_sigma, valid[:, 0], offsets, first, second)
    arrived = move(send, "vel", 1)

    keep_own, send_edge, keep_edge = pl.pallas_call(
        functools.partial(own_kernel, epochs, tile, block, n_epoch, n_vel),
        out_shape=(
            jax.ShapeDtypeStruct((main_rows, tile), F32),
            jax.ShapeDtypeStruct((n_epoch * n_vel * edge_rows, tile), BF16),
            jax.ShapeDtypeStruct((n_epoch * n_vel * edge_rows, tile), F32),
        ),
        in_specs=[smem, vmem, vmem],
        out_specs=(vmem,) * 3,
        scratch_shapes=[plane],
        compiler_params=params,
    )(table, maps, side)
    edges = (keep_edge + move(send_edge, "vel", 1).astype(F32)).astype(BF16)

    far = (keep_far + arrived[:-main_rows].astype(F32)).astype(BF16)
    mains, sides = [], []
    for d in range(1, n_epoch):
        mains.append(move(far[(d - 1) * main_rows : d * main_rows], "epoch", d))
    for d in range(1, n_epoch + 1):
        at = (d - 1) * n_vel * edge_rows
        sides.append(beside_by_member(edges[at : at + n_vel * edge_rows], d % n_epoch))
    side = sum(s.astype(F32) for s in sides)
    member = lax.axis_index("vel")
    halves = side.astype(BF16).reshape(n_vel, edge_rows, tile)
    near = jnp.where(member == 0, halves[0], halves[1])
    other = move(jnp.where(member == 0, halves[1], halves[0]), "vel", 1)
    main = sum(m.astype(F32) for m in mains) if len(mains) > 1 else mains[0]

    shape = jax.ShapeDtypeStruct((block, tile, tile), F32)
    likelihood, flux = pl.pallas_call(
        functools.partial(finish_kernel, tile, block),
        out_shape=(shape, shape),
        in_specs=[vmem] * 5,
        out_specs=(vmem, vmem),
        compiler_params=params,
    )(keep_own, arrived[-main_rows:], main, near, other)
    return likelihood[:, None], flux[:, None]


def solution(mesh):
    placed = (
        P(("epoch", "vel"), ("field", "sky"), None, None),
        P(("epoch", "vel"), ("field", "sky"), None, None),
        P(("epoch", "vel"), ("field", "sky")),
        P(("field", "epoch", "vel")),
        P(None, None, "epoch"),
    )
    return jax.shard_map(
        on_device,
        mesh=mesh,
        in_specs=placed,
        out_specs=(
            P(("epoch", "vel"), ("field", "sky"), None, None),
            P(("epoch", "vel"), ("field", "sky"), None, None),
        ),
        check_vma=False,
    )
```

```python
import functools

import jax
import jax.numpy as jnp
from jax import lax
from jax.experimental import pallas as pl
from jax.experimental.pallas import tpu as pltpu
from jax.sharding import PartitionSpec as P

VELS = 16
REACH = 12
PSFR = 7
GRID_X = 4

phi_floor = 0.25

F32 = jnp.float32
BF16 = jnp.bfloat16
EDGE = REACH + PSFR
PAD = 16
HALO = 32
SIDE = 48
HALF = 64
CHUNK = 4
STEP = 8


def iota(shape, axis):
    return lax.broadcasted_iota(jnp.int32, shape, axis)


def pick_edges(tile, first_left):
    row, lane = iota((2 * SIDE, tile), 0), iota((2 * SIDE, tile), 1)
    within = row % SIDE
    left = (row >= SIDE) != first_left
    wanted = jnp.where(
        within < EDGE,
        jnp.where(left, tile - EDGE, 0) + within,
        jnp.where(left, HALF - EDGE, HALF) + within - EDGE,
    )
    return jnp.where((within < 2 * EDGE) & (lane == wanted), 1.0, 0.0).astype(BF16)


def segment_table(motion, epochs, first):
    code = (motion[0] + REACH) * 32 + motion[1] + REACH
    total = code.shape[1]
    lane = iota(code.shape, 1)
    later = jnp.roll(code, -1, axis=1) if total < 128 else pltpu.roll(code, total - 1, 1)
    stop = first + epochs
    end = jnp.where((later != code) | (lane == stop - 1), lane + 1, total)
    reach = 1
    while reach < epochs:
        end = jnp.minimum(end, jnp.where(lane + reach < total, jnp.roll(end, -reach, axis=1), total))
        reach *= 2
    return jnp.clip(end - first, 0, epochs) * 1024 + code


def stack_kernel(
    epochs, tile, block, n_epoch, n_vel, prepared,
    sigma_hbm, valid_hbm, motion_hbm, first_hbm, second_hbm,
    send_ref, keep_ref,
    sigma_ref, valid_ref, motion_ref, coded_ref, table_ref, first_ref, second_ref, maps_ref, sum_ref,
    small_sems, data_sems, table_sem,
):
    height = tile + 2 * PAD
    chunks = epochs // CHUNK
    column = lax.axis_index("epoch")
    member = lax.axis_index("vel")

    small = [
        pltpu.make_async_copy(motion_hbm, motion_ref, small_sems.at[0]),
        pltpu.make_async_copy(sigma_hbm, sigma_ref, small_sems.at[1]),
        pltpu.make_async_copy(valid_hbm, valid_ref, small_sems.at[2]),
    ]
    for copy in small:
        copy.start()

    def data_copy(c, i):
        at = pl.ds(c * CHUNK, CHUNK)
        source, target = ((first_hbm, first_ref), (second_hbm, second_ref))[i]
        return pltpu.make_async_copy(source.at[at], target.at[at], data_sems.at[2 * c + i])

    for c in range(chunks):
        for i in range(2):
            data_copy(c, i).start()

    row, lane = iota((tile, tile), 0), iota((tile, tile), 1)
    gap = jnp.abs(row - lane)
    ring = jnp.minimum(gap, tile - gap)
    outside = ring > PSFR
    far = gap >= tile // 2
    ring = ring.astype(F32)
    if prepared:
        depth = tile + 2 * HALO
        drop = jnp.abs(iota((height, depth), 1) - HALO - iota((height, depth), 0) + PAD)
        dropped = drop > PSFR
        drop = drop.astype(F32)

    maps_ref[0] = jnp.zeros(maps_ref.shape[1:], F32)

    def clear(slot, carry):
        sum_ref[slot] = jnp.zeros(sum_ref.shape[1:], F32)
        return carry

    lax.fori_loop(0, VELS, clear, 0)
    for copy in small:
        copy.wait()
    coded_ref[...] = segment_table(motion_ref[...], epochs, member * epochs)
    table = pltpu.make_async_copy(coded_ref, table_ref, table_sem)
    table.start()

    def weights(e):
        def profile(distance, beyond):
            scaled = distance * (1.0 / jnp.full((1, distance.shape[1]), sigma_ref[e], F32))
            return jnp.where(beyond, 0.0, jnp.exp(-0.5 * (scaled * scaled)))

        turned = profile(ring, outside)
        scale = 1.0 / jnp.sum(turned[:8], axis=1, keepdims=True)[:1]
        turned = turned * scale
        bands = profile(drop, dropped) * scale if prepared else None
        result = []
        for m in range(2):
            value = turned if m == 0 else turned * turned
            inside = jnp.where(far, 0.0, value)
            beyond = jnp.where(far, value, 0.0)
            top, bottom = beyond[:PAD], beyond[tile - PAD :]
            if prepared:
                band = (bands if m == 0 else bands * bands).astype(BF16)
            else:
                band = jnp.concatenate([bottom, inside, top], axis=0).astype(BF16)
            if m == 1:
                inside, top, bottom = (pltpu.roll(v, HALF, 1) for v in (inside, top, bottom))
            blank = jnp.zeros((tile - 2 * PAD, tile), F32)
            outer = jnp.concatenate([top, blank, bottom], axis=0)
            result.append((band, inside.astype(BF16), outer.astype(BF16)))
        return result

    def correlate(e):
        if prepared:
            pair = first_ref[e], second_ref[e]
        else:
            inverse = valid_ref[e].astype(F32) / second_ref[e].astype(F32)
            pair = (first_ref[e].astype(F32) * inverse).astype(BF16), inverse.astype(BF16)
        built = weights(e)
        rows = [
            jnp.dot(built[m][0], pair[m], preferred_element_type=F32).astype(BF16) for m in range(2)
        ]
        return (
            jnp.dot(rows[0], built[0][1], preferred_element_type=F32),
            jnp.dot(rows[1], built[1][1], preferred_element_type=F32),
            jnp.dot(
                jnp.concatenate(rows, axis=1),
                jnp.concatenate([built[0][2], built[1][2]], axis=0),
                preferred_element_type=F32,
            ),
        )

    def correlate_chunk(c, carry):
        for i in range(2):
            data_copy(c, i).wait()
        made = [correlate(c * CHUNK + u) for u in range(CHUNK)]
        for i in range(3):
            total = maps_ref[c * CHUNK, i]
            for u in range(CHUNK):
                total = total + made[u][i]
                maps_ref[c * CHUNK + u + 1, i] = total
        return carry

    lax.fori_loop(0, chunks, correlate_chunk, 0)
    table.wait()

    lane8 = iota((8, tile), 1)
    turned8 = (lane8 + HALF) % tile
    first_k = (column + 1) * n_vel * block

    def segment(slot, e):
        word = table_ref[lax.rem(first_k + slot, VELS), member * epochs + e]
        e_end = word >> 10
        start = PAD - REACH + ((word >> 5) & 31)
        dx = (word & 31) - REACH
        shift = jnp.where(dx > 0, tile - dx, -dx)
        out = (lane8 + dx < 0) | (lane8 + dx >= tile)
        out_turned = (turned8 + dx < 0) | (turned8 + dx >= tile)
        for r in range(0, tile, 8):
            window = pl.ds(start + r, 8)
            psi, phi, side = (
                pltpu.roll(maps_ref[e_end, m, window] - maps_ref[e, m, window], shift, 1)
                for m in range(3)
            )
            sum_ref[slot, 0, r : r + 8] += jnp.where(out, side, psi)
            sum_ref[slot, 1, r : r + 8] += jnp.where(out_turned, side, phi)
            sum_ref[slot, 2, r : r + 8] += jnp.where(out, psi, jnp.where(out_turned, phi, side))
        ended = e_end >= epochs
        return jnp.where(ended, jnp.minimum(slot + 1, VELS), slot), jnp.where(ended, 0, e_end)

    def some_segments(state):
        for _ in range(STEP):
            state = segment(*state)
        return state

    start = (jnp.int32(0), jnp.int32(0))
    lax.while_loop(lambda state: state[0] < VELS, some_segments, start)

    selector = pick_edges(tile, member == 1)
    mains = n_epoch * block * 2 * tile

    def write(group, carry):
        rank, whose = group // n_vel, lax.rem(group, n_vel)
        kept = whose == member
        for i in range(block):
            slot = group * block + i
            packed = lax.dot_general(
                selector, sum_ref[slot, 2].astype(BF16), (((1,), (1,)), ((), ())),
                preferred_element_type=F32,
            )
            rows = pl.ds(mains + slot * SIDE, SIDE)
            keep_ref[rows] = packed[:SIDE]
            send_ref[rows] = packed[SIDE:].astype(BF16)
            main = pl.ds((rank * block + i) * 2 * tile, 2 * tile)

            @pl.when(kept)
            def _():
                keep_ref[main] = sum_ref[slot, :2].reshape(2 * tile, tile)

            @pl.when(jnp.logical_not(kept))
            def _():
                send_ref[main] = sum_ref[slot, :2].reshape(2 * tile, tile).astype(BF16)

        return carry

    lax.fori_loop(0, n_epoch * n_vel, write, 0)


def add_kernel(n_mains, keep_ref, own_ref, *refs):
    arrived, (total_ref, near_ref, other_ref) = refs[:-3], refs[-3:]
    mains, sides = arrived[:n_mains], arrived[n_mains:]
    total = keep_ref[...] + own_ref[...].astype(F32)
    for main_ref in mains:
        total = total + main_ref[...].astype(F32)
    total_ref[...] = total
    side = sum(side_ref[...].astype(F32) for side_ref in sides)
    half = near_ref.shape[0]
    first = lax.axis_index("vel") == 0
    near_ref[...] = jnp.where(first, side[:half], side[half:]).astype(BF16)
    other_ref[...] = jnp.where(first, side[half:], side[:half]).astype(BF16)


def finish_kernel(tile, block, total_ref, near_ref, other_ref, like_ref, flux_ref):
    row, lane = iota((SIDE, tile), 0), iota((SIDE, tile), 1)
    member = lax.axis_index("vel")
    placed = []
    for m in range(2):
        at = row - m * EDGE
        used = (at >= 0) & (at < EDGE)
        for right in (1 - member, member):
            wanted = at + jnp.where(right == 1, 0, tile - EDGE) + m * HALF
            placed.append(jnp.where(used & (lane == wanted % tile), 1.0, 0.0).astype(BF16))
    for i in range(block):
        sums = []
        for m in range(2):
            rows = slice((2 * i + m) * tile, (2 * i + m + 1) * tile)
            total = total_ref[rows]
            for side_ref, put in zip((near_ref, other_ref), placed[2 * m : 2 * m + 2]):
                total = total + lax.dot_general(
                    side_ref[i * SIDE : (i + 1) * SIDE], put, (((0,), (0,)), ((), ())),
                    preferred_element_type=F32,
                )
            sums.append(total)
        root = lax.rsqrt(jnp.maximum(pltpu.roll(sums[1], HALF, 1), phi_floor))
        like = sums[0] * root
        like_ref[i] = like
        flux_ref[i] = like * root


def move(block, axis, distance):
    count = lax.axis_size(axis)
    return lax.ppermute(block, axis, [(i, (i + distance) % count) for i in range(count)])


def beside(block, step, keep):
    count = lax.axis_size("sky")
    device = [(q - GRID_X // 2) % count for q in range(count)]
    route = [(device[q], device[q + step]) for q in range(count) if keep(q)]
    return lax.ppermute(block, "sky", route)


def beside_by_member(block, distance):
    n_sky, n_epoch = lax.axis_size("sky"), lax.axis_size("epoch")
    device = [(q - GRID_X // 2) % n_sky for q in range(n_sky)]
    route = []
    for q in range(n_sky):
        for p in range(n_epoch):
            for v, step in ((0, 1), (1, -1)):
                if 0 <= q % GRID_X + step < GRID_X:
                    away = (p + distance) % n_epoch
                    route.append(
                        (
                            (device[q] * n_epoch + p) * 2 + v,
                            (device[q + step] * n_epoch + away) * 2 + v,
                        )
                    )
    return lax.ppermute(block, ("sky", "epoch", "vel"), route)


def on_device(images, variances, valid, psf_sigma, offsets):
    epochs, tile = images.shape[0], images.shape[-1]
    n_epoch, n_vel = lax.axis_size("epoch"), lax.axis_size("vel")
    n_sky = lax.axis_size("sky")
    assert n_vel == 2 and epochs % CHUNK == 0
    block = VELS // (n_epoch * n_vel)
    first, second = images[:, 0], variances[:, 0]
    prepared = n_sky > GRID_X
    if prepared:
        usable = valid[:, 0].astype(F32)[:, None, None]
        scaled = (first.astype(F32) / second.astype(F32) * usable).astype(BF16)
        inverse = (usable / second.astype(F32)).astype(BF16)
        pair = jnp.stack([scaled, inverse])
        above = beside(pair[:, :, tile - HALO :], GRID_X, lambda q: q + GRID_X < n_sky)
        below = beside(pair[:, :, :HALO], -GRID_X, lambda q: q >= GRID_X)
        first, second = jnp.concatenate([above, pair, below], axis=2)

    main_rows = block * 2 * tile
    edge_rows = block * SIDE
    hbm = pl.BlockSpec(memory_space=pltpu.HBM)
    vmem = pl.BlockSpec(memory_space=pltpu.VMEM)
    params = pltpu.CompilerParams(vmem_limit_bytes=32 * 1024 * 1024)
    mains_end = n_epoch * main_rows
    length = mains_end + n_epoch * n_vel * edge_rows
    operands = (psf_sigma, valid[:, 0], offsets, first, second)
    send, keep = pl.pallas_call(
        functools.partial(stack_kernel, epochs, tile, block, n_epoch, n_vel, prepared),
        out_shape=(
            jax.ShapeDtypeStruct((length, tile), BF16),
            jax.ShapeDtypeStruct((length, tile), F32),
        ),
        in_specs=[hbm] * 5,
        out_specs=(vmem,) * 2,
        scratch_shapes=[
            pltpu.SMEM((epochs,), F32),
            pltpu.SMEM((epochs,), jnp.int32),
            pltpu.VMEM(offsets.shape, jnp.int32),
            pltpu.VMEM(offsets.shape[1:], jnp.int32),
            pltpu.SMEM(offsets.shape[1:], jnp.int32),
            pltpu.VMEM(first.shape, BF16),
            pltpu.VMEM(second.shape, BF16),
            pltpu.VMEM((epochs + 1, 3, tile + 2 * PAD, tile), F32),
            pltpu.VMEM((VELS + 1, 3, tile, tile), F32),
            pltpu.SemaphoreType.DMA((3,)),
            pltpu.SemaphoreType.DMA((2 * (epochs // CHUNK),)),
            pltpu.SemaphoreType.DMA,
        ],
        compiler_params=params,
    )(*(pltpu.with_memory_space_constraint(a, pltpu.HBM) for a in operands))

    arrived = move(send, "vel", 1)
    joined = (keep + arrived.astype(F32)).astype(BF16)
    mains, sides = [], []
    for d in range(1, n_epoch):
        mains.append(move(joined[(d - 1) * main_rows : d * main_rows], "epoch", d))
    for d in range(1, n_epoch + 1):
        at = mains_end + (d - 1) * n_vel * edge_rows
        sides.append(beside_by_member(joined[at : at + n_vel * edge_rows], d % n_epoch))
    if not mains:
        mains.append(jnp.zeros((main_rows, tile), BF16))

    own = slice(mains_end - main_rows, mains_end)
    total, near, other = pl.pallas_call(
        functools.partial(add_kernel, len(mains)),
        out_shape=(
            jax.ShapeDtypeStruct((main_rows, tile), F32),
            jax.ShapeDtypeStruct((edge_rows, tile), BF16),
            jax.ShapeDtypeStruct((edge_rows, tile), BF16),
        ),
        in_specs=[vmem] * (2 + len(mains) + len(sides)),
        out_specs=(vmem,) * 3,
        compiler_params=params,
    )(keep[own], arrived[own], *mains, *sides)
    other = move(other, "vel", 1)
    shape = jax.ShapeDtypeStruct((block, tile, tile), F32)
    likelihood, flux = pl.pallas_call(
        functools.partial(finish_kernel, tile, block),
        out_shape=(shape, shape),
        in_specs=[vmem] * 3,
        out_specs=(vmem, vmem),
        compiler_params=params,
    )(total, near, other)
    return likelihood[:, None], flux[:, None]


def solution(mesh):
    placed = (
        P(("epoch", "vel"), ("field", "sky"), None, None),
        P(("epoch", "vel"), ("field", "sky"), None, None),
        P(("epoch", "vel"), ("field", "sky")),
        P(("field", "epoch", "vel")),
        P(None, None, "epoch"),
    )
    return jax.shard_map(
        on_device,
        mesh=mesh,
        in_specs=placed,
        out_specs=(
            P(("epoch", "vel"), ("field", "sky"), None, None),
            P(("epoch", "vel"), ("field", "sky"), None, None),
        ),
        check_vma=False,
    )
```

```python
import functools

import jax
import jax.numpy as jnp
from jax import lax
from jax.experimental import pallas as pl
from jax.experimental.pallas import tpu as pltpu
from jax.sharding import PartitionSpec as P

VELS = 16
REACH = 12
PSFR = 7
GRID_X = 4

phi_floor = 0.25

F32 = jnp.float32
BF16 = jnp.bfloat16
EDGE = REACH + PSFR
PAD = 16
HALO = 32
SIDE = 48
HALF = 64
CHUNK = 4
STEP = 8


def iota(shape, axis):
    return lax.broadcasted_iota(jnp.int32, shape, axis)


def pick_edges(tile, first_left):
    row, lane = iota((2 * SIDE, tile), 0), iota((2 * SIDE, tile), 1)
    within = row % SIDE
    left = (row >= SIDE) != first_left
    wanted = jnp.where(
        within < EDGE,
        jnp.where(left, tile - EDGE, 0) + within,
        jnp.where(left, HALF - EDGE, HALF) + within - EDGE,
    )
    return jnp.where((within < 2 * EDGE) & (lane == wanted), 1.0, 0.0).astype(BF16)


def segment_table(motion, epochs, first):
    code = (motion[0] + REACH) * 32 + motion[1] + REACH
    total = code.shape[1]
    lane = iota(code.shape, 1)
    later = jnp.roll(code, -1, axis=1) if total < 128 else pltpu.roll(code, total - 1, 1)
    stop = first + epochs
    end = jnp.where((later != code) | (lane == stop - 1), lane + 1, total)
    reach = 1
    while reach < epochs:
        end = jnp.minimum(end, jnp.where(lane + reach < total, jnp.roll(end, -reach, axis=1), total))
        reach *= 2
    return jnp.clip(end - first, 0, epochs) * 1024 + code


def stack_slots(
    epochs, tile, block, n_epoch, n_vel, ranks,
    table_ref, maps_ref, sum_ref, send_ref, keep_ref,
):
    column = lax.axis_index("epoch")
    member = lax.axis_index("vel")
    lane = iota((8, tile), 1)
    turned = (lane + HALF) % tile
    first_slot, last_slot = (r * n_vel * block for r in ranks)
    slots = last_slot - first_slot
    first_k = (column + 1) * n_vel * block + first_slot

    def segment(slot, e):
        word = table_ref[lax.rem(first_k + slot, VELS), member * epochs + e]
        e_end = word >> 10
        start = PAD - REACH + ((word >> 5) & 31)
        dx = (word & 31) - REACH
        shift = jnp.where(dx > 0, tile - dx, -dx)
        out = (lane + dx < 0) | (lane + dx >= tile)
        out_turned = (turned + dx < 0) | (turned + dx >= tile)
        for r in range(0, tile, 8):
            window = pl.ds(start + r, 8)
            psi, phi, side = (
                pltpu.roll(maps_ref[e_end, m, window] - maps_ref[e, m, window], shift, 1)
                for m in range(3)
            )
            sum_ref[slot, 0, r : r + 8] += jnp.where(out, side, psi)
            sum_ref[slot, 1, r : r + 8] += jnp.where(out_turned, side, phi)
            sum_ref[slot, 2, r : r + 8] += jnp.where(out, psi, jnp.where(out_turned, phi, side))
        ended = e_end >= epochs
        return jnp.where(ended, jnp.minimum(slot + 1, slots), slot), jnp.where(ended, 0, e_end)

    def some_segments(state):
        for _ in range(STEP):
            state = segment(*state)
        return state

    start = (jnp.int32(0), jnp.int32(0))
    lax.while_loop(lambda state: state[0] < slots, some_segments, start)

    selector = pick_edges(tile, member == 1)
    mains = slots // n_vel * 2 * tile

    def write(group, carry):
        rank, whose = group // n_vel, lax.rem(group, n_vel)
        kept = whose == member
        for i in range(block):
            slot = group * block + i
            packed = lax.dot_general(
                selector, sum_ref[slot, 2].astype(BF16), (((1,), (1,)), ((), ())),
                preferred_element_type=F32,
            )
            rows = pl.ds(mains + slot * SIDE, SIDE)
            keep_ref[rows] = packed[:SIDE]
            send_ref[rows] = packed[SIDE:].astype(BF16)
            main = pl.ds((rank * block + i) * 2 * tile, 2 * tile)

            @pl.when(kept)
            def _():
                keep_ref[main] = sum_ref[slot, :2].reshape(2 * tile, tile)

            @pl.when(jnp.logical_not(kept))
            def _():
                send_ref[main] = sum_ref[slot, :2].reshape(2 * tile, tile).astype(BF16)

        return carry

    lax.fori_loop(0, slots // block, write, 0)


def clear_sums(sum_ref):
    def clear(slot, carry):
        sum_ref[slot] = jnp.zeros(sum_ref.shape[1:], F32)
        return carry

    lax.fori_loop(0, sum_ref.shape[0] - 1, clear, 0)


def stack_kernel(
    epochs, tile, block, n_epoch, n_vel, prepared,
    sigma_hbm, valid_hbm, motion_hbm, first_hbm, second_hbm,
    send_ref, keep_ref, maps_ref, coded_ref,
    sigma_ref, valid_ref, motion_ref, table_ref, first_ref, second_ref, sum_ref,
    small_sems, data_sems, table_sem,
):
    height = tile + 2 * PAD
    chunks = epochs // CHUNK
    member = lax.axis_index("vel")

    small = [
        pltpu.make_async_copy(motion_hbm, motion_ref, small_sems.at[0]),
        pltpu.make_async_copy(sigma_hbm, sigma_ref, small_sems.at[1]),
        pltpu.make_async_copy(valid_hbm, valid_ref, small_sems.at[2]),
    ]
    for copy in small:
        copy.start()

    def data_copy(c, i):
        at = pl.ds(c * CHUNK, CHUNK)
        source, target = ((first_hbm, first_ref), (second_hbm, second_ref))[i]
        return pltpu.make_async_copy(source.at[at], target.at[at], data_sems.at[2 * c + i])

    for c in range(chunks):
        for i in range(2):
            data_copy(c, i).start()

    row, lane = iota((tile, tile), 0), iota((tile, tile), 1)
    gap = jnp.abs(row - lane)
    ring = jnp.minimum(gap, tile - gap)
    outside = ring > PSFR
    far = gap >= tile // 2
    ring = ring.astype(F32)
    if prepared:
        depth = tile + 2 * HALO
        drop = jnp.abs(iota((height, depth), 1) - HALO - iota((height, depth), 0) + PAD)
        dropped = drop > PSFR
        drop = drop.astype(F32)

    maps_ref[0] = jnp.zeros(maps_ref.shape[1:], F32)
    clear_sums(sum_ref)
    for copy in small:
        copy.wait()
    coded_ref[...] = segment_table(motion_ref[...], epochs, member * epochs)
    table = pltpu.make_async_copy(coded_ref, table_ref, table_sem)
    table.start()

    def weights(e):
        def profile(distance, beyond):
            scaled = distance * (1.0 / jnp.full((1, distance.shape[1]), sigma_ref[e], F32))
            return jnp.where(beyond, 0.0, jnp.exp(-0.5 * (scaled * scaled)))

        turned = profile(ring, outside)
        scale = 1.0 / jnp.sum(turned[:8], axis=1, keepdims=True)[:1]
        turned = turned * scale
        bands = profile(drop, dropped) * scale if prepared else None
        result = []
        for m in range(2):
            value = turned if m == 0 else turned * turned
            inside = jnp.where(far, 0.0, value)
            beyond = jnp.where(far, value, 0.0)
            top, bottom = beyond[:PAD], beyond[tile - PAD :]
            if prepared:
                band = (bands if m == 0 else bands * bands).astype(BF16)
            else:
                band = jnp.concatenate([bottom, inside, top], axis=0).astype(BF16)
            if m == 1:
                inside, top, bottom = (pltpu.roll(v, HALF, 1) for v in (inside, top, bottom))
            blank = jnp.zeros((tile - 2 * PAD, tile), F32)
            outer = jnp.concatenate([top, blank, bottom], axis=0)
            result.append((band, inside.astype(BF16), outer.astype(BF16)))
        return result

    def correlate(e):
        if prepared:
            pair = first_ref[e], second_ref[e]
        else:
            inverse = valid_ref[e].astype(F32) / second_ref[e].astype(F32)
            pair = (first_ref[e].astype(F32) * inverse).astype(BF16), inverse.astype(BF16)
        built = weights(e)
        rows = [
            jnp.dot(built[m][0], pair[m], preferred_element_type=F32).astype(BF16) for m in range(2)
        ]
        return (
            jnp.dot(rows[0], built[0][1], preferred_element_type=F32),
            jnp.dot(rows[1], built[1][1], preferred_element_type=F32),
            jnp.dot(
                jnp.concatenate(rows, axis=1),
                jnp.concatenate([built[0][2], built[1][2]], axis=0),
                preferred_element_type=F32,
            ),
        )

    def correlate_chunk(c, carry):
        for i in range(2):
            data_copy(c, i).wait()
        made = [correlate(c * CHUNK + u) for u in range(CHUNK)]
        for i in range(3):
            total = maps_ref[c * CHUNK, i]
            for u in range(CHUNK):
                total = total + made[u][i]
                maps_ref[c * CHUNK + u + 1, i] = total
        return carry

    lax.fori_loop(0, chunks, correlate_chunk, 0)
    table.wait()
    stack_slots(
        epochs, tile, block, n_epoch, n_vel, (0, n_epoch - 1),
        table_ref, maps_ref, sum_ref, send_ref, keep_ref,
    )


def own_kernel(
    epochs, tile, block, n_epoch, n_vel,
    table_hbm, maps_ref, send_ref, keep_ref, table_ref, sum_ref, table_sem,
):
    table = pltpu.make_async_copy(table_hbm, table_ref, table_sem)
    table.start()
    clear_sums(sum_ref)
    table.wait()
    stack_slots(
        epochs, tile, block, n_epoch, n_vel, (n_epoch - 1, n_epoch),
        table_ref, maps_ref, sum_ref, send_ref, keep_ref,
    )


def add_kernel(n_mains, keep_ref, own_ref, *refs):
    arrived, (total_ref, near_ref, other_ref) = refs[:-3], refs[-3:]
    mains, sides = arrived[:n_mains], arrived[n_mains:]
    total = keep_ref[...] + own_ref[...].astype(F32)
    for main_ref in mains:
        total = total + main_ref[...].astype(F32)
    total_ref[...] = total
    side = sum(side_ref[...].astype(F32) for side_ref in sides)
    half = near_ref.shape[0]
    first = lax.axis_index("vel") == 0
    near_ref[...] = jnp.where(first, side[:half], side[half:]).astype(BF16)
    other_ref[...] = jnp.where(first, side[half:], side[:half]).astype(BF16)


def finish_kernel(tile, block, total_ref, near_ref, other_ref, like_ref, flux_ref):
    row, lane = iota((SIDE, tile), 0), iota((SIDE, tile), 1)
    member = lax.axis_index("vel")
    placed = []
    for m in range(2):
        at = row - m * EDGE
        used = (at >= 0) & (at < EDGE)
        for right in (1 - member, member):
            wanted = at + jnp.where(right == 1, 0, tile - EDGE) + m * HALF
            placed.append(jnp.where(used & (lane == wanted % tile), 1.0, 0.0).astype(BF16))
    for i in range(block):
        sums = []
        for m in range(2):
            rows = slice((2 * i + m) * tile, (2 * i + m + 1) * tile)
            total = total_ref[rows]
            for side_ref, put in zip((near_ref, other_ref), placed[2 * m : 2 * m + 2]):
                total = total + lax.dot_general(
                    side_ref[i * SIDE : (i + 1) * SIDE], put, (((0,), (0,)), ((), ())),
                    preferred_element_type=F32,
                )
            sums.append(total)
        root = lax.rsqrt(jnp.maximum(pltpu.roll(sums[1], HALF, 1), phi_floor))
        like = sums[0] * root
        like_ref[i] = like
        flux_ref[i] = like * root


def move(block, axis, distance):
    count = lax.axis_size(axis)
    return lax.ppermute(block, axis, [(i, (i + distance) % count) for i in range(count)])


def beside(block, step, keep):
    count = lax.axis_size("sky")
    device = [(q - GRID_X // 2) % count for q in range(count)]
    route = [(device[q], device[q + step]) for q in range(count) if keep(q)]
    return lax.ppermute(block, "sky", route)


def beside_by_member(block, distance):
    n_sky, n_epoch = lax.axis_size("sky"), lax.axis_size("epoch")
    device = [(q - GRID_X // 2) % n_sky for q in range(n_sky)]
    route = []
    for q in range(n_sky):
        for p in range(n_epoch):
            for v, step in ((0, 1), (1, -1)):
                if 0 <= q % GRID_X + step < GRID_X:
                    away = (p + distance) % n_epoch
                    route.append(
                        (
                            (device[q] * n_epoch + p) * 2 + v,
                            (device[q + step] * n_epoch + away) * 2 + v,
                        )
                    )
    return lax.ppermute(block, ("sky", "epoch", "vel"), route)


def on_device(images, variances, valid, psf_sigma, offsets):
    epochs, tile = images.shape[0], images.shape[-1]
    n_epoch, n_vel = lax.axis_size("epoch"), lax.axis_size("vel")
    n_sky = lax.axis_size("sky")
    assert n_vel == 2 and epochs % CHUNK == 0
    block = VELS // (n_epoch * n_vel)
    first, second = images[:, 0], variances[:, 0]
    prepared = n_sky > GRID_X
    if prepared:
        usable = valid[:, 0].astype(F32)[:, None, None]
        scaled = (first.astype(F32) / second.astype(F32) * usable).astype(BF16)
        inverse = (usable / second.astype(F32)).astype(BF16)
        pair = jnp.stack([scaled, inverse])
        above = beside(pair[:, :, tile - HALO :], GRID_X, lambda q: q + GRID_X < n_sky)
        below = beside(pair[:, :, :HALO], -GRID_X, lambda q: q >= GRID_X)
        first, second = jnp.concatenate([above, pair, below], axis=2)

    main_rows = block * 2 * tile
    edge_rows = block * SIDE
    hbm = pl.BlockSpec(memory_space=pltpu.HBM)
    vmem = pl.BlockSpec(memory_space=pltpu.VMEM)
    params = pltpu.CompilerParams(vmem_limit_bytes=32 * 1024 * 1024)
    group_rows = main_rows + n_vel * edge_rows
    operands = (psf_sigma, valid[:, 0], offsets, first, second)
    far_send, far_keep, maps, table = pl.pallas_call(
        functools.partial(stack_kernel, epochs, tile, block, n_epoch, n_vel, prepared),
        out_shape=(
            jax.ShapeDtypeStruct(((n_epoch - 1) * group_rows, tile), BF16),
            jax.ShapeDtypeStruct(((n_epoch - 1) * group_rows, tile), F32),
            jax.ShapeDtypeStruct((epochs + 1, 3, tile + 2 * PAD, tile), F32),
            jax.ShapeDtypeStruct(offsets.shape[1:], jnp.int32),
        ),
        in_specs=[hbm] * 5,
        out_specs=(vmem,) * 4,
        scratch_shapes=[
            pltpu.SMEM((epochs,), F32),
            pltpu.SMEM((epochs,), jnp.int32),
            pltpu.VMEM(offsets.shape, jnp.int32),
            pltpu.SMEM(offsets.shape[1:], jnp.int32),
            pltpu.VMEM(first.shape, BF16),
            pltpu.VMEM(second.shape, BF16),
            pltpu.VMEM(((n_epoch - 1) * n_vel * block + 1, 3, tile, tile), F32),
            pltpu.SemaphoreType.DMA((3,)),
            pltpu.SemaphoreType.DMA((2 * (epochs // CHUNK),)),
            pltpu.SemaphoreType.DMA,
        ],
        compiler_params=params,
    )(*(pltpu.with_memory_space_constraint(a, pltpu.HBM) for a in operands))
    far = (far_keep + move(far_send, "vel", 1).astype(F32)).astype(BF16)
    mains, sides = [], []
    far_edges = (n_epoch - 1) * main_rows
    for d in range(1, n_epoch):
        mains.append(move(far[(d - 1) * main_rows : d * main_rows], "epoch", d))
    for d in range(1, n_epoch):
        at = far_edges + (d - 1) * n_vel * edge_rows
        sides.append(beside_by_member(far[at : at + n_vel * edge_rows], d))

    send, keep = pl.pallas_call(
        functools.partial(own_kernel, epochs, tile, block, n_epoch, n_vel),
        out_shape=(
            jax.ShapeDtypeStruct((group_rows, tile), BF16),
            jax.ShapeDtypeStruct((group_rows, tile), F32),
        ),
        in_specs=[pl.BlockSpec(memory_space=pl.ANY), vmem],
        out_specs=(vmem,) * 2,
        scratch_shapes=[
            pltpu.SMEM(offsets.shape[1:], jnp.int32),
            pltpu.VMEM((n_vel * block + 1, 3, tile, tile), F32),
            pltpu.SemaphoreType.DMA,
        ],
        compiler_params=params,
    )(table, maps)
    arrived = move(send, "vel", 1)
    edges = (keep[main_rows:] + arrived[main_rows:].astype(F32)).astype(BF16)
    sides.append(beside_by_member(edges, 0))
    if not mains:
        mains.append(jnp.zeros((main_rows, tile), BF16))

    total, near, other = pl.pallas_call(
        functools.partial(add_kernel, len(mains)),
        out_shape=(
            jax.ShapeDtypeStruct((main_rows, tile), F32),
            jax.ShapeDtypeStruct((edge_rows, tile), BF16),
            jax.ShapeDtypeStruct((edge_rows, tile), BF16),
        ),
        in_specs=[vmem] * (2 + len(mains) + len(sides)),
        out_specs=(vmem,) * 3,
        compiler_params=params,
    )(keep[:main_rows], arrived[:main_rows], *mains, *sides)
    other = move(other, "vel", 1)
    shape = jax.ShapeDtypeStruct((block, tile, tile), F32)
    likelihood, flux = pl.pallas_call(
        functools.partial(finish_kernel, tile, block),
        out_shape=(shape, shape),
        in_specs=[vmem] * 3,
        out_specs=(vmem, vmem),
        compiler_params=params,
    )(total, near, other)
    return likelihood[:, None], flux[:, None]


def solution(mesh):
    placed = (
        P(("epoch", "vel"), ("field", "sky"), None, None),
        P(("epoch", "vel"), ("field", "sky"), None, None),
        P(("epoch", "vel"), ("field", "sky")),
        P(("field", "epoch", "vel")),
        P(None, None, "epoch"),
    )
    return jax.shard_map(
        on_device,
        mesh=mesh,
        in_specs=placed,
        out_specs=(
            P(("epoch", "vel"), ("field", "sky"), None, None),
            P(("epoch", "vel"), ("field", "sky"), None, None),
        ),
        check_vma=False,
    )
```

```python
import functools

import jax
import jax.numpy as jnp
from jax import lax
from jax.experimental import pallas as pl
from jax.experimental.pallas import tpu as pltpu
from jax.sharding import PartitionSpec as P

VELS = 16
REACH = 12
PSFR = 7
GRID_X = 4

phi_floor = 0.25

F32 = jnp.float32
BF16 = jnp.bfloat16
EDGE = REACH + PSFR
PAD = 16
HALO = 32
SIDE = 48
HALF = 64
CHUNK = 4
STEP = 8


def iota(shape, axis):
    return lax.broadcasted_iota(jnp.int32, shape, axis)


def pick_edges(tile, first_left):
    row, lane = iota((2 * SIDE, tile), 0), iota((2 * SIDE, tile), 1)
    within = row % SIDE
    left = (row >= SIDE) != first_left
    wanted = jnp.where(
        within < EDGE,
        jnp.where(left, tile - EDGE, 0) + within,
        jnp.where(left, HALF - EDGE, HALF) + within - EDGE,
    )
    return jnp.where((within < 2 * EDGE) & (lane == wanted), 1.0, 0.0).astype(BF16)


def segment_table(motion, epochs, first):
    code = (motion[0] + REACH) * 32 + motion[1] + REACH
    total = code.shape[1]
    lane = iota(code.shape, 1)
    later = jnp.roll(code, -1, axis=1) if total < 128 else pltpu.roll(code, total - 1, 1)
    stop = first + epochs
    end = jnp.where((later != code) | (lane == stop - 1), lane + 1, total)
    reach = 1
    while reach < epochs:
        end = jnp.minimum(end, jnp.where(lane + reach < total, jnp.roll(end, -reach, axis=1), total))
        reach *= 2
    return jnp.clip(end - first, 0, epochs) * 1024 + code


def stack_slots(
    epochs, tile, block, n_epoch, n_vel, ranks,
    table_ref, maps_ref, sum_ref, send_ref, keep_ref,
):
    column = lax.axis_index("epoch")
    member = lax.axis_index("vel")
    lane = iota((8, tile), 1)
    turned = (lane + HALF) % tile
    first_slot, last_slot = (r * n_vel * block for r in ranks)
    slots = last_slot - first_slot
    first_k = (column + 1) * n_vel * block + first_slot

    def segment(slot, e):
        word = table_ref[lax.rem(first_k + slot, VELS), member * epochs + e]
        e_end = word >> 10
        start = PAD - REACH + ((word >> 5) & 31)
        dx = (word & 31) - REACH
        shift = jnp.where(dx > 0, tile - dx, -dx)
        out = (lane + dx < 0) | (lane + dx >= tile)
        out_turned = (turned + dx < 0) | (turned + dx >= tile)
        for r in range(0, tile, 8):
            window = pl.ds(start + r, 8)
            psi, phi, side = (
                pltpu.roll(maps_ref[e_end, m, window] - maps_ref[e, m, window], shift, 1)
                for m in range(3)
            )
            sum_ref[slot, 0, r : r + 8] += jnp.where(out, side, psi)
            sum_ref[slot, 1, r : r + 8] += jnp.where(out_turned, side, phi)
            sum_ref[slot, 2, r : r + 8] += jnp.where(out, psi, jnp.where(out_turned, phi, side))
        ended = e_end >= epochs
        return jnp.where(ended, jnp.minimum(slot + 1, slots), slot), jnp.where(ended, 0, e_end)

    def some_segments(state):
        for _ in range(STEP):
            state = segment(*state)
        return state

    start = (jnp.int32(0), jnp.int32(0))
    lax.while_loop(lambda state: state[0] < slots, some_segments, start)

    selector = pick_edges(tile, member == 1)
    mains = slots // n_vel * 2 * tile

    def write(group, carry):
        rank, whose = group // n_vel, lax.rem(group, n_vel)
        kept = whose == member
        for i in range(block):
            slot = group * block + i
            packed = lax.dot_general(
                selector, sum_ref[slot, 2].astype(BF16), (((1,), (1,)), ((), ())),
                preferred_element_type=F32,
            )
            rows = pl.ds(mains + slot * SIDE, SIDE)
            keep_ref[rows] = packed[:SIDE]
            send_ref[rows] = packed[SIDE:].astype(BF16)
            main = pl.ds((rank * block + i) * 2 * tile, 2 * tile)

            @pl.when(kept)
            def _():
                keep_ref[main] = sum_ref[slot, :2].reshape(2 * tile, tile)

            @pl.when(jnp.logical_not(kept))
            def _():
                send_ref[main] = sum_ref[slot, :2].reshape(2 * tile, tile).astype(BF16)

        return carry

    lax.fori_loop(0, slots // block, write, 0)


def clear_sums(sum_ref):
    def clear(slot, carry):
        sum_ref[slot] = jnp.zeros(sum_ref.shape[1:], F32)
        return carry

    lax.fori_loop(0, sum_ref.shape[0] - 1, clear, 0)


def stack_kernel(
    epochs, tile, block, n_epoch, n_vel, prepared,
    sigma_hbm, valid_hbm, motion_hbm, first_hbm, second_hbm,
    send_ref, keep_ref, maps_ref, coded_ref,
    sigma_ref, valid_ref, motion_ref, table_ref, first_ref, second_ref, sum_ref,
    small_sems, data_sems, table_sem,
):
    height = tile + 2 * PAD
    chunks = epochs // CHUNK
    member = lax.axis_index("vel")

    small = [
        pltpu.make_async_copy(motion_hbm, motion_ref, small_sems.at[0]),
        pltpu.make_async_copy(sigma_hbm, sigma_ref, small_sems.at[1]),
        pltpu.make_async_copy(valid_hbm, valid_ref, small_sems.at[2]),
    ]
    for copy in small:
        copy.start()

    def data_copy(c, i):
        at = pl.ds(c * CHUNK, CHUNK)
        source, target = ((first_hbm, first_ref), (second_hbm, second_ref))[i]
        return pltpu.make_async_copy(source.at[at], target.at[at], data_sems.at[2 * c + i])

    for c in range(chunks):
        for i in range(2):
            data_copy(c, i).start()

    row, lane = iota((tile, tile), 0), iota((tile, tile), 1)
    gap = jnp.abs(row - lane)
    ring = jnp.minimum(gap, tile - gap)
    outside = ring > PSFR
    far = gap >= tile // 2
    ring = ring.astype(F32)
    if prepared:
        depth = tile + 2 * HALO
        drop = jnp.abs(iota((height, depth), 1) - HALO - iota((height, depth), 0) + PAD)
        dropped = drop > PSFR
        drop = drop.astype(F32)

    maps_ref[0] = jnp.zeros(maps_ref.shape[1:], F32)
    clear_sums(sum_ref)
    for copy in small:
        copy.wait()
    coded_ref[...] = segment_table(motion_ref[...], epochs, member * epochs)
    table = pltpu.make_async_copy(coded_ref, table_ref, table_sem)
    table.start()

    def weights(e):
        def profile(distance, beyond):
            scaled = distance * (1.0 / jnp.full((1, distance.shape[1]), sigma_ref[e], F32))
            return jnp.where(beyond, 0.0, jnp.exp(-0.5 * (scaled * scaled)))

        turned = profile(ring, outside)
        scale = 1.0 / jnp.sum(turned[:8], axis=1, keepdims=True)[:1]
        turned = turned * scale
        bands = profile(drop, dropped) * scale if prepared else None
        result = []
        for m in range(2):
            value = turned if m == 0 else turned * turned
            inside = jnp.where(far, 0.0, value)
            beyond = jnp.where(far, value, 0.0)
            top, bottom = beyond[:PAD], beyond[tile - PAD :]
            if prepared:
                band = (bands if m == 0 else bands * bands).astype(BF16)
            else:
                band = jnp.concatenate([bottom, inside, top], axis=0).astype(BF16)
            if m == 1:
                inside, top, bottom = (pltpu.roll(v, HALF, 1) for v in (inside, top, bottom))
            blank = jnp.zeros((tile - 2 * PAD, tile), F32)
            outer = jnp.concatenate([top, blank, bottom], axis=0)
            result.append((band, inside.astype(BF16), outer.astype(BF16)))
        return result

    def correlate(e):
        if prepared:
            pair = first_ref[e], second_ref[e]
        else:
            inverse = valid_ref[e].astype(F32) / second_ref[e].astype(F32)
            pair = (first_ref[e].astype(F32) * inverse).astype(BF16), inverse.astype(BF16)
        built = weights(e)
        rows = [
            jnp.dot(built[m][0], pair[m], preferred_element_type=F32).astype(BF16) for m in range(2)
        ]
        return (
            jnp.dot(rows[0], built[0][1], preferred_element_type=F32),
            jnp.dot(rows[1], built[1][1], preferred_element_type=F32),
            jnp.dot(
                jnp.concatenate(rows, axis=1),
                jnp.concatenate([built[0][2], built[1][2]], axis=0),
                preferred_element_type=F32,
            ),
        )

    def correlate_chunk(c, carry):
        for i in range(2):
            data_copy(c, i).wait()
        made = [correlate(c * CHUNK + u) for u in range(CHUNK)]
        for i in range(3):
            total = maps_ref[c * CHUNK, i]
            for u in range(CHUNK):
                total = total + made[u][i]
                maps_ref[c * CHUNK + u + 1, i] = total
        return carry

    lax.fori_loop(0, chunks, correlate_chunk, 0)
    table.wait()
    stack_slots(
        epochs, tile, block, n_epoch, n_vel, (0, n_epoch - 1),
        table_ref, maps_ref, sum_ref, send_ref, keep_ref,
    )


def own_kernel(
    epochs, tile, block, n_epoch, n_vel,
    table_hbm, maps_ref, send_ref, keep_ref, table_ref, sum_ref, table_sem,
):
    table = pltpu.make_async_copy(table_hbm, table_ref, table_sem)
    table.start()
    clear_sums(sum_ref)
    table.wait()
    stack_slots(
        epochs, tile, block, n_epoch, n_vel, (n_epoch - 1, n_epoch),
        table_ref, maps_ref, sum_ref, send_ref, keep_ref,
    )


def add_kernel(n_mains, keep_ref, own_ref, *refs):
    arrived, (total_ref, near_ref, other_ref) = refs[:-3], refs[-3:]
    mains, sides = arrived[:n_mains], arrived[n_mains:]
    total = keep_ref[...] + own_ref[...].astype(F32)
    for main_ref in mains:
        total = total + main_ref[...].astype(F32)
    total_ref[...] = total
    side = sum(side_ref[...].astype(F32) for side_ref in sides)
    half = near_ref.shape[0]
    first = lax.axis_index("vel") == 0
    near_ref[...] = jnp.where(first, side[:half], side[half:]).astype(BF16)
    other_ref[...] = jnp.where(first, side[half:], side[:half]).astype(BF16)


def finish_kernel(tile, block, total_ref, near_ref, other_ref, like_ref, flux_ref):
    row, lane = iota((SIDE, tile), 0), iota((SIDE, tile), 1)
    member = lax.axis_index("vel")
    placed = []
    for m in range(2):
        at = row - m * EDGE
        used = (at >= 0) & (at < EDGE)
        for right in (1 - member, member):
            wanted = at + jnp.where(right == 1, 0, tile - EDGE) + m * HALF
            placed.append(jnp.where(used & (lane == wanted % tile), 1.0, 0.0).astype(BF16))
    for i in range(block):
        sums = []
        for m in range(2):
            rows = slice((2 * i + m) * tile, (2 * i + m + 1) * tile)
            total = total_ref[rows]
            for side_ref, put in zip((near_ref, other_ref), placed[2 * m : 2 * m + 2]):
                total = total + lax.dot_general(
                    side_ref[i * SIDE : (i + 1) * SIDE], put, (((0,), (0,)), ((), ())),
                    preferred_element_type=F32,
                )
            sums.append(total)
        root = lax.rsqrt(jnp.maximum(pltpu.roll(sums[1], HALF, 1), phi_floor))
        like = sums[0] * root
        like_ref[i] = like
        flux_ref[i] = like * root


def move(block, axis, distance):
    count = lax.axis_size(axis)
    return lax.ppermute(block, axis, [(i, (i + distance) % count) for i in range(count)])


def beside(block, step, keep):
    count = lax.axis_size("sky")
    device = [(q - GRID_X // 2) % count for q in range(count)]
    route = [(device[q], device[q + step]) for q in range(count) if keep(q)]
    return lax.ppermute(block, "sky", route)


def beside_by_member(block, distance):
    n_sky, n_epoch = lax.axis_size("sky"), lax.axis_size("epoch")
    device = [(q - GRID_X // 2) % n_sky for q in range(n_sky)]
    route = []
    for q in range(n_sky):
        for p in range(n_epoch):
            for v, step in ((0, 1), (1, -1)):
                if 0 <= q % GRID_X + step < GRID_X:
                    away = (p + distance) % n_epoch
                    route.append(
                        (
                            (device[q] * n_epoch + p) * 2 + v,
                            (device[q + step] * n_epoch + away) * 2 + v,
                        )
                    )
    return lax.ppermute(block, ("sky", "epoch", "vel"), route)


def on_device(images, variances, valid, psf_sigma, offsets):
    epochs, tile = images.shape[0], images.shape[-1]
    n_epoch, n_vel = lax.axis_size("epoch"), lax.axis_size("vel")
    n_sky = lax.axis_size("sky")
    assert n_vel == 2 and epochs % CHUNK == 0
    block = VELS // (n_epoch * n_vel)
    first, second = images[:, 0], variances[:, 0]
    prepared = n_sky > GRID_X
    if prepared:
        usable = valid[:, 0].astype(F32)[:, None, None]
        scaled = (first.astype(F32) / second.astype(F32) * usable).astype(BF16)
        inverse = (usable / second.astype(F32)).astype(BF16)
        pair = jnp.stack([scaled, inverse])
        above = beside(pair[:, :, tile - HALO :], GRID_X, lambda q: q + GRID_X < n_sky)
        below = beside(pair[:, :, :HALO], -GRID_X, lambda q: q >= GRID_X)
        first, second = jnp.concatenate([above, pair, below], axis=2)

    main_rows = block * 2 * tile
    edge_rows = block * SIDE
    hbm = pl.BlockSpec(memory_space=pltpu.HBM)
    vmem = pl.BlockSpec(memory_space=pltpu.VMEM)
    params = pltpu.CompilerParams(vmem_limit_bytes=32 * 1024 * 1024)
    group_rows = main_rows + n_vel * edge_rows
    operands = (psf_sigma, valid[:, 0], offsets, first, second)
    far_send, far_keep, maps, table = pl.pallas_call(
        functools.partial(stack_kernel, epochs, tile, block, n_epoch, n_vel, prepared),
        out_shape=(
            jax.ShapeDtypeStruct(((n_epoch - 1) * group_rows, tile), BF16),
            jax.ShapeDtypeStruct(((n_epoch - 1) * group_rows, tile), F32),
            jax.ShapeDtypeStruct((epochs + 1, 3, tile + 2 * PAD, tile), F32),
            jax.ShapeDtypeStruct(offsets.shape[1:], jnp.int32),
        ),
        in_specs=[hbm] * 5,
        out_specs=(vmem,) * 4,
        scratch_shapes=[
            pltpu.SMEM((epochs,), F32),
            pltpu.SMEM((epochs,), jnp.int32),
            pltpu.VMEM(offsets.shape, jnp.int32),
            pltpu.SMEM(offsets.shape[1:], jnp.int32),
            pltpu.VMEM(first.shape, BF16),
            pltpu.VMEM(second.shape, BF16),
            pltpu.VMEM(((n_epoch - 1) * n_vel * block + 1, 3, tile, tile), F32),
            pltpu.SemaphoreType.DMA((3,)),
            pltpu.SemaphoreType.DMA((2 * (epochs // CHUNK),)),
            pltpu.SemaphoreType.DMA,
        ],
        compiler_params=params,
    )(*(pltpu.with_memory_space_constraint(a, pltpu.HBM) for a in operands))
    far = (far_keep + move(far_send, "vel", 1).astype(F32)).astype(BF16)
    mains, sides = [], []
    far_edges = (n_epoch - 1) * main_rows
    for d in range(1, n_epoch):
        mains.append(move(far[(d - 1) * main_rows : d * main_rows], "epoch", d))
    for d in range(1, n_epoch):
        at = far_edges + (d - 1) * n_vel * edge_rows
        sides.append(beside_by_member(far[at : at + n_vel * edge_rows], d))

    send, keep = pl.pallas_call(
        functools.partial(own_kernel, epochs, tile, block, n_epoch, n_vel),
        out_shape=(
            jax.ShapeDtypeStruct((group_rows, tile), BF16),
            jax.ShapeDtypeStruct((group_rows, tile), F32),
        ),
        in_specs=[pl.BlockSpec(memory_space=pl.ANY), vmem],
        out_specs=(vmem,) * 2,
        scratch_shapes=[
            pltpu.SMEM(offsets.shape[1:], jnp.int32),
            pltpu.VMEM((n_vel * block + 1, 3, tile, tile), F32),
            pltpu.SemaphoreType.DMA,
        ],
        compiler_params=params,
    )(table, maps)

    def exchange(send, keep_edges):
        arrived = move(send, "vel", 1)
        edges = (keep_edges + arrived[main_rows:].astype(F32)).astype(BF16)
        return arrived[:main_rows], beside_by_member(edges, 0)

    def blank(*_):
        return jnp.zeros((main_rows, tile), BF16), jnp.zeros((n_vel * edge_rows, tile), BF16)

    arrived, side = lax.cond(psf_sigma[0] > 0, exchange, blank, send, keep[main_rows:])
    sides.append(side)
    if not mains:
        mains.append(jnp.zeros((main_rows, tile), BF16))

    total, near, other = pl.pallas_call(
        functools.partial(add_kernel, len(mains)),
        out_shape=(
            jax.ShapeDtypeStruct((main_rows, tile), F32),
            jax.ShapeDtypeStruct((edge_rows, tile), BF16),
            jax.ShapeDtypeStruct((edge_rows, tile), BF16),
        ),
        in_specs=[vmem] * (2 + len(mains) + len(sides)),
        out_specs=(vmem,) * 3,
        compiler_params=params,
    )(keep[:main_rows], arrived, *mains, *sides)
    other = move(other, "vel", 1)
    shape = jax.ShapeDtypeStruct((block, tile, tile), F32)
    likelihood, flux = pl.pallas_call(
        functools.partial(finish_kernel, tile, block),
        out_shape=(shape, shape),
        in_specs=[vmem] * 3,
        out_specs=(vmem, vmem),
        compiler_params=params,
    )(total, near, other)
    return likelihood[:, None], flux[:, None]


def solution(mesh):
    placed = (
        P(("epoch", "vel"), ("field", "sky"), None, None),
        P(("epoch", "vel"), ("field", "sky"), None, None),
        P(("epoch", "vel"), ("field", "sky")),
        P(("field", "epoch", "vel")),
        P(None, None, "epoch"),
    )
    return jax.shard_map(
        on_device,
        mesh=mesh,
        in_specs=placed,
        out_specs=(
            P(("epoch", "vel"), ("field", "sky"), None, None),
            P(("epoch", "vel"), ("field", "sky"), None, None),
        ),
        check_vma=False,
    )
```

```python
import functools

import jax
import jax.numpy as jnp
from jax import lax
from jax.experimental import pallas as pl
from jax.experimental.pallas import tpu as pltpu
from jax.sharding import PartitionSpec as P

VELS = 16
REACH = 12
PSFR = 7
GRID_X = 4

phi_floor = 0.25

F32 = jnp.float32
BF16 = jnp.bfloat16
EDGE = REACH + PSFR
PAD = 16
HALO = 32
SIDE = 48
HALF = 64
CHUNK = 4
PIECES = (2, 1, 1)
STEP = 8


def iota(shape, axis):
    return lax.broadcasted_iota(jnp.int32, shape, axis)


def pick_edges(tile, first_left):
    row, lane = iota((2 * SIDE, tile), 0), iota((2 * SIDE, tile), 1)
    within = row % SIDE
    left = (row >= SIDE) != first_left
    wanted = jnp.where(
        within < EDGE,
        jnp.where(left, tile - EDGE, 0) + within,
        jnp.where(left, HALF - EDGE, HALF) + within - EDGE,
    )
    return jnp.where((within < 2 * EDGE) & (lane == wanted), 1.0, 0.0).astype(BF16)


def segment_table(motion, epochs, first):
    code = (motion[0] + REACH) * 32 + motion[1] + REACH
    total = code.shape[1]
    lane = iota(code.shape, 1)
    later = jnp.roll(code, -1, axis=1) if total < 128 else pltpu.roll(code, total - 1, 1)
    stop = first + epochs
    end = jnp.where((later != code) | (lane == stop - 1), lane + 1, total)
    reach = 1
    while reach < epochs:
        end = jnp.minimum(end, jnp.where(lane + reach < total, jnp.roll(end, -reach, axis=1), total))
        reach *= 2
    return jnp.clip(end - first, 0, epochs) * 1024 + code


def stack_kernel(
    epochs, tile, block, n_epoch, n_vel, prepared,
    sigma_hbm, valid_hbm, motion_hbm, first_hbm, second_hbm,
    send_ref, keep_ref, send_edge_ref, keep_edge_ref,
    sigma_ref, valid_ref, motion_ref, coded_ref, table_ref, first_ref, second_ref, maps_ref, sum_ref,
    small_sems, data_sems, table_sem,
):
    height = tile + 2 * PAD
    chunks = epochs // CHUNK
    column = lax.axis_index("epoch")
    member = lax.axis_index("vel")

    small = [
        pltpu.make_async_copy(motion_hbm, motion_ref, small_sems.at[0]),
        pltpu.make_async_copy(sigma_hbm, sigma_ref, small_sems.at[1]),
        pltpu.make_async_copy(valid_hbm, valid_ref, small_sems.at[2]),
    ]
    for copy in small:
        copy.start()

    def data_copy(c, i):
        at = pl.ds(c * CHUNK, CHUNK)
        source, target = ((first_hbm, first_ref), (second_hbm, second_ref))[i]
        return pltpu.make_async_copy(source.at[at], target.at[at], data_sems.at[2 * c + i])

    for c in range(chunks):
        for i in range(2):
            data_copy(c, i).start()

    row, lane = iota((tile, tile), 0), iota((tile, tile), 1)
    gap = jnp.abs(row - lane)
    ring = jnp.minimum(gap, tile - gap)
    outside = ring > PSFR
    far = gap >= tile // 2
    ring = ring.astype(F32)
    if prepared:
        depth = tile + 2 * HALO
        drop = jnp.abs(iota((height, depth), 1) - HALO - iota((height, depth), 0) + PAD)
        dropped = drop > PSFR
        drop = drop.astype(F32)

    maps_ref[0] = jnp.zeros(maps_ref.shape[1:], F32)

    def clear(slot, carry):
        sum_ref[slot] = jnp.zeros(sum_ref.shape[1:], F32)
        return carry

    lax.fori_loop(0, VELS, clear, 0)
    for copy in small:
        copy.wait()
    coded_ref[...] = segment_table(motion_ref[...], epochs, member * epochs)
    table = pltpu.make_async_copy(coded_ref, table_ref, table_sem)
    table.start()

    def weights(e):
        def profile(distance, beyond):
            scaled = distance * (1.0 / jnp.full((1, distance.shape[1]), sigma_ref[e], F32))
            return jnp.where(beyond, 0.0, jnp.exp(-0.5 * (scaled * scaled)))

        turned = profile(ring, outside)
        scale = 1.0 / jnp.sum(turned[:8], axis=1, keepdims=True)[:1]
        turned = turned * scale
        bands = profile(drop, dropped) * scale if prepared else None
        result = []
        for m in range(2):
            value = turned if m == 0 else turned * turned
            inside = jnp.where(far, 0.0, value)
            beyond = jnp.where(far, value, 0.0)
            top, bottom = beyond[:PAD], beyond[tile - PAD :]
            if prepared:
                band = (bands if m == 0 else bands * bands).astype(BF16)
            else:
                band = jnp.concatenate([bottom, inside, top], axis=0).astype(BF16)
            if m == 1:
                inside, top, bottom = (pltpu.roll(v, HALF, 1) for v in (inside, top, bottom))
            blank = jnp.zeros((tile - 2 * PAD, tile), F32)
            outer = jnp.concatenate([top, blank, bottom], axis=0)
            result.append((band, inside.astype(BF16), outer.astype(BF16)))
        return result

    def correlate(e):
        if prepared:
            pair = first_ref[e], second_ref[e]
        else:
            inverse = valid_ref[e].astype(F32) / second_ref[e].astype(F32)
            pair = (first_ref[e].astype(F32) * inverse).astype(BF16), inverse.astype(BF16)
        built = weights(e)
        rows = [
            jnp.dot(built[m][0], pair[m], preferred_element_type=F32).astype(BF16) for m in range(2)
        ]
        return (
            jnp.dot(rows[0], built[0][1], preferred_element_type=F32),
            jnp.dot(rows[1], built[1][1], preferred_element_type=F32),
            jnp.dot(
                jnp.concatenate(rows, axis=1),
                jnp.concatenate([built[0][2], built[1][2]], axis=0),
                preferred_element_type=F32,
            ),
        )

    def correlate_chunk(c, carry):
        for i in range(2):
            data_copy(c, i).wait()
        made = [correlate(c * CHUNK + u) for u in range(CHUNK)]
        for i in range(3):
            total = maps_ref[c * CHUNK, i]
            for u in range(CHUNK):
                total = total + made[u][i]
                maps_ref[c * CHUNK + u + 1, i] = total
        return carry

    lax.fori_loop(0, chunks, correlate_chunk, 0)
    table.wait()

    row8, lane8 = iota((8, tile), 0), iota((8, tile), 1)
    turned8 = (lane8 + HALF) % tile
    first_k = (column + 1) * n_vel * block

    def segment(slot, e):
        word = table_ref[lax.rem(first_k + slot, VELS), member * epochs + e]
        e_end = word >> 10
        start = PAD - REACH + ((word >> 5) & 31)
        dx = (word & 31) - REACH
        shift = jnp.where(dx > 0, tile - dx, -dx)
        base = pl.multiple_of((start // 8) * 8, 8)
        above = start - base
        turn = lax.rem(8 - above, 8)
        same = row8 < 8 - above
        out = (lane8 + dx < 0) | (lane8 + dx >= tile)
        out_turned = (turned8 + dx < 0) | (turned8 + dx >= tile)

        def rows_at(r):
            window = pl.ds(base + r, 8)
            return [
                pltpu.roll(maps_ref[e_end, m, window] - maps_ref[e, m, window], turn, 0)
                for m in range(3)
            ]

        upper = rows_at(0)
        for r in range(0, tile, 8):
            lower = rows_at(r + 8)
            psi, phi, side = (
                pltpu.roll(jnp.where(same, a, b), shift, 1) for a, b in zip(upper, lower)
            )
            upper = lower
            sum_ref[slot, 0, r : r + 8] += jnp.where(out, side, psi)
            sum_ref[slot, 1, r : r + 8] += jnp.where(out_turned, side, phi)
            sum_ref[slot, 2, r : r + 8] += jnp.where(out, psi, jnp.where(out_turned, phi, side))
        ended = e_end >= epochs
        return jnp.where(ended, jnp.minimum(slot + 1, VELS), slot), jnp.where(ended, 0, e_end)

    def some_segments(state):
        for _ in range(STEP):
            state = segment(*state)
        return state

    start = (jnp.int32(0), jnp.int32(0))
    lax.while_loop(lambda state: state[0] < VELS, some_segments, start)

    selector = pick_edges(tile, member == 1)
    def write(group, carry):
        rank, whose = group // n_vel, lax.rem(group, n_vel)
        kept = whose == member
        for i in range(block):
            slot = group * block + i
            packed = lax.dot_general(
                selector, sum_ref[slot, 2].astype(BF16), (((1,), (1,)), ((), ())),
                preferred_element_type=F32,
            )
            rows = pl.ds(slot * SIDE, SIDE)
            keep_edge_ref[rows] = packed[:SIDE]
            send_edge_ref[rows] = packed[SIDE:].astype(BF16)
            main = pl.ds((rank * block + i) * 2 * tile, 2 * tile)

            @pl.when(kept)
            def _():
                keep_ref[main] = sum_ref[slot, :2].reshape(2 * tile, tile)

            @pl.when(jnp.logical_not(kept))
            def _():
                send_ref[main] = sum_ref[slot, :2].reshape(2 * tile, tile).astype(BF16)

        return carry

    lax.fori_loop(0, n_epoch * n_vel, write, 0)


def add_kernel(n_parts, keep_ref, own_ref, *refs):
    arrived, (total_ref, near_ref, other_ref) = refs[:-3], refs[-3:]
    parts, sides = arrived[:n_parts], arrived[n_parts:]
    at = 0
    for i, quarters in enumerate(PIECES):
        size = quarters * (total_ref.shape[0] // sum(PIECES))
        rows = slice(at, at + size)
        total = keep_ref[rows] + own_ref[rows].astype(F32)
        for part_ref in parts[i :: len(PIECES)]:
            total = total + part_ref[...].astype(F32)
        total_ref[rows] = total
        at += size
    side = sum(side_ref[...].astype(F32) for side_ref in sides)
    half = near_ref.shape[0]
    first = lax.axis_index("vel") == 0
    near_ref[...] = jnp.where(first, side[:half], side[half:]).astype(BF16)
    other_ref[...] = jnp.where(first, side[half:], side[:half]).astype(BF16)


def finish_kernel(tile, block, total_ref, near_ref, other_ref, like_ref, flux_ref):
    row, lane = iota((SIDE, tile), 0), iota((SIDE, tile), 1)
    member = lax.axis_index("vel")
    placed = []
    for m in range(2):
        at = row - m * EDGE
        used = (at >= 0) & (at < EDGE)
        for right in (1 - member, member):
            wanted = at + jnp.where(right == 1, 0, tile - EDGE) + m * HALF
            placed.append(jnp.where(used & (lane == wanted % tile), 1.0, 0.0).astype(BF16))
    for i in range(block):
        sums = []
        for m in range(2):
            rows = slice((2 * i + m) * tile, (2 * i + m + 1) * tile)
            total = total_ref[rows]
            for side_ref, put in zip((near_ref, other_ref), placed[2 * m : 2 * m + 2]):
                total = total + lax.dot_general(
                    side_ref[i * SIDE : (i + 1) * SIDE], put, (((0,), (0,)), ((), ())),
                    preferred_element_type=F32,
                )
            sums.append(total)
        root = lax.rsqrt(jnp.maximum(pltpu.roll(sums[1], HALF, 1), phi_floor))
        like = sums[0] * root
        like_ref[i] = like
        flux_ref[i] = like * root


def move(block, axis, distance):
    count = lax.axis_size(axis)
    return lax.ppermute(block, axis, [(i, (i + distance) % count) for i in range(count)])


def beside(block, step, keep):
    count = lax.axis_size("sky")
    device = [(q - GRID_X // 2) % count for q in range(count)]
    route = [(device[q], device[q + step]) for q in range(count) if keep(q)]
    return lax.ppermute(block, "sky", route)


def beside_by_member(block, distance):
    n_sky, n_epoch = lax.axis_size("sky"), lax.axis_size("epoch")
    device = [(q - GRID_X // 2) % n_sky for q in range(n_sky)]
    route = []
    for q in range(n_sky):
        for p in range(n_epoch):
            for v, step in ((0, 1), (1, -1)):
                if 0 <= q % GRID_X + step < GRID_X:
                    away = (p + distance) % n_epoch
                    route.append(
                        (
                            (device[q] * n_epoch + p) * 2 + v,
                            (device[q + step] * n_epoch + away) * 2 + v,
                        )
                    )
    return lax.ppermute(block, ("sky", "epoch", "vel"), route)


def on_device(images, variances, valid, psf_sigma, offsets):
    epochs, tile = images.shape[0], images.shape[-1]
    n_epoch, n_vel = lax.axis_size("epoch"), lax.axis_size("vel")
    n_sky = lax.axis_size("sky")
    assert n_vel == 2 and epochs % CHUNK == 0
    block = VELS // (n_epoch * n_vel)
    first, second = images[:, 0], variances[:, 0]
    prepared = n_sky > GRID_X
    if prepared:
        usable = valid[:, 0].astype(F32)[:, None, None]
        scaled = (first.astype(F32) / second.astype(F32) * usable).astype(BF16)
        inverse = (usable / second.astype(F32)).astype(BF16)
        pair = jnp.stack([scaled, inverse])
        above = beside(pair[:, :, tile - HALO :], GRID_X, lambda q: q + GRID_X < n_sky)
        below = beside(pair[:, :, :HALO], -GRID_X, lambda q: q >= GRID_X)
        first, second = jnp.concatenate([above, pair, below], axis=2)

    main_rows = block * 2 * tile
    edge_rows = block * SIDE
    hbm = pl.BlockSpec(memory_space=pltpu.HBM)
    vmem = pl.BlockSpec(memory_space=pltpu.VMEM)
    params = pltpu.CompilerParams(vmem_limit_bytes=32 * 1024 * 1024)
    mains_end = n_epoch * main_rows
    group_rows = n_vel * edge_rows
    operands = (psf_sigma, valid[:, 0], offsets, first, second)
    send, keep, send_edges, keep_edges = pl.pallas_call(
        functools.partial(stack_kernel, epochs, tile, block, n_epoch, n_vel, prepared),
        out_shape=(
            jax.ShapeDtypeStruct((mains_end, tile), BF16),
            jax.ShapeDtypeStruct((mains_end, tile), F32),
            jax.ShapeDtypeStruct((n_epoch * group_rows, tile), BF16),
            jax.ShapeDtypeStruct((n_epoch * group_rows, tile), F32),
        ),
        in_specs=[hbm] * 5,
        out_specs=(vmem,) * 4,
        scratch_shapes=[
            pltpu.SMEM((epochs,), F32),
            pltpu.SMEM((epochs,), jnp.int32),
            pltpu.VMEM(offsets.shape, jnp.int32),
            pltpu.VMEM(offsets.shape[1:], jnp.int32),
            pltpu.SMEM(offsets.shape[1:], jnp.int32),
            pltpu.VMEM(first.shape, BF16),
            pltpu.VMEM(second.shape, BF16),
            pltpu.VMEM((epochs + 1, 3, tile + 2 * PAD, tile), F32),
            pltpu.VMEM((VELS + 1, 3, tile, tile), F32),
            pltpu.SemaphoreType.DMA((3,)),
            pltpu.SemaphoreType.DMA((2 * (epochs // CHUNK),)),
            pltpu.SemaphoreType.DMA,
        ],
        compiler_params=params,
    )(*(pltpu.with_memory_space_constraint(a, pltpu.HBM) for a in operands))

    edges = (keep_edges + move(send_edges, "vel", 1).astype(F32)).astype(BF16)
    sides = []
    for d in range(1, n_epoch + 1):
        at = (d - 1) * group_rows
        sides.append(beside_by_member(edges[at : at + group_rows], d % n_epoch))

    arrived = move(send, "vel", 1)
    own = mains_end - main_rows
    far = (keep[:own] + arrived[:own].astype(F32)).astype(BF16)
    quarter = main_rows // sum(PIECES)
    parts = []
    for d in range(1, n_epoch):
        at = (d - 1) * main_rows
        for quarters in PIECES:
            parts.append(move(far[at : at + quarters * quarter], "epoch", d))
            at += quarters * quarter

    total, near, other = pl.pallas_call(
        functools.partial(add_kernel, len(parts)),
        out_shape=(
            jax.ShapeDtypeStruct((main_rows, tile), F32),
            jax.ShapeDtypeStruct((edge_rows, tile), BF16),
            jax.ShapeDtypeStruct((edge_rows, tile), BF16),
        ),
        in_specs=[vmem] * (2 + len(parts) + len(sides)),
        out_specs=(vmem,) * 3,
        compiler_params=params,
    )(keep[own:], arrived[own:], *parts, *sides)
    other = move(other, "vel", 1)
    shape = jax.ShapeDtypeStruct((block, tile, tile), F32)
    likelihood, flux = pl.pallas_call(
        functools.partial(finish_kernel, tile, block),
        out_shape=(shape, shape),
        in_specs=[vmem] * 3,
        out_specs=(vmem, vmem),
        compiler_params=params,
    )(total, near, other)
    return likelihood[:, None], flux[:, None]


def solution(mesh):
    placed = (
        P(("epoch", "vel"), ("field", "sky"), None, None),
        P(("epoch", "vel"), ("field", "sky"), None, None),
        P(("epoch", "vel"), ("field", "sky")),
        P(("field", "epoch", "vel")),
        P(None, None, "epoch"),
    )
    return jax.shard_map(
        on_device,
        mesh=mesh,
        in_specs=placed,
        out_specs=(
            P(("epoch", "vel"), ("field", "sky"), None, None),
            P(("epoch", "vel"), ("field", "sky"), None, None),
        ),
        check_vma=False,
    )
```

```python
import functools

import jax
import jax.numpy as jnp
from jax import lax
from jax.experimental import pallas as pl
from jax.experimental.pallas import tpu as pltpu
from jax.sharding import PartitionSpec as P

VELS = 16
REACH = 12
PSFR = 7
GRID_X = 4

phi_floor = 0.25

F32 = jnp.float32
BF16 = jnp.bfloat16
EDGE = REACH + PSFR
PAD = 16
HALO = 32
SIDE = 48
HALF = 64
CHUNK = 4
TAKEN = 1 << 24
STEP = 8


def iota(shape, axis):
    return lax.broadcasted_iota(jnp.int32, shape, axis)


def pick_edges(tile, first_left):
    row, lane = iota((2 * SIDE, tile), 0), iota((2 * SIDE, tile), 1)
    within = row % SIDE
    left = (row >= SIDE) != first_left
    wanted = jnp.where(
        within < EDGE,
        jnp.where(left, tile - EDGE, 0) + within,
        jnp.where(left, HALF - EDGE, HALF) + within - EDGE,
    )
    return jnp.where((within < 2 * EDGE) & (lane == wanted), 1.0, 0.0).astype(BF16)


def segment_table(motion, epochs, first):
    code = (motion[0] + REACH) * 32 + motion[1] + REACH
    total = code.shape[1]
    lane = iota(code.shape, 1)
    later = jnp.roll(code, -1, axis=1) if total < 128 else pltpu.roll(code, total - 1, 1)
    stop = first + epochs
    end = jnp.where((later != code) | (lane == stop - 1), lane + 1, total)
    reach = 1
    while reach < epochs:
        end = jnp.minimum(end, jnp.where(lane + reach < total, jnp.roll(end, -reach, axis=1), total))
        reach *= 2
    return TAKEN + jnp.clip(end - first, 0, epochs) * 1024 + code


def stack_slots(
    epochs, tile, block, n_epoch, n_vel, ranks,
    table_ref, maps_ref, sum_ref, send_ref, keep_ref,
):
    column = lax.axis_index("epoch")
    member = lax.axis_index("vel")
    row, lane = iota((8, tile), 0), iota((8, tile), 1)
    turned = (lane + HALF) % tile
    first_slot, last_slot = (r * n_vel * block for r in ranks)
    slots = last_slot - first_slot
    first_k = (column + 1) * n_vel * block + first_slot

    def segment(slot, e):
        word = table_ref[lax.rem(first_k + slot, VELS), member * epochs + e]
        e_end = (word & (TAKEN - 1)) >> 10
        start = PAD - REACH + ((word >> 5) & 31)
        dx = (word & 31) - REACH
        shift = jnp.where(dx > 0, tile - dx, -dx)
        base = pl.multiple_of((start // 8) * 8, 8)
        above = start - base
        turn = lax.rem(8 - above, 8)
        same = row < 8 - above
        out = (lane + dx < 0) | (lane + dx >= tile)
        out_turned = (turned + dx < 0) | (turned + dx >= tile)

        def rows_at(r):
            window = pl.ds(base + r, 8)
            return [
                pltpu.roll(maps_ref[e_end, m, window] - maps_ref[e, m, window], turn, 0)
                for m in range(3)
            ]

        upper = rows_at(0)
        for r in range(0, tile, 8):
            lower = rows_at(r + 8)
            psi, phi, side = (
                pltpu.roll(jnp.where(same, a, b), shift, 1) for a, b in zip(upper, lower)
            )
            upper = lower
            sum_ref[slot, 0, r : r + 8] += jnp.where(out, side, psi)
            sum_ref[slot, 1, r : r + 8] += jnp.where(out_turned, side, phi)
            sum_ref[slot, 2, r : r + 8] += jnp.where(out, psi, jnp.where(out_turned, phi, side))
        ended = e_end >= epochs
        return jnp.where(ended, jnp.minimum(slot + 1, slots), slot), jnp.where(ended, 0, e_end)

    def some_segments(state):
        for _ in range(STEP):
            state = segment(*state)
        return state

    start = (jnp.int32(0), jnp.int32(0))
    lax.while_loop(lambda state: state[0] < slots, some_segments, start)

    selector = pick_edges(tile, member == 1)
    main_rows = block * 2 * tile
    rank_rows = main_rows + n_vel * block * SIDE

    def write(group, carry):
        rank, whose = group // n_vel, lax.rem(group, n_vel)
        kept = whose == member
        for i in range(block):
            slot = group * block + i
            packed = lax.dot_general(
                selector, sum_ref[slot, 2].astype(BF16), (((1,), (1,)), ((), ())),
                preferred_element_type=F32,
            )
            rows = pl.ds(rank * rank_rows + main_rows + (whose * block + i) * SIDE, SIDE)
            keep_ref[rows] = packed[:SIDE]
            send_ref[rows] = packed[SIDE:].astype(BF16)
            main = pl.ds(rank * rank_rows + i * 2 * tile, 2 * tile)

            @pl.when(kept)
            def _():
                keep_ref[main] = sum_ref[slot, :2].reshape(2 * tile, tile)

            @pl.when(jnp.logical_not(kept))
            def _():
                send_ref[main] = sum_ref[slot, :2].reshape(2 * tile, tile).astype(BF16)

        return carry

    lax.fori_loop(0, slots // block, write, 0)


def clear_sums(sum_ref):
    def clear(slot, carry):
        sum_ref[slot] = jnp.zeros(sum_ref.shape[1:], F32)
        return carry

    lax.fori_loop(0, sum_ref.shape[0] - 1, clear, 0)


def stack_kernel(
    epochs, tile, block, n_epoch, n_vel, prepared,
    sigma_hbm, valid_hbm, motion_hbm, first_hbm, second_hbm,
    send_ref, keep_ref, maps_ref, coded_ref,
    sigma_ref, valid_ref, motion_ref, table_ref, first_ref, second_ref, sum_ref,
    small_sems, data_sems, table_sem,
):
    height = tile + 2 * PAD
    chunks = epochs // CHUNK
    member = lax.axis_index("vel")

    small = [
        pltpu.make_async_copy(motion_hbm, motion_ref, small_sems.at[0]),
        pltpu.make_async_copy(sigma_hbm, sigma_ref, small_sems.at[1]),
        pltpu.make_async_copy(valid_hbm, valid_ref, small_sems.at[2]),
    ]
    for copy in small:
        copy.start()

    def data_copy(c, i):
        at = pl.ds(c * CHUNK, CHUNK)
        source, target = ((first_hbm, first_ref), (second_hbm, second_ref))[i]
        return pltpu.make_async_copy(source.at[at], target.at[at], data_sems.at[2 * c + i])

    for c in range(chunks):
        for i in range(2):
            data_copy(c, i).start()

    row, lane = iota((tile, tile), 0), iota((tile, tile), 1)
    gap = jnp.abs(row - lane)
    ring = jnp.minimum(gap, tile - gap)
    outside = ring > PSFR
    far = gap >= tile // 2
    ring = ring.astype(F32)
    if prepared:
        depth = tile + 2 * HALO
        drop = jnp.abs(iota((height, depth), 1) - HALO - iota((height, depth), 0) + PAD)
        dropped = drop > PSFR
        drop = drop.astype(F32)

    maps_ref[0] = jnp.zeros(maps_ref.shape[1:], F32)
    clear_sums(sum_ref)
    for copy in small:
        copy.wait()
    coded_ref[...] = segment_table(motion_ref[...], epochs, member * epochs)
    table = pltpu.make_async_copy(coded_ref, table_ref, table_sem)
    table.start()

    def weights(e):
        def profile(distance, beyond):
            scaled = distance * (1.0 / jnp.full((1, distance.shape[1]), sigma_ref[e], F32))
            return jnp.where(beyond, 0.0, jnp.exp(-0.5 * (scaled * scaled)))

        turned = profile(ring, outside)
        scale = 1.0 / jnp.sum(turned[:8], axis=1, keepdims=True)[:1]
        turned = turned * scale
        bands = profile(drop, dropped) * scale if prepared else None
        result = []
        for m in range(2):
            value = turned if m == 0 else turned * turned
            inside = jnp.where(far, 0.0, value)
            beyond = jnp.where(far, value, 0.0)
            top, bottom = beyond[:PAD], beyond[tile - PAD :]
            if prepared:
                band = (bands if m == 0 else bands * bands).astype(BF16)
            else:
                band = jnp.concatenate([bottom, inside, top], axis=0).astype(BF16)
            if m == 1:
                inside, top, bottom = (pltpu.roll(v, HALF, 1) for v in (inside, top, bottom))
            blank = jnp.zeros((tile - 2 * PAD, tile), F32)
            outer = jnp.concatenate([top, blank, bottom], axis=0)
            result.append((band, inside.astype(BF16), outer.astype(BF16)))
        return result

    def correlate(e):
        if prepared:
            pair = first_ref[e], second_ref[e]
        else:
            inverse = valid_ref[e].astype(F32) / second_ref[e].astype(F32)
            pair = (first_ref[e].astype(F32) * inverse).astype(BF16), inverse.astype(BF16)
        built = weights(e)
        rows = [
            jnp.dot(built[m][0], pair[m], preferred_element_type=F32).astype(BF16) for m in range(2)
        ]
        return (
            jnp.dot(rows[0], built[0][1], preferred_element_type=F32),
            jnp.dot(rows[1], built[1][1], preferred_element_type=F32),
            jnp.dot(
                jnp.concatenate(rows, axis=1),
                jnp.concatenate([built[0][2], built[1][2]], axis=0),
                preferred_element_type=F32,
            ),
        )

    def correlate_chunk(c, carry):
        for i in range(2):
            data_copy(c, i).wait()
        made = [correlate(c * CHUNK + u) for u in range(CHUNK)]
        for i in range(3):
            total = maps_ref[c * CHUNK, i]
            for u in range(CHUNK):
                total = total + made[u][i]
                maps_ref[c * CHUNK + u + 1, i] = total
        return carry

    lax.fori_loop(0, chunks, correlate_chunk, 0)
    table.wait()
    stack_slots(
        epochs, tile, block, n_epoch, n_vel, (0, n_epoch - 1),
        table_ref, maps_ref, sum_ref, send_ref, keep_ref,
    )


def own_kernel(
    epochs, tile, block, n_epoch, n_vel,
    table_hbm, maps_ref, send_ref, keep_ref, table_ref, sum_ref, table_sem,
):
    table = pltpu.make_async_copy(table_hbm, table_ref, table_sem)
    table.start()
    clear_sums(sum_ref)
    table.wait()
    stack_slots(
        epochs, tile, block, n_epoch, n_vel, (n_epoch - 1, n_epoch),
        table_ref, maps_ref, sum_ref, send_ref, keep_ref,
    )


def finish_kernel(tile, block, keep_ref, own_ref, near_ref, other_ref, *refs):
    mains, (like_ref, flux_ref) = refs[:-2], refs[-2:]
    row, lane = iota((SIDE, tile), 0), iota((SIDE, tile), 1)
    member = lax.axis_index("vel")
    placed = []
    for m in range(2):
        at = row - m * EDGE
        used = (at >= 0) & (at < EDGE)
        for right in (1 - member, member):
            wanted = at + jnp.where(right == 1, 0, tile - EDGE) + m * HALF
            placed.append(jnp.where(used & (lane == wanted % tile), 1.0, 0.0).astype(BF16))
    for i in range(block):
        sums = []
        for m in range(2):
            rows = slice((2 * i + m) * tile, (2 * i + m + 1) * tile)
            total = keep_ref[rows] + own_ref[rows].astype(F32)
            for main_ref in mains:
                total = total + main_ref[rows].astype(F32)
            for side_ref, put in zip((near_ref, other_ref), placed[2 * m : 2 * m + 2]):
                total = total + lax.dot_general(
                    side_ref[i * SIDE : (i + 1) * SIDE], put, (((0,), (0,)), ((), ())),
                    preferred_element_type=F32,
                )
            sums.append(total)
        root = lax.rsqrt(jnp.maximum(pltpu.roll(sums[1], HALF, 1), phi_floor))
        like = sums[0] * root
        like_ref[i] = like
        flux_ref[i] = like * root


def move(block, axis, distance):
    count = lax.axis_size(axis)
    return lax.ppermute(block, axis, [(i, (i + distance) % count) for i in range(count)])


def beside(block, step, keep):
    count = lax.axis_size("sky")
    device = [(q - GRID_X // 2) % count for q in range(count)]
    route = [(device[q], device[q + step]) for q in range(count) if keep(q)]
    return lax.ppermute(block, "sky", route)


def beside_by_member(block, distance):
    n_sky, n_epoch = lax.axis_size("sky"), lax.axis_size("epoch")
    device = [(q - GRID_X // 2) % n_sky for q in range(n_sky)]
    route = []
    for q in range(n_sky):
        for p in range(n_epoch):
            for v, step in ((0, 1), (1, -1)):
                if 0 <= q % GRID_X + step < GRID_X:
                    away = (p + distance) % n_epoch
                    route.append(
                        (
                            (device[q] * n_epoch + p) * 2 + v,
                            (device[q + step] * n_epoch + away) * 2 + v,
                        )
                    )
    return lax.ppermute(block, ("sky", "epoch", "vel"), route)


def on_device(images, variances, valid, psf_sigma, offsets):
    epochs, tile = images.shape[0], images.shape[-1]
    n_epoch, n_vel = lax.axis_size("epoch"), lax.axis_size("vel")
    n_sky = lax.axis_size("sky")
    assert n_vel == 2 and epochs % CHUNK == 0
    block = VELS // (n_epoch * n_vel)
    first, second = images[:, 0], variances[:, 0]
    prepared = n_sky > GRID_X
    if prepared:
        usable = valid[:, 0].astype(F32)[:, None, None]
        scaled = (first.astype(F32) / second.astype(F32) * usable).astype(BF16)
        inverse = (usable / second.astype(F32)).astype(BF16)
        pair = jnp.stack([scaled, inverse])
        above = beside(pair[:, :, tile - HALO :], GRID_X, lambda q: q + GRID_X < n_sky)
        below = beside(pair[:, :, :HALO], -GRID_X, lambda q: q >= GRID_X)
        first, second = jnp.concatenate([above, pair, below], axis=2)

    main_rows = block * 2 * tile
    edge_rows = block * SIDE
    hbm = pl.BlockSpec(memory_space=pltpu.HBM)
    vmem = pl.BlockSpec(memory_space=pltpu.VMEM)
    params = pltpu.CompilerParams(vmem_limit_bytes=32 * 1024 * 1024)
    group_rows = main_rows + n_vel * edge_rows
    operands = (psf_sigma, valid[:, 0], offsets, first, second)
    far_send, far_keep, maps, table = pl.pallas_call(
        functools.partial(stack_kernel, epochs, tile, block, n_epoch, n_vel, prepared),
        out_shape=(
            jax.ShapeDtypeStruct(((n_epoch - 1) * group_rows, tile), BF16),
            jax.ShapeDtypeStruct(((n_epoch - 1) * group_rows, tile), F32),
            jax.ShapeDtypeStruct((epochs + 1, 3, tile + 2 * PAD, tile), F32),
            jax.ShapeDtypeStruct(offsets.shape[1:], jnp.int32),
        ),
        in_specs=[hbm] * 5,
        out_specs=(vmem,) * 4,
        scratch_shapes=[
            pltpu.SMEM((epochs,), F32),
            pltpu.SMEM((epochs,), jnp.int32),
            pltpu.VMEM(offsets.shape, jnp.int32),
            pltpu.SMEM(offsets.shape[1:], jnp.int32),
            pltpu.VMEM(first.shape, BF16),
            pltpu.VMEM(second.shape, BF16),
            pltpu.VMEM(((n_epoch - 1) * n_vel * block + 1, 3, tile, tile), F32),
            pltpu.SemaphoreType.DMA((3,)),
            pltpu.SemaphoreType.DMA((2 * (epochs // CHUNK),)),
            pltpu.SemaphoreType.DMA,
        ],
        compiler_params=params,
    )(*(pltpu.with_memory_space_constraint(a, pltpu.HBM) for a in operands))
    far = (far_keep + move(far_send, "vel", 1).astype(F32)).astype(BF16)
    beyond = [
        move(far[(d - 1) * group_rows : d * group_rows], "epoch", d) for d in range(1, n_epoch)
    ]

    send, keep = pl.pallas_call(
        functools.partial(own_kernel, epochs, tile, block, n_epoch, n_vel),
        out_shape=(
            jax.ShapeDtypeStruct((group_rows, tile), BF16),
            jax.ShapeDtypeStruct((group_rows, tile), F32),
        ),
        in_specs=[pl.BlockSpec(memory_space=pl.ANY), vmem],
        out_specs=(vmem,) * 2,
        scratch_shapes=[
            pltpu.SMEM(offsets.shape[1:], jnp.int32),
            pltpu.VMEM((n_vel * block + 1, 3, tile, tile), F32),
            pltpu.SemaphoreType.DMA,
        ],
        compiler_params=params,
    )(table, maps)

    def exchange(send, keep):
        arrived = move(send, "vel", 1)
        return arrived[:main_rows], keep[main_rows:] + arrived[main_rows:].astype(F32)

    def nothing(send, keep):
        return send[:main_rows], keep[main_rows:]

    arrived, edges = lax.cond(table[0, 0] >= TAKEN, exchange, nothing, send, keep)
    for block_sums in beyond:
        edges = edges + block_sums[main_rows:].astype(F32)
    edges = beside_by_member(edges.astype(BF16), 0)
    first = lax.axis_index("vel") == 0
    near = jnp.where(first, edges[:edge_rows], edges[edge_rows:])
    other = jnp.where(first, edges[edge_rows:], edges[:edge_rows])
    other = move(other, "vel", 1)
    mains = [block_sums[:main_rows] for block_sums in beyond]

    shape = jax.ShapeDtypeStruct((block, tile, tile), F32)
    likelihood, flux = pl.pallas_call(
        functools.partial(finish_kernel, tile, block),
        out_shape=(shape, shape),
        in_specs=[vmem] * (4 + len(mains)),
        out_specs=(vmem, vmem),
        compiler_params=params,
    )(keep[:main_rows], arrived, near, other, *mains)
    return likelihood[:, None], flux[:, None]


def solution(mesh):
    placed = (
        P(("epoch", "vel"), ("field", "sky"), None, None),
        P(("epoch", "vel"), ("field", "sky"), None, None),
        P(("epoch", "vel"), ("field", "sky")),
        P(("field", "epoch", "vel")),
        P(None, None, "epoch"),
    )
    return jax.shard_map(
        on_device,
        mesh=mesh,
        in_specs=placed,
        out_specs=(
            P(("epoch", "vel"), ("field", "sky"), None, None),
            P(("epoch", "vel"), ("field", "sky"), None, None),
        ),
        check_vma=False,
    )
```

```python
import functools

import jax
import jax.numpy as jnp
from jax import lax
from jax.experimental import pallas as pl
from jax.experimental.pallas import tpu as pltpu
from jax.sharding import PartitionSpec as P

VELS = 16
REACH = 12
PSFR = 7
GRID_X = 4

phi_floor = 0.25

F32 = jnp.float32
BF16 = jnp.bfloat16
EDGE = REACH + PSFR
PAD = 16
HALO = 32
SIDE = 48
HALF = 64
SPAN = 32
CHUNK = 4
STEP = 8


def iota(shape, axis):
    return lax.broadcasted_iota(jnp.int32, shape, axis)


def pick_edges(tile, first_left):
    row, lane = iota((2 * SIDE, tile), 0), iota((2 * SIDE, tile), 1)
    within = row % SIDE
    left = (row >= SIDE) != first_left
    wanted = within % EDGE + jnp.where(left, 0, SPAN + REACH) + jnp.where(within < EDGE, 0, HALF)
    return jnp.where((within < 2 * EDGE) & (lane == wanted), 1.0, 0.0).astype(BF16)


def segment_table(motion, epochs, first):
    code = (motion[0] + REACH) * 32 + motion[1] + REACH
    total = code.shape[1]
    lane = iota(code.shape, 1)
    later = jnp.roll(code, -1, axis=1) if total < 128 else pltpu.roll(code, total - 1, 1)
    stop = first + epochs
    end = jnp.where((later != code) | (lane == stop - 1), lane + 1, total)
    reach = 1
    while reach < epochs:
        end = jnp.minimum(end, jnp.where(lane + reach < total, jnp.roll(end, -reach, axis=1), total))
        reach *= 2
    return jnp.clip(end - first, 0, epochs) * 1024 + code


def over_segments(epochs, table_ref, maps_ref, chosen, slots, first_k, add):
    member = lax.axis_index("vel")
    row = iota((8, maps_ref.shape[-1]), 0)

    def segment(slot, e):
        word = table_ref[lax.rem(first_k + slot, VELS), member * epochs + e]
        e_end = word >> 10
        start = PAD - REACH + ((word >> 5) & 31)
        dx = (word & 31) - REACH
        tile = maps_ref.shape[-1]
        shift = jnp.where(dx > 0, tile - dx, -dx)
        base = pl.multiple_of((start // 8) * 8, 8)
        above = start - base
        turn = lax.rem(8 - above, 8)
        same = row < 8 - above
        put = add(slot, dx)

        def rows_at(r):
            window = pl.ds(base + r, 8)
            return [
                pltpu.roll(maps_ref[e_end, m, window] - maps_ref[e, m, window], turn, 0)
                for m in chosen
            ]

        upper = rows_at(0)
        for r in range(0, tile, 8):
            lower = rows_at(r + 8)
            put(r, [pltpu.roll(jnp.where(same, a, b), shift, 1) for a, b in zip(upper, lower)])
            upper = lower
        ended = e_end >= epochs
        return jnp.where(ended, jnp.minimum(slot + 1, slots), slot), jnp.where(ended, 0, e_end)

    def some_segments(state):
        for _ in range(STEP):
            state = segment(*state)
        return state

    start = (jnp.int32(0), jnp.int32(0))
    lax.while_loop(lambda state: state[0] < slots, some_segments, start)


def clear_sums(sum_ref):
    def clear(slot, carry):
        sum_ref[slot] = jnp.zeros(sum_ref.shape[1:], F32)
        return carry

    lax.fori_loop(0, sum_ref.shape[0] - 1, clear, 0)


def stack_edges(
    epochs, tile, block, n_epoch, n_vel, table_ref, maps_ref, sum_ref, send_ref, keep_ref
):
    column = lax.axis_index("epoch")
    member = lax.axis_index("vel")
    lane = iota((8, tile), 1)
    place = lane % SPAN - jnp.where(lane // SPAN % 2 == 0, REACH, 0)

    def add(slot, dx):
        held = (place + dx >= 0) & (place + dx < EDGE)

        def put(r, pieces):
            sum_ref[slot, r : r + 8] += jnp.where(held, pieces[0], 0.0)

        return put

    first_k = (column + 1) * n_vel * block
    over_segments(epochs, table_ref, maps_ref, (3,), VELS, first_k, add)

    selector = pick_edges(tile, member == 1)

    def pack(group, carry):
        for i in range(block):
            slot = group * block + i
            packed = lax.dot_general(
                selector, sum_ref[slot].astype(BF16), (((1,), (1,)), ((), ())),
                preferred_element_type=F32,
            )
            rows = pl.ds(slot * SIDE, SIDE)
            keep_ref[rows] = packed[:SIDE]
            send_ref[rows] = packed[SIDE:].astype(BF16)
        return carry

    lax.fori_loop(0, VELS // block, pack, 0)


def main_kernel(
    epochs, tile, block, n_epoch, n_vel, ranks,
    table_hbm, maps_ref, send_ref, keep_ref, table_ref, sum_ref, table_sem,
):
    table = pltpu.make_async_copy(table_hbm, table_ref, table_sem)
    table.start()
    clear_sums(sum_ref)
    column = lax.axis_index("epoch")
    member = lax.axis_index("vel")
    lane = iota((8, tile), 1)
    turned = (lane + HALF) % tile
    first_slot, last_slot = (r * n_vel * block for r in ranks)
    slots = last_slot - first_slot

    def add(slot, dx):
        out = (lane + dx < 0) | (lane + dx >= tile)
        out_turned = (turned + dx < 0) | (turned + dx >= tile)

        def put(r, pieces):
            psi, phi, side = pieces
            sum_ref[slot, 0, r : r + 8] += jnp.where(out, side, psi)
            sum_ref[slot, 1, r : r + 8] += jnp.where(out_turned, side, phi)

        return put

    table.wait()
    first_k = (column + 1) * n_vel * block + first_slot
    over_segments(epochs, table_ref, maps_ref, (0, 1, 2), slots, first_k, add)

    def write(j, carry):
        rank, i = j // block, lax.rem(j, block)
        kept = (rank * n_vel + member) * block + i
        sent = (rank * n_vel + 1 - member) * block + i
        rows = pl.ds(j * 2 * tile, 2 * tile)
        keep_ref[rows] = sum_ref[kept].reshape(2 * tile, tile)
        send_ref[rows] = sum_ref[sent].reshape(2 * tile, tile).astype(BF16)
        return carry

    lax.fori_loop(0, slots // n_vel, write, 0)


def stack_kernel(
    epochs, tile, block, n_epoch, n_vel, prepared,
    sigma_hbm, valid_hbm, motion_hbm, first_hbm, second_hbm,
    send_ref, keep_ref, maps_ref, coded_ref,
    sigma_ref, valid_ref, motion_ref, table_ref, first_ref, second_ref, sum_ref,
    small_sems, data_sems, table_sem,
):
    height = tile + 2 * PAD
    chunks = epochs // CHUNK
    member = lax.axis_index("vel")

    small = [
        pltpu.make_async_copy(motion_hbm, motion_ref, small_sems.at[0]),
        pltpu.make_async_copy(sigma_hbm, sigma_ref, small_sems.at[1]),
        pltpu.make_async_copy(valid_hbm, valid_ref, small_sems.at[2]),
    ]
    for copy in small:
        copy.start()

    def data_copy(c, i):
        at = pl.ds(c * CHUNK, CHUNK)
        source, target = ((first_hbm, first_ref), (second_hbm, second_ref))[i]
        return pltpu.make_async_copy(source.at[at], target.at[at], data_sems.at[2 * c + i])

    for c in range(chunks):
        for i in range(2):
            data_copy(c, i).start()

    row, lane = iota((tile, tile), 0), iota((tile, tile), 1)
    gap = jnp.abs(row - lane)
    ring = jnp.minimum(gap, tile - gap)
    outside = ring > PSFR
    far = gap >= tile // 2
    ring = ring.astype(F32)

    def edge_distance(first_row):
        at, ln = iota((SPAN, tile), 0) + first_row, iota((SPAN, tile), 1)
        left, place = ln // SPAN % 2 == 0, ln % SPAN
        source = place + jnp.where(left, -EDGE, tile - REACH)
        place = place - jnp.where(left, REACH, 0)
        away = jnp.abs(at - source)
        return away.astype(F32), (away > PSFR) | (place < 0) | (place >= EDGE)

    edge_gaps = [edge_distance(0), edge_distance(tile - SPAN)]
    of_psi = iota((SPAN, tile), 1) < HALF
    if prepared:
        depth = tile + 2 * HALO
        drop = jnp.abs(iota((height, depth), 1) - HALO - iota((height, depth), 0) + PAD)
        dropped = drop > PSFR
        drop = drop.astype(F32)

    maps_ref[0] = jnp.zeros(maps_ref.shape[1:], F32)
    clear_sums(sum_ref)
    for copy in small:
        copy.wait()
    coded_ref[...] = segment_table(motion_ref[...], epochs, member * epochs)
    table = pltpu.make_async_copy(coded_ref, table_ref, table_sem)
    table.start()

    def weights(e):
        def profile(distance, beyond):
            scaled = distance * (1.0 / jnp.full((1, distance.shape[1]), sigma_ref[e], F32))
            return jnp.where(beyond, 0.0, jnp.exp(-0.5 * (scaled * scaled)))

        turned = profile(ring, outside)
        scale = 1.0 / jnp.sum(turned[:8], axis=1, keepdims=True)[:1]
        turned = turned * scale
        bands = profile(drop, dropped) * scale if prepared else None
        ends = [profile(*gap) * scale for gap in edge_gaps]
        result = []
        blank = jnp.zeros((tile - 2 * PAD, tile), F32)
        for m in range(2):
            value = turned if m == 0 else turned * turned
            inside = jnp.where(far, 0.0, value)
            beyond = jnp.where(far, value, 0.0)
            top, bottom = beyond[:PAD], beyond[tile - PAD :]
            if prepared:
                band = (bands if m == 0 else bands * bands).astype(BF16)
            else:
                band = jnp.concatenate([bottom, inside, top], axis=0).astype(BF16)
            if m == 1:
                inside, top, bottom = (pltpu.roll(v, HALF, 1) for v in (inside, top, bottom))
            outer = jnp.concatenate([top, blank, bottom], axis=0)
            if m == 0:
                first, last = (jnp.where(of_psi, end, 0.0) for end in ends)
            else:
                first, last = (jnp.where(of_psi, 0.0, end * end) for end in ends)
            gap_rows = jnp.zeros((tile - 2 * SPAN, tile), F32)
            edge = jnp.concatenate([first, gap_rows, last], axis=0)
            result.append((band, *(v.astype(BF16) for v in (inside, outer, edge))))
        return result

    def correlate(e):
        if prepared:
            pair = first_ref[e], second_ref[e]
        else:
            inverse = valid_ref[e].astype(F32) / second_ref[e].astype(F32)
            pair = (first_ref[e].astype(F32) * inverse).astype(BF16), inverse.astype(BF16)
        (band, inside, outer, edge), (band2, inside2, outer2, edge2) = weights(e)

        def apart(a, b):
            wide = [jnp.concatenate([a, jnp.zeros_like(a)], axis=1)]
            wide.append(jnp.concatenate([jnp.zeros_like(b), b], axis=1))
            return jnp.concatenate(wide, axis=0)

        rows = jnp.dot(
            jnp.concatenate([band, band2], axis=1), apart(*pair), preferred_element_type=F32
        ).astype(BF16)
        maps = jnp.dot(rows, apart(inside, inside2), preferred_element_type=F32)
        sides = jnp.dot(
            rows,
            jnp.concatenate(
                [
                    jnp.concatenate([outer, edge], axis=1),
                    jnp.concatenate([outer2, edge2], axis=1),
                ],
                axis=0,
            ),
            preferred_element_type=F32,
        )
        return maps[:, :tile], maps[:, tile:], sides[:, :tile], sides[:, tile:]

    def correlate_chunk(c, carry):
        for i in range(2):
            data_copy(c, i).wait()
        made = [correlate(c * CHUNK + u) for u in range(CHUNK)]
        for i in range(4):
            total = maps_ref[c * CHUNK, i]
            for u in range(CHUNK):
                total = total + made[u][i]
                maps_ref[c * CHUNK + u + 1, i] = total
        return carry

    lax.fori_loop(0, chunks, correlate_chunk, 0)
    table.wait()
    stack_edges(
        epochs, tile, block, n_epoch, n_vel, table_ref, maps_ref, sum_ref, send_ref, keep_ref
    )


def finish_kernel(tile, block, keep_ref, own_ref, both_ref, *refs):
    mains, (like_ref, flux_ref) = refs[:-2], refs[-2:]
    row, lane = iota((SIDE, tile), 0), iota((SIDE, tile), 1)
    member = lax.axis_index("vel")
    placed = []
    for m in range(2):
        at = row - m * EDGE
        used = (at >= 0) & (at < EDGE)
        for right in (1 - member, member):
            wanted = at + jnp.where(right == 1, 0, tile - EDGE) + m * HALF
            placed.append(jnp.where(used & (lane == wanted % tile), 1.0, 0.0).astype(BF16))
    for i in range(block):
        sums = []
        for m in range(2):
            rows = slice((2 * i + m) * tile, (2 * i + m + 1) * tile)
            total = keep_ref[rows] + own_ref[rows].astype(F32)
            for main_ref in mains:
                total = total + main_ref[rows].astype(F32)
            for near, put in enumerate(placed[2 * m : 2 * m + 2]):
                at = (near * block + i) * SIDE
                total = total + lax.dot_general(
                    both_ref[at : at + SIDE], put, (((0,), (0,)), ((), ())),
                    preferred_element_type=F32,
                )
            sums.append(total)
        root = lax.rsqrt(jnp.maximum(pltpu.roll(sums[1], HALF, 1), phi_floor))
        like = sums[0] * root
        like_ref[i] = like
        flux_ref[i] = like * root


def move(block, axis, distance):
    count = lax.axis_size(axis)
    return lax.ppermute(block, axis, [(i, (i + distance) % count) for i in range(count)])


def beside(block, step, keep):
    count = lax.axis_size("sky")
    device = [(q - GRID_X // 2) % count for q in range(count)]
    route = [(device[q], device[q + step]) for q in range(count) if keep(q)]
    return lax.ppermute(block, "sky", route)


def beside_by_member(block, distance):
    n_sky, n_epoch = lax.axis_size("sky"), lax.axis_size("epoch")
    device = [(q - GRID_X // 2) % n_sky for q in range(n_sky)]
    route = []
    for q in range(n_sky):
        for p in range(n_epoch):
            for v, step in ((0, 1), (1, -1)):
                if 0 <= q % GRID_X + step < GRID_X:
                    away = (p + distance) % n_epoch
                    route.append(
                        (
                            (device[q] * n_epoch + p) * 2 + v,
                            (device[q + step] * n_epoch + away) * 2 + v,
                        )
                    )
    return lax.ppermute(block, ("sky", "epoch", "vel"), route)


def on_device(images, variances, valid, psf_sigma, offsets):
    epochs, tile = images.shape[0], images.shape[-1]
    n_epoch, n_vel = lax.axis_size("epoch"), lax.axis_size("vel")
    n_sky = lax.axis_size("sky")
    assert n_vel == 2 and epochs % CHUNK == 0
    block = VELS // (n_epoch * n_vel)
    first, second = images[:, 0], variances[:, 0]
    prepared = n_sky > GRID_X
    if prepared:
        usable = valid[:, 0].astype(F32)[:, None, None]
        scaled = (first.astype(F32) / second.astype(F32) * usable).astype(BF16)
        inverse = (usable / second.astype(F32)).astype(BF16)
        pair = jnp.stack([scaled, inverse])
        above = beside(pair[:, :, tile - HALO :], GRID_X, lambda q: q + GRID_X < n_sky)
        below = beside(pair[:, :, :HALO], -GRID_X, lambda q: q >= GRID_X)
        first, second = jnp.concatenate([above, pair, below], axis=2)

    main_rows = block * 2 * tile
    edge_rows = block * SIDE
    hbm = pl.BlockSpec(memory_space=pltpu.HBM)
    vmem = pl.BlockSpec(memory_space=pltpu.VMEM)
    params = pltpu.CompilerParams(vmem_limit_bytes=32 * 1024 * 1024)
    group_rows = n_vel * edge_rows
    operands = (psf_sigma, valid[:, 0], offsets, first, second)
    send_edges, keep_edges, maps, table = pl.pallas_call(
        functools.partial(stack_kernel, epochs, tile, block, n_epoch, n_vel, prepared),
        out_shape=(
            jax.ShapeDtypeStruct((n_epoch * group_rows, tile), BF16),
            jax.ShapeDtypeStruct((n_epoch * group_rows, tile), F32),
            jax.ShapeDtypeStruct((epochs + 1, 4, tile + 2 * PAD, tile), F32),
            jax.ShapeDtypeStruct(offsets.shape[1:], jnp.int32),
        ),
        in_specs=[hbm] * 5,
        out_specs=(vmem,) * 4,
        scratch_shapes=[
            pltpu.SMEM((epochs,), F32),
            pltpu.SMEM((epochs,), jnp.int32),
            pltpu.VMEM(offsets.shape, jnp.int32),
            pltpu.SMEM(offsets.shape[1:], jnp.int32),
            pltpu.VMEM(first.shape, BF16),
            pltpu.VMEM(second.shape, BF16),
            pltpu.VMEM((VELS + 1, tile, tile), F32),
            pltpu.SemaphoreType.DMA((3,)),
            pltpu.SemaphoreType.DMA((2 * (epochs // CHUNK),)),
            pltpu.SemaphoreType.DMA,
        ],
        compiler_params=params,
    )(*(pltpu.with_memory_space_constraint(a, pltpu.HBM) for a in operands))
    edges = (keep_edges + move(send_edges, "vel", 1).astype(F32)).astype(BF16)
    sides = []
    for d in range(1, n_epoch + 1):
        at = (d - 1) * group_rows
        sides.append(beside_by_member(edges[at : at + group_rows], d % n_epoch))

    def main_sums(ranks):
        rows = (ranks[1] - ranks[0]) * main_rows
        slots = (ranks[1] - ranks[0]) * n_vel * block
        return pl.pallas_call(
            functools.partial(main_kernel, epochs, tile, block, n_epoch, n_vel, ranks),
            out_shape=(
                jax.ShapeDtypeStruct((rows, tile), BF16),
                jax.ShapeDtypeStruct((rows, tile), F32),
            ),
            in_specs=[pl.BlockSpec(memory_space=pl.ANY), vmem],
            out_specs=(vmem,) * 2,
            scratch_shapes=[
                pltpu.SMEM(offsets.shape[1:], jnp.int32),
                pltpu.VMEM((slots + 1, 2, tile, tile), F32),
                pltpu.SemaphoreType.DMA,
            ],
            compiler_params=params,
        )(table, maps)

    taken = lax.axis_index("sky") < n_sky

    def pass_far(send, keep):
        return (keep + move(send, "vel", 1).astype(F32)).astype(BF16)

    far = lax.cond(taken, pass_far, lambda send, keep: send, *main_sums((0, n_epoch - 1)))
    mains = [
        move(far[(d - 1) * main_rows : d * main_rows], "epoch", d) for d in range(1, n_epoch)
    ]

    def pass_own(send, *sides):
        arrived = move(send, "vel", 1)
        side = sum(s.astype(F32) for s in sides).astype(BF16)
        is_first = lax.axis_index("vel") == 0
        near = jnp.where(is_first, side[:edge_rows], side[edge_rows:])
        other = jnp.where(is_first, side[edge_rows:], side[:edge_rows])
        return arrived, jnp.concatenate([near, move(other, "vel", 1)])

    def pass_nothing(send, *sides):
        return send, sides[0]

    send, keep = main_sums((n_epoch - 1, n_epoch))
    arrived, side = lax.cond(taken, pass_own, pass_nothing, send, *sides)

    shape = jax.ShapeDtypeStruct((block, tile, tile), F32)
    likelihood, flux = pl.pallas_call(
        functools.partial(finish_kernel, tile, block),
        out_shape=(shape, shape),
        in_specs=[vmem] * (3 + len(mains)),
        out_specs=(vmem, vmem),
        compiler_params=params,
    )(keep, arrived, side, *mains)
    return likelihood[:, None], flux[:, None]


def solution(mesh):
    placed = (
        P(("epoch", "vel"), ("field", "sky"), None, None),
        P(("epoch", "vel"), ("field", "sky"), None, None),
        P(("epoch", "vel"), ("field", "sky")),
        P(("field", "epoch", "vel")),
        P(None, None, "epoch"),
    )
    return jax.shard_map(
        on_device,
        mesh=mesh,
        in_specs=placed,
        out_specs=(
            P(("epoch", "vel"), ("field", "sky"), None, None),
            P(("epoch", "vel"), ("field", "sky"), None, None),
        ),
        check_vma=False,
    )
```

```python
import functools

import jax
import jax.numpy as jnp
from jax import lax
from jax.experimental import pallas as pl
from jax.experimental.pallas import tpu as pltpu
from jax.sharding import PartitionSpec as P

VELS = 16
REACH = 12
PSFR = 7
GRID_X = 4

phi_floor = 0.25

F32 = jnp.float32
BF16 = jnp.bfloat16
EDGE = REACH + PSFR
PAD = 16
HALO = 32
SIDE = 48
HALF = 64
SPAN = 32
CHUNK = 4
STEP = 8


def iota(shape, axis):
    return lax.broadcasted_iota(jnp.int32, shape, axis)


def pick_edges(tile, first_left):
    row, lane = iota((2 * SIDE, tile), 0), iota((2 * SIDE, tile), 1)
    within = row % SIDE
    left = (row >= SIDE) != first_left
    wanted = within % EDGE + jnp.where(left, 0, SPAN + REACH) + jnp.where(within < EDGE, 0, HALF)
    return jnp.where((within < 2 * EDGE) & (lane == wanted), 1.0, 0.0).astype(BF16)


def segment_table(motion, epochs, first):
    code = (motion[0] + REACH) * 32 + motion[1] + REACH
    total = code.shape[1]
    lane = iota(code.shape, 1)
    later = jnp.roll(code, -1, axis=1) if total < 128 else pltpu.roll(code, total - 1, 1)
    stop = first + epochs
    end = jnp.where((later != code) | (lane == stop - 1), lane + 1, total)
    reach = 1
    while reach < epochs:
        end = jnp.minimum(end, jnp.where(lane + reach < total, jnp.roll(end, -reach, axis=1), total))
        reach *= 2
    return jnp.clip(end - first, 0, epochs) * 1024 + code


def over_segments(epochs, table_ref, maps_ref, chosen, slots, first_k, add):
    member = lax.axis_index("vel")
    row = iota((8, maps_ref.shape[-1]), 0)

    def segment(slot, e):
        word = table_ref[lax.rem(first_k + slot, VELS), member * epochs + e]
        e_end = word >> 10
        start = PAD - REACH + ((word >> 5) & 31)
        dx = (word & 31) - REACH
        tile = maps_ref.shape[-1]
        shift = jnp.where(dx > 0, tile - dx, -dx)
        base = pl.multiple_of((start // 8) * 8, 8)
        above = start - base
        turn = lax.rem(8 - above, 8)
        same = row < 8 - above
        put = add(slot, dx)

        def rows_at(r):
            window = pl.ds(base + r, 8)
            return [
                pltpu.roll(maps_ref[e_end, m, window] - maps_ref[e, m, window], turn, 0)
                for m in chosen
            ]

        upper = rows_at(0)
        for r in range(0, tile, 8):
            lower = rows_at(r + 8)
            put(r, [pltpu.roll(jnp.where(same, a, b), shift, 1) for a, b in zip(upper, lower)])
            upper = lower
        ended = e_end >= epochs
        return jnp.where(ended, jnp.minimum(slot + 1, slots), slot), jnp.where(ended, 0, e_end)

    def some_segments(state):
        for _ in range(STEP):
            state = segment(*state)
        return state

    start = (jnp.int32(0), jnp.int32(0))
    lax.while_loop(lambda state: state[0] < slots, some_segments, start)


def clear_sums(sum_ref):
    def clear(slot, carry):
        sum_ref[slot] = jnp.zeros(sum_ref.shape[1:], F32)
        return carry

    lax.fori_loop(0, sum_ref.shape[0] - 1, clear, 0)


def stack_edges(
    epochs, tile, block, n_epoch, n_vel, table_ref, maps_ref, sum_ref, send_ref, keep_ref
):
    column = lax.axis_index("epoch")
    member = lax.axis_index("vel")
    lane = iota((8, tile), 1)
    place = lane % SPAN - jnp.where(lane // SPAN % 2 == 0, REACH, 0)

    def add(slot, dx):
        held = (place + dx >= 0) & (place + dx < EDGE)

        def put(r, pieces):
            sum_ref[slot, r : r + 8] += jnp.where(held, pieces[0], 0.0)

        return put

    first_k = (column + 1) * n_vel * block
    over_segments(epochs, table_ref, maps_ref, (0,), VELS, first_k, add)

    selector = pick_edges(tile, member == 1)

    def pack(group, carry):
        for i in range(block):
            slot = group * block + i
            packed = lax.dot_general(
                selector, sum_ref[slot].astype(BF16), (((1,), (1,)), ((), ())),
                preferred_element_type=F32,
            )
            rows = pl.ds(slot * SIDE, SIDE)
            keep_ref[rows] = packed[:SIDE]
            send_ref[rows] = packed[SIDE:].astype(BF16)
        return carry

    lax.fori_loop(0, VELS // block, pack, 0)


def main_kernel(
    epochs, tile, block, n_epoch, n_vel, ranks,
    table_ref, maps_ref, send_ref, keep_ref, sum_ref,
):
    clear_sums(sum_ref)
    column = lax.axis_index("epoch")
    member = lax.axis_index("vel")
    lane = iota((8, tile), 1)
    turned = (lane + HALF) % tile
    first_slot, last_slot = (r * n_vel * block for r in ranks)
    slots = last_slot - first_slot

    def add(slot, dx):
        out = (lane + dx < 0) | (lane + dx >= tile)
        out_turned = (turned + dx < 0) | (turned + dx >= tile)

        def put(r, pieces):
            psi, phi, side = pieces
            sum_ref[slot, 0, r : r + 8] += jnp.where(out, side, psi)
            sum_ref[slot, 1, r : r + 8] += jnp.where(out_turned, side, phi)

        return put

    first_k = (column + 1) * n_vel * block + first_slot
    over_segments(epochs, table_ref, maps_ref, (0, 1, 2), slots, first_k, add)

    def write(j, carry):
        rank, i = j // block, lax.rem(j, block)
        kept = (rank * n_vel + member) * block + i
        sent = (rank * n_vel + 1 - member) * block + i
        rows = pl.ds(j * 2 * tile, 2 * tile)
        keep_ref[rows] = sum_ref[kept].reshape(2 * tile, tile)
        send_ref[rows] = sum_ref[sent].reshape(2 * tile, tile).astype(BF16)
        return carry

    lax.fori_loop(0, slots // n_vel, write, 0)


def stack_kernel(
    epochs, tile, block, n_epoch, n_vel, prepared,
    sigma_hbm, valid_hbm, motion_hbm, first_hbm, second_hbm,
    send_ref, keep_ref, maps_ref, coded_ref,
    sigma_ref, valid_ref, motion_ref, table_ref, first_ref, second_ref, edges_ref, sum_ref,
    small_sems, data_sems, table_sem,
):
    height = tile + 2 * PAD
    chunks = epochs // CHUNK
    member = lax.axis_index("vel")

    small = [
        pltpu.make_async_copy(motion_hbm, motion_ref, small_sems.at[0]),
        pltpu.make_async_copy(sigma_hbm, sigma_ref, small_sems.at[1]),
        pltpu.make_async_copy(valid_hbm, valid_ref, small_sems.at[2]),
    ]
    for copy in small:
        copy.start()

    def data_copy(c, i):
        at = pl.ds(c * CHUNK, CHUNK)
        source, target = ((first_hbm, first_ref), (second_hbm, second_ref))[i]
        return pltpu.make_async_copy(source.at[at], target.at[at], data_sems.at[2 * c + i])

    for c in range(chunks):
        for i in range(2):
            data_copy(c, i).start()

    row, lane = iota((tile, tile), 0), iota((tile, tile), 1)
    gap = jnp.abs(row - lane)
    ring = jnp.minimum(gap, tile - gap)
    outside = ring > PSFR
    far = gap >= tile // 2
    ring = ring.astype(F32)

    def edge_distance(first_row):
        at, ln = iota((SPAN, tile), 0) + first_row, iota((SPAN, tile), 1)
        left, place = ln // SPAN % 2 == 0, ln % SPAN
        source = place + jnp.where(left, -EDGE, tile - REACH)
        place = place - jnp.where(left, REACH, 0)
        away = jnp.abs(at - source)
        return away.astype(F32), (away > PSFR) | (place < 0) | (place >= EDGE)

    edge_gaps = [edge_distance(0), edge_distance(tile - SPAN)]
    of_psi = iota((SPAN, tile), 1) < HALF
    if prepared:
        depth = tile + 2 * HALO
        drop = jnp.abs(iota((height, depth), 1) - HALO - iota((height, depth), 0) + PAD)
        dropped = drop > PSFR
        drop = drop.astype(F32)

    maps_ref[0] = jnp.zeros(maps_ref.shape[1:], F32)
    edges_ref[0] = jnp.zeros(edges_ref.shape[1:], F32)
    clear_sums(sum_ref)
    for copy in small:
        copy.wait()
    coded_ref[...] = segment_table(motion_ref[...], epochs, member * epochs)
    table = pltpu.make_async_copy(coded_ref, table_ref, table_sem)
    table.start()

    def weights(e):
        def profile(distance, beyond):
            scaled = distance * (1.0 / jnp.full((1, distance.shape[1]), sigma_ref[e], F32))
            return jnp.where(beyond, 0.0, jnp.exp(-0.5 * (scaled * scaled)))

        turned = profile(ring, outside)
        scale = 1.0 / jnp.sum(turned[:8], axis=1, keepdims=True)[:1]
        turned = turned * scale
        bands = profile(drop, dropped) * scale if prepared else None
        ends = [profile(*gap) * scale for gap in edge_gaps]
        result = []
        blank = jnp.zeros((tile - 2 * PAD, tile), F32)
        for m in range(2):
            value = turned if m == 0 else turned * turned
            inside = jnp.where(far, 0.0, value)
            beyond = jnp.where(far, value, 0.0)
            top, bottom = beyond[:PAD], beyond[tile - PAD :]
            if prepared:
                band = (bands if m == 0 else bands * bands).astype(BF16)
            else:
                band = jnp.concatenate([bottom, inside, top], axis=0).astype(BF16)
            if m == 1:
                inside, top, bottom = (pltpu.roll(v, HALF, 1) for v in (inside, top, bottom))
            outer = jnp.concatenate([top, blank, bottom], axis=0)
            if m == 0:
                first, last = (jnp.where(of_psi, end, 0.0) for end in ends)
            else:
                first, last = (jnp.where(of_psi, 0.0, end * end) for end in ends)
            gap_rows = jnp.zeros((tile - 2 * SPAN, tile), F32)
            edge = jnp.concatenate([first, gap_rows, last], axis=0)
            result.append((band, *(v.astype(BF16) for v in (inside, outer, edge))))
        return result

    def correlate(e):
        if prepared:
            pair = first_ref[e], second_ref[e]
        else:
            inverse = valid_ref[e].astype(F32) / second_ref[e].astype(F32)
            pair = (first_ref[e].astype(F32) * inverse).astype(BF16), inverse.astype(BF16)
        (band, inside, outer, edge), (band2, inside2, outer2, edge2) = weights(e)

        def apart(a, b):
            wide = [jnp.concatenate([a, jnp.zeros_like(a)], axis=1)]
            wide.append(jnp.concatenate([jnp.zeros_like(b), b], axis=1))
            return jnp.concatenate(wide, axis=0)

        rows = jnp.dot(
            jnp.concatenate([band, band2], axis=1), apart(*pair), preferred_element_type=F32
        ).astype(BF16)
        maps = jnp.dot(rows, apart(inside, inside2), preferred_element_type=F32)
        sides = jnp.dot(
            rows,
            jnp.concatenate(
                [
                    jnp.concatenate([outer, edge], axis=1),
                    jnp.concatenate([outer2, edge2], axis=1),
                ],
                axis=0,
            ),
            preferred_element_type=F32,
        )
        return maps[:, :tile], maps[:, tile:], sides[:, :tile], sides[:, tile:]

    def correlate_chunk(c, carry):
        for i in range(2):
            data_copy(c, i).wait()
        made = [correlate(c * CHUNK + u) for u in range(CHUNK)]
        for i in range(4):
            held, at = (maps_ref, i) if i < 3 else (edges_ref, 0)
            total = held[c * CHUNK, at]
            for u in range(CHUNK):
                total = total + made[u][i]
                held[c * CHUNK + u + 1, at] = total
        return carry

    lax.fori_loop(0, chunks, correlate_chunk, 0)
    table.wait()
    stack_edges(
        epochs, tile, block, n_epoch, n_vel, table_ref, edges_ref, sum_ref, send_ref, keep_ref
    )


def finish_kernel(tile, block, keep_ref, own_ref, both_ref, *refs):
    mains, (like_ref, flux_ref) = refs[:-2], refs[-2:]
    row, lane = iota((SIDE, tile), 0), iota((SIDE, tile), 1)
    member = lax.axis_index("vel")
    placed = []
    for m in range(2):
        at = row - m * EDGE
        used = (at >= 0) & (at < EDGE)
        for right in (1 - member, member):
            wanted = at + jnp.where(right == 1, 0, tile - EDGE) + m * HALF
            placed.append(jnp.where(used & (lane == wanted % tile), 1.0, 0.0).astype(BF16))
    for i in range(block):
        sums = []
        for m in range(2):
            rows = slice((2 * i + m) * tile, (2 * i + m + 1) * tile)
            total = keep_ref[rows] + own_ref[rows].astype(F32)
            for main_ref in mains:
                total = total + main_ref[rows].astype(F32)
            for near, put in enumerate(placed[2 * m : 2 * m + 2]):
                at = (near * block + i) * SIDE
                total = total + lax.dot_general(
                    both_ref[at : at + SIDE], put, (((0,), (0,)), ((), ())),
                    preferred_element_type=F32,
                )
            sums.append(total)
        root = lax.rsqrt(jnp.maximum(pltpu.roll(sums[1], HALF, 1), phi_floor))
        like = sums[0] * root
        like_ref[i] = like
        flux_ref[i] = like * root


def move(block, axis, distance):
    count = lax.axis_size(axis)
    return lax.ppermute(block, axis, [(i, (i + distance) % count) for i in range(count)])


def beside(block, step, keep):
    count = lax.axis_size("sky")
    device = [(q - GRID_X // 2) % count for q in range(count)]
    route = [(device[q], device[q + step]) for q in range(count) if keep(q)]
    return lax.ppermute(block, "sky", route)


def beside_by_member(block, distance):
    n_sky, n_epoch = lax.axis_size("sky"), lax.axis_size("epoch")
    device = [(q - GRID_X // 2) % n_sky for q in range(n_sky)]
    route = []
    for q in range(n_sky):
        for p in range(n_epoch):
            for v, step in ((0, 1), (1, -1)):
                if 0 <= q % GRID_X + step < GRID_X:
                    away = (p + distance) % n_epoch
                    route.append(
                        (
                            (device[q] * n_epoch + p) * 2 + v,
                            (device[q + step] * n_epoch + away) * 2 + v,
                        )
                    )
    return lax.ppermute(block, ("sky", "epoch", "vel"), route)


def on_device(images, variances, valid, psf_sigma, offsets):
    epochs, tile = images.shape[0], images.shape[-1]
    n_epoch, n_vel = lax.axis_size("epoch"), lax.axis_size("vel")
    n_sky = lax.axis_size("sky")
    assert n_vel == 2 and epochs % CHUNK == 0
    block = VELS // (n_epoch * n_vel)
    first, second = images[:, 0], variances[:, 0]
    prepared = n_sky > GRID_X
    if prepared:
        usable = valid[:, 0].astype(F32)[:, None, None]
        scaled = (first.astype(F32) / second.astype(F32) * usable).astype(BF16)
        inverse = (usable / second.astype(F32)).astype(BF16)
        pair = jnp.stack([scaled, inverse])
        above = beside(pair[:, :, tile - HALO :], GRID_X, lambda q: q + GRID_X < n_sky)
        below = beside(pair[:, :, :HALO], -GRID_X, lambda q: q >= GRID_X)
        first, second = jnp.concatenate([above, pair, below], axis=2)

    main_rows = block * 2 * tile
    edge_rows = block * SIDE
    hbm = pl.BlockSpec(memory_space=pltpu.HBM)
    vmem = pl.BlockSpec(memory_space=pltpu.VMEM)
    params = pltpu.CompilerParams(vmem_limit_bytes=16 * 1024 * 1024)
    group_rows = n_vel * edge_rows
    operands = (psf_sigma, valid[:, 0], offsets, first, second)
    send_edges, keep_edges, maps, table = pl.pallas_call(
        functools.partial(stack_kernel, epochs, tile, block, n_epoch, n_vel, prepared),
        out_shape=(
            jax.ShapeDtypeStruct((n_epoch * group_rows, tile), BF16),
            jax.ShapeDtypeStruct((n_epoch * group_rows, tile), F32),
            jax.ShapeDtypeStruct((epochs + 1, 3, tile + 2 * PAD, tile), F32),
            jax.ShapeDtypeStruct(offsets.shape[1:], jnp.int32),
        ),
        in_specs=[hbm] * 5,
        out_specs=(vmem,) * 4,
        scratch_shapes=[
            pltpu.SMEM((epochs,), F32),
            pltpu.SMEM((epochs,), jnp.int32),
            pltpu.VMEM(offsets.shape, jnp.int32),
            pltpu.SMEM(offsets.shape[1:], jnp.int32),
            pltpu.VMEM(first.shape, BF16),
            pltpu.VMEM(second.shape, BF16),
            pltpu.VMEM((epochs + 1, 1, tile + 2 * PAD, tile), F32),
            pltpu.VMEM((VELS + 1, tile, tile), F32),
            pltpu.SemaphoreType.DMA((3,)),
            pltpu.SemaphoreType.DMA((2 * (epochs // CHUNK),)),
            pltpu.SemaphoreType.DMA,
        ],
        compiler_params=params,
    )(*(pltpu.with_memory_space_constraint(a, pltpu.HBM) for a in operands))
    edges = (keep_edges + move(send_edges, "vel", 1).astype(F32)).astype(BF16)
    sides = []
    for d in range(1, n_epoch + 1):
        at = (d - 1) * group_rows
        sides.append(beside_by_member(edges[at : at + group_rows], d % n_epoch))

    def main_sums(ranks):
        rows = (ranks[1] - ranks[0]) * main_rows
        slots = (ranks[1] - ranks[0]) * n_vel * block
        return pl.pallas_call(
            functools.partial(main_kernel, epochs, tile, block, n_epoch, n_vel, ranks),
            out_shape=(
                jax.ShapeDtypeStruct((rows, tile), BF16),
                jax.ShapeDtypeStruct((rows, tile), F32),
            ),
            in_specs=[pl.BlockSpec(memory_space=pltpu.SMEM), vmem],
            out_specs=(vmem,) * 2,
            scratch_shapes=[pltpu.VMEM((slots + 1, 2, tile, tile), F32)],
            compiler_params=pltpu.CompilerParams(vmem_limit_bytes=8 * 1024 * 1024),
        )(table, maps)

    taken = lax.axis_index("sky") < n_sky

    def pass_far(send, keep):
        return (keep + move(send, "vel", 1).astype(F32)).astype(BF16)

    far = lax.cond(taken, pass_far, lambda send, keep: send, *main_sums((0, n_epoch - 1)))
    mains = [
        move(far[(d - 1) * main_rows : d * main_rows], "epoch", d) for d in range(1, n_epoch)
    ]

    def pass_own(send, *sides):
        arrived = move(send, "vel", 1)
        side = sum(s.astype(F32) for s in sides).astype(BF16)
        is_first = lax.axis_index("vel") == 0
        near = jnp.where(is_first, side[:edge_rows], side[edge_rows:])
        other = jnp.where(is_first, side[edge_rows:], side[:edge_rows])
        return arrived, jnp.concatenate([near, move(other, "vel", 1)])

    def pass_nothing(send, *sides):
        return send, sides[0]

    send, keep = main_sums((n_epoch - 1, n_epoch))
    arrived, side = lax.cond(taken, pass_own, pass_nothing, send, *sides)

    shape = jax.ShapeDtypeStruct((block, tile, tile), F32)
    likelihood, flux = pl.pallas_call(
        functools.partial(finish_kernel, tile, block),
        out_shape=(shape, shape),
        in_specs=[vmem] * (3 + len(mains)),
        out_specs=(vmem, vmem),
        compiler_params=params,
    )(keep, arrived, side, *mains)
    return likelihood[:, None], flux[:, None]


def solution(mesh):
    placed = (
        P(("epoch", "vel"), ("field", "sky"), None, None),
        P(("epoch", "vel"), ("field", "sky"), None, None),
        P(("epoch", "vel"), ("field", "sky")),
        P(("field", "epoch", "vel")),
        P(None, None, "epoch"),
    )
    return jax.shard_map(
        on_device,
        mesh=mesh,
        in_specs=placed,
        out_specs=(
            P(("epoch", "vel"), ("field", "sky"), None, None),
            P(("epoch", "vel"), ("field", "sky"), None, None),
        ),
        check_vma=False,
    )
```

```python
import functools

import jax
import jax.numpy as jnp
from jax import lax
from jax.experimental import pallas as pl
from jax.experimental.pallas import tpu as pltpu
from jax.sharding import PartitionSpec as P

VELS = 16
REACH = 12
PSFR = 7
GRID_X = 4

phi_floor = 0.25

F32 = jnp.float32
BF16 = jnp.bfloat16
EDGE = REACH + PSFR
PAD = 16
HALO = 32
SIDE = 48
HALF = 64
SPAN = 32
CHUNK = 4
STEP = 8


def iota(shape, axis):
    return lax.broadcasted_iota(jnp.int32, shape, axis)


def pick_edges(tile, first_left):
    row, lane = iota((2 * SIDE, tile), 0), iota((2 * SIDE, tile), 1)
    within = row % SIDE
    left = (row >= SIDE) != first_left
    wanted = within % EDGE + jnp.where(left, 0, SPAN + REACH) + jnp.where(within < EDGE, 0, HALF)
    return jnp.where((within < 2 * EDGE) & (lane == wanted), 1.0, 0.0).astype(BF16)


def segment_table(motion, epochs, first):
    code = (motion[0] + REACH) * 32 + motion[1] + REACH
    total = code.shape[1]
    lane = iota(code.shape, 1)
    later = jnp.roll(code, -1, axis=1) if total < 128 else pltpu.roll(code, total - 1, 1)
    stop = first + epochs
    end = jnp.where((later != code) | (lane == stop - 1), lane + 1, total)
    reach = 1
    while reach < epochs:
        end = jnp.minimum(end, jnp.where(lane + reach < total, jnp.roll(end, -reach, axis=1), total))
        reach *= 2
    return jnp.clip(end - first, 0, epochs) * 1024 + code


def over_segments(epochs, table_ref, maps_ref, chosen, slots, first_k, add):
    member = lax.axis_index("vel")
    row = iota((8, maps_ref.shape[-1]), 0)

    def segment(slot, e):
        word = table_ref[lax.rem(first_k + slot, VELS), member * epochs + e]
        e_end = word >> 10
        start = PAD - REACH + ((word >> 5) & 31)
        dx = (word & 31) - REACH
        tile = maps_ref.shape[-1]
        shift = jnp.where(dx > 0, tile - dx, -dx)
        base = pl.multiple_of((start // 8) * 8, 8)
        above = start - base
        turn = lax.rem(8 - above, 8)
        same = row < 8 - above
        put = add(slot, dx)

        def rows_at(r):
            window = pl.ds(base + r, 8)
            return [
                pltpu.roll(maps_ref[e_end, m, window] - maps_ref[e, m, window], turn, 0)
                for m in chosen
            ]

        upper = rows_at(0)
        for r in range(0, tile, 8):
            lower = rows_at(r + 8)
            put(r, [pltpu.roll(jnp.where(same, a, b), shift, 1) for a, b in zip(upper, lower)])
            upper = lower
        ended = e_end >= epochs
        return jnp.where(ended, jnp.minimum(slot + 1, slots), slot), jnp.where(ended, 0, e_end)

    def some_segments(state):
        for _ in range(STEP):
            state = segment(*state)
        return state

    start = (jnp.int32(0), jnp.int32(0))
    lax.while_loop(lambda state: state[0] < slots, some_segments, start)


def clear_sums(sum_ref):
    def clear(slot, carry):
        sum_ref[slot] = jnp.zeros(sum_ref.shape[1:], F32)
        return carry

    lax.fori_loop(0, sum_ref.shape[0] - 1, clear, 0)


def stack_edges(
    epochs, tile, block, n_epoch, n_vel, table_ref, maps_ref, sum_ref, send_ref, keep_ref
):
    column = lax.axis_index("epoch")
    member = lax.axis_index("vel")
    lane = iota((8, tile), 1)
    place = lane % SPAN - jnp.where(lane // SPAN % 2 == 0, REACH, 0)

    def add(slot, dx):
        held = (place + dx >= 0) & (place + dx < EDGE)

        def put(r, pieces):
            sum_ref[slot, r : r + 8] += jnp.where(held, pieces[0], 0.0)

        return put

    first_k = (column + 1) * n_vel * block
    over_segments(epochs, table_ref, maps_ref, (0,), VELS, first_k, add)

    selector = pick_edges(tile, member == 1)

    def pack(group, carry):
        for i in range(block):
            slot = group * block + i
            packed = lax.dot_general(
                selector, sum_ref[slot].astype(BF16), (((1,), (1,)), ((), ())),
                preferred_element_type=F32,
            )
            rows = pl.ds(slot * SIDE, SIDE)
            keep_ref[rows] = packed[:SIDE]
            send_ref[rows] = packed[SIDE:].astype(BF16)
        return carry

    lax.fori_loop(0, VELS // block, pack, 0)


def main_kernel(
    epochs, tile, block, n_epoch, n_vel, ranks,
    table_ref, maps_ref, send_ref, keep_ref, sum_ref,
):
    clear_sums(sum_ref)
    column = lax.axis_index("epoch")
    member = lax.axis_index("vel")
    lane = iota((8, tile), 1)
    turned = (lane + HALF) % tile
    first_slot, last_slot = (r * n_vel * block for r in ranks)
    slots = last_slot - first_slot

    def add(slot, dx):
        out = (lane + dx < 0) | (lane + dx >= tile)
        out_turned = (turned + dx < 0) | (turned + dx >= tile)

        def put(r, pieces):
            psi, phi, side = pieces
            sum_ref[slot, 0, r : r + 8] += jnp.where(out, side, psi)
            sum_ref[slot, 1, r : r + 8] += jnp.where(out_turned, side, phi)

        return put

    first_k = (column + 1) * n_vel * block + first_slot
    over_segments(epochs, table_ref, maps_ref, (0, 1, 2), slots, first_k, add)

    def write(j, carry):
        rank, i = j // block, lax.rem(j, block)
        kept = (rank * n_vel + member) * block + i
        sent = (rank * n_vel + 1 - member) * block + i
        rows = pl.ds(j * 2 * tile, 2 * tile)
        keep_ref[rows] = sum_ref[kept].reshape(2 * tile, tile)
        send_ref[rows] = sum_ref[sent].reshape(2 * tile, tile).astype(BF16)
        return carry

    lax.fori_loop(0, slots // n_vel, write, 0)


def stack_kernel(
    epochs, tile, block, n_epoch, n_vel, prepared,
    sigma_hbm, valid_hbm, motion_hbm, first_hbm, second_hbm,
    send_ref, keep_ref, maps_ref, coded_ref,
    sigma_ref, valid_ref, motion_ref, table_ref, first_ref, second_ref, edges_ref, sum_ref,
    small_sems, data_sems, table_sem,
):
    height = tile + 2 * PAD
    chunks = epochs // CHUNK
    member = lax.axis_index("vel")

    small = [
        pltpu.make_async_copy(motion_hbm, motion_ref, small_sems.at[0]),
        pltpu.make_async_copy(sigma_hbm, sigma_ref, small_sems.at[1]),
        pltpu.make_async_copy(valid_hbm, valid_ref, small_sems.at[2]),
    ]
    for copy in small:
        copy.start()

    def data_copy(c, i):
        at = pl.ds(c * CHUNK, CHUNK)
        source, target = ((first_hbm, first_ref), (second_hbm, second_ref))[i]
        return pltpu.make_async_copy(source.at[at], target.at[at], data_sems.at[2 * c + i])

    for c in range(chunks):
        for i in range(2):
            data_copy(c, i).start()

    row, lane = iota((tile, tile), 0), iota((tile, tile), 1)
    gap = jnp.abs(row - lane)
    ring = jnp.minimum(gap, tile - gap)
    outside = ring > PSFR
    far = gap >= tile // 2
    ring = ring.astype(F32)

    def edge_distance(first_row):
        at, ln = iota((SPAN, tile), 0) + first_row, iota((SPAN, tile), 1)
        left, place = ln // SPAN % 2 == 0, ln % SPAN
        source = place + jnp.where(left, -EDGE, tile - REACH)
        place = place - jnp.where(left, REACH, 0)
        away = jnp.abs(at - source)
        return away.astype(F32), (away > PSFR) | (place < 0) | (place >= EDGE)

    edge_gaps = [edge_distance(0), edge_distance(tile - SPAN)]
    of_psi = iota((SPAN, tile), 1) < HALF
    if prepared:
        depth = tile + 2 * HALO
        drop = jnp.abs(iota((height, depth), 1) - HALO - iota((height, depth), 0) + PAD)
        dropped = drop > PSFR
        drop = drop.astype(F32)

    maps_ref[0] = jnp.zeros(maps_ref.shape[1:], F32)
    edges_ref[0] = jnp.zeros(edges_ref.shape[1:], F32)
    clear_sums(sum_ref)
    for copy in small:
        copy.wait()
    coded_ref[...] = segment_table(motion_ref[...], epochs, member * epochs)
    table = pltpu.make_async_copy(coded_ref, table_ref, table_sem)
    table.start()

    def weights(e):
        def profile(distance, beyond):
            scaled = distance * (1.0 / jnp.full((1, distance.shape[1]), sigma_ref[e], F32))
            return jnp.where(beyond, 0.0, jnp.exp(-0.5 * (scaled * scaled)))

        turned = profile(ring, outside)
        scale = 1.0 / jnp.sum(turned[:8], axis=1, keepdims=True)[:1]
        turned = turned * scale
        bands = profile(drop, dropped) * scale if prepared else None
        ends = [profile(*gap) * scale for gap in edge_gaps]
        result = []
        blank = jnp.zeros((tile - 2 * PAD, tile), F32)
        for m in range(2):
            value = turned if m == 0 else turned * turned
            inside = jnp.where(far, 0.0, value)
            beyond = jnp.where(far, value, 0.0)
            top, bottom = beyond[:PAD], beyond[tile - PAD :]
            if prepared:
                band = (bands if m == 0 else bands * bands).astype(BF16)
            else:
                band = jnp.concatenate([bottom, inside, top], axis=0).astype(BF16)
            if m == 1:
                inside, top, bottom = (pltpu.roll(v, HALF, 1) for v in (inside, top, bottom))
            outer = jnp.concatenate([top, blank, bottom], axis=0)
            if m == 0:
                first, last = (jnp.where(of_psi, end, 0.0) for end in ends)
            else:
                first, last = (jnp.where(of_psi, 0.0, end * end) for end in ends)
            gap_rows = jnp.zeros((tile - 2 * SPAN, tile), F32)
            edge = jnp.concatenate([first, gap_rows, last], axis=0)
            result.append((band, *(v.astype(BF16) for v in (inside, outer, edge))))
        return result

    def correlate(e):
        if prepared:
            pair = first_ref[e], second_ref[e]
        else:
            inverse = valid_ref[e].astype(F32) / second_ref[e].astype(F32)
            pair = (first_ref[e].astype(F32) * inverse).astype(BF16), inverse.astype(BF16)
        (band, inside, outer, edge), (band2, inside2, outer2, edge2) = weights(e)

        def apart(a, b):
            wide = [jnp.concatenate([a, jnp.zeros_like(a)], axis=1)]
            wide.append(jnp.concatenate([jnp.zeros_like(b), b], axis=1))
            return jnp.concatenate(wide, axis=0)

        rows = jnp.dot(
            jnp.concatenate([band, band2], axis=1), apart(*pair), preferred_element_type=F32
        ).astype(BF16)
        maps = jnp.dot(rows, apart(inside, inside2), preferred_element_type=F32)
        sides = jnp.dot(
            rows,
            jnp.concatenate(
                [
                    jnp.concatenate([outer, edge], axis=1),
                    jnp.concatenate([outer2, edge2], axis=1),
                ],
                axis=0,
            ),
            preferred_element_type=F32,
        )
        return maps[:, :tile], maps[:, tile:], sides[:, :tile], sides[:, tile:]

    def correlate_chunk(c, carry):
        for i in range(2):
            data_copy(c, i).wait()
        made = [correlate(c * CHUNK + u) for u in range(CHUNK)]
        for i in range(4):
            held, at = (maps_ref, i) if i < 3 else (edges_ref, 0)
            total = held[c * CHUNK, at]
            for u in range(CHUNK):
                total = total + made[u][i]
                held[c * CHUNK + u + 1, at] = total
        return carry

    lax.fori_loop(0, chunks, correlate_chunk, 0)
    table.wait()
    stack_edges(
        epochs, tile, block, n_epoch, n_vel, table_ref, edges_ref, sum_ref, send_ref, keep_ref
    )


def finish_kernel(tile, block, keep_ref, own_ref, both_ref, *refs):
    mains, (like_ref, flux_ref) = refs[:-2], refs[-2:]
    row, lane = iota((SIDE, tile), 0), iota((SIDE, tile), 1)
    member = lax.axis_index("vel")
    placed = []
    for m in range(2):
        at = row - m * EDGE
        used = (at >= 0) & (at < EDGE)
        for right in (1 - member, member):
            wanted = at + jnp.where(right == 1, 0, tile - EDGE) + m * HALF
            placed.append(jnp.where(used & (lane == wanted % tile), 1.0, 0.0).astype(BF16))
    for i in range(block):
        sums = []
        for m in range(2):
            rows = slice((2 * i + m) * tile, (2 * i + m + 1) * tile)
            total = keep_ref[rows] + own_ref[rows].astype(F32)
            for main_ref in mains:
                total = total + main_ref[rows].astype(F32)
            for near, put in enumerate(placed[2 * m : 2 * m + 2]):
                at = (near * block + i) * SIDE
                total = total + lax.dot_general(
                    both_ref[at : at + SIDE], put, (((0,), (0,)), ((), ())),
                    preferred_element_type=F32,
                )
            sums.append(total)
        root = lax.rsqrt(jnp.maximum(pltpu.roll(sums[1], HALF, 1), phi_floor))
        like = sums[0] * root
        like_ref[i] = like
        flux_ref[i] = like * root


def move(block, axis, distance):
    count = lax.axis_size(axis)
    return lax.ppermute(block, axis, [(i, (i + distance) % count) for i in range(count)])


def beside(block, step, keep):
    count = lax.axis_size("sky")
    device = [(q - GRID_X // 2) % count for q in range(count)]
    route = [(device[q], device[q + step]) for q in range(count) if keep(q)]
    return lax.ppermute(block, "sky", route)


def beside_by_member(block):
    n_sky = lax.axis_size("sky")
    device = [(q - GRID_X // 2) % n_sky for q in range(n_sky)]
    route = []
    for q in range(n_sky):
        for v, step in ((0, 1), (1, -1)):
            if 0 <= q % GRID_X + step < GRID_X:
                route.append((device[q] * 2 + v, device[q + step] * 2 + v))
    return lax.ppermute(block, ("sky", "vel"), route)


def on_device(images, variances, valid, psf_sigma, offsets):
    epochs, tile = images.shape[0], images.shape[-1]
    n_epoch, n_vel = lax.axis_size("epoch"), lax.axis_size("vel")
    n_sky = lax.axis_size("sky")
    assert n_vel == 2 and epochs % CHUNK == 0
    block = VELS // (n_epoch * n_vel)
    first, second = images[:, 0], variances[:, 0]
    prepared = n_sky > GRID_X
    if prepared:
        usable = valid[:, 0].astype(F32)[:, None, None]
        scaled = (first.astype(F32) / second.astype(F32) * usable).astype(BF16)
        inverse = (usable / second.astype(F32)).astype(BF16)
        pair = jnp.stack([scaled, inverse])
        above = beside(pair[:, :, tile - HALO :], GRID_X, lambda q: q + GRID_X < n_sky)
        below = beside(pair[:, :, :HALO], -GRID_X, lambda q: q >= GRID_X)
        first, second = jnp.concatenate([above, pair, below], axis=2)

    main_rows = block * 2 * tile
    edge_rows = block * SIDE
    hbm = pl.BlockSpec(memory_space=pltpu.HBM)
    vmem = pl.BlockSpec(memory_space=pltpu.VMEM)
    params = pltpu.CompilerParams(vmem_limit_bytes=16 * 1024 * 1024)
    group_rows = n_vel * edge_rows
    operands = (psf_sigma, valid[:, 0], offsets, first, second)
    send_edges, keep_edges, maps, table = pl.pallas_call(
        functools.partial(stack_kernel, epochs, tile, block, n_epoch, n_vel, prepared),
        out_shape=(
            jax.ShapeDtypeStruct((n_epoch * group_rows, tile), BF16),
            jax.ShapeDtypeStruct((n_epoch * group_rows, tile), F32),
            pltpu.VMEM((epochs + 1, 3, tile + 2 * PAD, tile), F32),
            jax.ShapeDtypeStruct(offsets.shape[1:], jnp.int32),
        ),
        in_specs=[hbm] * 5,
        out_specs=(vmem,) * 4,
        scratch_shapes=[
            pltpu.SMEM((epochs,), F32),
            pltpu.SMEM((epochs,), jnp.int32),
            pltpu.VMEM(offsets.shape, jnp.int32),
            pltpu.SMEM(offsets.shape[1:], jnp.int32),
            pltpu.VMEM(first.shape, BF16),
            pltpu.VMEM(second.shape, BF16),
            pltpu.VMEM((epochs + 1, 1, tile + 2 * PAD, tile), F32),
            pltpu.VMEM((VELS + 1, tile, tile), F32),
            pltpu.SemaphoreType.DMA((3,)),
            pltpu.SemaphoreType.DMA((2 * (epochs // CHUNK),)),
            pltpu.SemaphoreType.DMA,
        ],
        compiler_params=params,
    )(*(pltpu.with_memory_space_constraint(a, pltpu.HBM) for a in operands))
    edges = (keep_edges + move(send_edges, "vel", 1).astype(F32)).astype(BF16)
    own_edges = edges[(n_epoch - 1) * group_rows :].astype(F32)
    for d in range(1, n_epoch):
        own_edges += move(edges[(d - 1) * group_rows : d * group_rows], "epoch", d).astype(F32)
    side = beside_by_member(own_edges.astype(BF16))

    def main_sums(ranks):
        rows = (ranks[1] - ranks[0]) * main_rows
        slots = (ranks[1] - ranks[0]) * n_vel * block
        return pl.pallas_call(
            functools.partial(main_kernel, epochs, tile, block, n_epoch, n_vel, ranks),
            out_shape=(
                jax.ShapeDtypeStruct((rows, tile), BF16),
                jax.ShapeDtypeStruct((rows, tile), F32),
            ),
            in_specs=[pl.BlockSpec(memory_space=pltpu.SMEM), vmem],
            out_specs=(vmem,) * 2,
            scratch_shapes=[pltpu.VMEM((slots + 1, 2, tile, tile), F32)],
            compiler_params=pltpu.CompilerParams(vmem_limit_bytes=8 * 1024 * 1024),
        )(table, pltpu.with_memory_space_constraint(maps, pltpu.VMEM))

    taken = lax.axis_index("sky") < n_sky

    def pass_far(send, keep):
        return (keep + move(send, "vel", 1).astype(F32)).astype(BF16)

    far = lax.cond(taken, pass_far, lambda send, keep: send, *main_sums((0, n_epoch - 1)))
    mains = [
        move(far[(d - 1) * main_rows : d * main_rows], "epoch", d) for d in range(1, n_epoch)
    ]

    def pass_own(send, side):
        arrived = move(send, "vel", 1)
        is_first = lax.axis_index("vel") == 0
        near = jnp.where(is_first, side[:edge_rows], side[edge_rows:])
        other = jnp.where(is_first, side[edge_rows:], side[:edge_rows])
        return arrived, jnp.concatenate([near, move(other, "vel", 1)])

    send, keep = main_sums((n_epoch - 1, n_epoch))
    arrived, side = lax.cond(taken, pass_own, lambda send, side: (send, side), send, side)

    shape = jax.ShapeDtypeStruct((block, tile, tile), F32)
    likelihood, flux = pl.pallas_call(
        functools.partial(finish_kernel, tile, block),
        out_shape=(shape, shape),
        in_specs=[vmem] * (3 + len(mains)),
        out_specs=(vmem, vmem),
        compiler_params=params,
    )(keep, arrived, side, *mains)
    return likelihood[:, None], flux[:, None]


def solution(mesh):
    placed = (
        P(("epoch", "vel"), ("field", "sky"), None, None),
        P(("epoch", "vel"), ("field", "sky"), None, None),
        P(("epoch", "vel"), ("field", "sky")),
        P(("field", "epoch", "vel")),
        P(None, None, "epoch"),
    )
    return jax.shard_map(
        on_device,
        mesh=mesh,
        in_specs=placed,
        out_specs=(
            P(("epoch", "vel"), ("field", "sky"), None, None),
            P(("epoch", "vel"), ("field", "sky"), None, None),
        ),
        check_vma=False,
    )
```

```python
import functools

import jax
import jax.numpy as jnp
from jax import lax
from jax.experimental import pallas as pl
from jax.experimental.pallas import tpu as pltpu
from jax.sharding import PartitionSpec as P

VELS = 16
REACH = 12
PSFR = 7
GRID_X = 4

phi_floor = 0.25

F32 = jnp.float32
BF16 = jnp.bfloat16
EDGE = REACH + PSFR
PAD = 16
HALO = 32
SIDE = 48
HALF = 64
SPAN = 32
CHUNK = 4
STEP = 8


def iota(shape, axis):
    return lax.broadcasted_iota(jnp.int32, shape, axis)


def pick_edges(tile, first_left):
    row, lane = iota((2 * SIDE, tile), 0), iota((2 * SIDE, tile), 1)
    within = row % SIDE
    left = (row >= SIDE) != first_left
    wanted = within % EDGE + jnp.where(left, 0, SPAN + REACH) + jnp.where(within < EDGE, 0, HALF)
    return jnp.where((within < 2 * EDGE) & (lane == wanted), 1.0, 0.0).astype(BF16)


def segment_table(motion, epochs, first):
    code = (motion[0] + REACH) * 32 + motion[1] + REACH
    total = code.shape[1]
    lane = iota(code.shape, 1)
    later = jnp.roll(code, -1, axis=1) if total < 128 else pltpu.roll(code, total - 1, 1)
    stop = first + epochs
    end = jnp.where((later != code) | (lane == stop - 1), lane + 1, total)
    reach = 1
    while reach < epochs:
        end = jnp.minimum(end, jnp.where(lane + reach < total, jnp.roll(end, -reach, axis=1), total))
        reach *= 2
    return jnp.clip(end - first, 0, epochs) * 1024 + code


def over_segments(epochs, table_ref, maps_ref, chosen, slots, first_k, add):
    member = lax.axis_index("vel")
    row = iota((8, maps_ref.shape[-1]), 0)

    def segment(slot, e):
        word = table_ref[lax.rem(first_k + slot, VELS), member * epochs + e]
        e_end = word >> 10
        start = PAD - REACH + ((word >> 5) & 31)
        dx = (word & 31) - REACH
        tile = maps_ref.shape[-1]
        shift = jnp.where(dx > 0, tile - dx, -dx)
        base = pl.multiple_of((start // 8) * 8, 8)
        above = start - base
        turn = lax.rem(8 - above, 8)
        same = row < 8 - above
        put = add(slot, dx)

        def rows_at(r):
            window = pl.ds(base + r, 8)
            return [
                pltpu.roll(maps_ref[e_end, m, window] - maps_ref[e, m, window], turn, 0)
                for m in chosen
            ]

        upper = rows_at(0)
        for r in range(0, tile, 8):
            lower = rows_at(r + 8)
            put(r, [pltpu.roll(jnp.where(same, a, b), shift, 1) for a, b in zip(upper, lower)])
            upper = lower
        ended = e_end >= epochs
        return jnp.where(ended, jnp.minimum(slot + 1, slots), slot), jnp.where(ended, 0, e_end)

    def some_segments(state):
        for _ in range(STEP):
            state = segment(*state)
        return state

    start = (jnp.int32(0), jnp.int32(0))
    lax.while_loop(lambda state: state[0] < slots, some_segments, start)


def clear_sums(sum_ref):
    def clear(slot, carry):
        sum_ref[slot] = jnp.zeros(sum_ref.shape[1:], F32)
        return carry

    lax.fori_loop(0, sum_ref.shape[0] - 1, clear, 0)


def stack_edges(
    epochs, tile, block, n_epoch, n_vel, table_ref, maps_ref, sum_ref, send_ref, keep_ref
):
    column = lax.axis_index("epoch")
    member = lax.axis_index("vel")
    lane = iota((8, tile), 1)
    place = lane % SPAN - jnp.where(lane // SPAN % 2 == 0, REACH, 0)

    def add(slot, dx):
        held = (place + dx >= 0) & (place + dx < EDGE)

        def put(r, pieces):
            sum_ref[slot, r : r + 8] += jnp.where(held, pieces[0], 0.0)

        return put

    first_k = (column + 1) * n_vel * block
    over_segments(epochs, table_ref, maps_ref, (0,), VELS, first_k, add)

    selector = pick_edges(tile, member == 1)

    def pack(group, carry):
        for i in range(block):
            slot = group * block + i
            packed = lax.dot_general(
                selector, sum_ref[slot].astype(BF16), (((1,), (1,)), ((), ())),
                preferred_element_type=F32,
            )
            rows = pl.ds(slot * SIDE, SIDE)
            keep_ref[rows] = packed[:SIDE]
            send_ref[rows] = packed[SIDE:].astype(BF16)
        return carry

    lax.fori_loop(0, VELS // block, pack, 0)


def main_kernel(
    epochs, tile, block, n_epoch, n_vel, ranks,
    table_ref, maps_ref, send_ref, keep_ref, *refs,
):
    sum_ref = refs[-1]
    clear_sums(sum_ref)
    column = lax.axis_index("epoch")
    member = lax.axis_index("vel")
    lane = iota((8, tile), 1)
    turned = (lane + HALF) % tile
    first_slot, last_slot = (r * n_vel * block for r in ranks)
    slots = last_slot - first_slot

    def add(slot, dx):
        out = (lane + dx < 0) | (lane + dx >= tile)
        out_turned = (turned + dx < 0) | (turned + dx >= tile)

        def put(r, pieces):
            psi, phi, side = pieces
            sum_ref[slot, 0, r : r + 8] += jnp.where(out, side, psi)
            sum_ref[slot, 1, r : r + 8] += jnp.where(out_turned, side, phi)

        return put

    first_k = (column + 1) * n_vel * block + first_slot
    over_segments(epochs, table_ref, maps_ref, (0, 1, 2), slots, first_k, add)

    def write(j, carry):
        rank, i = j // block, lax.rem(j, block)
        kept = (rank * n_vel + member) * block + i
        sent = (rank * n_vel + 1 - member) * block + i
        rows = pl.ds(j * 2 * tile, 2 * tile)
        keep_ref[rows] = sum_ref[kept].reshape(2 * tile, tile)
        send_ref[rows] = sum_ref[sent].reshape(2 * tile, tile).astype(BF16)
        return carry

    lax.fori_loop(0, slots // n_vel, write, 0)


def stack_kernel(
    epochs, tile, block, n_epoch, n_vel, prepared,
    sigma_hbm, valid_hbm, motion_hbm, first_hbm, second_hbm,
    send_ref, keep_ref, maps_ref, coded_ref,
    sigma_ref, valid_ref, motion_ref, table_ref, first_ref, second_ref, edges_ref, sum_ref,
    small_sems, data_sems, table_sem,
):
    height = tile + 2 * PAD
    chunks = epochs // CHUNK
    member = lax.axis_index("vel")

    small = [
        pltpu.make_async_copy(motion_hbm, motion_ref, small_sems.at[0]),
        pltpu.make_async_copy(sigma_hbm, sigma_ref, small_sems.at[1]),
        pltpu.make_async_copy(valid_hbm, valid_ref, small_sems.at[2]),
    ]
    for copy in small:
        copy.start()

    def data_copy(c, i):
        at = pl.ds(c * CHUNK, CHUNK)
        source, target = ((first_hbm, first_ref), (second_hbm, second_ref))[i]
        return pltpu.make_async_copy(source.at[at], target.at[at], data_sems.at[2 * c + i])

    for c in range(chunks):
        for i in range(2):
            data_copy(c, i).start()

    row, lane = iota((tile, tile), 0), iota((tile, tile), 1)
    gap = jnp.abs(row - lane)
    ring = jnp.minimum(gap, tile - gap)
    outside = ring > PSFR
    far = gap >= tile // 2
    ring = ring.astype(F32)

    def edge_distance(first_row):
        at, ln = iota((SPAN, tile), 0) + first_row, iota((SPAN, tile), 1)
        left, place = ln // SPAN % 2 == 0, ln % SPAN
        source = place + jnp.where(left, -EDGE, tile - REACH)
        place = place - jnp.where(left, REACH, 0)
        away = jnp.abs(at - source)
        return away.astype(F32), (away > PSFR) | (place < 0) | (place >= EDGE)

    edge_gaps = [edge_distance(0), edge_distance(tile - SPAN)]
    of_psi = iota((SPAN, tile), 1) < HALF
    if prepared:
        depth = tile + 2 * HALO
        drop = jnp.abs(iota((height, depth), 1) - HALO - iota((height, depth), 0) + PAD)
        dropped = drop > PSFR
        drop = drop.astype(F32)

    maps_ref[0] = jnp.zeros(maps_ref.shape[1:], F32)
    edges_ref[0] = jnp.zeros(edges_ref.shape[1:], F32)
    clear_sums(sum_ref)
    for copy in small:
        copy.wait()
    coded_ref[...] = segment_table(motion_ref[...], epochs, member * epochs)
    table = pltpu.make_async_copy(coded_ref, table_ref, table_sem)
    table.start()

    def weights(e):
        def profile(distance, beyond):
            scaled = distance * (1.0 / jnp.full((1, distance.shape[1]), sigma_ref[e], F32))
            return jnp.where(beyond, 0.0, jnp.exp(-0.5 * (scaled * scaled)))

        turned = profile(ring, outside)
        scale = 1.0 / jnp.sum(turned[:8], axis=1, keepdims=True)[:1]
        turned = turned * scale
        bands = profile(drop, dropped) * scale if prepared else None
        ends = [profile(*gap) * scale for gap in edge_gaps]
        result = []
        blank = jnp.zeros((tile - 2 * PAD, tile), F32)
        for m in range(2):
            value = turned if m == 0 else turned * turned
            inside = jnp.where(far, 0.0, value)
            beyond = jnp.where(far, value, 0.0)
            top, bottom = beyond[:PAD], beyond[tile - PAD :]
            if prepared:
                band = (bands if m == 0 else bands * bands).astype(BF16)
            else:
                band = jnp.concatenate([bottom, inside, top], axis=0).astype(BF16)
            if m == 1:
                inside, top, bottom = (pltpu.roll(v, HALF, 1) for v in (inside, top, bottom))
            outer = jnp.concatenate([top, blank, bottom], axis=0)
            if m == 0:
                first, last = (jnp.where(of_psi, end, 0.0) for end in ends)
            else:
                first, last = (jnp.where(of_psi, 0.0, end * end) for end in ends)
            gap_rows = jnp.zeros((tile - 2 * SPAN, tile), F32)
            edge = jnp.concatenate([first, gap_rows, last], axis=0)
            result.append((band, *(v.astype(BF16) for v in (inside, outer, edge))))
        return result

    def correlate(e):
        if prepared:
            pair = first_ref[e], second_ref[e]
        else:
            inverse = valid_ref[e].astype(F32) / second_ref[e].astype(F32)
            pair = (first_ref[e].astype(F32) * inverse).astype(BF16), inverse.astype(BF16)
        (band, inside, outer, edge), (band2, inside2, outer2, edge2) = weights(e)

        def apart(a, b):
            wide = [jnp.concatenate([a, jnp.zeros_like(a)], axis=1)]
            wide.append(jnp.concatenate([jnp.zeros_like(b), b], axis=1))
            return jnp.concatenate(wide, axis=0)

        rows = jnp.dot(
            jnp.concatenate([band, band2], axis=1), apart(*pair), preferred_element_type=F32
        ).astype(BF16)
        maps = jnp.dot(rows, apart(inside, inside2), preferred_element_type=F32)
        sides = jnp.dot(
            rows,
            jnp.concatenate(
                [
                    jnp.concatenate([outer, edge], axis=1),
                    jnp.concatenate([outer2, edge2], axis=1),
                ],
                axis=0,
            ),
            preferred_element_type=F32,
        )
        return maps[:, :tile], maps[:, tile:], sides[:, :tile], sides[:, tile:]

    def correlate_chunk(c, carry):
        for i in range(2):
            data_copy(c, i).wait()
        made = [correlate(c * CHUNK + u) for u in range(CHUNK)]
        for i in range(4):
            held, at = (maps_ref, i) if i < 3 else (edges_ref, 0)
            total = held[c * CHUNK, at]
            for u in range(CHUNK):
                total = total + made[u][i]
                held[c * CHUNK + u + 1, at] = total
        return carry

    lax.fori_loop(0, chunks, correlate_chunk, 0)
    table.wait()
    stack_edges(
        epochs, tile, block, n_epoch, n_vel, table_ref, edges_ref, sum_ref, send_ref, keep_ref
    )


def finish_kernel(tile, block, keep_ref, own_ref, both_ref, *refs):
    mains, (like_ref, flux_ref) = refs[:-2], refs[-2:]
    row, lane = iota((SIDE, tile), 0), iota((SIDE, tile), 1)
    member = lax.axis_index("vel")
    placed = []
    for m in range(2):
        at = row - m * EDGE
        used = (at >= 0) & (at < EDGE)
        for right in (1 - member, member):
            wanted = at + jnp.where(right == 1, 0, tile - EDGE) + m * HALF
            placed.append(jnp.where(used & (lane == wanted % tile), 1.0, 0.0).astype(BF16))
    for i in range(block):
        sums = []
        for m in range(2):
            rows = slice((2 * i + m) * tile, (2 * i + m + 1) * tile)
            total = keep_ref[rows] + own_ref[rows].astype(F32)
            for main_ref in mains:
                total = total + main_ref[rows].astype(F32)
            for near, put in enumerate(placed[2 * m : 2 * m + 2]):
                at = (near * block + i) * SIDE
                total = total + lax.dot_general(
                    both_ref[at : at + SIDE], put, (((0,), (0,)), ((), ())),
                    preferred_element_type=F32,
                )
            sums.append(total)
        root = lax.rsqrt(jnp.maximum(pltpu.roll(sums[1], HALF, 1), phi_floor))
        like = sums[0] * root
        like_ref[i] = like
        flux_ref[i] = like * root


def move(block, axis, distance):
    count = lax.axis_size(axis)
    return lax.ppermute(block, axis, [(i, (i + distance) % count) for i in range(count)])


def beside(block, step, keep):
    count = lax.axis_size("sky")
    device = [(q - GRID_X // 2) % count for q in range(count)]
    route = [(device[q], device[q + step]) for q in range(count) if keep(q)]
    return lax.ppermute(block, "sky", route)


def beside_by_member(block):
    n_sky = lax.axis_size("sky")
    device = [(q - GRID_X // 2) % n_sky for q in range(n_sky)]
    route = []
    for q in range(n_sky):
        for v, step in ((0, 1), (1, -1)):
            if 0 <= q % GRID_X + step < GRID_X:
                route.append((device[q] * 2 + v, device[q + step] * 2 + v))
    return lax.ppermute(block, ("sky", "vel"), route)


def on_device(images, variances, valid, psf_sigma, offsets):
    epochs, tile = images.shape[0], images.shape[-1]
    n_epoch, n_vel = lax.axis_size("epoch"), lax.axis_size("vel")
    n_sky = lax.axis_size("sky")
    assert n_vel == 2 and epochs % CHUNK == 0
    block = VELS // (n_epoch * n_vel)
    first, second = images[:, 0], variances[:, 0]
    prepared = n_sky > GRID_X
    if prepared:
        usable = valid[:, 0].astype(F32)[:, None, None]
        scaled = (first.astype(F32) / second.astype(F32) * usable).astype(BF16)
        inverse = (usable / second.astype(F32)).astype(BF16)
        pair = jnp.stack([scaled, inverse])
        above = beside(pair[:, :, tile - HALO :], GRID_X, lambda q: q + GRID_X < n_sky)
        below = beside(pair[:, :, :HALO], -GRID_X, lambda q: q >= GRID_X)
        first, second = jnp.concatenate([above, pair, below], axis=2)

    main_rows = block * 2 * tile
    edge_rows = block * SIDE
    hbm = pl.BlockSpec(memory_space=pltpu.HBM)
    vmem = pl.BlockSpec(memory_space=pltpu.VMEM)
    params = pltpu.CompilerParams(vmem_limit_bytes=16 * 1024 * 1024)
    group_rows = n_vel * edge_rows
    operands = (psf_sigma, valid[:, 0], offsets, first, second)
    send_edges, keep_edges, maps, table = pl.pallas_call(
        functools.partial(stack_kernel, epochs, tile, block, n_epoch, n_vel, prepared),
        out_shape=(
            jax.ShapeDtypeStruct((n_epoch * group_rows, tile), BF16),
            jax.ShapeDtypeStruct((n_epoch * group_rows, tile), F32),
            jax.ShapeDtypeStruct((epochs + 1, 3, tile + 2 * PAD, tile), F32),
            jax.ShapeDtypeStruct(offsets.shape[1:], jnp.int32),
        ),
        in_specs=[hbm] * 5,
        out_specs=(vmem,) * 4,
        scratch_shapes=[
            pltpu.SMEM((epochs,), F32),
            pltpu.SMEM((epochs,), jnp.int32),
            pltpu.VMEM(offsets.shape, jnp.int32),
            pltpu.SMEM(offsets.shape[1:], jnp.int32),
            pltpu.VMEM(first.shape, BF16),
            pltpu.VMEM(second.shape, BF16),
            pltpu.VMEM((epochs + 1, 1, tile + 2 * PAD, tile), F32),
            pltpu.VMEM((VELS + 1, tile, tile), F32),
            pltpu.SemaphoreType.DMA((3,)),
            pltpu.SemaphoreType.DMA((2 * (epochs // CHUNK),)),
            pltpu.SemaphoreType.DMA,
        ],
        compiler_params=params,
    )(*(pltpu.with_memory_space_constraint(a, pltpu.HBM) for a in operands))
    edges = (keep_edges + move(send_edges, "vel", 1).astype(F32)).astype(BF16)
    own_edges = edges[(n_epoch - 1) * group_rows :].astype(F32)
    for d in range(1, n_epoch):
        own_edges += move(edges[(d - 1) * group_rows : d * group_rows], "epoch", d).astype(F32)
    side = beside_by_member(own_edges.astype(BF16))

    def main_sums(ranks, maps, hand_on):
        rows = (ranks[1] - ranks[0]) * main_rows
        slots = (ranks[1] - ranks[0]) * n_vel * block
        handed = [jax.ShapeDtypeStruct(maps.shape, F32)] if hand_on else []
        return pl.pallas_call(
            functools.partial(main_kernel, epochs, tile, block, n_epoch, n_vel, ranks),
            out_shape=[
                jax.ShapeDtypeStruct((rows, tile), BF16),
                jax.ShapeDtypeStruct((rows, tile), F32),
                *handed,
            ],
            in_specs=[pl.BlockSpec(memory_space=pltpu.SMEM), vmem],
            out_specs=[vmem] * (2 + len(handed)),
            input_output_aliases={1: 2} if hand_on else {},
            scratch_shapes=[pltpu.VMEM((slots + 1, 2, tile, tile), F32)],
            compiler_params=pltpu.CompilerParams(vmem_limit_bytes=8 * 1024 * 1024),
        )(table, maps)

    send, keep, maps = main_sums((0, n_epoch - 1), maps, True)
    far = (keep + move(send, "vel", 1).astype(F32)).astype(BF16)
    mains = [
        move(far[(d - 1) * main_rows : d * main_rows], "epoch", d) for d in range(1, n_epoch)
    ]

    def pass_own(send, side):
        arrived = move(send, "vel", 1)
        is_first = lax.axis_index("vel") == 0
        near = jnp.where(is_first, side[:edge_rows], side[edge_rows:])
        other = jnp.where(is_first, side[edge_rows:], side[:edge_rows])
        return arrived, jnp.concatenate([near, move(other, "vel", 1)])

    send, keep = main_sums((n_epoch - 1, n_epoch), maps, False)
    taken = lax.axis_index("sky") < n_sky
    arrived, side = lax.cond(taken, pass_own, lambda send, side: (send, side), send, side)

    shape = jax.ShapeDtypeStruct((block, tile, tile), F32)
    likelihood, flux = pl.pallas_call(
        functools.partial(finish_kernel, tile, block),
        out_shape=(shape, shape),
        in_specs=[vmem] * (3 + len(mains)),
        out_specs=(vmem, vmem),
        compiler_params=params,
    )(keep, arrived, side, *mains)
    return likelihood[:, None], flux[:, None]


def solution(mesh):
    placed = (
        P(("epoch", "vel"), ("field", "sky"), None, None),
        P(("epoch", "vel"), ("field", "sky"), None, None),
        P(("epoch", "vel"), ("field", "sky")),
        P(("field", "epoch", "vel")),
        P(None, None, "epoch"),
    )
    return jax.shard_map(
        on_device,
        mesh=mesh,
        in_specs=placed,
        out_specs=(
            P(("epoch", "vel"), ("field", "sky"), None, None),
            P(("epoch", "vel"), ("field", "sky"), None, None),
        ),
        check_vma=False,
    )
```

```python
import functools

import jax
import jax.numpy as jnp
from jax import lax
from jax.experimental import pallas as pl
from jax.experimental.pallas import tpu as pltpu
from jax.sharding import PartitionSpec as P

VELS = 16
REACH = 12
PSFR = 7
GRID_X = 4

phi_floor = 0.25

F32 = jnp.float32
BF16 = jnp.bfloat16
EDGE = REACH + PSFR
PAD = 16
HALO = 32
SIDE = 48
HALF = 64
SPAN = 32
CHUNK = 4
STEP = 8


def iota(shape, axis):
    return lax.broadcasted_iota(jnp.int32, shape, axis)


def pick_edges(tile, first_left):
    row, lane = iota((2 * SIDE, tile), 0), iota((2 * SIDE, tile), 1)
    within = row % SIDE
    left = (row >= SIDE) != first_left
    wanted = within % EDGE + jnp.where(left, 0, SPAN + REACH) + jnp.where(within < EDGE, 0, HALF)
    return jnp.where((within < 2 * EDGE) & (lane == wanted), 1.0, 0.0).astype(BF16)


def segment_table(motion, epochs, first):
    code = (motion[0] + REACH) * 32 + motion[1] + REACH
    total = code.shape[1]
    lane = iota(code.shape, 1)
    later = jnp.roll(code, -1, axis=1) if total < 128 else pltpu.roll(code, total - 1, 1)
    stop = first + epochs
    end = jnp.where((later != code) | (lane == stop - 1), lane + 1, total)
    reach = 1
    while reach < epochs:
        end = jnp.minimum(end, jnp.where(lane + reach < total, jnp.roll(end, -reach, axis=1), total))
        reach *= 2
    return jnp.clip(end - first, 0, epochs) * 1024 + code


def over_segments(epochs, table_ref, maps_ref, chosen, slots, k_of, add):
    member = lax.axis_index("vel")
    row = iota((8, maps_ref.shape[-1]), 0)

    def segment(slot, e):
        word = table_ref[k_of(slot), member * epochs + e]
        e_end = word >> 10
        start = PAD - REACH + ((word >> 5) & 31)
        dx = (word & 31) - REACH
        tile = maps_ref.shape[-1]
        shift = jnp.where(dx > 0, tile - dx, -dx)
        base = pl.multiple_of((start // 8) * 8, 8)
        above = start - base
        turn = lax.rem(8 - above, 8)
        same = row < 8 - above
        put = add(slot, dx)

        def rows_at(r):
            window = pl.ds(base + r, 8)
            return [
                pltpu.roll(maps_ref[e_end, m, window] - maps_ref[e, m, window], turn, 0)
                for m in chosen
            ]

        upper = rows_at(0)
        for r in range(0, tile, 8):
            lower = rows_at(r + 8)
            put(r, [pltpu.roll(jnp.where(same, a, b), shift, 1) for a, b in zip(upper, lower)])
            upper = lower
        ended = e_end >= epochs
        return jnp.where(ended, jnp.minimum(slot + 1, slots), slot), jnp.where(ended, 0, e_end)

    def some_segments(state):
        for _ in range(STEP):
            state = segment(*state)
        return state

    start = (jnp.int32(0), jnp.int32(0))
    lax.while_loop(lambda state: state[0] < slots, some_segments, start)


def clear_sums(sum_ref):
    def clear(slot, carry):
        sum_ref[slot] = jnp.zeros(sum_ref.shape[1:], F32)
        return carry

    lax.fori_loop(0, sum_ref.shape[0] - 1, clear, 0)


def stack_edges(
    epochs, tile, block, n_epoch, n_vel, table_ref, maps_ref, sum_ref, send_ref, keep_ref
):
    column = lax.axis_index("epoch")
    member = lax.axis_index("vel")
    lane = iota((8, tile), 1)
    place = lane % SPAN - jnp.where(lane // SPAN % 2 == 0, REACH, 0)

    def add(slot, dx):
        held = (place + dx >= 0) & (place + dx < EDGE)

        def put(r, pieces):
            sum_ref[slot, r : r + 8] += jnp.where(held, pieces[0], 0.0)

        return put

    first_k = (column + 1) * n_vel * block
    over_segments(
        epochs, table_ref, maps_ref, (0,), VELS, lambda slot: lax.rem(first_k + slot, VELS), add
    )

    selector = pick_edges(tile, member == 1)

    def pack(group, carry):
        for i in range(block):
            slot = group * block + i
            packed = lax.dot_general(
                selector, sum_ref[slot].astype(BF16), (((1,), (1,)), ((), ())),
                preferred_element_type=F32,
            )
            rows = pl.ds(slot * SIDE, SIDE)
            keep_ref[rows] = packed[:SIDE]
            send_ref[rows] = packed[SIDE:].astype(BF16)
        return carry

    lax.fori_loop(0, VELS // block, pack, 0)


def main_kernel(epochs, tile, block, n_epoch, n_vel, ranks, sent, kept, table_ref, maps_ref, *refs):
    sum_ref = refs[-1]
    clear_sums(sum_ref)
    column = lax.axis_index("epoch")
    member = lax.axis_index("vel")
    lane = iota((8, tile), 1)
    turned = (lane + HALF) % tile
    share = (ranks[1] - ranks[0]) * block
    slots = (sent + kept) * share

    def k_of(slot):
        whose = jnp.where(slot < sent * share, 1 - member, member)
        rank = ranks[0] + lax.rem(slot, share) // block
        owner = lax.rem(column + 1 + rank, n_epoch)
        return (owner * n_vel + whose) * block + lax.rem(slot, block)

    def add(slot, dx):
        out = (lane + dx < 0) | (lane + dx >= tile)
        out_turned = (turned + dx < 0) | (turned + dx >= tile)

        def put(r, pieces):
            psi, phi, side = pieces
            sum_ref[slot, 0, r : r + 8] += jnp.where(out, side, psi)
            sum_ref[slot, 1, r : r + 8] += jnp.where(out_turned, side, phi)

        return put

    over_segments(epochs, table_ref, maps_ref, (0, 1, 2), slots, k_of, add)

    def write(target_ref, first):
        def one(j, carry):
            rows = pl.ds(j * 2 * tile, 2 * tile)
            value = sum_ref[first + j].reshape(2 * tile, tile)
            target_ref[rows] = value.astype(target_ref.dtype)
            return carry

        lax.fori_loop(0, share, one, 0)

    if sent:
        write(refs[0], 0)
    if kept:
        write(refs[sent], sent * share)


def stack_kernel(
    epochs, tile, block, n_epoch, n_vel, prepared,
    sigma_hbm, valid_hbm, motion_hbm, first_hbm, second_hbm,
    send_ref, keep_ref, maps_ref, coded_ref,
    sigma_ref, valid_ref, motion_ref, table_ref, first_ref, second_ref, edges_ref, sum_ref,
    small_sems, data_sems, table_sem,
):
    height = tile + 2 * PAD
    chunks = epochs // CHUNK
    member = lax.axis_index("vel")

    small = [
        pltpu.make_async_copy(motion_hbm, motion_ref, small_sems.at[0]),
        pltpu.make_async_copy(sigma_hbm, sigma_ref, small_sems.at[1]),
        pltpu.make_async_copy(valid_hbm, valid_ref, small_sems.at[2]),
    ]
    for copy in small:
        copy.start()

    def data_copy(c, i):
        at = pl.ds(c * CHUNK, CHUNK)
        source, target = ((first_hbm, first_ref), (second_hbm, second_ref))[i]
        return pltpu.make_async_copy(source.at[at], target.at[at], data_sems.at[2 * c + i])

    for c in range(chunks):
        for i in range(2):
            data_copy(c, i).start()

    row, lane = iota((tile, tile), 0), iota((tile, tile), 1)
    gap = jnp.abs(row - lane)
    ring = jnp.minimum(gap, tile - gap)
    outside = ring > PSFR
    far = gap >= tile // 2
    ring = ring.astype(F32)

    def edge_distance(first_row):
        at, ln = iota((SPAN, tile), 0) + first_row, iota((SPAN, tile), 1)
        left, place = ln // SPAN % 2 == 0, ln % SPAN
        source = place + jnp.where(left, -EDGE, tile - REACH)
        place = place - jnp.where(left, REACH, 0)
        away = jnp.abs(at - source)
        return away.astype(F32), (away > PSFR) | (place < 0) | (place >= EDGE)

    edge_gaps = [edge_distance(0), edge_distance(tile - SPAN)]
    of_psi = iota((SPAN, tile), 1) < HALF
    if prepared:
        depth = tile + 2 * HALO
        drop = jnp.abs(iota((height, depth), 1) - HALO - iota((height, depth), 0) + PAD)
        dropped = drop > PSFR
        drop = drop.astype(F32)

    maps_ref[0] = jnp.zeros(maps_ref.shape[1:], F32)
    edges_ref[0] = jnp.zeros(edges_ref.shape[1:], F32)
    clear_sums(sum_ref)
    for copy in small:
        copy.wait()
    coded_ref[...] = segment_table(motion_ref[...], epochs, member * epochs)
    table = pltpu.make_async_copy(coded_ref, table_ref, table_sem)
    table.start()

    def weights(e):
        def profile(distance, beyond):
            scaled = distance * (1.0 / jnp.full((1, distance.shape[1]), sigma_ref[e], F32))
            return jnp.where(beyond, 0.0, jnp.exp(-0.5 * (scaled * scaled)))

        turned = profile(ring, outside)
        scale = 1.0 / jnp.sum(turned[:8], axis=1, keepdims=True)[:1]
        turned = turned * scale
        bands = profile(drop, dropped) * scale if prepared else None
        ends = [profile(*gap) * scale for gap in edge_gaps]
        result = []
        blank = jnp.zeros((tile - 2 * PAD, tile), F32)
        for m in range(2):
            value = turned if m == 0 else turned * turned
            inside = jnp.where(far, 0.0, value)
            beyond = jnp.where(far, value, 0.0)
            top, bottom = beyond[:PAD], beyond[tile - PAD :]
            if prepared:
                band = (bands if m == 0 else bands * bands).astype(BF16)
            else:
                band = jnp.concatenate([bottom, inside, top], axis=0).astype(BF16)
            if m == 1:
                inside, top, bottom = (pltpu.roll(v, HALF, 1) for v in (inside, top, bottom))
            outer = jnp.concatenate([top, blank, bottom], axis=0)
            if m == 0:
                first, last = (jnp.where(of_psi, end, 0.0) for end in ends)
            else:
                first, last = (jnp.where(of_psi, 0.0, end * end) for end in ends)
            gap_rows = jnp.zeros((tile - 2 * SPAN, tile), F32)
            edge = jnp.concatenate([first, gap_rows, last], axis=0)
            result.append((band, *(v.astype(BF16) for v in (inside, outer, edge))))
        return result

    def correlate(e):
        if prepared:
            pair = first_ref[e], second_ref[e]
        else:
            inverse = valid_ref[e].astype(F32) / second_ref[e].astype(F32)
            pair = (first_ref[e].astype(F32) * inverse).astype(BF16), inverse.astype(BF16)
        (band, inside, outer, edge), (band2, inside2, outer2, edge2) = weights(e)

        def apart(a, b):
            wide = [jnp.concatenate([a, jnp.zeros_like(a)], axis=1)]
            wide.append(jnp.concatenate([jnp.zeros_like(b), b], axis=1))
            return jnp.concatenate(wide, axis=0)

        rows = jnp.dot(
            jnp.concatenate([band, band2], axis=1), apart(*pair), preferred_element_type=F32
        ).astype(BF16)
        maps = jnp.dot(rows, apart(inside, inside2), preferred_element_type=F32)
        sides = jnp.dot(
            rows,
            jnp.concatenate(
                [
                    jnp.concatenate([outer, edge], axis=1),
                    jnp.concatenate([outer2, edge2], axis=1),
                ],
                axis=0,
            ),
            preferred_element_type=F32,
        )
        return maps[:, :tile], maps[:, tile:], sides[:, :tile], sides[:, tile:]

    def correlate_chunk(c, carry):
        for i in range(2):
            data_copy(c, i).wait()
        made = [correlate(c * CHUNK + u) for u in range(CHUNK)]
        for i in range(4):
            held, at = (maps_ref, i) if i < 3 else (edges_ref, 0)
            total = held[c * CHUNK, at]
            for u in range(CHUNK):
                total = total + made[u][i]
                held[c * CHUNK + u + 1, at] = total
        return carry

    lax.fori_loop(0, chunks, correlate_chunk, 0)
    table.wait()
    stack_edges(
        epochs, tile, block, n_epoch, n_vel, table_ref, edges_ref, sum_ref, send_ref, keep_ref
    )


def join_kernel(keep_ref, arrived_ref, own_ref, *refs):
    beyond, (far_ref, side_ref) = refs[:-2], refs[-2:]
    far_ref[...] = (keep_ref[...] + arrived_ref[...].astype(F32)).astype(BF16)
    side = own_ref[...].astype(F32)
    for edge_ref in beyond:
        side = side + edge_ref[...].astype(F32)
    side_ref[...] = side.astype(BF16)


def finish_kernel(tile, block, keep_ref, own_ref, both_ref, *refs):
    mains, (like_hbm, flux_hbm, like_ref, flux_ref, sems) = refs[:-5], refs[-5:]
    copies = []
    row, lane = iota((SIDE, tile), 0), iota((SIDE, tile), 1)
    member = lax.axis_index("vel")
    placed = []
    for m in range(2):
        at = row - m * EDGE
        used = (at >= 0) & (at < EDGE)
        for right in (1 - member, member):
            wanted = at + jnp.where(right == 1, 0, tile - EDGE) + m * HALF
            placed.append(jnp.where(used & (lane == wanted % tile), 1.0, 0.0).astype(BF16))
    for i in range(block):
        sums = []
        for m in range(2):
            rows = slice((2 * i + m) * tile, (2 * i + m + 1) * tile)
            total = keep_ref[rows] + own_ref[rows].astype(F32)
            for main_ref in mains:
                total = total + main_ref[rows].astype(F32)
            for near, put in enumerate(placed[2 * m : 2 * m + 2]):
                at = (near * block + i) * SIDE
                total = total + lax.dot_general(
                    both_ref[at : at + SIDE], put, (((0,), (0,)), ((), ())),
                    preferred_element_type=F32,
                )
            sums.append(total)
        root = lax.rsqrt(jnp.maximum(pltpu.roll(sums[1], HALF, 1), phi_floor))
        like = sums[0] * root
        like_ref[i] = like
        flux_ref[i] = like * root
        for j, (source, target) in enumerate(((like_ref, like_hbm), (flux_ref, flux_hbm))):
            copies.append(pltpu.make_async_copy(source.at[i], target.at[i], sems.at[2 * i + j]))
            copies[-1].start()
    for copy in copies:
        copy.wait()


def move(block, axis, distance):
    count = lax.axis_size(axis)
    return lax.ppermute(block, axis, [(i, (i + distance) % count) for i in range(count)])


def beside(block, step, keep):
    count = lax.axis_size("sky")
    device = [(q - GRID_X // 2) % count for q in range(count)]
    route = [(device[q], device[q + step]) for q in range(count) if keep(q)]
    return lax.ppermute(block, "sky", route)


def beside_by_member(block):
    n_sky = lax.axis_size("sky")
    device = [(q - GRID_X // 2) % n_sky for q in range(n_sky)]
    route = []
    for q in range(n_sky):
        for v, step in ((0, 1), (1, -1)):
            if 0 <= q % GRID_X + step < GRID_X:
                route.append((device[q] * 2 + v, device[q + step] * 2 + v))
    return lax.ppermute(block, ("sky", "vel"), route)


def on_device(images, variances, valid, psf_sigma, offsets):
    epochs, tile = images.shape[0], images.shape[-1]
    n_epoch, n_vel = lax.axis_size("epoch"), lax.axis_size("vel")
    n_sky = lax.axis_size("sky")
    assert n_vel == 2 and epochs % CHUNK == 0
    block = VELS // (n_epoch * n_vel)
    first, second = images[:, 0], variances[:, 0]
    prepared = n_sky > GRID_X
    if prepared:
        usable = valid[:, 0].astype(F32)[:, None, None]
        scaled = (first.astype(F32) / second.astype(F32) * usable).astype(BF16)
        inverse = (usable / second.astype(F32)).astype(BF16)
        pair = jnp.stack([scaled, inverse])
        above = beside(pair[:, :, tile - HALO :], GRID_X, lambda q: q + GRID_X < n_sky)
        below = beside(pair[:, :, :HALO], -GRID_X, lambda q: q >= GRID_X)
        first, second = jnp.concatenate([above, pair, below], axis=2)

    main_rows = block * 2 * tile
    edge_rows = block * SIDE
    hbm = pl.BlockSpec(memory_space=pltpu.HBM)
    vmem = pl.BlockSpec(memory_space=pltpu.VMEM)
    params = pltpu.CompilerParams(vmem_limit_bytes=16 * 1024 * 1024)
    group_rows = n_vel * edge_rows
    operands = (psf_sigma, valid[:, 0], offsets, first, second)
    send_edges, keep_edges, maps, table = pl.pallas_call(
        functools.partial(stack_kernel, epochs, tile, block, n_epoch, n_vel, prepared),
        out_shape=(
            jax.ShapeDtypeStruct((n_epoch * group_rows, tile), BF16),
            jax.ShapeDtypeStruct((n_epoch * group_rows, tile), F32),
            jax.ShapeDtypeStruct((epochs + 1, 3, tile + 2 * PAD, tile), F32),
            jax.ShapeDtypeStruct(offsets.shape[1:], jnp.int32),
        ),
        in_specs=[hbm] * 5,
        out_specs=(vmem,) * 4,
        scratch_shapes=[
            pltpu.SMEM((epochs,), F32),
            pltpu.SMEM((epochs,), jnp.int32),
            pltpu.VMEM(offsets.shape, jnp.int32),
            pltpu.SMEM(offsets.shape[1:], jnp.int32),
            pltpu.VMEM(first.shape, BF16),
            pltpu.VMEM(second.shape, BF16),
            pltpu.VMEM((epochs + 1, 1, tile + 2 * PAD, tile), F32),
            pltpu.VMEM((VELS + 1, tile, tile), F32),
            pltpu.SemaphoreType.DMA((3,)),
            pltpu.SemaphoreType.DMA((2 * (epochs // CHUNK),)),
            pltpu.SemaphoreType.DMA,
        ],
        compiler_params=params,
    )(*(pltpu.with_memory_space_constraint(a, pltpu.HBM) for a in operands))
    edges = (keep_edges + move(send_edges, "vel", 1).astype(F32)).astype(BF16)
    beyond = [
        move(edges[(d - 1) * group_rows : d * group_rows], "epoch", d) for d in range(1, n_epoch)
    ]

    def main_sums(ranks, sent, kept, maps, hand_on):
        rows = (ranks[1] - ranks[0]) * main_rows
        results = [jax.ShapeDtypeStruct((rows, tile), BF16)] * sent
        results += [jax.ShapeDtypeStruct((rows, tile), F32)] * kept
        aliases = {1: len(results)} if hand_on else {}
        results += [jax.ShapeDtypeStruct(maps.shape, F32)] * hand_on
        slots = (sent + kept) * (ranks[1] - ranks[0]) * block
        return pl.pallas_call(
            functools.partial(
                main_kernel, epochs, tile, block, n_epoch, n_vel, ranks, sent, kept
            ),
            out_shape=results,
            in_specs=[pl.BlockSpec(memory_space=pltpu.SMEM), vmem],
            out_specs=[vmem] * len(results),
            input_output_aliases=aliases,
            scratch_shapes=[pltpu.VMEM((slots + 1, 2, tile, tile), F32)],
            compiler_params=pltpu.CompilerParams(vmem_limit_bytes=8 * 1024 * 1024),
        )(table, maps)

    far_ranks, own_ranks = (0, n_epoch - 1), (n_epoch - 1, n_epoch)
    send, maps = main_sums(far_ranks, 1, 0, maps, 1)
    keep, maps = main_sums(far_ranks, 0, 1, maps, 1)
    far, side = pl.pallas_call(
        join_kernel,
        out_shape=(
            jax.ShapeDtypeStruct(keep.shape, BF16),
            jax.ShapeDtypeStruct((group_rows, tile), BF16),
        ),
        in_specs=[vmem] * (3 + len(beyond)),
        out_specs=(vmem, vmem),
        compiler_params=params,
    )(keep, move(send, "vel", 1), edges[(n_epoch - 1) * group_rows :], *beyond)
    side = beside_by_member(side)
    mains = [
        move(far[(d - 1) * main_rows : d * main_rows], "epoch", d) for d in range(1, n_epoch)
    ]

    def pass_own(send, side):
        arrived = move(send, "vel", 1)
        is_first = lax.axis_index("vel") == 0
        near = jnp.where(is_first, side[:edge_rows], side[edge_rows:])
        other = jnp.where(is_first, side[edge_rows:], side[:edge_rows])
        return arrived, jnp.concatenate([near, move(other, "vel", 1)])

    send, keep = main_sums(own_ranks, 1, 1, maps, 0)
    taken = lax.axis_index("sky") < n_sky
    arrived, side = lax.cond(taken, pass_own, lambda send, side: (send, side), send, side)

    shape = jax.ShapeDtypeStruct((block, tile, tile), F32)
    likelihood, flux = pl.pallas_call(
        functools.partial(finish_kernel, tile, block),
        out_shape=(shape, shape),
        in_specs=[vmem] * (3 + len(mains)),
        out_specs=(hbm, hbm),
        scratch_shapes=[
            pltpu.VMEM(shape.shape, F32),
            pltpu.VMEM(shape.shape, F32),
            pltpu.SemaphoreType.DMA((2 * block,)),
        ],
        compiler_params=params,
    )(keep, arrived, side, *mains)
    return likelihood[:, None], flux[:, None]


def solution(mesh):
    placed = (
        P(("epoch", "vel"), ("field", "sky"), None, None),
        P(("epoch", "vel"), ("field", "sky"), None, None),
        P(("epoch", "vel"), ("field", "sky")),
        P(("field", "epoch", "vel")),
        P(None, None, "epoch"),
    )
    return jax.shard_map(
        on_device,
        mesh=mesh,
        in_specs=placed,
        out_specs=(
            P(("epoch", "vel"), ("field", "sky"), None, None),
            P(("epoch", "vel"), ("field", "sky"), None, None),
        ),
        check_vma=False,
    )
```

```python
import functools

import jax
import jax.numpy as jnp
from jax import lax
from jax.experimental import pallas as pl
from jax.experimental.pallas import tpu as pltpu
from jax.sharding import PartitionSpec as P

VELS = 16
REACH = 12
PSFR = 7
GRID_X = 4

phi_floor = 0.25

F32 = jnp.float32
BF16 = jnp.bfloat16
EDGE = REACH + PSFR
PAD = 16
HALO = 32
SIDE = 48
HALF = 64
SPAN = 32
CHUNK = 4
STEP = 8


def iota(shape, axis):
    return lax.broadcasted_iota(jnp.int32, shape, axis)


def pick_edges(tile, first_left):
    row, lane = iota((2 * SIDE, tile), 0), iota((2 * SIDE, tile), 1)
    within = row % SIDE
    left = (row >= SIDE) != first_left
    wanted = within % EDGE + jnp.where(left, 0, SPAN + REACH) + jnp.where(within < EDGE, 0, HALF)
    return jnp.where((within < 2 * EDGE) & (lane == wanted), 1.0, 0.0).astype(BF16)


def segment_table(motion, epochs, first):
    code = (motion[0] + REACH) * 32 + motion[1] + REACH
    total = code.shape[1]
    lane = iota(code.shape, 1)
    later = jnp.roll(code, -1, axis=1) if total < 128 else pltpu.roll(code, total - 1, 1)
    stop = first + epochs
    end = jnp.where((later != code) | (lane == stop - 1), lane + 1, total)
    reach = 1
    while reach < epochs:
        end = jnp.minimum(end, jnp.where(lane + reach < total, jnp.roll(end, -reach, axis=1), total))
        reach *= 2
    return jnp.clip(end - first, 0, epochs) * 1024 + code


def over_segments(epochs, table_ref, maps_ref, chosen, slots, k_of, add):
    member = lax.axis_index("vel")
    row = iota((8, maps_ref.shape[-1]), 0)

    def segment(slot, e):
        word = table_ref[k_of(slot), member * epochs + e]
        e_end = word >> 10
        start = PAD - REACH + ((word >> 5) & 31)
        dx = (word & 31) - REACH
        tile = maps_ref.shape[-1]
        shift = jnp.where(dx > 0, tile - dx, -dx)
        base = pl.multiple_of((start // 8) * 8, 8)
        above = start - base
        turn = lax.rem(8 - above, 8)
        same = row < 8 - above
        put = add(slot, dx)

        def rows_at(r):
            window = pl.ds(base + r, 8)
            return [
                pltpu.roll(maps_ref[e_end, m, window] - maps_ref[e, m, window], turn, 0)
                for m in chosen
            ]

        upper = rows_at(0)
        for r in range(0, tile, 8):
            lower = rows_at(r + 8)
            put(r, [pltpu.roll(jnp.where(same, a, b), shift, 1) for a, b in zip(upper, lower)])
            upper = lower
        ended = e_end >= epochs
        return jnp.where(ended, jnp.minimum(slot + 1, slots), slot), jnp.where(ended, 0, e_end)

    def some_segments(state):
        for _ in range(STEP):
            state = segment(*state)
        return state

    start = (jnp.int32(0), jnp.int32(0))
    lax.while_loop(lambda state: state[0] < slots, some_segments, start)


def clear_sums(sum_ref):
    def clear(slot, carry):
        sum_ref[slot] = jnp.zeros(sum_ref.shape[1:], F32)
        return carry

    lax.fori_loop(0, sum_ref.shape[0] - 1, clear, 0)


def stack_edges(
    epochs, tile, block, n_epoch, n_vel, table_ref, maps_ref, sum_ref, send_ref, keep_ref
):
    column = lax.axis_index("epoch")
    member = lax.axis_index("vel")
    lane = iota((8, tile), 1)
    place = lane % SPAN - jnp.where(lane // SPAN % 2 == 0, REACH, 0)

    def add(slot, dx):
        held = (place + dx >= 0) & (place + dx < EDGE)

        def put(r, pieces):
            sum_ref[slot, r : r + 8] += jnp.where(held, pieces[0], 0.0)

        return put

    first_k = (column + 1) * n_vel * block
    over_segments(
        epochs, table_ref, maps_ref, (0,), VELS, lambda slot: lax.rem(first_k + slot, VELS), add
    )

    selector = pick_edges(tile, member == 1)

    def pack(group, carry):
        for i in range(block):
            slot = group * block + i
            packed = lax.dot_general(
                selector, sum_ref[slot].astype(BF16), (((1,), (1,)), ((), ())),
                preferred_element_type=F32,
            )
            rows = pl.ds(slot * SIDE, SIDE)
            keep_ref[rows] = packed[:SIDE]
            send_ref[rows] = packed[SIDE:].astype(BF16)
        return carry

    lax.fori_loop(0, VELS // block, pack, 0)


def main_kernel(epochs, tile, block, n_epoch, n_vel, ranks, sent, kept, table_ref, maps_ref, *refs):
    sum_ref = refs[-1]
    clear_sums(sum_ref)
    column = lax.axis_index("epoch")
    member = lax.axis_index("vel")
    lane = iota((8, tile), 1)
    turned = (lane + HALF) % tile
    share = (ranks[1] - ranks[0]) * block
    slots = (sent + kept) * share

    def k_of(slot):
        whose = jnp.where(slot < sent * share, 1 - member, member)
        rank = ranks[0] + lax.rem(slot, share) // block
        owner = lax.rem(column + 1 + rank, n_epoch)
        return (owner * n_vel + whose) * block + lax.rem(slot, block)

    def add(slot, dx):
        out = (lane + dx < 0) | (lane + dx >= tile)
        out_turned = (turned + dx < 0) | (turned + dx >= tile)

        def put(r, pieces):
            psi, phi, side = pieces
            sum_ref[slot, 0, r : r + 8] += jnp.where(out, side, psi)
            sum_ref[slot, 1, r : r + 8] += jnp.where(out_turned, side, phi)

        return put

    over_segments(epochs, table_ref, maps_ref, (0, 1, 2), slots, k_of, add)

    def write(target_ref, first):
        def one(j, carry):
            rows = pl.ds(j * 2 * tile, 2 * tile)
            value = sum_ref[first + j].reshape(2 * tile, tile)
            target_ref[rows] = value.astype(target_ref.dtype)
            return carry

        lax.fori_loop(0, share, one, 0)

    if sent:
        write(refs[0], 0)
    if kept:
        write(refs[sent], sent * share)


def stack_kernel(
    epochs, tile, block, n_epoch, n_vel, prepared,
    sigma_hbm, valid_hbm, motion_hbm, first_hbm, second_hbm,
    send_ref, keep_ref, maps_ref, coded_ref,
    sigma_ref, valid_ref, motion_ref, table_ref, first_ref, second_ref, edges_ref, sum_ref,
    small_sems, data_sems, table_sem,
):
    height = tile + 2 * PAD
    chunks = epochs // CHUNK
    member = lax.axis_index("vel")

    small = [
        pltpu.make_async_copy(motion_hbm, motion_ref, small_sems.at[0]),
        pltpu.make_async_copy(sigma_hbm, sigma_ref, small_sems.at[1]),
        pltpu.make_async_copy(valid_hbm, valid_ref, small_sems.at[2]),
    ]
    for copy in small:
        copy.start()

    def data_copy(c, i):
        at = pl.ds(c * CHUNK, CHUNK)
        source, target = ((first_hbm, first_ref), (second_hbm, second_ref))[i]
        return pltpu.make_async_copy(source.at[at], target.at[at], data_sems.at[2 * c + i])

    for c in range(chunks):
        for i in range(2):
            data_copy(c, i).start()

    row, lane = iota((tile, tile), 0), iota((tile, tile), 1)
    gap = jnp.abs(row - lane)
    ring = jnp.minimum(gap, tile - gap)
    outside = ring > PSFR
    far = gap >= tile // 2
    ring = ring.astype(F32)

    def edge_distance(first_row):
        at, ln = iota((SPAN, tile), 0) + first_row, iota((SPAN, tile), 1)
        left, place = ln // SPAN % 2 == 0, ln % SPAN
        source = place + jnp.where(left, -EDGE, tile - REACH)
        place = place - jnp.where(left, REACH, 0)
        away = jnp.abs(at - source)
        return away.astype(F32), (away > PSFR) | (place < 0) | (place >= EDGE)

    edge_gaps = [edge_distance(0), edge_distance(tile - SPAN)]
    of_psi = iota((SPAN, tile), 1) < HALF
    if prepared:
        depth = tile + 2 * HALO
        drop = jnp.abs(iota((height, depth), 1) - HALO - iota((height, depth), 0) + PAD)
        dropped = drop > PSFR
        drop = drop.astype(F32)

    maps_ref[0] = jnp.zeros(maps_ref.shape[1:], F32)
    edges_ref[0] = jnp.zeros(edges_ref.shape[1:], F32)
    clear_sums(sum_ref)
    for copy in small:
        copy.wait()
    coded_ref[...] = segment_table(motion_ref[...], epochs, member * epochs)
    table = pltpu.make_async_copy(coded_ref, table_ref, table_sem)
    table.start()

    def weights(e):
        def profile(distance, beyond):
            scaled = distance * (1.0 / jnp.full((1, distance.shape[1]), sigma_ref[e], F32))
            return jnp.where(beyond, 0.0, jnp.exp(-0.5 * (scaled * scaled)))

        turned = profile(ring, outside)
        scale = 1.0 / jnp.sum(turned[:8], axis=1, keepdims=True)[:1]
        turned = turned * scale
        bands = profile(drop, dropped) * scale if prepared else None
        ends = [profile(*gap) * scale for gap in edge_gaps]
        result = []
        blank = jnp.zeros((tile - 2 * PAD, tile), F32)
        for m in range(2):
            value = turned if m == 0 else turned * turned
            inside = jnp.where(far, 0.0, value)
            beyond = jnp.where(far, value, 0.0)
            top, bottom = beyond[:PAD], beyond[tile - PAD :]
            if prepared:
                band = (bands if m == 0 else bands * bands).astype(BF16)
            else:
                band = jnp.concatenate([bottom, inside, top], axis=0).astype(BF16)
            if m == 1:
                inside, top, bottom = (pltpu.roll(v, HALF, 1) for v in (inside, top, bottom))
            outer = jnp.concatenate([top, blank, bottom], axis=0)
            if m == 0:
                first, last = (jnp.where(of_psi, end, 0.0) for end in ends)
            else:
                first, last = (jnp.where(of_psi, 0.0, end * end) for end in ends)
            gap_rows = jnp.zeros((tile - 2 * SPAN, tile), F32)
            edge = jnp.concatenate([first, gap_rows, last], axis=0)
            result.append((band, *(v.astype(BF16) for v in (inside, outer, edge))))
        return result

    def correlate(e):
        if prepared:
            pair = first_ref[e], second_ref[e]
        else:
            inverse = valid_ref[e].astype(F32) / second_ref[e].astype(F32)
            pair = (first_ref[e].astype(F32) * inverse).astype(BF16), inverse.astype(BF16)
        (band, inside, outer, edge), (band2, inside2, outer2, edge2) = weights(e)

        def apart(a, b):
            wide = [jnp.concatenate([a, jnp.zeros_like(a)], axis=1)]
            wide.append(jnp.concatenate([jnp.zeros_like(b), b], axis=1))
            return jnp.concatenate(wide, axis=0)

        rows = jnp.dot(
            jnp.concatenate([band, band2], axis=1), apart(*pair), preferred_element_type=F32
        ).astype(BF16)
        maps = jnp.dot(rows, apart(inside, inside2), preferred_element_type=F32)
        sides = jnp.dot(
            rows,
            jnp.concatenate(
                [
                    jnp.concatenate([outer, edge], axis=1),
                    jnp.concatenate([outer2, edge2], axis=1),
                ],
                axis=0,
            ),
            preferred_element_type=F32,
        )
        return maps[:, :tile], maps[:, tile:], sides[:, :tile], sides[:, tile:]

    def correlate_chunk(c, carry):
        for i in range(2):
            data_copy(c, i).wait()
        made = [correlate(c * CHUNK + u) for u in range(CHUNK)]
        for i in range(4):
            held, at = (maps_ref, i) if i < 3 else (edges_ref, 0)
            total = held[c * CHUNK, at]
            for u in range(CHUNK):
                total = total + made[u][i]
                held[c * CHUNK + u + 1, at] = total
        return carry

    lax.fori_loop(0, chunks, correlate_chunk, 0)
    table.wait()
    stack_edges(
        epochs, tile, block, n_epoch, n_vel, table_ref, edges_ref, sum_ref, send_ref, keep_ref
    )


def join_kernel(keep_ref, arrived_ref, own_ref, *refs):
    beyond, (far_ref, side_ref) = refs[:-2], refs[-2:]
    far_ref[...] = (keep_ref[...] + arrived_ref[...].astype(F32)).astype(BF16)
    side = own_ref[...].astype(F32)
    for edge_ref in beyond:
        side = side + edge_ref[...].astype(F32)
    side_ref[...] = side.astype(BF16)


def finish_kernel(tile, block, keep_ref, own_ref, both_ref, *refs):
    mains, (like_hbm, flux_hbm, like_ref, flux_ref, sems) = refs[:-5], refs[-5:]
    copies = []
    row, lane = iota((SIDE, tile), 0), iota((SIDE, tile), 1)
    member = lax.axis_index("vel")
    placed = []
    for m in range(2):
        at = row - m * EDGE
        used = (at >= 0) & (at < EDGE)
        for right in (1 - member, member):
            wanted = at + jnp.where(right == 1, 0, tile - EDGE) + m * HALF
            placed.append(jnp.where(used & (lane == wanted % tile), 1.0, 0.0).astype(BF16))
    for i in range(block):
        sums = []
        for m in range(2):
            rows = slice((2 * i + m) * tile, (2 * i + m + 1) * tile)
            total = keep_ref[rows] + own_ref[rows].astype(F32)
            for main_ref in mains:
                total = total + main_ref[rows].astype(F32)
            for near, put in enumerate(placed[2 * m : 2 * m + 2]):
                at = (near * block + i) * SIDE
                total = total + lax.dot_general(
                    both_ref[at : at + SIDE], put, (((0,), (0,)), ((), ())),
                    preferred_element_type=F32,
                )
            sums.append(total)
        root = lax.rsqrt(jnp.maximum(pltpu.roll(sums[1], HALF, 1), phi_floor))
        like = sums[0] * root
        like_ref[i] = like
        flux_ref[i] = like * root
        for j, (source, target) in enumerate(((like_ref, like_hbm), (flux_ref, flux_hbm))):
            copies.append(pltpu.make_async_copy(source.at[i], target.at[i], sems.at[2 * i + j]))
            copies[-1].start()
    for copy in copies:
        copy.wait()


def move(block, axis, distance):
    count = lax.axis_size(axis)
    return lax.ppermute(block, axis, [(i, (i + distance) % count) for i in range(count)])


def beside(block, step, keep):
    count = lax.axis_size("sky")
    device = [(q - GRID_X // 2) % count for q in range(count)]
    route = [(device[q], device[q + step]) for q in range(count) if keep(q)]
    return lax.ppermute(block, "sky", route)


def beside_by_member(block):
    n_sky = lax.axis_size("sky")
    device = [(q - GRID_X // 2) % n_sky for q in range(n_sky)]
    route = []
    for q in range(n_sky):
        for v, step in ((0, 1), (1, -1)):
            if 0 <= q % GRID_X + step < GRID_X:
                route.append((device[q] * 2 + v, device[q + step] * 2 + v))
    return lax.ppermute(block, ("sky", "vel"), route)


def on_device(images, variances, valid, psf_sigma, offsets):
    epochs, tile = images.shape[0], images.shape[-1]
    n_epoch, n_vel = lax.axis_size("epoch"), lax.axis_size("vel")
    n_sky = lax.axis_size("sky")
    assert n_vel == 2 and epochs % CHUNK == 0
    block = VELS // (n_epoch * n_vel)
    first, second = images[:, 0], variances[:, 0]
    prepared = n_sky > GRID_X
    if prepared:
        usable = valid[:, 0].astype(F32)[:, None, None]
        scaled = (first.astype(F32) / second.astype(F32) * usable).astype(BF16)
        inverse = (usable / second.astype(F32)).astype(BF16)
        pair = jnp.stack([scaled, inverse])
        above = beside(pair[:, :, tile - HALO :], GRID_X, lambda q: q + GRID_X < n_sky)
        below = beside(pair[:, :, :HALO], -GRID_X, lambda q: q >= GRID_X)
        first, second = jnp.concatenate([above, pair, below], axis=2)

    main_rows = block * 2 * tile
    edge_rows = block * SIDE
    hbm = pl.BlockSpec(memory_space=pltpu.HBM)
    vmem = pl.BlockSpec(memory_space=pltpu.VMEM)
    params = pltpu.CompilerParams(vmem_limit_bytes=16 * 1024 * 1024)
    small_params = pltpu.CompilerParams(vmem_limit_bytes=8 * 1024 * 1024)
    group_rows = n_vel * edge_rows
    operands = (psf_sigma, valid[:, 0], offsets, first, second)
    send_edges, keep_edges, maps, table = pl.pallas_call(
        functools.partial(stack_kernel, epochs, tile, block, n_epoch, n_vel, prepared),
        out_shape=(
            jax.ShapeDtypeStruct((n_epoch * group_rows, tile), BF16),
            jax.ShapeDtypeStruct((n_epoch * group_rows, tile), F32),
            jax.ShapeDtypeStruct((epochs + 1, 3, tile + 2 * PAD, tile), F32),
            jax.ShapeDtypeStruct(offsets.shape[1:], jnp.int32),
        ),
        in_specs=[hbm] * 5,
        out_specs=(vmem,) * 4,
        scratch_shapes=[
            pltpu.SMEM((epochs,), F32),
            pltpu.SMEM((epochs,), jnp.int32),
            pltpu.VMEM(offsets.shape, jnp.int32),
            pltpu.SMEM(offsets.shape[1:], jnp.int32),
            pltpu.VMEM(first.shape, BF16),
            pltpu.VMEM(second.shape, BF16),
            pltpu.VMEM((epochs + 1, 1, tile + 2 * PAD, tile), F32),
            pltpu.VMEM((VELS + 1, tile, tile), F32),
            pltpu.SemaphoreType.DMA((3,)),
            pltpu.SemaphoreType.DMA((2 * (epochs // CHUNK),)),
            pltpu.SemaphoreType.DMA,
        ],
        compiler_params=params,
    )(*(pltpu.with_memory_space_constraint(a, pltpu.HBM) for a in operands))
    edges = (keep_edges + move(send_edges, "vel", 1).astype(F32)).astype(BF16)
    beyond = [
        move(edges[(d - 1) * group_rows : d * group_rows], "epoch", d) for d in range(1, n_epoch)
    ]

    def main_sums(ranks, sent, kept, maps, hand_on):
        rows = (ranks[1] - ranks[0]) * main_rows
        results = [jax.ShapeDtypeStruct((rows, tile), BF16)] * sent
        results += [jax.ShapeDtypeStruct((rows, tile), F32)] * kept
        aliases = {1: len(results)} if hand_on else {}
        results += [jax.ShapeDtypeStruct(maps.shape, F32)] * hand_on
        slots = (sent + kept) * (ranks[1] - ranks[0]) * block
        return pl.pallas_call(
            functools.partial(
                main_kernel, epochs, tile, block, n_epoch, n_vel, ranks, sent, kept
            ),
            out_shape=results,
            in_specs=[pl.BlockSpec(memory_space=pltpu.SMEM), vmem],
            out_specs=[vmem] * len(results),
            input_output_aliases=aliases,
            scratch_shapes=[pltpu.VMEM((slots + 1, 2, tile, tile), F32)],
            compiler_params=small_params,
        )(table, maps)

    far_ranks, own_ranks = (0, n_epoch - 1), (n_epoch - 1, n_epoch)
    send, maps = main_sums(far_ranks, 1, 0, maps, 1)
    keep, maps = main_sums(far_ranks, 0, 1, maps, 1)
    far, side = pl.pallas_call(
        join_kernel,
        out_shape=(
            jax.ShapeDtypeStruct(keep.shape, BF16),
            jax.ShapeDtypeStruct((group_rows, tile), BF16),
        ),
        in_specs=[vmem] * (3 + len(beyond)),
        out_specs=(vmem, vmem),
        compiler_params=small_params,
    )(keep, move(send, "vel", 1), edges[(n_epoch - 1) * group_rows :], *beyond)
    side = beside_by_member(side)
    mains = [
        move(far[(d - 1) * main_rows : d * main_rows], "epoch", d) for d in range(1, n_epoch)
    ]

    def pass_own(send, side):
        arrived = move(send, "vel", 1)
        is_first = lax.axis_index("vel") == 0
        near = jnp.where(is_first, side[:edge_rows], side[edge_rows:])
        other = jnp.where(is_first, side[edge_rows:], side[:edge_rows])
        return arrived, jnp.concatenate([near, move(other, "vel", 1)])

    send, keep = main_sums(own_ranks, 1, 1, maps, 0)
    taken = lax.axis_index("sky") < n_sky
    arrived, side = lax.cond(taken, pass_own, lambda send, side: (send, side), send, side)

    shape = jax.ShapeDtypeStruct((block, tile, tile), F32)
    likelihood, flux = pl.pallas_call(
        functools.partial(finish_kernel, tile, block),
        out_shape=(shape, shape),
        in_specs=[vmem] * (3 + len(mains)),
        out_specs=(hbm, hbm),
        scratch_shapes=[
            pltpu.VMEM(shape.shape, F32),
            pltpu.VMEM(shape.shape, F32),
            pltpu.SemaphoreType.DMA((2 * block,)),
        ],
        compiler_params=params,
    )(keep, arrived, side, *mains)
    return likelihood[:, None], flux[:, None]


def solution(mesh):
    placed = (
        P(("epoch", "vel"), ("field", "sky"), None, None),
        P(("epoch", "vel"), ("field", "sky"), None, None),
        P(("epoch", "vel"), ("field", "sky")),
        P(("field", "epoch", "vel")),
        P(None, None, "epoch"),
    )
    return jax.shard_map(
        on_device,
        mesh=mesh,
        in_specs=placed,
        out_specs=(
            P(("epoch", "vel"), ("field", "sky"), None, None),
            P(("epoch", "vel"), ("field", "sky"), None, None),
        ),
        check_vma=False,
    )
```

```python
import functools

import jax
import jax.numpy as jnp
from jax import lax
from jax.experimental import pallas as pl
from jax.experimental.pallas import tpu as pltpu
from jax.sharding import PartitionSpec as P

VELS = 16
REACH = 12
PSFR = 7
GRID_X = 4

phi_floor = 0.25

F32 = jnp.float32
BF16 = jnp.bfloat16
EDGE = REACH + PSFR
PAD = 16
HALO = 32
SIDE = 48
HALF = 64
SPAN = 32
CHUNK = 4
STEP = 8


def iota(shape, axis):
    return lax.broadcasted_iota(jnp.int32, shape, axis)


def pick_edges(tile, first_left):
    row, lane = iota((2 * SIDE, tile), 0), iota((2 * SIDE, tile), 1)
    within = row % SIDE
    left = (row >= SIDE) != first_left
    wanted = within % EDGE + jnp.where(left, 0, SPAN + REACH) + jnp.where(within < EDGE, 0, HALF)
    return jnp.where((within < 2 * EDGE) & (lane == wanted), 1.0, 0.0).astype(BF16)


def segment_table(motion, epochs, first):
    code = (motion[0] + REACH) * 32 + motion[1] + REACH
    total = code.shape[1]
    lane = iota(code.shape, 1)
    later = jnp.roll(code, -1, axis=1) if total < 128 else pltpu.roll(code, total - 1, 1)
    stop = first + epochs
    end = jnp.where((later != code) | (lane == stop - 1), lane + 1, total)
    reach = 1
    while reach < epochs:
        end = jnp.minimum(end, jnp.where(lane + reach < total, jnp.roll(end, -reach, axis=1), total))
        reach *= 2
    return jnp.clip(end - first, 0, epochs) * 1024 + code


def over_segments(epochs, table_ref, maps_ref, chosen, slots, k_of, add):
    member = lax.axis_index("vel")
    row = iota((8, maps_ref.shape[-1]), 0)

    def segment(slot, e):
        word = table_ref[k_of(slot), member * epochs + e]
        e_end = word >> 10
        start = PAD - REACH + ((word >> 5) & 31)
        dx = (word & 31) - REACH
        tile = maps_ref.shape[-1]
        shift = jnp.where(dx > 0, tile - dx, -dx)
        base = pl.multiple_of((start // 8) * 8, 8)
        above = start - base
        turn = lax.rem(8 - above, 8)
        same = row < 8 - above
        put = add(slot, dx)

        def rows_at(r):
            window = pl.ds(base + r, 8)
            return [
                pltpu.roll(maps_ref[e_end, m, window] - maps_ref[e, m, window], turn, 0)
                for m in chosen
            ]

        upper = rows_at(0)
        for r in range(0, tile, 8):
            lower = rows_at(r + 8)
            put(r, [pltpu.roll(jnp.where(same, a, b), shift, 1) for a, b in zip(upper, lower)])
            upper = lower
        ended = e_end >= epochs
        return jnp.where(ended, jnp.minimum(slot + 1, slots), slot), jnp.where(ended, 0, e_end)

    def some_segments(state):
        for _ in range(STEP):
            state = segment(*state)
        return state

    start = (jnp.int32(0), jnp.int32(0))
    lax.while_loop(lambda state: state[0] < slots, some_segments, start)


def clear_sums(sum_ref):
    def clear(slot, carry):
        sum_ref[slot] = jnp.zeros(sum_ref.shape[1:], F32)
        return carry

    lax.fori_loop(0, sum_ref.shape[0] - 1, clear, 0)


def stack_edges(
    epochs, tile, block, n_epoch, n_vel, table_ref, maps_ref, sum_ref, send_ref, keep_ref
):
    column = lax.axis_index("epoch")
    member = lax.axis_index("vel")
    lane = iota((8, tile), 1)
    place = lane % SPAN - jnp.where(lane // SPAN % 2 == 0, REACH, 0)

    def add(slot, dx):
        held = (place + dx >= 0) & (place + dx < EDGE)

        def put(r, pieces):
            sum_ref[slot, r : r + 8] += jnp.where(held, pieces[0], 0.0)

        return put

    first_k = (column + 1) * n_vel * block
    over_segments(
        epochs, table_ref, maps_ref, (0,), VELS, lambda slot: lax.rem(first_k + slot, VELS), add
    )

    selector = pick_edges(tile, member == 1)

    def pack(group, carry):
        for i in range(block):
            slot = group * block + i
            packed = lax.dot_general(
                selector, sum_ref[slot].astype(BF16), (((1,), (1,)), ((), ())),
                preferred_element_type=F32,
            )
            rows = pl.ds(slot * SIDE, SIDE)
            keep_ref[rows] = packed[:SIDE]
            send_ref[rows] = packed[SIDE:].astype(BF16)
        return carry

    lax.fori_loop(0, VELS // block, pack, 0)


def main_kernel(epochs, tile, block, n_epoch, n_vel, ranks, sent, kept, table_ref, maps_ref, *refs):
    sum_ref = refs[-1]
    clear_sums(sum_ref)
    column = lax.axis_index("epoch")
    member = lax.axis_index("vel")
    lane = iota((8, tile), 1)
    turned = (lane + HALF) % tile
    share = (ranks[1] - ranks[0]) * block
    slots = (sent + kept) * share

    def k_of(slot):
        whose = jnp.where(slot < sent * share, 1 - member, member)
        rank = ranks[0] + lax.rem(slot, share) // block
        owner = lax.rem(column + 1 + rank, n_epoch)
        return (owner * n_vel + whose) * block + lax.rem(slot, block)

    def add(slot, dx):
        out = (lane + dx < 0) | (lane + dx >= tile)
        out_turned = (turned + dx < 0) | (turned + dx >= tile)

        def put(r, pieces):
            psi, phi, side = pieces
            sum_ref[slot, 0, r : r + 8] += jnp.where(out, side, psi)
            sum_ref[slot, 1, r : r + 8] += jnp.where(out_turned, side, phi)

        return put

    over_segments(epochs, table_ref, maps_ref, (0, 1, 2), slots, k_of, add)

    def write(target_ref, first):
        def one(j, carry):
            rows = pl.ds(j * 2 * tile, 2 * tile)
            value = sum_ref[first + j].reshape(2 * tile, tile)
            target_ref[rows] = value.astype(target_ref.dtype)
            return carry

        lax.fori_loop(0, share, one, 0)

    if sent:
        write(refs[0], 0)
    if kept:
        write(refs[sent], sent * share)


def stack_kernel(
    epochs, tile, block, n_epoch, n_vel, prepared,
    taken_ref, sigma_hbm, valid_hbm, motion_hbm, first_hbm, second_hbm,
    send_ref, keep_ref, maps_ref, coded_ref,
    sigma_ref, valid_ref, motion_ref, table_ref, first_ref, second_ref, edges_ref, sum_ref,
    small_sems, data_sems, table_sem,
):
    height = tile + 2 * PAD
    chunks = epochs // CHUNK
    member = lax.axis_index("vel")

    small = [
        pltpu.make_async_copy(motion_hbm, motion_ref, small_sems.at[0]),
        pltpu.make_async_copy(sigma_hbm, sigma_ref, small_sems.at[1]),
        pltpu.make_async_copy(valid_hbm, valid_ref, small_sems.at[2]),
    ]
    for copy in small:
        copy.start()

    def data_copy(c, i):
        at = pl.ds(c * CHUNK, CHUNK)
        source, target = ((first_hbm, first_ref), (second_hbm, second_ref))[i]
        return pltpu.make_async_copy(source.at[at], target.at[at], data_sems.at[2 * c + i])

    for c in range(chunks):
        for i in range(2):
            data_copy(c, i).start()

    row, lane = iota((tile, tile), 0), iota((tile, tile), 1)
    gap = jnp.abs(row - lane)
    ring = jnp.minimum(gap, tile - gap)
    outside = ring > PSFR
    far = gap >= tile // 2
    ring = ring.astype(F32)

    def edge_distance(first_row):
        at, ln = iota((SPAN, tile), 0) + first_row, iota((SPAN, tile), 1)
        left, place = ln // SPAN % 2 == 0, ln % SPAN
        source = place + jnp.where(left, -EDGE, tile - REACH)
        place = place - jnp.where(left, REACH, 0)
        away = jnp.abs(at - source)
        return away.astype(F32), (away > PSFR) | (place < 0) | (place >= EDGE)

    edge_gaps = [edge_distance(0), edge_distance(tile - SPAN)]
    of_psi = iota((SPAN, tile), 1) < HALF
    if prepared:
        depth = tile + 2 * HALO
        drop = jnp.abs(iota((height, depth), 1) - HALO - iota((height, depth), 0) + PAD)
        dropped = drop > PSFR
        drop = drop.astype(F32)

    maps_ref[0] = jnp.zeros(maps_ref.shape[1:], F32)
    edges_ref[0] = jnp.zeros(edges_ref.shape[1:], F32)
    clear_sums(sum_ref)
    for copy in small:
        copy.wait()
    coded_ref[...] = segment_table(motion_ref[...], epochs, member * epochs)
    table = pltpu.make_async_copy(coded_ref, table_ref, table_sem)
    table.start()

    def weights(e):
        def profile(distance, beyond):
            scaled = distance * (1.0 / jnp.full((1, distance.shape[1]), sigma_ref[e], F32))
            return jnp.where(beyond, 0.0, jnp.exp(-0.5 * (scaled * scaled)))

        turned = profile(ring, outside)
        scale = 1.0 / jnp.sum(turned[:8], axis=1, keepdims=True)[:1]
        turned = turned * scale
        bands = profile(drop, dropped) * scale if prepared else None
        ends = [profile(*gap) * scale for gap in edge_gaps]
        result = []
        blank = jnp.zeros((tile - 2 * PAD, tile), F32)
        for m in range(2):
            value = turned if m == 0 else turned * turned
            inside = jnp.where(far, 0.0, value)
            beyond = jnp.where(far, value, 0.0)
            top, bottom = beyond[:PAD], beyond[tile - PAD :]
            if prepared:
                band = (bands if m == 0 else bands * bands).astype(BF16)
            else:
                band = jnp.concatenate([bottom, inside, top], axis=0).astype(BF16)
            if m == 1:
                inside, top, bottom = (pltpu.roll(v, HALF, 1) for v in (inside, top, bottom))
            outer = jnp.concatenate([top, blank, bottom], axis=0)
            if m == 0:
                first, last = (jnp.where(of_psi, end, 0.0) for end in ends)
            else:
                first, last = (jnp.where(of_psi, 0.0, end * end) for end in ends)
            gap_rows = jnp.zeros((tile - 2 * SPAN, tile), F32)
            edge = jnp.concatenate([first, gap_rows, last], axis=0)
            result.append((band, *(v.astype(BF16) for v in (inside, outer, edge))))
        return result

    def correlate(e):
        if prepared:
            pair = first_ref[e], second_ref[e]
        else:
            inverse = valid_ref[e].astype(F32) / second_ref[e].astype(F32)
            pair = (first_ref[e].astype(F32) * inverse).astype(BF16), inverse.astype(BF16)
        (band, inside, outer, edge), (band2, inside2, outer2, edge2) = weights(e)

        def apart(a, b):
            wide = [jnp.concatenate([a, jnp.zeros_like(a)], axis=1)]
            wide.append(jnp.concatenate([jnp.zeros_like(b), b], axis=1))
            return jnp.concatenate(wide, axis=0)

        rows = jnp.dot(
            jnp.concatenate([band, band2], axis=1), apart(*pair), preferred_element_type=F32
        ).astype(BF16)
        maps = jnp.dot(rows, apart(inside, inside2), preferred_element_type=F32)
        sides = jnp.dot(
            rows,
            jnp.concatenate(
                [
                    jnp.concatenate([outer, edge], axis=1),
                    jnp.concatenate([outer2, edge2], axis=1),
                ],
                axis=0,
            ),
            preferred_element_type=F32,
        )
        return maps[:, :tile], maps[:, tile:], sides[:, :tile], sides[:, tile:]

    def correlate_chunk(c, carry):
        for i in range(2):
            data_copy(c, i).wait()
        made = [correlate(c * CHUNK + u) for u in range(CHUNK)]
        for i in range(4):
            held, at = (maps_ref, i) if i < 3 else (edges_ref, 0)
            total = held[c * CHUNK, at]
            for u in range(CHUNK):
                total = total + made[u][i]
                held[c * CHUNK + u + 1, at] = total
        return carry

    lax.fori_loop(0, chunks, correlate_chunk, 0)
    table.wait()
    stack_edges(
        epochs, tile, block, n_epoch, n_vel, table_ref, edges_ref, sum_ref, send_ref, keep_ref
    )


def join_kernel(keep_ref, arrived_ref, own_ref, *refs):
    beyond, (far_ref, side_ref) = refs[:-2], refs[-2:]
    far_ref[...] = (keep_ref[...] + arrived_ref[...].astype(F32)).astype(BF16)
    side = own_ref[...].astype(F32)
    for edge_ref in beyond:
        side = side + edge_ref[...].astype(F32)
    side_ref[...] = side.astype(BF16)


def finish_kernel(tile, block, keep_ref, own_ref, both_ref, *refs):
    mains, (like_hbm, flux_hbm, like_ref, flux_ref, sems) = refs[:-5], refs[-5:]
    copies = []
    row, lane = iota((SIDE, tile), 0), iota((SIDE, tile), 1)
    member = lax.axis_index("vel")
    placed = []
    for m in range(2):
        at = row - m * EDGE
        used = (at >= 0) & (at < EDGE)
        for right in (1 - member, member):
            wanted = at + jnp.where(right == 1, 0, tile - EDGE) + m * HALF
            placed.append(jnp.where(used & (lane == wanted % tile), 1.0, 0.0).astype(BF16))
    for i in range(block):
        sums = []
        for m in range(2):
            rows = slice((2 * i + m) * tile, (2 * i + m + 1) * tile)
            total = keep_ref[rows] + own_ref[rows].astype(F32)
            for main_ref in mains:
                total = total + main_ref[rows].astype(F32)
            for near, put in enumerate(placed[2 * m : 2 * m + 2]):
                at = (near * block + i) * SIDE
                total = total + lax.dot_general(
                    both_ref[at : at + SIDE], put, (((0,), (0,)), ((), ())),
                    preferred_element_type=F32,
                )
            sums.append(total)
        root = lax.rsqrt(jnp.maximum(pltpu.roll(sums[1], HALF, 1), phi_floor))
        like = sums[0] * root
        like_ref[i] = like
        flux_ref[i] = like * root
        for j, (source, target) in enumerate(((like_ref, like_hbm), (flux_ref, flux_hbm))):
            copies.append(pltpu.make_async_copy(source.at[i], target.at[i], sems.at[2 * i + j]))
            copies[-1].start()
    for copy in copies:
        copy.wait()


def move(block, axis, distance):
    count = lax.axis_size(axis)
    return lax.ppermute(block, axis, [(i, (i + distance) % count) for i in range(count)])


def beside(block, step, keep):
    count = lax.axis_size("sky")
    device = [(q - GRID_X // 2) % count for q in range(count)]
    route = [(device[q], device[q + step]) for q in range(count) if keep(q)]
    return lax.ppermute(block, "sky", route)


def beside_by_member(block):
    n_sky = lax.axis_size("sky")
    device = [(q - GRID_X // 2) % n_sky for q in range(n_sky)]
    route = []
    for q in range(n_sky):
        for v, step in ((0, 1), (1, -1)):
            if 0 <= q % GRID_X + step < GRID_X:
                route.append((device[q] * 2 + v, device[q + step] * 2 + v))
    return lax.ppermute(block, ("sky", "vel"), route)


def on_device(images, variances, valid, psf_sigma, offsets):
    epochs, tile = images.shape[0], images.shape[-1]
    n_epoch, n_vel = lax.axis_size("epoch"), lax.axis_size("vel")
    n_sky = lax.axis_size("sky")
    assert n_vel == 2 and epochs % CHUNK == 0
    block = VELS // (n_epoch * n_vel)
    first, second = images[:, 0], variances[:, 0]
    prepared = n_sky > GRID_X
    if prepared:
        usable = valid[:, 0].astype(F32)[:, None, None]
        scaled = (first.astype(F32) / second.astype(F32) * usable).astype(BF16)
        inverse = (usable / second.astype(F32)).astype(BF16)
        pair = jnp.stack([scaled, inverse])
        above = beside(pair[:, :, tile - HALO :], GRID_X, lambda q: q + GRID_X < n_sky)
        below = beside(pair[:, :, :HALO], -GRID_X, lambda q: q >= GRID_X)
        first, second = jnp.concatenate([above, pair, below], axis=2)

    main_rows = block * 2 * tile
    edge_rows = block * SIDE
    hbm = pl.BlockSpec(memory_space=pltpu.HBM)
    vmem = pl.BlockSpec(memory_space=pltpu.VMEM)
    params = pltpu.CompilerParams(vmem_limit_bytes=16 * 1024 * 1024)
    small_params = pltpu.CompilerParams(vmem_limit_bytes=8 * 1024 * 1024)
    group_rows = n_vel * edge_rows
    operands = (psf_sigma, valid[:, 0], offsets, first, second)
    taken = lax.axis_index("sky") < n_sky
    flag = taken.astype(jnp.int32)[None]
    send_edges, keep_edges, maps, table = pl.pallas_call(
        functools.partial(stack_kernel, epochs, tile, block, n_epoch, n_vel, prepared),
        out_shape=(
            jax.ShapeDtypeStruct((n_epoch * group_rows, tile), BF16),
            jax.ShapeDtypeStruct((n_epoch * group_rows, tile), F32),
            jax.ShapeDtypeStruct((epochs + 1, 3, tile + 2 * PAD, tile), F32),
            jax.ShapeDtypeStruct(offsets.shape[1:], jnp.int32),
        ),
        in_specs=[pl.BlockSpec(memory_space=pltpu.SMEM)] + [hbm] * 5,
        out_specs=(vmem,) * 4,
        scratch_shapes=[
            pltpu.SMEM((epochs,), F32),
            pltpu.SMEM((epochs,), jnp.int32),
            pltpu.VMEM(offsets.shape, jnp.int32),
            pltpu.SMEM(offsets.shape[1:], jnp.int32),
            pltpu.VMEM(first.shape, BF16),
            pltpu.VMEM(second.shape, BF16),
            pltpu.VMEM((epochs + 1, 1, tile + 2 * PAD, tile), F32),
            pltpu.VMEM((VELS + 1, tile, tile), F32),
            pltpu.SemaphoreType.DMA((3,)),
            pltpu.SemaphoreType.DMA((2 * (epochs // CHUNK),)),
            pltpu.SemaphoreType.DMA,
        ],
        compiler_params=params,
    )(flag, *(pltpu.with_memory_space_constraint(a, pltpu.HBM) for a in operands))
    edges = (keep_edges + move(send_edges, "vel", 1).astype(F32)).astype(BF16)
    beyond = [
        move(edges[(d - 1) * group_rows : d * group_rows], "epoch", d) for d in range(1, n_epoch)
    ]

    def main_sums(ranks, sent, kept, maps, hand_on):
        rows = (ranks[1] - ranks[0]) * main_rows
        results = [jax.ShapeDtypeStruct((rows, tile), BF16)] * sent
        results += [jax.ShapeDtypeStruct((rows, tile), F32)] * kept
        aliases = {1: len(results)} if hand_on else {}
        results += [jax.ShapeDtypeStruct(maps.shape, F32)] * hand_on
        slots = (sent + kept) * (ranks[1] - ranks[0]) * block
        return pl.pallas_call(
            functools.partial(
                main_kernel, epochs, tile, block, n_epoch, n_vel, ranks, sent, kept
            ),
            out_shape=results,
            in_specs=[pl.BlockSpec(memory_space=pltpu.SMEM), vmem],
            out_specs=[vmem] * len(results),
            input_output_aliases=aliases,
            scratch_shapes=[pltpu.VMEM((slots + 1, 2, tile, tile), F32)],
            compiler_params=small_params,
        )(table, maps)

    far_ranks, own_ranks = (0, n_epoch - 1), (n_epoch - 1, n_epoch)
    send, maps = main_sums(far_ranks, 1, 0, maps, 1)
    keep, maps = main_sums(far_ranks, 0, 1, maps, 1)
    far, side = pl.pallas_call(
        join_kernel,
        out_shape=(
            jax.ShapeDtypeStruct(keep.shape, BF16),
            jax.ShapeDtypeStruct((group_rows, tile), BF16),
        ),
        in_specs=[vmem] * (3 + len(beyond)),
        out_specs=(vmem, vmem),
        compiler_params=small_params,
    )(keep, move(send, "vel", 1), edges[(n_epoch - 1) * group_rows :], *beyond)
    side = beside_by_member(side)
    mains = [
        move(far[(d - 1) * main_rows : d * main_rows], "epoch", d) for d in range(1, n_epoch)
    ]

    def pass_own(send, side):
        arrived = move(send, "vel", 1)
        is_first = lax.axis_index("vel") == 0
        near = jnp.where(is_first, side[:edge_rows], side[edge_rows:])
        other = jnp.where(is_first, side[edge_rows:], side[:edge_rows])
        return arrived, jnp.concatenate([near, move(other, "vel", 1)])

    send, keep = main_sums(own_ranks, 1, 1, maps, 0)
    arrived, side = lax.cond(taken, pass_own, lambda send, side: (send, side), send, side)

    shape = jax.ShapeDtypeStruct((block, tile, tile), F32)
    likelihood, flux = pl.pallas_call(
        functools.partial(finish_kernel, tile, block),
        out_shape=(shape, shape),
        in_specs=[vmem] * (3 + len(mains)),
        out_specs=(hbm, hbm),
        scratch_shapes=[
            pltpu.VMEM(shape.shape, F32),
            pltpu.VMEM(shape.shape, F32),
            pltpu.SemaphoreType.DMA((2 * block,)),
        ],
        compiler_params=params,
    )(keep, arrived, side, *mains)
    return likelihood[:, None], flux[:, None]


def solution(mesh):
    placed = (
        P(("epoch", "vel"), ("field", "sky"), None, None),
        P(("epoch", "vel"), ("field", "sky"), None, None),
        P(("epoch", "vel"), ("field", "sky")),
        P(("field", "epoch", "vel")),
        P(None, None, "epoch"),
    )
    return jax.shard_map(
        on_device,
        mesh=mesh,
        in_specs=placed,
        out_specs=(
            P(("epoch", "vel"), ("field", "sky"), None, None),
            P(("epoch", "vel"), ("field", "sky"), None, None),
        ),
        check_vma=False,
    )
```

```python
import functools

import jax
import jax.numpy as jnp
from jax import lax
from jax.experimental import pallas as pl
from jax.experimental.pallas import tpu as pltpu
from jax.sharding import PartitionSpec as P

VELS = 16
REACH = 12
PSFR = 7
GRID_X = 4

phi_floor = 0.25

F32 = jnp.float32
BF16 = jnp.bfloat16
EDGE = REACH + PSFR
PAD = 16
HALO = 32
SIDE = 48
HALF = 64
SPAN = 32
CHUNK = 4
STEP = 8
EDGE_STEP = 16
PIECE = 11


def iota(shape, axis):
    return lax.broadcasted_iota(jnp.int32, shape, axis)


def pick_edges(tile, first_left):
    row, lane = iota((2 * SIDE, tile), 0), iota((2 * SIDE, tile), 1)
    within = row % SIDE
    left = (row >= SIDE) != first_left
    wanted = within % EDGE + jnp.where(left, 0, SPAN + REACH) + jnp.where(within < EDGE, 0, HALF)
    return jnp.where((within < 2 * EDGE) & (lane == wanted), 1.0, 0.0).astype(BF16)


def segment_table(motion, epochs, first):
    code = (motion[0] + REACH) * 32 + motion[1] + REACH
    total = code.shape[1]
    lane = iota(code.shape, 1)
    later = jnp.roll(code, -1, axis=1) if total < 128 else pltpu.roll(code, total - 1, 1)
    stop = first + epochs
    end = jnp.where((later != code) | (lane == stop - 1), lane + 1, total)
    reach = 1
    while reach < epochs:
        end = jnp.minimum(end, jnp.where(lane + reach < total, jnp.roll(end, -reach, axis=1), total))
        reach *= 2
    return jnp.clip(end - first, 0, epochs) * 1024 + code


def over_segments(epochs, table_ref, maps_ref, chosen, slots, k_of, step, add):
    member = lax.axis_index("vel")
    row = iota((8, maps_ref.shape[-1]), 0)

    def segment(slot, e):
        word = table_ref[k_of(slot), member * epochs + e]
        e_end = word >> 10
        start = PAD - REACH + ((word >> 5) & 31)
        dx = (word & 31) - REACH
        tile = maps_ref.shape[-1]
        shift = jnp.where(dx > 0, tile - dx, -dx)
        base = pl.multiple_of((start // 8) * 8, 8)
        above = start - base
        turn = lax.rem(8 - above, 8)
        same = row < 8 - above
        put = add(slot, dx)

        def rows_at(r):
            window = pl.ds(base + r, 8)
            return [
                pltpu.roll(maps_ref[e_end, m, window] - maps_ref[e, m, window], turn, 0)
                for m in chosen
            ]

        upper = rows_at(0)
        for r in range(0, tile, 8):
            lower = rows_at(r + 8)
            put(r, [pltpu.roll(jnp.where(same, a, b), shift, 1) for a, b in zip(upper, lower)])
            upper = lower
        ended = e_end >= epochs
        return jnp.where(ended, jnp.minimum(slot + 1, slots), slot), jnp.where(ended, 0, e_end)

    def some_segments(state):
        for _ in range(step):
            state = segment(*state)
        return state

    start = (jnp.int32(0), jnp.int32(0))
    lax.while_loop(lambda state: state[0] < slots, some_segments, start)


def clear_sums(sum_ref):
    def clear(slot, carry):
        sum_ref[slot] = jnp.zeros(sum_ref.shape[1:], F32)
        return carry

    lax.fori_loop(0, sum_ref.shape[0] - 1, clear, 0)


def stack_edges(
    epochs, tile, block, n_epoch, n_vel, table_ref, maps_ref, sum_ref, send_ref, keep_ref
):
    column = lax.axis_index("epoch")
    member = lax.axis_index("vel")
    lane = iota((8, tile), 1)
    place = lane % SPAN - jnp.where(lane // SPAN % 2 == 0, REACH, 0)

    def add(slot, dx):
        held = (place + dx >= 0) & (place + dx < EDGE)

        def put(r, pieces):
            sum_ref[slot, r : r + 8] += jnp.where(held, pieces[0], 0.0)

        return put

    first_k = (column + 1) * n_vel * block
    over_segments(
        epochs, table_ref, maps_ref, (0,), VELS, lambda slot: lax.rem(first_k + slot, VELS),
        EDGE_STEP, add,
    )

    selector = pick_edges(tile, member == 1)

    def pack(group, carry):
        for i in range(block):
            slot = group * block + i
            packed = lax.dot_general(
                selector, sum_ref[slot].astype(BF16), (((1,), (1,)), ((), ())),
                preferred_element_type=F32,
            )
            rows = pl.ds(slot * SIDE, SIDE)
            keep_ref[rows] = packed[:SIDE]
            send_ref[rows] = packed[SIDE:].astype(BF16)
        return carry

    lax.fori_loop(0, VELS // block, pack, 0)


def main_kernel(epochs, tile, block, n_epoch, n_vel, ranks, sent, kept, table_ref, maps_ref, *refs):
    sum_ref = refs[-1]
    clear_sums(sum_ref)
    column = lax.axis_index("epoch")
    member = lax.axis_index("vel")
    lane = iota((8, tile), 1)
    turned = (lane + HALF) % tile
    share = (ranks[1] - ranks[0]) * block
    slots = (sent + kept) * share

    def k_of(slot):
        whose = jnp.where(slot < sent * share, 1 - member, member)
        rank = ranks[0] + lax.rem(slot, share) // block
        owner = lax.rem(column + 1 + rank, n_epoch)
        return (owner * n_vel + whose) * block + lax.rem(slot, block)

    def add(slot, dx):
        out = (lane + dx < 0) | (lane + dx >= tile)
        out_turned = (turned + dx < 0) | (turned + dx >= tile)

        def put(r, pieces):
            psi, phi, side = pieces
            sum_ref[slot, 0, r : r + 8] += jnp.where(out, side, psi)
            sum_ref[slot, 1, r : r + 8] += jnp.where(out_turned, side, phi)

        return put

    over_segments(epochs, table_ref, maps_ref, (0, 1, 2), slots, k_of, STEP, add)

    def write(target_ref, first):
        def one(j, carry):
            rows = pl.ds(j * 2 * tile, 2 * tile)
            value = sum_ref[first + j].reshape(2 * tile, tile)
            target_ref[rows] = value.astype(target_ref.dtype)
            return carry

        lax.fori_loop(0, share, one, 0)

    if sent:
        write(refs[0], 0)
    if kept:
        write(refs[sent], sent * share)


def stack_kernel(
    epochs, tile, block, n_epoch, n_vel, prepared,
    taken_ref, sigma_hbm, valid_hbm, motion_hbm, first_hbm, second_hbm,
    send_ref, keep_ref, maps_ref, coded_ref,
    sigma_ref, valid_ref, motion_ref, table_ref, first_ref, second_ref, edges_ref, sum_ref,
    small_sems, data_sems, table_sem,
):
    height = tile + 2 * PAD
    chunks = epochs // CHUNK
    member = lax.axis_index("vel")

    small = [
        pltpu.make_async_copy(motion_hbm, motion_ref, small_sems.at[0]),
        pltpu.make_async_copy(sigma_hbm, sigma_ref, small_sems.at[1]),
        pltpu.make_async_copy(valid_hbm, valid_ref, small_sems.at[2]),
    ]
    for copy in small:
        copy.start()

    def data_copy(c, i):
        at = pl.ds(c * CHUNK, CHUNK)
        source, target = ((first_hbm, first_ref), (second_hbm, second_ref))[i]
        return pltpu.make_async_copy(source.at[at], target.at[at], data_sems.at[2 * c + i])

    for c in range(chunks):
        for i in range(2):
            data_copy(c, i).start()

    row, lane = iota((tile, tile), 0), iota((tile, tile), 1)
    gap = jnp.abs(row - lane)
    ring = jnp.minimum(gap, tile - gap)
    outside = ring > PSFR
    far = gap >= tile // 2
    ring = ring.astype(F32)

    def edge_distance(first_row):
        at, ln = iota((SPAN, tile), 0) + first_row, iota((SPAN, tile), 1)
        left, place = ln // SPAN % 2 == 0, ln % SPAN
        source = place + jnp.where(left, -EDGE, tile - REACH)
        place = place - jnp.where(left, REACH, 0)
        away = jnp.abs(at - source)
        return away.astype(F32), (away > PSFR) | (place < 0) | (place >= EDGE)

    edge_gaps = [edge_distance(0), edge_distance(tile - SPAN)]
    of_psi = iota((SPAN, tile), 1) < HALF
    if prepared:
        depth = tile + 2 * HALO
        drop = jnp.abs(iota((height, depth), 1) - HALO - iota((height, depth), 0) + PAD)
        dropped = drop > PSFR
        drop = drop.astype(F32)

    maps_ref[0] = jnp.zeros(maps_ref.shape[1:], F32)
    edges_ref[0] = jnp.zeros(edges_ref.shape[1:], F32)
    clear_sums(sum_ref)
    for copy in small:
        copy.wait()
    coded_ref[...] = segment_table(motion_ref[...], epochs, member * epochs)
    table = pltpu.make_async_copy(coded_ref, table_ref, table_sem)
    table.start()

    def weights(e):
        def profile(distance, beyond):
            scaled = distance * (1.0 / jnp.full((1, distance.shape[1]), sigma_ref[e], F32))
            return jnp.where(beyond, 0.0, jnp.exp(-0.5 * (scaled * scaled)))

        turned = profile(ring, outside)
        scale = 1.0 / jnp.sum(turned[:8], axis=1, keepdims=True)[:1]
        turned = turned * scale
        bands = profile(drop, dropped) * scale if prepared else None
        ends = [profile(*gap) * scale for gap in edge_gaps]
        result = []
        blank = jnp.zeros((tile - 2 * PAD, tile), F32)
        for m in range(2):
            value = turned if m == 0 else turned * turned
            inside = jnp.where(far, 0.0, value)
            beyond = jnp.where(far, value, 0.0)
            top, bottom = beyond[:PAD], beyond[tile - PAD :]
            if prepared:
                band = (bands if m == 0 else bands * bands).astype(BF16)
            else:
                band = jnp.concatenate([bottom, inside, top], axis=0).astype(BF16)
            if m == 1:
                inside, top, bottom = (pltpu.roll(v, HALF, 1) for v in (inside, top, bottom))
            outer = jnp.concatenate([top, blank, bottom], axis=0)
            if m == 0:
                first, last = (jnp.where(of_psi, end, 0.0) for end in ends)
            else:
                first, last = (jnp.where(of_psi, 0.0, end * end) for end in ends)
            gap_rows = jnp.zeros((tile - 2 * SPAN, tile), F32)
            edge = jnp.concatenate([first, gap_rows, last], axis=0)
            result.append((band, *(v.astype(BF16) for v in (inside, outer, edge))))
        return result

    def correlate(e):
        if prepared:
            pair = first_ref[e], second_ref[e]
        else:
            inverse = valid_ref[e].astype(F32) / second_ref[e].astype(F32)
            pair = (first_ref[e].astype(F32) * inverse).astype(BF16), inverse.astype(BF16)
        (band, inside, outer, edge), (band2, inside2, outer2, edge2) = weights(e)

        def apart(a, b):
            wide = [jnp.concatenate([a, jnp.zeros_like(a)], axis=1)]
            wide.append(jnp.concatenate([jnp.zeros_like(b), b], axis=1))
            return jnp.concatenate(wide, axis=0)

        rows = jnp.dot(
            jnp.concatenate([band, band2], axis=1), apart(*pair), preferred_element_type=F32
        ).astype(BF16)
        maps = jnp.dot(rows, apart(inside, inside2), preferred_element_type=F32)
        sides = jnp.dot(
            rows,
            jnp.concatenate(
                [
                    jnp.concatenate([outer, edge], axis=1),
                    jnp.concatenate([outer2, edge2], axis=1),
                ],
                axis=0,
            ),
            preferred_element_type=F32,
        )
        return maps[:, :tile], maps[:, tile:], sides[:, :tile], sides[:, tile:]

    def correlate_chunk(c, carry):
        for i in range(2):
            data_copy(c, i).wait()
        made = [correlate(c * CHUNK + u) for u in range(CHUNK)]
        for i in range(4):
            held, at = (maps_ref, i) if i < 3 else (edges_ref, 0)
            total = held[c * CHUNK, at]
            for u in range(CHUNK):
                total = total + made[u][i]
                held[c * CHUNK + u + 1, at] = total
        return carry

    lax.fori_loop(0, chunks, correlate_chunk, 0)
    table.wait()
    stack_edges(
        epochs, tile, block, n_epoch, n_vel, table_ref, edges_ref, sum_ref, send_ref, keep_ref
    )


def join_kernel(keep_ref, arrived_ref, own_ref, *refs):
    beyond, (far_ref, side_ref) = refs[:-2], refs[-2:]
    far_ref[...] = (keep_ref[...] + arrived_ref[...].astype(F32)).astype(BF16)
    side = own_ref[...].astype(F32)
    for edge_ref in beyond:
        side = side + edge_ref[...].astype(F32)
    side_ref[...] = side.astype(BF16)


def finish_kernel(tile, block, keep_ref, own_ref, both_ref, *refs):
    mains, (like_hbm, flux_hbm, like_ref, flux_ref, sems) = refs[:-5], refs[-5:]
    copies = []
    row, lane = iota((SIDE, tile), 0), iota((SIDE, tile), 1)
    member = lax.axis_index("vel")
    placed = []
    for m in range(2):
        at = row - m * EDGE
        used = (at >= 0) & (at < EDGE)
        for right in (1 - member, member):
            wanted = at + jnp.where(right == 1, 0, tile - EDGE) + m * HALF
            placed.append(jnp.where(used & (lane == wanted % tile), 1.0, 0.0).astype(BF16))
    for i in range(block):
        sums = []
        for m in range(2):
            rows = slice((2 * i + m) * tile, (2 * i + m + 1) * tile)
            total = keep_ref[rows] + own_ref[rows].astype(F32)
            for main_ref, rest_ref in zip(mains[: len(mains) // 2], mains[len(mains) // 2 :]):
                cut = main_ref.shape[0]
                split = min(max(cut, rows.start), rows.stop)
                held = []
                if split > rows.start:
                    held.append(main_ref[rows.start : split])
                if split < rows.stop:
                    held.append(rest_ref[split - cut : rows.stop - cut])
                total = total + jnp.concatenate([h.astype(F32) for h in held], axis=0)
            for near, put in enumerate(placed[2 * m : 2 * m + 2]):
                at = (near * block + i) * SIDE
                total = total + lax.dot_general(
                    both_ref[at : at + SIDE], put, (((0,), (0,)), ((), ())),
                    preferred_element_type=F32,
                )
            sums.append(total)
        root = lax.rsqrt(jnp.maximum(pltpu.roll(sums[1], HALF, 1), phi_floor))
        like = sums[0] * root
        like_ref[i] = like
        flux_ref[i] = like * root
        for j, (source, target) in enumerate(((like_ref, like_hbm), (flux_ref, flux_hbm))):
            copies.append(pltpu.make_async_copy(source.at[i], target.at[i], sems.at[2 * i + j]))
            copies[-1].start()
    for copy in copies:
        copy.wait()


def move(block, axis, distance):
    count = lax.axis_size(axis)
    return lax.ppermute(block, axis, [(i, (i + distance) % count) for i in range(count)])


def beside(block, step, keep):
    count = lax.axis_size("sky")
    device = [(q - GRID_X // 2) % count for q in range(count)]
    route = [(device[q], device[q + step]) for q in range(count) if keep(q)]
    return lax.ppermute(block, "sky", route)


def beside_by_member(block):
    n_sky = lax.axis_size("sky")
    device = [(q - GRID_X // 2) % n_sky for q in range(n_sky)]
    route = []
    for q in range(n_sky):
        for v, step in ((0, 1), (1, -1)):
            if 0 <= q % GRID_X + step < GRID_X:
                route.append((device[q] * 2 + v, device[q + step] * 2 + v))
    return lax.ppermute(block, ("sky", "vel"), route)


def on_device(images, variances, valid, psf_sigma, offsets):
    epochs, tile = images.shape[0], images.shape[-1]
    n_epoch, n_vel = lax.axis_size("epoch"), lax.axis_size("vel")
    n_sky = lax.axis_size("sky")
    assert n_vel == 2 and epochs % CHUNK == 0
    block = VELS // (n_epoch * n_vel)
    first, second = images[:, 0], variances[:, 0]
    prepared = n_sky > GRID_X
    if prepared:
        usable = valid[:, 0].astype(F32)[:, None, None]
        scaled = (first.astype(F32) / second.astype(F32) * usable).astype(BF16)
        inverse = (usable / second.astype(F32)).astype(BF16)
        pair = jnp.stack([scaled, inverse])
        above = beside(pair[:, :, tile - HALO :], GRID_X, lambda q: q + GRID_X < n_sky)
        below = beside(pair[:, :, :HALO], -GRID_X, lambda q: q >= GRID_X)
        first, second = jnp.concatenate([above, pair, below], axis=2)

    main_rows = block * 2 * tile
    edge_rows = block * SIDE
    hbm = pl.BlockSpec(memory_space=pltpu.HBM)
    vmem = pl.BlockSpec(memory_space=pltpu.VMEM)
    params = pltpu.CompilerParams(vmem_limit_bytes=16 * 1024 * 1024)
    small_params = pltpu.CompilerParams(vmem_limit_bytes=8 * 1024 * 1024)
    group_rows = n_vel * edge_rows
    operands = (psf_sigma, valid[:, 0], offsets, first, second)
    taken = lax.axis_index("sky") < n_sky
    flag = taken.astype(jnp.int32)[None]
    send_edges, keep_edges, maps, table = pl.pallas_call(
        functools.partial(stack_kernel, epochs, tile, block, n_epoch, n_vel, prepared),
        out_shape=(
            jax.ShapeDtypeStruct((n_epoch * group_rows, tile), BF16),
            jax.ShapeDtypeStruct((n_epoch * group_rows, tile), F32),
            jax.ShapeDtypeStruct((epochs + 1, 3, tile + 2 * PAD, tile), F32),
            jax.ShapeDtypeStruct(offsets.shape[1:], jnp.int32),
        ),
        in_specs=[pl.BlockSpec(memory_space=pltpu.SMEM)] + [hbm] * 5,
        out_specs=(vmem,) * 4,
        scratch_shapes=[
            pltpu.SMEM((epochs,), F32),
            pltpu.SMEM((epochs,), jnp.int32),
            pltpu.VMEM(offsets.shape, jnp.int32),
            pltpu.SMEM(offsets.shape[1:], jnp.int32),
            pltpu.VMEM(first.shape, BF16),
            pltpu.VMEM(second.shape, BF16),
            pltpu.VMEM((epochs + 1, 1, tile + 2 * PAD, tile), F32),
            pltpu.VMEM((VELS + 1, tile, tile), F32),
            pltpu.SemaphoreType.DMA((3,)),
            pltpu.SemaphoreType.DMA((2 * (epochs // CHUNK),)),
            pltpu.SemaphoreType.DMA,
        ],
        compiler_params=params,
    )(flag, *(pltpu.with_memory_space_constraint(a, pltpu.HBM) for a in operands))
    edges = (keep_edges + move(send_edges, "vel", 1).astype(F32)).astype(BF16)
    beyond = [
        move(edges[(d - 1) * group_rows : d * group_rows], "epoch", d) for d in range(1, n_epoch)
    ]

    def main_sums(ranks, sent, kept, maps, hand_on):
        rows = (ranks[1] - ranks[0]) * main_rows
        results = [jax.ShapeDtypeStruct((rows, tile), BF16)] * sent
        results += [jax.ShapeDtypeStruct((rows, tile), F32)] * kept
        aliases = {1: len(results)} if hand_on else {}
        results += [jax.ShapeDtypeStruct(maps.shape, F32)] * hand_on
        slots = (sent + kept) * (ranks[1] - ranks[0]) * block
        return pl.pallas_call(
            functools.partial(
                main_kernel, epochs, tile, block, n_epoch, n_vel, ranks, sent, kept
            ),
            out_shape=results,
            in_specs=[pl.BlockSpec(memory_space=pltpu.SMEM), vmem],
            out_specs=[vmem] * len(results),
            input_output_aliases=aliases,
            scratch_shapes=[pltpu.VMEM((slots + 1, 2, tile, tile), F32)],
            compiler_params=small_params,
        )(table, maps)

    far_ranks, own_ranks = (0, n_epoch - 1), (n_epoch - 1, n_epoch)
    send, maps = main_sums(far_ranks, 1, 0, maps, 1)
    keep, maps = main_sums(far_ranks, 0, 1, maps, 1)
    far, side = pl.pallas_call(
        join_kernel,
        out_shape=(
            jax.ShapeDtypeStruct(keep.shape, BF16),
            jax.ShapeDtypeStruct((group_rows, tile), BF16),
        ),
        in_specs=[vmem] * (3 + len(beyond)),
        out_specs=(vmem, vmem),
        compiler_params=small_params,
    )(keep, move(send, "vel", 1), edges[(n_epoch - 1) * group_rows :], *beyond)
    side = beside_by_member(side)
    piece = main_rows * PIECE // 16
    mains, rests = [], []
    for d in range(1, n_epoch):
        at = (d - 1) * main_rows
        mains.append(move(far[at : at + piece], "epoch", d))
        rests.append(move(far[at + piece : at + main_rows], "epoch", d))

    def pass_own(send, side):
        arrived = move(send, "vel", 1)
        is_first = lax.axis_index("vel") == 0
        near = jnp.where(is_first, side[:edge_rows], side[edge_rows:])
        other = jnp.where(is_first, side[edge_rows:], side[:edge_rows])
        return arrived, jnp.concatenate([near, move(other, "vel", 1)])

    send, keep = main_sums(own_ranks, 1, 1, maps, 0)
    arrived, side = lax.cond(taken, pass_own, lambda send, side: (send, side), send, side)

    shape = jax.ShapeDtypeStruct((block, tile, tile), F32)
    likelihood, flux = pl.pallas_call(
        functools.partial(finish_kernel, tile, block),
        out_shape=(shape, shape),
        in_specs=[vmem] * (3 + 2 * len(mains)),
        out_specs=(hbm, hbm),
        scratch_shapes=[
            pltpu.VMEM(shape.shape, F32),
            pltpu.VMEM(shape.shape, F32),
            pltpu.SemaphoreType.DMA((2 * block,)),
        ],
        compiler_params=params,
    )(keep, arrived, side, *mains, *rests)
    return likelihood[:, None], flux[:, None]


def solution(mesh):
    placed = (
        P(("epoch", "vel"), ("field", "sky"), None, None),
        P(("epoch", "vel"), ("field", "sky"), None, None),
        P(("epoch", "vel"), ("field", "sky")),
        P(("field", "epoch", "vel")),
        P(None, None, "epoch"),
    )
    return jax.shard_map(
        on_device,
        mesh=mesh,
        in_specs=placed,
        out_specs=(
            P(("epoch", "vel"), ("field", "sky"), None, None),
            P(("epoch", "vel"), ("field", "sky"), None, None),
        ),
        check_vma=False,
    )
```

```python
import functools

import jax
import jax.numpy as jnp
from jax import lax
from jax.experimental import pallas as pl
from jax.experimental.pallas import tpu as pltpu
from jax.sharding import PartitionSpec as P

VELS = 16
REACH = 12
PSFR = 7
GRID_X = 4

phi_floor = 0.25

F32 = jnp.float32
BF16 = jnp.bfloat16
EDGE = REACH + PSFR
PAD = 16
HALO = 32
SIDE = 48
HALF = 64
SPAN = 32
CHUNK = 4
STEP = 8


def iota(shape, axis):
    return lax.broadcasted_iota(jnp.int32, shape, axis)


def pick_edges(tile, first_left):
    row, lane = iota((2 * SIDE, tile), 0), iota((2 * SIDE, tile), 1)
    within = row % SIDE
    left = (row >= SIDE) != first_left
    wanted = within % EDGE + jnp.where(left, 0, SPAN + REACH) + jnp.where(within < EDGE, 0, HALF)
    return jnp.where((within < 2 * EDGE) & (lane == wanted), 1.0, 0.0).astype(BF16)


def segment_table(motion, epochs, first):
    code = (motion[0] + REACH) * 32 + motion[1] + REACH
    total = code.shape[1]
    lane = iota(code.shape, 1)
    later = jnp.roll(code, -1, axis=1) if total < 128 else pltpu.roll(code, total - 1, 1)
    stop = first + epochs
    end = jnp.where((later != code) | (lane == stop - 1), lane + 1, total)
    reach = 1
    while reach < epochs:
        end = jnp.minimum(end, jnp.where(lane + reach < total, jnp.roll(end, -reach, axis=1), total))
        reach *= 2
    return jnp.clip(end - first, 0, epochs) * 1024 + code


def over_segments(epochs, table_ref, maps_ref, chosen, slots, k_of, add):
    member = lax.axis_index("vel")
    row = iota((8, maps_ref.shape[-1]), 0)

    def segment(slot, e, turn_of):
        word = table_ref[k_of(slot), member * epochs + e]
        e_end = word >> 10
        start = PAD - REACH + ((word >> 5) & 31)
        dx = (word & 31) - REACH
        tile = maps_ref.shape[-1]
        shift = jnp.where(dx > 0, tile - dx, -dx)
        base = pl.multiple_of((start // 8) * 8, 8)
        above = start - base
        turn = lax.rem(8 - above, 8)
        same = row < 8 - above
        put = add(slot, dx, turn_of)

        def rows_at(r):
            window = pl.ds(base + r, 8)
            return [
                pltpu.roll(maps_ref[e_end, m, window] - maps_ref[e, m, window], turn, 0)
                for m in chosen
            ]

        upper = rows_at(0)
        for r in range(0, tile, 8):
            lower = rows_at(r + 8)
            put(r, [pltpu.roll(jnp.where(same, a, b), shift, 1) for a, b in zip(upper, lower)])
            upper = lower
        ended = e_end >= epochs
        return jnp.where(ended, jnp.minimum(slot + 1, slots), slot), jnp.where(ended, 0, e_end)

    def some_segments(state):
        for u in range(STEP):
            state = segment(*state, u % 2)
        return state

    start = (jnp.int32(0), jnp.int32(0))
    lax.while_loop(lambda state: state[0] < slots, some_segments, start)


def clear_sums(sum_refs):
    def clear(slot, carry):
        for sum_ref in sum_refs:
            sum_ref[slot] = jnp.zeros(sum_ref.shape[1:], F32)
        return carry

    lax.fori_loop(0, sum_refs[0].shape[0] - 1, clear, 0)


def stack_edges(
    epochs, tile, block, n_epoch, n_vel, table_ref, maps_ref, sum_refs, send_ref, keep_ref
):
    column = lax.axis_index("epoch")
    member = lax.axis_index("vel")
    lane = iota((8, tile), 1)
    place = lane % SPAN - jnp.where(lane // SPAN % 2 == 0, REACH, 0)

    def add(slot, dx, turn_of):
        sum_ref = sum_refs[turn_of]
        held = (place + dx >= 0) & (place + dx < EDGE)

        def put(r, pieces):
            sum_ref[slot, r : r + 8] += jnp.where(held, pieces[0], 0.0)

        return put

    first_k = (column + 1) * n_vel * block
    over_segments(
        epochs, table_ref, maps_ref, (0,), VELS, lambda slot: lax.rem(first_k + slot, VELS), add
    )

    selector = pick_edges(tile, member == 1)

    def pack(group, carry):
        for i in range(block):
            slot = group * block + i
            packed = lax.dot_general(
                selector, (sum_refs[0][slot] + sum_refs[1][slot]).astype(BF16), (((1,), (1,)), ((), ())),
                preferred_element_type=F32,
            )
            rows = pl.ds(slot * SIDE, SIDE)
            keep_ref[rows] = packed[:SIDE]
            send_ref[rows] = packed[SIDE:].astype(BF16)
        return carry

    lax.fori_loop(0, VELS // block, pack, 0)


def main_kernel(epochs, tile, block, n_epoch, n_vel, ranks, sent, kept, table_ref, maps_ref, *refs):
    sum_refs = refs[-2:]
    clear_sums(sum_refs)
    column = lax.axis_index("epoch")
    member = lax.axis_index("vel")
    lane = iota((8, tile), 1)
    turned = (lane + HALF) % tile
    share = (ranks[1] - ranks[0]) * block
    slots = (sent + kept) * share

    def k_of(slot):
        whose = jnp.where(slot < sent * share, 1 - member, member)
        rank = ranks[0] + lax.rem(slot, share) // block
        owner = lax.rem(column + 1 + rank, n_epoch)
        return (owner * n_vel + whose) * block + lax.rem(slot, block)

    def add(slot, dx, turn_of):
        sum_ref = sum_refs[turn_of]
        out = (lane + dx < 0) | (lane + dx >= tile)
        out_turned = (turned + dx < 0) | (turned + dx >= tile)

        def put(r, pieces):
            psi, phi, side = pieces
            sum_ref[slot, 0, r : r + 8] += jnp.where(out, side, psi)
            sum_ref[slot, 1, r : r + 8] += jnp.where(out_turned, side, phi)

        return put

    over_segments(epochs, table_ref, maps_ref, (0, 1, 2), slots, k_of, add)

    def write(target_ref, first):
        def one(j, carry):
            rows = pl.ds(j * 2 * tile, 2 * tile)
            value = (sum_refs[0][first + j] + sum_refs[1][first + j]).reshape(2 * tile, tile)
            target_ref[rows] = value.astype(target_ref.dtype)
            return carry

        lax.fori_loop(0, share, one, 0)

    if sent:
        write(refs[0], 0)
    if kept:
        write(refs[sent], sent * share)


def stack_kernel(
    epochs, tile, block, n_epoch, n_vel, prepared,
    taken_ref, sigma_hbm, valid_hbm, motion_hbm, first_hbm, second_hbm,
    send_ref, keep_ref, maps_ref, coded_ref,
    sigma_ref, valid_ref, motion_ref, table_ref, first_ref, second_ref, edges_ref, even_ref, odd_ref,
    small_sems, data_sems, table_sem,
):
    height = tile + 2 * PAD
    chunks = epochs // CHUNK
    member = lax.axis_index("vel")

    small = [
        pltpu.make_async_copy(motion_hbm, motion_ref, small_sems.at[0]),
        pltpu.make_async_copy(sigma_hbm, sigma_ref, small_sems.at[1]),
        pltpu.make_async_copy(valid_hbm, valid_ref, small_sems.at[2]),
    ]
    for copy in small:
        copy.start()

    def data_copy(c, i):
        at = pl.ds(c * CHUNK, CHUNK)
        source, target = ((first_hbm, first_ref), (second_hbm, second_ref))[i]
        return pltpu.make_async_copy(source.at[at], target.at[at], data_sems.at[2 * c + i])

    for c in range(chunks):
        for i in range(2):
            data_copy(c, i).start()

    row, lane = iota((tile, tile), 0), iota((tile, tile), 1)
    gap = jnp.abs(row - lane)
    ring = jnp.minimum(gap, tile - gap)
    outside = ring > PSFR
    far = gap >= tile // 2
    ring = ring.astype(F32)

    def edge_distance(first_row):
        at, ln = iota((SPAN, tile), 0) + first_row, iota((SPAN, tile), 1)
        left, place = ln // SPAN % 2 == 0, ln % SPAN
        source = place + jnp.where(left, -EDGE, tile - REACH)
        place = place - jnp.where(left, REACH, 0)
        away = jnp.abs(at - source)
        return away.astype(F32), (away > PSFR) | (place < 0) | (place >= EDGE)

    edge_gaps = [edge_distance(0), edge_distance(tile - SPAN)]
    of_psi = iota((SPAN, tile), 1) < HALF
    if prepared:
        depth = tile + 2 * HALO
        drop = jnp.abs(iota((height, depth), 1) - HALO - iota((height, depth), 0) + PAD)
        dropped = drop > PSFR
        drop = drop.astype(F32)

    maps_ref[0] = jnp.zeros(maps_ref.shape[1:], F32)
    edges_ref[0] = jnp.zeros(edges_ref.shape[1:], F32)
    sum_refs = even_ref, odd_ref
    clear_sums(sum_refs)
    for copy in small:
        copy.wait()
    coded_ref[...] = segment_table(motion_ref[...], epochs, member * epochs)
    table = pltpu.make_async_copy(coded_ref, table_ref, table_sem)
    table.start()

    def weights(e):
        def profile(distance, beyond):
            scaled = distance * (1.0 / jnp.full((1, distance.shape[1]), sigma_ref[e], F32))
            return jnp.where(beyond, 0.0, jnp.exp(-0.5 * (scaled * scaled)))

        turned = profile(ring, outside)
        scale = 1.0 / jnp.sum(turned[:8], axis=1, keepdims=True)[:1]
        turned = turned * scale
        bands = profile(drop, dropped) * scale if prepared else None
        ends = [profile(*gap) * scale for gap in edge_gaps]
        result = []
        blank = jnp.zeros((tile - 2 * PAD, tile), F32)
        for m in range(2):
            value = turned if m == 0 else turned * turned
            inside = jnp.where(far, 0.0, value)
            beyond = jnp.where(far, value, 0.0)
            top, bottom = beyond[:PAD], beyond[tile - PAD :]
            if prepared:
                band = (bands if m == 0 else bands * bands).astype(BF16)
            else:
                band = jnp.concatenate([bottom, inside, top], axis=0).astype(BF16)
            if m == 1:
                inside, top, bottom = (pltpu.roll(v, HALF, 1) for v in (inside, top, bottom))
            outer = jnp.concatenate([top, blank, bottom], axis=0)
            if m == 0:
                first, last = (jnp.where(of_psi, end, 0.0) for end in ends)
            else:
                first, last = (jnp.where(of_psi, 0.0, end * end) for end in ends)
            gap_rows = jnp.zeros((tile - 2 * SPAN, tile), F32)
            edge = jnp.concatenate([first, gap_rows, last], axis=0)
            result.append((band, *(v.astype(BF16) for v in (inside, outer, edge))))
        return result

    def correlate(e):
        if prepared:
            pair = first_ref[e], second_ref[e]
        else:
            inverse = valid_ref[e].astype(F32) / second_ref[e].astype(F32)
            pair = (first_ref[e].astype(F32) * inverse).astype(BF16), inverse.astype(BF16)
        (band, inside, outer, edge), (band2, inside2, outer2, edge2) = weights(e)

        def apart(a, b):
            wide = [jnp.concatenate([a, jnp.zeros_like(a)], axis=1)]
            wide.append(jnp.concatenate([jnp.zeros_like(b), b], axis=1))
            return jnp.concatenate(wide, axis=0)

        rows = jnp.dot(
            jnp.concatenate([band, band2], axis=1), apart(*pair), preferred_element_type=F32
        ).astype(BF16)
        maps = jnp.dot(rows, apart(inside, inside2), preferred_element_type=F32)
        sides = jnp.dot(
            rows,
            jnp.concatenate(
                [
                    jnp.concatenate([outer, edge], axis=1),
                    jnp.concatenate([outer2, edge2], axis=1),
                ],
                axis=0,
            ),
            preferred_element_type=F32,
        )
        return maps[:, :tile], maps[:, tile:], sides[:, :tile], sides[:, tile:]

    def correlate_chunk(c, carry):
        for i in range(2):
            data_copy(c, i).wait()
        made = [correlate(c * CHUNK + u) for u in range(CHUNK)]
        for i in range(4):
            held, at = (maps_ref, i) if i < 3 else (edges_ref, 0)
            total = held[c * CHUNK, at]
            for u in range(CHUNK):
                total = total + made[u][i]
                held[c * CHUNK + u + 1, at] = total
        return carry

    lax.fori_loop(0, chunks, correlate_chunk, 0)
    table.wait()
    stack_edges(
        epochs, tile, block, n_epoch, n_vel, table_ref, edges_ref, sum_refs, send_ref, keep_ref
    )


def join_kernel(keep_ref, arrived_ref, own_ref, *refs):
    beyond, (far_ref, side_ref) = refs[:-2], refs[-2:]
    far_ref[...] = (keep_ref[...] + arrived_ref[...].astype(F32)).astype(BF16)
    side = own_ref[...].astype(F32)
    for edge_ref in beyond:
        side = side + edge_ref[...].astype(F32)
    side_ref[...] = side.astype(BF16)


def finish_kernel(tile, block, keep_ref, own_ref, both_ref, *refs):
    mains, (like_hbm, flux_hbm, like_ref, flux_ref, sems) = refs[:-5], refs[-5:]
    copies = []
    row, lane = iota((SIDE, tile), 0), iota((SIDE, tile), 1)
    member = lax.axis_index("vel")
    placed = []
    for m in range(2):
        at = row - m * EDGE
        used = (at >= 0) & (at < EDGE)
        for right in (1 - member, member):
            wanted = at + jnp.where(right == 1, 0, tile - EDGE) + m * HALF
            placed.append(jnp.where(used & (lane == wanted % tile), 1.0, 0.0).astype(BF16))
    for i in range(block):
        sums = []
        for m in range(2):
            rows = slice((2 * i + m) * tile, (2 * i + m + 1) * tile)
            total = keep_ref[rows] + own_ref[rows].astype(F32)
            for main_ref in mains:
                total = total + main_ref[rows].astype(F32)
            for near, put in enumerate(placed[2 * m : 2 * m + 2]):
                at = (near * block + i) * SIDE
                total = total + lax.dot_general(
                    both_ref[at : at + SIDE], put, (((0,), (0,)), ((), ())),
                    preferred_element_type=F32,
                )
            sums.append(total)
        root = lax.rsqrt(jnp.maximum(pltpu.roll(sums[1], HALF, 1), phi_floor))
        like = sums[0] * root
        like_ref[i] = like
        flux_ref[i] = like * root
        for j, (source, target) in enumerate(((like_ref, like_hbm), (flux_ref, flux_hbm))):
            copies.append(pltpu.make_async_copy(source.at[i], target.at[i], sems.at[2 * i + j]))
            copies[-1].start()
    for copy in copies:
        copy.wait()


def move(block, axis, distance):
    count = lax.axis_size(axis)
    return lax.ppermute(block, axis, [(i, (i + distance) % count) for i in range(count)])


def beside(block, step, keep):
    count = lax.axis_size("sky")
    device = [(q - GRID_X // 2) % count for q in range(count)]
    route = [(device[q], device[q + step]) for q in range(count) if keep(q)]
    return lax.ppermute(block, "sky", route)


def beside_by_member(block):
    n_sky = lax.axis_size("sky")
    device = [(q - GRID_X // 2) % n_sky for q in range(n_sky)]
    route = []
    for q in range(n_sky):
        for v, step in ((0, 1), (1, -1)):
            if 0 <= q % GRID_X + step < GRID_X:
                route.append((device[q] * 2 + v, device[q + step] * 2 + v))
    return lax.ppermute(block, ("sky", "vel"), route)


def on_device(images, variances, valid, psf_sigma, offsets):
    epochs, tile = images.shape[0], images.shape[-1]
    n_epoch, n_vel = lax.axis_size("epoch"), lax.axis_size("vel")
    n_sky = lax.axis_size("sky")
    assert n_vel == 2 and epochs % CHUNK == 0
    block = VELS // (n_epoch * n_vel)
    first, second = images[:, 0], variances[:, 0]
    prepared = n_sky > GRID_X
    if prepared:
        usable = valid[:, 0].astype(F32)[:, None, None]
        scaled = (first.astype(F32) / second.astype(F32) * usable).astype(BF16)
        inverse = (usable / second.astype(F32)).astype(BF16)
        pair = jnp.stack([scaled, inverse])
        above = beside(pair[:, :, tile - HALO :], GRID_X, lambda q: q + GRID_X < n_sky)
        below = beside(pair[:, :, :HALO], -GRID_X, lambda q: q >= GRID_X)
        first, second = jnp.concatenate([above, pair, below], axis=2)

    main_rows = block * 2 * tile
    edge_rows = block * SIDE
    hbm = pl.BlockSpec(memory_space=pltpu.HBM)
    vmem = pl.BlockSpec(memory_space=pltpu.VMEM)
    params = pltpu.CompilerParams(vmem_limit_bytes=16 * 1024 * 1024)
    small_params = pltpu.CompilerParams(vmem_limit_bytes=8 * 1024 * 1024)
    group_rows = n_vel * edge_rows
    operands = (psf_sigma, valid[:, 0], offsets, first, second)
    taken = lax.axis_index("sky") < n_sky
    flag = taken.astype(jnp.int32)[None]
    send_edges, keep_edges, maps, table = pl.pallas_call(
        functools.partial(stack_kernel, epochs, tile, block, n_epoch, n_vel, prepared),
        out_shape=(
            jax.ShapeDtypeStruct((n_epoch * group_rows, tile), BF16),
            jax.ShapeDtypeStruct((n_epoch * group_rows, tile), F32),
            jax.ShapeDtypeStruct((epochs + 1, 3, tile + 2 * PAD, tile), F32),
            jax.ShapeDtypeStruct(offsets.shape[1:], jnp.int32),
        ),
        in_specs=[pl.BlockSpec(memory_space=pltpu.SMEM)] + [hbm] * 5,
        out_specs=(vmem,) * 4,
        scratch_shapes=[
            pltpu.SMEM((epochs,), F32),
            pltpu.SMEM((epochs,), jnp.int32),
            pltpu.VMEM(offsets.shape, jnp.int32),
            pltpu.SMEM(offsets.shape[1:], jnp.int32),
            pltpu.VMEM(first.shape, BF16),
            pltpu.VMEM(second.shape, BF16),
            pltpu.VMEM((epochs + 1, 1, tile + 2 * PAD, tile), F32),
            pltpu.VMEM((VELS + 1, tile, tile), F32),
            pltpu.VMEM((VELS + 1, tile, tile), F32),
            pltpu.SemaphoreType.DMA((3,)),
            pltpu.SemaphoreType.DMA((2 * (epochs // CHUNK),)),
            pltpu.SemaphoreType.DMA,
        ],
        compiler_params=params,
    )(flag, *(pltpu.with_memory_space_constraint(a, pltpu.HBM) for a in operands))
    edges = (keep_edges + move(send_edges, "vel", 1).astype(F32)).astype(BF16)
    beyond = [
        move(edges[(d - 1) * group_rows : d * group_rows], "epoch", d) for d in range(1, n_epoch)
    ]

    def main_sums(ranks, sent, kept, maps, hand_on):
        rows = (ranks[1] - ranks[0]) * main_rows
        results = [jax.ShapeDtypeStruct((rows, tile), BF16)] * sent
        results += [jax.ShapeDtypeStruct((rows, tile), F32)] * kept
        aliases = {1: len(results)} if hand_on else {}
        results += [jax.ShapeDtypeStruct(maps.shape, F32)] * hand_on
        slots = (sent + kept) * (ranks[1] - ranks[0]) * block
        return pl.pallas_call(
            functools.partial(
                main_kernel, epochs, tile, block, n_epoch, n_vel, ranks, sent, kept
            ),
            out_shape=results,
            in_specs=[pl.BlockSpec(memory_space=pltpu.SMEM), vmem],
            out_specs=[vmem] * len(results),
            input_output_aliases=aliases,
            scratch_shapes=[pltpu.VMEM((slots + 1, 2, tile, tile), F32)] * 2,
            compiler_params=small_params,
        )(table, maps)

    far_ranks, own_ranks = (0, n_epoch - 1), (n_epoch - 1, n_epoch)
    send, maps = main_sums(far_ranks, 1, 0, maps, 1)
    keep, maps = main_sums(far_ranks, 0, 1, maps, 1)
    far, side = pl.pallas_call(
        join_kernel,
        out_shape=(
            jax.ShapeDtypeStruct(keep.shape, BF16),
            jax.ShapeDtypeStruct((group_rows, tile), BF16),
        ),
        in_specs=[vmem] * (3 + len(beyond)),
        out_specs=(vmem, vmem),
        compiler_params=small_params,
    )(keep, move(send, "vel", 1), edges[(n_epoch - 1) * group_rows :], *beyond)
    side = beside_by_member(side)
    mains = [
        move(far[(d - 1) * main_rows : d * main_rows], "epoch", d) for d in range(1, n_epoch)
    ]

    def pass_own(send, side):
        arrived = move(send, "vel", 1)
        is_first = lax.axis_index("vel") == 0
        near = jnp.where(is_first, side[:edge_rows], side[edge_rows:])
        other = jnp.where(is_first, side[edge_rows:], side[:edge_rows])
        return arrived, jnp.concatenate([near, move(other, "vel", 1)])

    send, keep = main_sums(own_ranks, 1, 1, maps, 0)
    arrived, side = lax.cond(taken, pass_own, lambda send, side: (send, side), send, side)

    shape = jax.ShapeDtypeStruct((block, tile, tile), F32)
    likelihood, flux = pl.pallas_call(
        functools.partial(finish_kernel, tile, block),
        out_shape=(shape, shape),
        in_specs=[vmem] * (3 + len(mains)),
        out_specs=(hbm, hbm),
        scratch_shapes=[
            pltpu.VMEM(shape.shape, F32),
            pltpu.VMEM(shape.shape, F32),
            pltpu.SemaphoreType.DMA((2 * block,)),
        ],
        compiler_params=params,
    )(keep, arrived, side, *mains)
    return likelihood[:, None], flux[:, None]


def solution(mesh):
    placed = (
        P(("epoch", "vel"), ("field", "sky"), None, None),
        P(("epoch", "vel"), ("field", "sky"), None, None),
        P(("epoch", "vel"), ("field", "sky")),
        P(("field", "epoch", "vel")),
        P(None, None, "epoch"),
    )
    return jax.shard_map(
        on_device,
        mesh=mesh,
        in_specs=placed,
        out_specs=(
            P(("epoch", "vel"), ("field", "sky"), None, None),
            P(("epoch", "vel"), ("field", "sky"), None, None),
        ),
        check_vma=False,
    )
```

```python
import functools

import jax
import jax.numpy as jnp
from jax import lax
from jax.experimental import pallas as pl
from jax.experimental.pallas import tpu as pltpu
from jax.sharding import PartitionSpec as P

VELS = 16
REACH = 12
PSFR = 7
GRID_X = 4

phi_floor = 0.25

F32 = jnp.float32
BF16 = jnp.bfloat16
EDGE = REACH + PSFR
PAD = 16
HALO = 32
SIDE = 48
HALF = 64
SPAN = 32
CHUNK = 4
STEP = 8


def iota(shape, axis):
    return lax.broadcasted_iota(jnp.int32, shape, axis)


def pick_edges(tile, first_left):
    row, lane = iota((2 * SIDE, tile), 0), iota((2 * SIDE, tile), 1)
    within = row % SIDE
    left = (row >= SIDE) != first_left
    wanted = within % EDGE + jnp.where(left, 0, SPAN + REACH) + jnp.where(within < EDGE, 0, HALF)
    return jnp.where((within < 2 * EDGE) & (lane == wanted), 1.0, 0.0).astype(BF16)


def segment_table(motion, epochs, first):
    code = (motion[0] + REACH) * 32 + motion[1] + REACH
    total = code.shape[1]
    lane = iota(code.shape, 1)
    later = jnp.roll(code, -1, axis=1) if total < 128 else pltpu.roll(code, total - 1, 1)
    stop = first + epochs
    end = jnp.where((later != code) | (lane == stop - 1), lane + 1, total)
    reach = 1
    while reach < epochs:
        end = jnp.minimum(end, jnp.where(lane + reach < total, jnp.roll(end, -reach, axis=1), total))
        reach *= 2
    return jnp.clip(end - first, 0, epochs) * 1024 + code


def over_segments(epochs, table_ref, maps_ref, chosen, slots, k_of, add):
    member = lax.axis_index("vel")
    row = iota((8, maps_ref.shape[-1]), 0)

    def segment(slot, e):
        word = table_ref[k_of(slot), member * epochs + e]
        e_end = word >> 10
        start = PAD - REACH + ((word >> 5) & 31)
        dx = (word & 31) - REACH
        tile = maps_ref.shape[-1]
        shift = jnp.where(dx > 0, tile - dx, -dx)
        base = pl.multiple_of((start // 8) * 8, 8)
        above = start - base
        turn = lax.rem(8 - above, 8)
        same = row < 8 - above
        put = add(slot, dx)

        def rows_at(r):
            window = pl.ds(base + r, 8)
            return [
                pltpu.roll(maps_ref[e_end, m, window] - maps_ref[e, m, window], turn, 0)
                for m in chosen
            ]

        upper = rows_at(0)
        for r in range(0, tile, 8):
            lower = rows_at(r + 8)
            put(r, [pltpu.roll(jnp.where(same, a, b), shift, 1) for a, b in zip(upper, lower)])
            upper = lower
        ended = e_end >= epochs
        return jnp.where(ended, jnp.minimum(slot + 1, slots), slot), jnp.where(ended, 0, e_end)

    def some_segments(state):
        for _ in range(STEP):
            state = segment(*state)
        return state

    start = (jnp.int32(0), jnp.int32(0))
    lax.while_loop(lambda state: state[0] < slots, some_segments, start)


def clear_sums(sum_ref):
    def clear(slot, carry):
        sum_ref[slot] = jnp.zeros(sum_ref.shape[1:], F32)
        return carry

    lax.fori_loop(0, sum_ref.shape[0] - 1, clear, 0)


def stack_edges(
    epochs, tile, block, n_epoch, n_vel, table_ref, maps_ref, sum_ref, send_ref, keep_ref
):
    column = lax.axis_index("epoch")
    member = lax.axis_index("vel")
    lane = iota((8, tile), 1)
    place = lane % SPAN - jnp.where(lane // SPAN % 2 == 0, REACH, 0)

    def add(slot, dx):
        held = (place + dx >= 0) & (place + dx < EDGE)

        def put(r, pieces):
            sum_ref[slot, r : r + 8] += jnp.where(held, pieces[0], 0.0)

        return put

    first_k = (column + 1) * n_vel * block
    over_segments(
        epochs, table_ref, maps_ref, (0,), VELS, lambda slot: lax.rem(first_k + slot, VELS), add
    )

    selector = pick_edges(tile, member == 1)

    def pack(group, carry):
        for i in range(block):
            slot = group * block + i
            packed = lax.dot_general(
                selector, sum_ref[slot].astype(BF16), (((1,), (1,)), ((), ())),
                preferred_element_type=F32,
            )
            rows = pl.ds(slot * SIDE, SIDE)
            keep_ref[rows] = packed[:SIDE]
            send_ref[rows] = packed[SIDE:].astype(BF16)
        return carry

    lax.fori_loop(0, VELS // block, pack, 0)


def main_kernel(epochs, tile, block, n_epoch, n_vel, ranks, sent, kept, table_ref, maps_ref, *refs):
    sum_ref = refs[-1]
    clear_sums(sum_ref)
    column = lax.axis_index("epoch")
    member = lax.axis_index("vel")
    lane = iota((8, tile), 1)
    turned = (lane + HALF) % tile
    share = (ranks[1] - ranks[0]) * block
    slots = (sent + kept) * share

    def k_of(slot):
        whose = jnp.where(slot < sent * share, 1 - member, member)
        rank = ranks[0] + lax.rem(slot, share) // block
        owner = lax.rem(column + 1 + rank, n_epoch)
        return (owner * n_vel + whose) * block + lax.rem(slot, block)

    def add(slot, dx):
        out = (lane + dx < 0) | (lane + dx >= tile)
        out_turned = (turned + dx < 0) | (turned + dx >= tile)

        def put(r, pieces):
            psi, phi, side = pieces
            sum_ref[slot, 0, r : r + 8] += jnp.where(out, side, psi)
            sum_ref[slot, 1, r : r + 8] += jnp.where(out_turned, side, phi)

        return put

    over_segments(epochs, table_ref, maps_ref, (0, 1, 2), slots, k_of, add)

    def write(target_ref, first):
        def one(j, carry):
            rows = pl.ds(j * 2 * tile, 2 * tile)
            value = sum_ref[first + j].reshape(2 * tile, tile)
            target_ref[rows] = value.astype(target_ref.dtype)
            return carry

        lax.fori_loop(0, share, one, 0)

    if sent:
        write(refs[0], 0)
    if kept:
        write(refs[sent], sent * share)


def stack_kernel(
    epochs, tile, block, n_epoch, n_vel, prepared,
    taken_ref, sigma_hbm, valid_hbm, motion_hbm, first_hbm, second_hbm,
    send_ref, keep_ref, maps_ref, coded_ref,
    sigma_ref, valid_ref, motion_ref, table_ref, first_ref, second_ref, edges_ref, sum_ref,
    small_sems, data_sems, table_sem,
):
    height = tile + 2 * PAD
    chunks = epochs // CHUNK
    member = lax.axis_index("vel")

    small = [
        pltpu.make_async_copy(motion_hbm, motion_ref, small_sems.at[0]),
        pltpu.make_async_copy(sigma_hbm, sigma_ref, small_sems.at[1]),
        pltpu.make_async_copy(valid_hbm, valid_ref, small_sems.at[2]),
    ]
    for copy in small:
        copy.start()

    def data_copy(c, i):
        at = pl.ds(c * CHUNK, CHUNK)
        source, target = ((first_hbm, first_ref), (second_hbm, second_ref))[i]
        return pltpu.make_async_copy(source.at[at], target.at[at], data_sems.at[2 * c + i])

    for c in range(chunks):
        for i in range(2):
            data_copy(c, i).start()

    row, lane = iota((tile, tile), 0), iota((tile, tile), 1)
    gap = jnp.abs(row - lane)
    ring = jnp.minimum(gap, tile - gap)
    outside = ring > PSFR
    far = gap >= tile // 2
    ring = ring.astype(F32)

    def edge_distance(first_row):
        at, ln = iota((SPAN, tile), 0) + first_row, iota((SPAN, tile), 1)
        left, place = ln // SPAN % 2 == 0, ln % SPAN
        source = place + jnp.where(left, -EDGE, tile - REACH)
        place = place - jnp.where(left, REACH, 0)
        away = jnp.abs(at - source)
        return away.astype(F32), (away > PSFR) | (place < 0) | (place >= EDGE)

    edge_gaps = [edge_distance(0), edge_distance(tile - SPAN)]
    of_psi = iota((SPAN, tile), 1) < HALF
    if prepared:
        depth = tile + 2 * HALO
        drop = jnp.abs(iota((height, depth), 1) - HALO - iota((height, depth), 0) + PAD)
        dropped = drop > PSFR
        drop = drop.astype(F32)

    maps_ref[0] = jnp.zeros(maps_ref.shape[1:], F32)
    edges_ref[0] = jnp.zeros(edges_ref.shape[1:], F32)
    clear_sums(sum_ref)
    for copy in small:
        copy.wait()
    coded_ref[...] = segment_table(motion_ref[...], epochs, member * epochs)
    table = pltpu.make_async_copy(coded_ref, table_ref, table_sem)
    table.start()

    def weights(e):
        def profile(distance, beyond):
            scaled = distance * (1.0 / jnp.full((1, distance.shape[1]), sigma_ref[e], F32))
            return jnp.where(beyond, 0.0, jnp.exp(-0.5 * (scaled * scaled)))

        turned = profile(ring, outside)
        scale = 1.0 / jnp.sum(turned[:8], axis=1, keepdims=True)[:1]
        turned = turned * scale
        bands = profile(drop, dropped) * scale if prepared else None
        ends = [profile(*gap) * scale for gap in edge_gaps]
        result = []
        blank = jnp.zeros((tile - 2 * PAD, tile), F32)
        for m in range(2):
            value = turned if m == 0 else turned * turned
            inside = jnp.where(far, 0.0, value)
            beyond = jnp.where(far, value, 0.0)
            top, bottom = beyond[:PAD], beyond[tile - PAD :]
            if prepared:
                band = (bands if m == 0 else bands * bands).astype(BF16)
            else:
                band = jnp.concatenate([bottom, inside, top], axis=0).astype(BF16)
            if m == 1:
                inside, top, bottom = (pltpu.roll(v, HALF, 1) for v in (inside, top, bottom))
            outer = jnp.concatenate([top, blank, bottom], axis=0)
            if m == 0:
                first, last = (jnp.where(of_psi, end, 0.0) for end in ends)
            else:
                first, last = (jnp.where(of_psi, 0.0, end * end) for end in ends)
            gap_rows = jnp.zeros((tile - 2 * SPAN, tile), F32)
            edge = jnp.concatenate([first, gap_rows, last], axis=0)
            result.append((band, *(v.astype(BF16) for v in (inside, outer, edge))))
        return result

    def correlate(e):
        if prepared:
            pair = first_ref[e], second_ref[e]
        else:
            inverse = valid_ref[e].astype(F32) / second_ref[e].astype(F32)
            pair = (first_ref[e].astype(F32) * inverse).astype(BF16), inverse.astype(BF16)
        (band, inside, outer, edge), (band2, inside2, outer2, edge2) = weights(e)

        def apart(a, b):
            wide = [jnp.concatenate([a, jnp.zeros_like(a)], axis=1)]
            wide.append(jnp.concatenate([jnp.zeros_like(b), b], axis=1))
            return jnp.concatenate(wide, axis=0)

        rows = jnp.dot(
            jnp.concatenate([band, band2], axis=1), apart(*pair), preferred_element_type=F32
        ).astype(BF16)
        maps = jnp.dot(rows, apart(inside, inside2), preferred_element_type=F32)
        sides = jnp.dot(
            rows,
            jnp.concatenate(
                [
                    jnp.concatenate([outer, edge], axis=1),
                    jnp.concatenate([outer2, edge2], axis=1),
                ],
                axis=0,
            ),
            preferred_element_type=F32,
        )
        return maps[:, :tile], maps[:, tile:], sides[:, :tile], sides[:, tile:]

    def correlate_chunk(c, carry):
        for i in range(2):
            data_copy(c, i).wait()
        made = [correlate(c * CHUNK + u) for u in range(CHUNK)]
        for i in range(4):
            held, at = (maps_ref, i) if i < 3 else (edges_ref, 0)
            total = held[c * CHUNK, at]
            for u in range(CHUNK):
                total = total + made[u][i]
                held[c * CHUNK + u + 1, at] = total
        return carry

    lax.fori_loop(0, chunks, correlate_chunk, 0)
    table.wait()
    stack_edges(
        epochs, tile, block, n_epoch, n_vel, table_ref, edges_ref, sum_ref, send_ref, keep_ref
    )


def join_kernel(keep_ref, arrived_ref, own_ref, *refs):
    beyond, (far_ref, side_ref) = refs[:-2], refs[-2:]
    far_ref[...] = (keep_ref[...] + arrived_ref[...].astype(F32)).astype(BF16)
    side = own_ref[...].astype(F32)
    for edge_ref in beyond:
        side = side + edge_ref[...].astype(F32)
    side_ref[...] = side.astype(BF16)


def finish_kernel(tile, block, own_ref, both_ref, *refs):
    mains, (like_hbm, flux_hbm, like_ref, flux_ref, sems) = refs[:-5], refs[-5:]
    copies = []
    row, lane = iota((SIDE, tile), 0), iota((SIDE, tile), 1)
    member = lax.axis_index("vel")
    placed = []
    for m in range(2):
        at = row - m * EDGE
        used = (at >= 0) & (at < EDGE)
        for right in (1 - member, member):
            wanted = at + jnp.where(right == 1, 0, tile - EDGE) + m * HALF
            placed.append(jnp.where(used & (lane == wanted % tile), 1.0, 0.0).astype(BF16))
    for i in range(block):
        sums = []
        for m in range(2):
            rows = slice((2 * i + m) * tile, (2 * i + m + 1) * tile)
            total = own_ref[rows]
            for main_ref in mains:
                total = total + main_ref[rows].astype(F32)
            for near, put in enumerate(placed[2 * m : 2 * m + 2]):
                at = (near * block + i) * SIDE
                total = total + lax.dot_general(
                    both_ref[at : at + SIDE], put, (((0,), (0,)), ((), ())),
                    preferred_element_type=F32,
                )
            sums.append(total)
        root = lax.rsqrt(jnp.maximum(pltpu.roll(sums[1], HALF, 1), phi_floor))
        like = sums[0] * root
        like_ref[i] = like
        flux_ref[i] = like * root
        for j, (source, target) in enumerate(((like_ref, like_hbm), (flux_ref, flux_hbm))):
            copies.append(pltpu.make_async_copy(source.at[i], target.at[i], sems.at[2 * i + j]))
            copies[-1].start()
    for copy in copies:
        copy.wait()


def move(block, axis, distance):
    count = lax.axis_size(axis)
    return lax.ppermute(block, axis, [(i, (i + distance) % count) for i in range(count)])


def beside(block, step, keep):
    count = lax.axis_size("sky")
    device = [(q - GRID_X // 2) % count for q in range(count)]
    route = [(device[q], device[q + step]) for q in range(count) if keep(q)]
    return lax.ppermute(block, "sky", route)


def beside_by_member(block):
    n_sky = lax.axis_size("sky")
    device = [(q - GRID_X // 2) % n_sky for q in range(n_sky)]
    route = []
    for q in range(n_sky):
        for v, step in ((0, 1), (1, -1)):
            if 0 <= q % GRID_X + step < GRID_X:
                route.append((device[q] * 2 + v, device[q + step] * 2 + v))
    return lax.ppermute(block, ("sky", "vel"), route)


def on_device(images, variances, valid, psf_sigma, offsets):
    epochs, tile = images.shape[0], images.shape[-1]
    n_epoch, n_vel = lax.axis_size("epoch"), lax.axis_size("vel")
    n_sky = lax.axis_size("sky")
    assert n_vel == 2 and epochs % CHUNK == 0
    block = VELS // (n_epoch * n_vel)
    first, second = images[:, 0], variances[:, 0]
    prepared = n_sky > GRID_X
    if prepared:
        usable = valid[:, 0].astype(F32)[:, None, None]
        scaled = (first.astype(F32) / second.astype(F32) * usable).astype(BF16)
        inverse = (usable / second.astype(F32)).astype(BF16)
        pair = jnp.stack([scaled, inverse])
        above = beside(pair[:, :, tile - HALO :], GRID_X, lambda q: q + GRID_X < n_sky)
        below = beside(pair[:, :, :HALO], -GRID_X, lambda q: q >= GRID_X)
        first, second = jnp.concatenate([above, pair, below], axis=2)

    main_rows = block * 2 * tile
    edge_rows = block * SIDE
    hbm = pl.BlockSpec(memory_space=pltpu.HBM)
    vmem = pl.BlockSpec(memory_space=pltpu.VMEM)
    params = pltpu.CompilerParams(vmem_limit_bytes=16 * 1024 * 1024)
    small_params = pltpu.CompilerParams(vmem_limit_bytes=8 * 1024 * 1024)
    group_rows = n_vel * edge_rows
    operands = (psf_sigma, valid[:, 0], offsets, first, second)
    taken = lax.axis_index("sky") < n_sky
    flag = taken.astype(jnp.int32)[None]
    send_edges, keep_edges, maps, table = pl.pallas_call(
        functools.partial(stack_kernel, epochs, tile, block, n_epoch, n_vel, prepared),
        out_shape=(
            jax.ShapeDtypeStruct((n_epoch * group_rows, tile), BF16),
            jax.ShapeDtypeStruct((n_epoch * group_rows, tile), F32),
            jax.ShapeDtypeStruct((epochs + 1, 3, tile + 2 * PAD, tile), F32),
            jax.ShapeDtypeStruct(offsets.shape[1:], jnp.int32),
        ),
        in_specs=[pl.BlockSpec(memory_space=pltpu.SMEM)] + [hbm] * 5,
        out_specs=(vmem,) * 4,
        scratch_shapes=[
            pltpu.SMEM((epochs,), F32),
            pltpu.SMEM((epochs,), jnp.int32),
            pltpu.VMEM(offsets.shape, jnp.int32),
            pltpu.SMEM(offsets.shape[1:], jnp.int32),
            pltpu.VMEM(first.shape, BF16),
            pltpu.VMEM(second.shape, BF16),
            pltpu.VMEM((epochs + 1, 1, tile + 2 * PAD, tile), F32),
            pltpu.VMEM((VELS + 1, tile, tile), F32),
            pltpu.SemaphoreType.DMA((3,)),
            pltpu.SemaphoreType.DMA((2 * (epochs // CHUNK),)),
            pltpu.SemaphoreType.DMA,
        ],
        compiler_params=params,
    )(flag, *(pltpu.with_memory_space_constraint(a, pltpu.HBM) for a in operands))
    edges = (keep_edges + move(send_edges, "vel", 1).astype(F32)).astype(BF16)
    beyond = [
        move(edges[(d - 1) * group_rows : d * group_rows], "epoch", d) for d in range(1, n_epoch)
    ]

    def main_sums(ranks, sent, kept, maps, hand_on):
        rows = (ranks[1] - ranks[0]) * main_rows
        results = [jax.ShapeDtypeStruct((rows, tile), BF16)] * sent
        results += [jax.ShapeDtypeStruct((rows, tile), F32)] * kept
        aliases = {1: len(results)} if hand_on else {}
        results += [jax.ShapeDtypeStruct(maps.shape, F32)] * hand_on
        slots = (sent + kept) * (ranks[1] - ranks[0]) * block
        return pl.pallas_call(
            functools.partial(
                main_kernel, epochs, tile, block, n_epoch, n_vel, ranks, sent, kept
            ),
            out_shape=results,
            in_specs=[pl.BlockSpec(memory_space=pltpu.SMEM), vmem],
            out_specs=[vmem] * len(results),
            input_output_aliases=aliases,
            scratch_shapes=[pltpu.VMEM((slots + 1, 2, tile, tile), F32)],
            compiler_params=small_params,
        )(table, maps)

    far_ranks, own_ranks = (0, n_epoch - 1), (n_epoch - 1, n_epoch)
    send, maps = main_sums(far_ranks, 1, 0, maps, 1)
    keep, maps = main_sums(far_ranks, 0, 1, maps, 1)
    far, side = pl.pallas_call(
        join_kernel,
        out_shape=(
            jax.ShapeDtypeStruct(keep.shape, BF16),
            jax.ShapeDtypeStruct((group_rows, tile), BF16),
        ),
        in_specs=[vmem] * (3 + len(beyond)),
        out_specs=(vmem, vmem),
        compiler_params=small_params,
    )(keep, move(send, "vel", 1), edges[(n_epoch - 1) * group_rows :], *beyond)
    side = beside_by_member(side)
    mains = [
        move(far[(d - 1) * main_rows : d * main_rows], "epoch", d) for d in range(1, n_epoch)
    ]

    def pass_edges(own, arrived, side):
        is_first = lax.axis_index("vel") == 0
        near = jnp.where(is_first, side[:edge_rows], side[edge_rows:])
        other = jnp.where(is_first, side[edge_rows:], side[:edge_rows])
        total = own + arrived.astype(F32)
        return total, jnp.concatenate([near, move(other, "vel", 1)])

    send, keep = main_sums(own_ranks, 1, 1, maps, 0)
    arrived = lax.cond(taken, lambda v: move(v, "vel", 1), lambda v: v, send)
    total, side = lax.cond(
        taken, pass_edges, lambda own, arrived, side: (own, side), keep, arrived, side
    )

    shape = jax.ShapeDtypeStruct((block, tile, tile), F32)
    likelihood, flux = pl.pallas_call(
        functools.partial(finish_kernel, tile, block),
        out_shape=(shape, shape),
        in_specs=[vmem] * (2 + len(mains)),
        out_specs=(hbm, hbm),
        scratch_shapes=[
            pltpu.VMEM(shape.shape, F32),
            pltpu.VMEM(shape.shape, F32),
            pltpu.SemaphoreType.DMA((2 * block,)),
        ],
        compiler_params=params,
    )(total, side, *mains)
    return likelihood[:, None], flux[:, None]


def solution(mesh):
    placed = (
        P(("epoch", "vel"), ("field", "sky"), None, None),
        P(("epoch", "vel"), ("field", "sky"), None, None),
        P(("epoch", "vel"), ("field", "sky")),
        P(("field", "epoch", "vel")),
        P(None, None, "epoch"),
    )
    return jax.shard_map(
        on_device,
        mesh=mesh,
        in_specs=placed,
        out_specs=(
            P(("epoch", "vel"), ("field", "sky"), None, None),
            P(("epoch", "vel"), ("field", "sky"), None, None),
        ),
        check_vma=False,
    )
```

```python
import functools

import jax
import jax.numpy as jnp
from jax import lax
from jax.experimental import pallas as pl
from jax.experimental.pallas import tpu as pltpu
from jax.sharding import PartitionSpec as P

VELS = 16
REACH = 12
PSFR = 7
GRID_X = 4

phi_floor = 0.25

F32 = jnp.float32
BF16 = jnp.bfloat16
EDGE = REACH + PSFR
PAD = 16
HALO = 32
SIDE = 48
HALF = 64
SPAN = 32
CHUNK = 2
STEP = 8


def iota(shape, axis):
    return lax.broadcasted_iota(jnp.int32, shape, axis)


def pick_edges(tile, first_left):
    row, lane = iota((2 * SIDE, tile), 0), iota((2 * SIDE, tile), 1)
    within = row % SIDE
    left = (row >= SIDE) != first_left
    wanted = within % EDGE + jnp.where(left, 0, SPAN + REACH) + jnp.where(within < EDGE, 0, HALF)
    return jnp.where((within < 2 * EDGE) & (lane == wanted), 1.0, 0.0).astype(BF16)


def segment_table(motion, epochs, first):
    code = (motion[0] + REACH) * 32 + motion[1] + REACH
    total = code.shape[1]
    lane = iota(code.shape, 1)
    later = jnp.roll(code, -1, axis=1) if total < 128 else pltpu.roll(code, total - 1, 1)
    stop = first + epochs
    end = jnp.where((later != code) | (lane == stop - 1), lane + 1, total)
    reach = 1
    while reach < epochs:
        end = jnp.minimum(end, jnp.where(lane + reach < total, jnp.roll(end, -reach, axis=1), total))
        reach *= 2
    return jnp.clip(end - first, 0, epochs) * 1024 + code


def over_segments(epochs, table_ref, maps_ref, chosen, slots, k_of, add):
    member = lax.axis_index("vel")
    row = iota((8, maps_ref.shape[-1]), 0)

    def segment(slot, e):
        word = table_ref[k_of(slot), member * epochs + e]
        e_end = word >> 10
        start = PAD - REACH + ((word >> 5) & 31)
        dx = (word & 31) - REACH
        tile = maps_ref.shape[-1]
        shift = jnp.where(dx > 0, tile - dx, -dx)
        base = pl.multiple_of((start // 8) * 8, 8)
        above = start - base
        turn = lax.rem(8 - above, 8)
        same = row < 8 - above
        put = add(slot, dx)

        def rows_at(r):
            window = pl.ds(base + r, 8)
            return [
                pltpu.roll(maps_ref[e_end, m, window] - maps_ref[e, m, window], turn, 0)
                for m in chosen
            ]

        upper = rows_at(0)
        for r in range(0, tile, 8):
            lower = rows_at(r + 8)
            put(r, [pltpu.roll(jnp.where(same, a, b), shift, 1) for a, b in zip(upper, lower)])
            upper = lower
        ended = e_end >= epochs
        return jnp.where(ended, jnp.minimum(slot + 1, slots), slot), jnp.where(ended, 0, e_end)

    def some_segments(state):
        for _ in range(STEP):
            state = segment(*state)
        return state

    start = (jnp.int32(0), jnp.int32(0))
    lax.while_loop(lambda state: state[0] < slots, some_segments, start)


def clear_sums(sum_ref):
    def clear(slot, carry):
        sum_ref[slot] = jnp.zeros(sum_ref.shape[1:], F32)
        return carry

    lax.fori_loop(0, sum_ref.shape[0] - 1, clear, 0)


def stack_edges(
    epochs, tile, block, n_epoch, n_vel, table_ref, maps_ref, sum_ref, send_ref, keep_ref
):
    column = lax.axis_index("epoch")
    member = lax.axis_index("vel")
    lane = iota((8, tile), 1)
    place = lane % SPAN - jnp.where(lane // SPAN % 2 == 0, REACH, 0)

    def add(slot, dx):
        held = (place + dx >= 0) & (place + dx < EDGE)

        def put(r, pieces):
            sum_ref[slot, r : r + 8] += jnp.where(held, pieces[0], 0.0)

        return put

    first_k = (column + 1) * n_vel * block
    over_segments(
        epochs, table_ref, maps_ref, (0,), VELS, lambda slot: lax.rem(first_k + slot, VELS), add
    )

    selector = pick_edges(tile, member == 1)

    def pack(group, carry):
        for i in range(block):
            slot = group * block + i
            packed = lax.dot_general(
                selector, sum_ref[slot].astype(BF16), (((1,), (1,)), ((), ())),
                preferred_element_type=F32,
            )
            rows = pl.ds(slot * SIDE, SIDE)
            keep_ref[rows] = packed[:SIDE]
            send_ref[rows] = packed[SIDE:].astype(BF16)
        return carry

    lax.fori_loop(0, VELS // block, pack, 0)


def main_kernel(epochs, tile, block, n_epoch, n_vel, ranks, sent, kept, table_ref, maps_ref, *refs):
    sum_ref = refs[-1]
    clear_sums(sum_ref)
    column = lax.axis_index("epoch")
    member = lax.axis_index("vel")
    lane = iota((8, tile), 1)
    turned = (lane + HALF) % tile
    share = (ranks[1] - ranks[0]) * block
    slots = (sent + kept) * share

    def k_of(slot):
        whose = jnp.where(slot < sent * share, 1 - member, member)
        rank = ranks[0] + lax.rem(slot, share) // block
        owner = lax.rem(column + 1 + rank, n_epoch)
        return (owner * n_vel + whose) * block + lax.rem(slot, block)

    def add(slot, dx):
        out = (lane + dx < 0) | (lane + dx >= tile)
        out_turned = (turned + dx < 0) | (turned + dx >= tile)

        def put(r, pieces):
            psi, phi, side = pieces
            sum_ref[slot, 0, r : r + 8] += jnp.where(out, side, psi)
            sum_ref[slot, 1, r : r + 8] += jnp.where(out_turned, side, phi)

        return put

    over_segments(epochs, table_ref, maps_ref, (0, 1, 2), slots, k_of, add)

    def write(target_ref, first):
        def one(j, carry):
            rows = pl.ds(j * 2 * tile, 2 * tile)
            value = sum_ref[first + j].reshape(2 * tile, tile)
            target_ref[rows] = value.astype(target_ref.dtype)
            return carry

        lax.fori_loop(0, share, one, 0)

    if sent:
        write(refs[0], 0)
    if kept:
        write(refs[sent], sent * share)


def stack_kernel(
    epochs, tile, block, n_epoch, n_vel, prepared,
    taken_ref, sigma_hbm, valid_hbm, motion_hbm, first_hbm, second_hbm,
    send_ref, keep_ref, maps_ref, coded_ref,
    sigma_ref, valid_ref, motion_ref, table_ref, first_ref, second_ref, edges_ref, sum_ref,
    small_sems, data_sems, table_sem,
):
    height = tile + 2 * PAD
    chunks = epochs // CHUNK
    member = lax.axis_index("vel")

    small = [
        pltpu.make_async_copy(motion_hbm, motion_ref, small_sems.at[0]),
        pltpu.make_async_copy(sigma_hbm, sigma_ref, small_sems.at[1]),
        pltpu.make_async_copy(valid_hbm, valid_ref, small_sems.at[2]),
    ]
    for copy in small:
        copy.start()

    def data_copy(c, i):
        at = pl.ds(c * CHUNK, CHUNK)
        source, target = ((first_hbm, first_ref), (second_hbm, second_ref))[i]
        return pltpu.make_async_copy(source.at[at], target.at[at], data_sems.at[2 * c + i])

    for c in range(chunks):
        for i in range(2):
            data_copy(c, i).start()

    row, lane = iota((tile, tile), 0), iota((tile, tile), 1)
    gap = jnp.abs(row - lane)
    ring = jnp.minimum(gap, tile - gap)
    outside = ring > PSFR
    far = gap >= tile // 2
    ring = ring.astype(F32)

    def edge_distance(first_row):
        at, ln = iota((SPAN, tile), 0) + first_row, iota((SPAN, tile), 1)
        left, place = ln // SPAN % 2 == 0, ln % SPAN
        source = place + jnp.where(left, -EDGE, tile - REACH)
        place = place - jnp.where(left, REACH, 0)
        away = jnp.abs(at - source)
        return away.astype(F32), (away > PSFR) | (place < 0) | (place >= EDGE)

    edge_gaps = [edge_distance(0), edge_distance(tile - SPAN)]
    of_psi = iota((SPAN, tile), 1) < HALF
    if prepared:
        depth = tile + 2 * HALO
        drop = jnp.abs(iota((height, depth), 1) - HALO - iota((height, depth), 0) + PAD)
        dropped = drop > PSFR
        drop = drop.astype(F32)

    maps_ref[0] = jnp.zeros(maps_ref.shape[1:], F32)
    edges_ref[0] = jnp.zeros(edges_ref.shape[1:], F32)
    clear_sums(sum_ref)
    for copy in small:
        copy.wait()
    coded_ref[...] = segment_table(motion_ref[...], epochs, member * epochs)
    table = pltpu.make_async_copy(coded_ref, table_ref, table_sem)
    table.start()

    def weights(e):
        def profile(distance, beyond):
            scaled = distance * (1.0 / jnp.full((1, distance.shape[1]), sigma_ref[e], F32))
            return jnp.where(beyond, 0.0, jnp.exp(-0.5 * (scaled * scaled)))

        turned = profile(ring, outside)
        scale = 1.0 / jnp.sum(turned[:8], axis=1, keepdims=True)[:1]
        turned = turned * scale
        bands = profile(drop, dropped) * scale if prepared else None
        ends = [profile(*gap) * scale for gap in edge_gaps]
        result = []
        blank = jnp.zeros((tile - 2 * PAD, tile), F32)
        for m in range(2):
            value = turned if m == 0 else turned * turned
            inside = jnp.where(far, 0.0, value)
            beyond = jnp.where(far, value, 0.0)
            top, bottom = beyond[:PAD], beyond[tile - PAD :]
            if prepared:
                band = (bands if m == 0 else bands * bands).astype(BF16)
            else:
                band = jnp.concatenate([bottom, inside, top], axis=0).astype(BF16)
            if m == 1:
                inside, top, bottom = (pltpu.roll(v, HALF, 1) for v in (inside, top, bottom))
            outer = jnp.concatenate([top, blank, bottom], axis=0)
            if m == 0:
                first, last = (jnp.where(of_psi, end, 0.0) for end in ends)
            else:
                first, last = (jnp.where(of_psi, 0.0, end * end) for end in ends)
            gap_rows = jnp.zeros((tile - 2 * SPAN, tile), F32)
            edge = jnp.concatenate([first, gap_rows, last], axis=0)
            result.append((band, *(v.astype(BF16) for v in (inside, outer, edge))))
        return result

    def correlate(e):
        if prepared:
            pair = first_ref[e], second_ref[e]
        else:
            inverse = valid_ref[e].astype(F32) / second_ref[e].astype(F32)
            pair = (first_ref[e].astype(F32) * inverse).astype(BF16), inverse.astype(BF16)
        (band, inside, outer, edge), (band2, inside2, outer2, edge2) = weights(e)

        def apart(a, b):
            wide = [jnp.concatenate([a, jnp.zeros_like(a)], axis=1)]
            wide.append(jnp.concatenate([jnp.zeros_like(b), b], axis=1))
            return jnp.concatenate(wide, axis=0)

        rows = jnp.dot(
            jnp.concatenate([band, band2], axis=1), apart(*pair), preferred_element_type=F32
        ).astype(BF16)
        maps = jnp.dot(rows, apart(inside, inside2), preferred_element_type=F32)
        sides = jnp.dot(
            rows,
            jnp.concatenate(
                [
                    jnp.concatenate([outer, edge], axis=1),
                    jnp.concatenate([outer2, edge2], axis=1),
                ],
                axis=0,
            ),
            preferred_element_type=F32,
        )
        return maps[:, :tile], maps[:, tile:], sides[:, :tile], sides[:, tile:]

    def correlate_chunk(c, carry):
        for i in range(2):
            data_copy(c, i).wait()
        made = [correlate(c * CHUNK + u) for u in range(CHUNK)]
        for i in range(4):
            held, at = (maps_ref, i) if i < 3 else (edges_ref, 0)
            total = held[c * CHUNK, at]
            for u in range(CHUNK):
                total = total + made[u][i]
                held[c * CHUNK + u + 1, at] = total
        return carry

    lax.fori_loop(0, chunks, correlate_chunk, 0)
    table.wait()
    stack_edges(
        epochs, tile, block, n_epoch, n_vel, table_ref, edges_ref, sum_ref, send_ref, keep_ref
    )


def join_kernel(keep_ref, arrived_ref, own_ref, *refs):
    beyond, (far_ref, side_ref) = refs[:-2], refs[-2:]
    far_ref[...] = (keep_ref[...] + arrived_ref[...].astype(F32)).astype(BF16)
    side = own_ref[...].astype(F32)
    for edge_ref in beyond:
        side = side + edge_ref[...].astype(F32)
    side_ref[...] = side.astype(BF16)


def finish_kernel(tile, block, keep_ref, own_ref, both_ref, *refs):
    mains, (like_hbm, flux_hbm, like_ref, flux_ref, sems) = refs[:-5], refs[-5:]
    copies = []
    row, lane = iota((SIDE, tile), 0), iota((SIDE, tile), 1)
    member = lax.axis_index("vel")
    placed = []
    for m in range(2):
        at = row - m * EDGE
        used = (at >= 0) & (at < EDGE)
        for right in (1 - member, member):
            wanted = at + jnp.where(right == 1, 0, tile - EDGE) + m * HALF
            placed.append(jnp.where(used & (lane == wanted % tile), 1.0, 0.0).astype(BF16))
    for i in range(block):
        sums = []
        for m in range(2):
            rows = slice((2 * i + m) * tile, (2 * i + m + 1) * tile)
            total = keep_ref[rows] + own_ref[rows].astype(F32)
            for main_ref in mains:
                total = total + main_ref[rows].astype(F32)
            for near, put in enumerate(placed[2 * m : 2 * m + 2]):
                at = (near * block + i) * SIDE
                total = total + lax.dot_general(
                    both_ref[at : at + SIDE], put, (((0,), (0,)), ((), ())),
                    preferred_element_type=F32,
                )
            sums.append(total)
        root = lax.rsqrt(jnp.maximum(pltpu.roll(sums[1], HALF, 1), phi_floor))
        like = sums[0] * root
        like_ref[i] = like
        flux_ref[i] = like * root
        for j, (source, target) in enumerate(((like_ref, like_hbm), (flux_ref, flux_hbm))):
            copies.append(pltpu.make_async_copy(source.at[i], target.at[i], sems.at[2 * i + j]))
            copies[-1].start()
    for copy in copies:
        copy.wait()


def move(block, axis, distance):
    count = lax.axis_size(axis)
    return lax.ppermute(block, axis, [(i, (i + distance) % count) for i in range(count)])


def beside(block, step, keep):
    count = lax.axis_size("sky")
    device = [(q - GRID_X // 2) % count for q in range(count)]
    route = [(device[q], device[q + step]) for q in range(count) if keep(q)]
    return lax.ppermute(block, "sky", route)


def beside_by_member(block):
    n_sky = lax.axis_size("sky")
    device = [(q - GRID_X // 2) % n_sky for q in range(n_sky)]
    route = []
    for q in range(n_sky):
        for v, step in ((0, 1), (1, -1)):
            if 0 <= q % GRID_X + step < GRID_X:
                route.append((device[q] * 2 + v, device[q + step] * 2 + v))
    return lax.ppermute(block, ("sky", "vel"), route)


def on_device(images, variances, valid, psf_sigma, offsets):
    epochs, tile = images.shape[0], images.shape[-1]
    n_epoch, n_vel = lax.axis_size("epoch"), lax.axis_size("vel")
    n_sky = lax.axis_size("sky")
    assert n_vel == 2 and epochs % CHUNK == 0
    block = VELS // (n_epoch * n_vel)
    first, second = images[:, 0], variances[:, 0]
    prepared = n_sky > GRID_X
    if prepared:
        usable = valid[:, 0].astype(F32)[:, None, None]
        scaled = (first.astype(F32) / second.astype(F32) * usable).astype(BF16)
        inverse = (usable / second.astype(F32)).astype(BF16)
        pair = jnp.stack([scaled, inverse])
        above = beside(pair[:, :, tile - HALO :], GRID_X, lambda q: q + GRID_X < n_sky)
        below = beside(pair[:, :, :HALO], -GRID_X, lambda q: q >= GRID_X)
        first, second = jnp.concatenate([above, pair, below], axis=2)

    main_rows = block * 2 * tile
    edge_rows = block * SIDE
    hbm = pl.BlockSpec(memory_space=pltpu.HBM)
    vmem = pl.BlockSpec(memory_space=pltpu.VMEM)
    params = pltpu.CompilerParams(vmem_limit_bytes=16 * 1024 * 1024)
    small_params = pltpu.CompilerParams(vmem_limit_bytes=8 * 1024 * 1024)
    group_rows = n_vel * edge_rows
    operands = (psf_sigma, valid[:, 0], offsets, first, second)
    taken = lax.axis_index("sky") < n_sky
    flag = taken.astype(jnp.int32)[None]
    send_edges, keep_edges, maps, table = pl.pallas_call(
        functools.partial(stack_kernel, epochs, tile, block, n_epoch, n_vel, prepared),
        out_shape=(
            jax.ShapeDtypeStruct((n_epoch * group_rows, tile), BF16),
            jax.ShapeDtypeStruct((n_epoch * group_rows, tile), F32),
            jax.ShapeDtypeStruct((epochs + 1, 3, tile + 2 * PAD, tile), F32),
            jax.ShapeDtypeStruct(offsets.shape[1:], jnp.int32),
        ),
        in_specs=[pl.BlockSpec(memory_space=pltpu.SMEM)] + [hbm] * 5,
        out_specs=(vmem,) * 4,
        scratch_shapes=[
            pltpu.SMEM((epochs,), F32),
            pltpu.SMEM((epochs,), jnp.int32),
            pltpu.VMEM(offsets.shape, jnp.int32),
            pltpu.SMEM(offsets.shape[1:], jnp.int32),
            pltpu.VMEM(first.shape, BF16),
            pltpu.VMEM(second.shape, BF16),
            pltpu.VMEM((epochs + 1, 1, tile + 2 * PAD, tile), F32),
            pltpu.VMEM((VELS + 1, tile, tile), F32),
            pltpu.SemaphoreType.DMA((3,)),
            pltpu.SemaphoreType.DMA((2 * (epochs // CHUNK),)),
            pltpu.SemaphoreType.DMA,
        ],
        compiler_params=params,
    )(flag, *(pltpu.with_memory_space_constraint(a, pltpu.HBM) for a in operands))
    edges = (keep_edges + move(send_edges, "vel", 1).astype(F32)).astype(BF16)
    beyond = [
        move(edges[(d - 1) * group_rows : d * group_rows], "epoch", d) for d in range(1, n_epoch)
    ]

    def main_sums(ranks, sent, kept, maps, hand_on):
        rows = (ranks[1] - ranks[0]) * main_rows
        results = [jax.ShapeDtypeStruct((rows, tile), BF16)] * sent
        results += [jax.ShapeDtypeStruct((rows, tile), F32)] * kept
        aliases = {1: len(results)} if hand_on else {}
        results += [jax.ShapeDtypeStruct(maps.shape, F32)] * hand_on
        slots = (sent + kept) * (ranks[1] - ranks[0]) * block
        return pl.pallas_call(
            functools.partial(
                main_kernel, epochs, tile, block, n_epoch, n_vel, ranks, sent, kept
            ),
            out_shape=results,
            in_specs=[pl.BlockSpec(memory_space=pltpu.SMEM), vmem],
            out_specs=[vmem] * len(results),
            input_output_aliases=aliases,
            scratch_shapes=[pltpu.VMEM((slots + 1, 2, tile, tile), F32)],
            compiler_params=small_params,
        )(table, maps)

    far_ranks, own_ranks = (0, n_epoch - 1), (n_epoch - 1, n_epoch)
    send, maps = main_sums(far_ranks, 1, 0, maps, 1)
    keep, maps = main_sums(far_ranks, 0, 1, maps, 1)
    far, side = pl.pallas_call(
        join_kernel,
        out_shape=(
            jax.ShapeDtypeStruct(keep.shape, BF16),
            jax.ShapeDtypeStruct((group_rows, tile), BF16),
        ),
        in_specs=[vmem] * (3 + len(beyond)),
        out_specs=(vmem, vmem),
        compiler_params=small_params,
    )(keep, move(send, "vel", 1), edges[(n_epoch - 1) * group_rows :], *beyond)
    side = beside_by_member(side)
    mains = [
        move(far[(d - 1) * main_rows : d * main_rows], "epoch", d) for d in range(1, n_epoch)
    ]

    def pass_own(send, side):
        arrived = move(send, "vel", 1)
        is_first = lax.axis_index("vel") == 0
        near = jnp.where(is_first, side[:edge_rows], side[edge_rows:])
        other = jnp.where(is_first, side[edge_rows:], side[:edge_rows])
        return arrived, jnp.concatenate([near, move(other, "vel", 1)])

    send, keep = main_sums(own_ranks, 1, 1, maps, 0)
    arrived, side = lax.cond(taken, pass_own, lambda send, side: (send, side), send, side)

    shape = jax.ShapeDtypeStruct((block, tile, tile), F32)
    likelihood, flux = pl.pallas_call(
        functools.partial(finish_kernel, tile, block),
        out_shape=(shape, shape),
        in_specs=[vmem] * (3 + len(mains)),
        out_specs=(hbm, hbm),
        scratch_shapes=[
            pltpu.VMEM(shape.shape, F32),
            pltpu.VMEM(shape.shape, F32),
            pltpu.SemaphoreType.DMA((2 * block,)),
        ],
        compiler_params=params,
    )(keep, arrived, side, *mains)
    return likelihood[:, None], flux[:, None]


def solution(mesh):
    placed = (
        P(("epoch", "vel"), ("field", "sky"), None, None),
        P(("epoch", "vel"), ("field", "sky"), None, None),
        P(("epoch", "vel"), ("field", "sky")),
        P(("field", "epoch", "vel")),
        P(None, None, "epoch"),
    )
    return jax.shard_map(
        on_device,
        mesh=mesh,
        in_specs=placed,
        out_specs=(
            P(("epoch", "vel"), ("field", "sky"), None, None),
            P(("epoch", "vel"), ("field", "sky"), None, None),
        ),
        check_vma=False,
    )
```

```python
import functools

import jax
import jax.numpy as jnp
from jax import lax
from jax.experimental import pallas as pl
from jax.experimental.pallas import tpu as pltpu
from jax.sharding import PartitionSpec as P

VELS = 16
REACH = 12
PSFR = 7
GRID_X = 4

phi_floor = 0.25

F32 = jnp.float32
BF16 = jnp.bfloat16
EDGE = REACH + PSFR
PAD = 16
HALO = 32
SIDE = 48
HALF = 64
SPAN = 32
CHUNK = 8
STEP = 8


def iota(shape, axis):
    return lax.broadcasted_iota(jnp.int32, shape, axis)


def pick_edges(tile, first_left):
    row, lane = iota((2 * SIDE, tile), 0), iota((2 * SIDE, tile), 1)
    within = row % SIDE
    left = (row >= SIDE) != first_left
    wanted = within % EDGE + jnp.where(left, 0, SPAN + REACH) + jnp.where(within < EDGE, 0, HALF)
    return jnp.where((within < 2 * EDGE) & (lane == wanted), 1.0, 0.0).astype(BF16)


def segment_table(motion, epochs, first):
    code = (motion[0] + REACH) * 32 + motion[1] + REACH
    total = code.shape[1]
    lane = iota(code.shape, 1)
    later = jnp.roll(code, -1, axis=1) if total < 128 else pltpu.roll(code, total - 1, 1)
    stop = first + epochs
    end = jnp.where((later != code) | (lane == stop - 1), lane + 1, total)
    reach = 1
    while reach < epochs:
        end = jnp.minimum(end, jnp.where(lane + reach < total, jnp.roll(end, -reach, axis=1), total))
        reach *= 2
    return jnp.clip(end - first, 0, epochs) * 1024 + code


def over_segments(epochs, table_ref, maps_ref, chosen, slots, k_of, add):
    member = lax.axis_index("vel")
    row = iota((8, maps_ref.shape[-1]), 0)

    def segment(slot, e):
        word = table_ref[k_of(slot), member * epochs + e]
        e_end = word >> 10
        start = PAD - REACH + ((word >> 5) & 31)
        dx = (word & 31) - REACH
        tile = maps_ref.shape[-1]
        shift = jnp.where(dx > 0, tile - dx, -dx)
        base = pl.multiple_of((start // 8) * 8, 8)
        above = start - base
        turn = lax.rem(8 - above, 8)
        same = row < 8 - above
        put = add(slot, dx)

        def rows_at(r):
            window = pl.ds(base + r, 8)
            return [
                pltpu.roll(maps_ref[e_end, m, window] - maps_ref[e, m, window], turn, 0)
                for m in chosen
            ]

        upper = rows_at(0)
        for r in range(0, tile, 8):
            lower = rows_at(r + 8)
            put(r, [pltpu.roll(jnp.where(same, a, b), shift, 1) for a, b in zip(upper, lower)])
            upper = lower
        ended = e_end >= epochs
        return jnp.where(ended, jnp.minimum(slot + 1, slots), slot), jnp.where(ended, 0, e_end)

    def some_segments(state):
        for _ in range(STEP):
            state = segment(*state)
        return state

    start = (jnp.int32(0), jnp.int32(0))
    lax.while_loop(lambda state: state[0] < slots, some_segments, start)


def clear_sums(sum_ref):
    def clear(slot, carry):
        sum_ref[slot] = jnp.zeros(sum_ref.shape[1:], F32)
        return carry

    lax.fori_loop(0, sum_ref.shape[0] - 1, clear, 0)


def stack_edges(
    epochs, tile, block, n_epoch, n_vel, table_ref, maps_ref, sum_ref, send_ref, keep_ref
):
    column = lax.axis_index("epoch")
    member = lax.axis_index("vel")
    lane = iota((8, tile), 1)
    place = lane % SPAN - jnp.where(lane // SPAN % 2 == 0, REACH, 0)

    def add(slot, dx):
        held = (place + dx >= 0) & (place + dx < EDGE)

        def put(r, pieces):
            sum_ref[slot, r : r + 8] += jnp.where(held, pieces[0], 0.0)

        return put

    first_k = (column + 1) * n_vel * block
    over_segments(
        epochs, table_ref, maps_ref, (0,), VELS, lambda slot: lax.rem(first_k + slot, VELS), add
    )

    selector = pick_edges(tile, member == 1)

    def pack(group, carry):
        for i in range(block):
            slot = group * block + i
            packed = lax.dot_general(
                selector, sum_ref[slot].astype(BF16), (((1,), (1,)), ((), ())),
                preferred_element_type=F32,
            )
            rows = pl.ds(slot * SIDE, SIDE)
            keep_ref[rows] = packed[:SIDE]
            send_ref[rows] = packed[SIDE:].astype(BF16)
        return carry

    lax.fori_loop(0, VELS // block, pack, 0)


def main_kernel(epochs, tile, block, n_epoch, n_vel, ranks, sent, kept, table_ref, maps_ref, *refs):
    sum_ref = refs[-1]
    clear_sums(sum_ref)
    column = lax.axis_index("epoch")
    member = lax.axis_index("vel")
    lane = iota((8, tile), 1)
    turned = (lane + HALF) % tile
    share = (ranks[1] - ranks[0]) * block
    slots = (sent + kept) * share

    def k_of(slot):
        whose = jnp.where(slot < sent * share, 1 - member, member)
        rank = ranks[0] + lax.rem(slot, share) // block
        owner = lax.rem(column + 1 + rank, n_epoch)
        return (owner * n_vel + whose) * block + lax.rem(slot, block)

    def add(slot, dx):
        out = (lane + dx < 0) | (lane + dx >= tile)
        out_turned = (turned + dx < 0) | (turned + dx >= tile)

        def put(r, pieces):
            psi, phi, side = pieces
            sum_ref[slot, 0, r : r + 8] += jnp.where(out, side, psi)
            sum_ref[slot, 1, r : r + 8] += jnp.where(out_turned, side, phi)

        return put

    over_segments(epochs, table_ref, maps_ref, (0, 1, 2), slots, k_of, add)

    def write(target_ref, first):
        def one(j, carry):
            rows = pl.ds(j * 2 * tile, 2 * tile)
            value = sum_ref[first + j].reshape(2 * tile, tile)
            target_ref[rows] = value.astype(target_ref.dtype)
            return carry

        lax.fori_loop(0, share, one, 0)

    if sent:
        write(refs[0], 0)
    if kept:
        write(refs[sent], sent * share)


def stack_kernel(
    epochs, tile, block, n_epoch, n_vel, prepared,
    taken_ref, sigma_hbm, valid_hbm, motion_hbm, first_hbm, second_hbm,
    send_ref, keep_ref, maps_ref, coded_ref,
    sigma_ref, valid_ref, motion_ref, table_ref, first_ref, second_ref, edges_ref, sum_ref,
    small_sems, data_sems, table_sem,
):
    height = tile + 2 * PAD
    chunks = epochs // CHUNK
    member = lax.axis_index("vel")

    small = [
        pltpu.make_async_copy(motion_hbm, motion_ref, small_sems.at[0]),
        pltpu.make_async_copy(sigma_hbm, sigma_ref, small_sems.at[1]),
        pltpu.make_async_copy(valid_hbm, valid_ref, small_sems.at[2]),
    ]
    for copy in small:
        copy.start()

    def data_copy(c, i):
        at = pl.ds(c * CHUNK, CHUNK)
        source, target = ((first_hbm, first_ref), (second_hbm, second_ref))[i]
        return pltpu.make_async_copy(source.at[at], target.at[at], data_sems.at[2 * c + i])

    for c in range(chunks):
        for i in range(2):
            data_copy(c, i).start()

    row, lane = iota((tile, tile), 0), iota((tile, tile), 1)
    gap = jnp.abs(row - lane)
    ring = jnp.minimum(gap, tile - gap)
    outside = ring > PSFR
    far = gap >= tile // 2
    ring = ring.astype(F32)

    def edge_distance(first_row):
        at, ln = iota((SPAN, tile), 0) + first_row, iota((SPAN, tile), 1)
        left, place = ln // SPAN % 2 == 0, ln % SPAN
        source = place + jnp.where(left, -EDGE, tile - REACH)
        place = place - jnp.where(left, REACH, 0)
        away = jnp.abs(at - source)
        return away.astype(F32), (away > PSFR) | (place < 0) | (place >= EDGE)

    edge_gaps = [edge_distance(0), edge_distance(tile - SPAN)]
    of_psi = iota((SPAN, tile), 1) < HALF
    if prepared:
        depth = tile + 2 * HALO
        drop = jnp.abs(iota((height, depth), 1) - HALO - iota((height, depth), 0) + PAD)
        dropped = drop > PSFR
        drop = drop.astype(F32)

    maps_ref[0] = jnp.zeros(maps_ref.shape[1:], F32)
    edges_ref[0] = jnp.zeros(edges_ref.shape[1:], F32)
    clear_sums(sum_ref)
    for copy in small:
        copy.wait()
    coded_ref[...] = segment_table(motion_ref[...], epochs, member * epochs)
    table = pltpu.make_async_copy(coded_ref, table_ref, table_sem)
    table.start()

    def weights(e):
        def profile(distance, beyond):
            scaled = distance * (1.0 / jnp.full((1, distance.shape[1]), sigma_ref[e], F32))
            return jnp.where(beyond, 0.0, jnp.exp(-0.5 * (scaled * scaled)))

        turned = profile(ring, outside)
        scale = 1.0 / jnp.sum(turned[:8], axis=1, keepdims=True)[:1]
        turned = turned * scale
        bands = profile(drop, dropped) * scale if prepared else None
        ends = [profile(*gap) * scale for gap in edge_gaps]
        result = []
        blank = jnp.zeros((tile - 2 * PAD, tile), F32)
        for m in range(2):
            value = turned if m == 0 else turned * turned
            inside = jnp.where(far, 0.0, value)
            beyond = jnp.where(far, value, 0.0)
            top, bottom = beyond[:PAD], beyond[tile - PAD :]
            if prepared:
                band = (bands if m == 0 else bands * bands).astype(BF16)
            else:
                band = jnp.concatenate([bottom, inside, top], axis=0).astype(BF16)
            if m == 1:
                inside, top, bottom = (pltpu.roll(v, HALF, 1) for v in (inside, top, bottom))
            outer = jnp.concatenate([top, blank, bottom], axis=0)
            if m == 0:
                first, last = (jnp.where(of_psi, end, 0.0) for end in ends)
            else:
                first, last = (jnp.where(of_psi, 0.0, end * end) for end in ends)
            gap_rows = jnp.zeros((tile - 2 * SPAN, tile), F32)
            edge = jnp.concatenate([first, gap_rows, last], axis=0)
            result.append((band, *(v.astype(BF16) for v in (inside, outer, edge))))
        return result

    def correlate(e):
        if prepared:
            pair = first_ref[e], second_ref[e]
        else:
            inverse = valid_ref[e].astype(F32) / second_ref[e].astype(F32)
            pair = (first_ref[e].astype(F32) * inverse).astype(BF16), inverse.astype(BF16)
        (band, inside, outer, edge), (band2, inside2, outer2, edge2) = weights(e)

        def apart(a, b):
            wide = [jnp.concatenate([a, jnp.zeros_like(a)], axis=1)]
            wide.append(jnp.concatenate([jnp.zeros_like(b), b], axis=1))
            return jnp.concatenate(wide, axis=0)

        rows = jnp.dot(
            jnp.concatenate([band, band2], axis=1), apart(*pair), preferred_element_type=F32
        ).astype(BF16)
        maps = jnp.dot(rows, apart(inside, inside2), preferred_element_type=F32)
        sides = jnp.dot(
            rows,
            jnp.concatenate(
                [
                    jnp.concatenate([outer, edge], axis=1),
                    jnp.concatenate([outer2, edge2], axis=1),
                ],
                axis=0,
            ),
            preferred_element_type=F32,
        )
        return maps[:, :tile], maps[:, tile:], sides[:, :tile], sides[:, tile:]

    def correlate_chunk(c, carry):
        for i in range(2):
            data_copy(c, i).wait()
        made = [correlate(c * CHUNK + u) for u in range(CHUNK)]
        for i in range(4):
            held, at = (maps_ref, i) if i < 3 else (edges_ref, 0)
            total = held[c * CHUNK, at]
            for u in range(CHUNK):
                total = total + made[u][i]
                held[c * CHUNK + u + 1, at] = total
        return carry

    lax.fori_loop(0, chunks, correlate_chunk, 0)
    table.wait()
    stack_edges(
        epochs, tile, block, n_epoch, n_vel, table_ref, edges_ref, sum_ref, send_ref, keep_ref
    )


def join_kernel(keep_ref, arrived_ref, own_ref, *refs):
    beyond, (far_ref, side_ref) = refs[:-2], refs[-2:]
    far_ref[...] = (keep_ref[...] + arrived_ref[...].astype(F32)).astype(BF16)
    side = own_ref[...].astype(F32)
    for edge_ref in beyond:
        side = side + edge_ref[...].astype(F32)
    side_ref[...] = side.astype(BF16)


def finish_kernel(tile, block, keep_ref, own_ref, both_ref, *refs):
    mains, (like_hbm, flux_hbm, like_ref, flux_ref, sems) = refs[:-5], refs[-5:]
    copies = []
    row, lane = iota((SIDE, tile), 0), iota((SIDE, tile), 1)
    member = lax.axis_index("vel")
    placed = []
    for m in range(2):
        at = row - m * EDGE
        used = (at >= 0) & (at < EDGE)
        for right in (1 - member, member):
            wanted = at + jnp.where(right == 1, 0, tile - EDGE) + m * HALF
            placed.append(jnp.where(used & (lane == wanted % tile), 1.0, 0.0).astype(BF16))
    for i in range(block):
        sums = []
        for m in range(2):
            rows = slice((2 * i + m) * tile, (2 * i + m + 1) * tile)
            total = keep_ref[rows] + own_ref[rows].astype(F32)
            for main_ref in mains:
                total = total + main_ref[rows].astype(F32)
            for near, put in enumerate(placed[2 * m : 2 * m + 2]):
                at = (near * block + i) * SIDE
                total = total + lax.dot_general(
                    both_ref[at : at + SIDE], put, (((0,), (0,)), ((), ())),
                    preferred_element_type=F32,
                )
            sums.append(total)
        root = lax.rsqrt(jnp.maximum(pltpu.roll(sums[1], HALF, 1), phi_floor))
        like = sums[0] * root
        like_ref[i] = like
        flux_ref[i] = like * root
        for j, (source, target) in enumerate(((like_ref, like_hbm), (flux_ref, flux_hbm))):
            copies.append(pltpu.make_async_copy(source.at[i], target.at[i], sems.at[2 * i + j]))
            copies[-1].start()
    for copy in copies:
        copy.wait()


def move(block, axis, distance):
    count = lax.axis_size(axis)
    return lax.ppermute(block, axis, [(i, (i + distance) % count) for i in range(count)])


def beside(block, step, keep):
    count = lax.axis_size("sky")
    device = [(q - GRID_X // 2) % count for q in range(count)]
    route = [(device[q], device[q + step]) for q in range(count) if keep(q)]
    return lax.ppermute(block, "sky", route)


def beside_by_member(block):
    n_sky = lax.axis_size("sky")
    device = [(q - GRID_X // 2) % n_sky for q in range(n_sky)]
    route = []
    for q in range(n_sky):
        for v, step in ((0, 1), (1, -1)):
            if 0 <= q % GRID_X + step < GRID_X:
                route.append((device[q] * 2 + v, device[q + step] * 2 + v))
    return lax.ppermute(block, ("sky", "vel"), route)


def on_device(images, variances, valid, psf_sigma, offsets):
    epochs, tile = images.shape[0], images.shape[-1]
    n_epoch, n_vel = lax.axis_size("epoch"), lax.axis_size("vel")
    n_sky = lax.axis_size("sky")
    assert n_vel == 2 and epochs % CHUNK == 0
    block = VELS // (n_epoch * n_vel)
    first, second = images[:, 0], variances[:, 0]
    prepared = n_sky > GRID_X
    if prepared:
        usable = valid[:, 0].astype(F32)[:, None, None]
        scaled = (first.astype(F32) / second.astype(F32) * usable).astype(BF16)
        inverse = (usable / second.astype(F32)).astype(BF16)
        pair = jnp.stack([scaled, inverse])
        above = beside(pair[:, :, tile - HALO :], GRID_X, lambda q: q + GRID_X < n_sky)
        below = beside(pair[:, :, :HALO], -GRID_X, lambda q: q >= GRID_X)
        first, second = jnp.concatenate([above, pair, below], axis=2)

    main_rows = block * 2 * tile
    edge_rows = block * SIDE
    hbm = pl.BlockSpec(memory_space=pltpu.HBM)
    vmem = pl.BlockSpec(memory_space=pltpu.VMEM)
    params = pltpu.CompilerParams(vmem_limit_bytes=16 * 1024 * 1024)
    small_params = pltpu.CompilerParams(vmem_limit_bytes=8 * 1024 * 1024)
    group_rows = n_vel * edge_rows
    operands = (psf_sigma, valid[:, 0], offsets, first, second)
    taken = lax.axis_index("sky") < n_sky
    flag = taken.astype(jnp.int32)[None]
    send_edges, keep_edges, maps, table = pl.pallas_call(
        functools.partial(stack_kernel, epochs, tile, block, n_epoch, n_vel, prepared),
        out_shape=(
            jax.ShapeDtypeStruct((n_epoch * group_rows, tile), BF16),
            jax.ShapeDtypeStruct((n_epoch * group_rows, tile), F32),
            jax.ShapeDtypeStruct((epochs + 1, 3, tile + 2 * PAD, tile), F32),
            jax.ShapeDtypeStruct(offsets.shape[1:], jnp.int32),
        ),
        in_specs=[pl.BlockSpec(memory_space=pltpu.SMEM)] + [hbm] * 5,
        out_specs=(vmem,) * 4,
        scratch_shapes=[
            pltpu.SMEM((epochs,), F32),
            pltpu.SMEM((epochs,), jnp.int32),
            pltpu.VMEM(offsets.shape, jnp.int32),
            pltpu.SMEM(offsets.shape[1:], jnp.int32),
            pltpu.VMEM(first.shape, BF16),
            pltpu.VMEM(second.shape, BF16),
            pltpu.VMEM((epochs + 1, 1, tile + 2 * PAD, tile), F32),
            pltpu.VMEM((VELS + 1, tile, tile), F32),
            pltpu.SemaphoreType.DMA((3,)),
            pltpu.SemaphoreType.DMA((2 * (epochs // CHUNK),)),
            pltpu.SemaphoreType.DMA,
        ],
        compiler_params=params,
    )(flag, *(pltpu.with_memory_space_constraint(a, pltpu.HBM) for a in operands))
    edges = (keep_edges + move(send_edges, "vel", 1).astype(F32)).astype(BF16)
    beyond = [
        move(edges[(d - 1) * group_rows : d * group_rows], "epoch", d) for d in range(1, n_epoch)
    ]

    def main_sums(ranks, sent, kept, maps, hand_on):
        rows = (ranks[1] - ranks[0]) * main_rows
        results = [jax.ShapeDtypeStruct((rows, tile), BF16)] * sent
        results += [jax.ShapeDtypeStruct((rows, tile), F32)] * kept
        aliases = {1: len(results)} if hand_on else {}
        results += [jax.ShapeDtypeStruct(maps.shape, F32)] * hand_on
        slots = (sent + kept) * (ranks[1] - ranks[0]) * block
        return pl.pallas_call(
            functools.partial(
                main_kernel, epochs, tile, block, n_epoch, n_vel, ranks, sent, kept
            ),
            out_shape=results,
            in_specs=[pl.BlockSpec(memory_space=pltpu.SMEM), vmem],
            out_specs=[vmem] * len(results),
            input_output_aliases=aliases,
            scratch_shapes=[pltpu.VMEM((slots + 1, 2, tile, tile), F32)],
            compiler_params=small_params,
        )(table, maps)

    far_ranks, own_ranks = (0, n_epoch - 1), (n_epoch - 1, n_epoch)
    send, maps = main_sums(far_ranks, 1, 0, maps, 1)
    keep, maps = main_sums(far_ranks, 0, 1, maps, 1)
    far, side = pl.pallas_call(
        join_kernel,
        out_shape=(
            jax.ShapeDtypeStruct(keep.shape, BF16),
            jax.ShapeDtypeStruct((group_rows, tile), BF16),
        ),
        in_specs=[vmem] * (3 + len(beyond)),
        out_specs=(vmem, vmem),
        compiler_params=small_params,
    )(keep, move(send, "vel", 1), edges[(n_epoch - 1) * group_rows :], *beyond)
    side = beside_by_member(side)
    mains = [
        move(far[(d - 1) * main_rows : d * main_rows], "epoch", d) for d in range(1, n_epoch)
    ]

    def pass_own(send, side):
        arrived = move(send, "vel", 1)
        is_first = lax.axis_index("vel") == 0
        near = jnp.where(is_first, side[:edge_rows], side[edge_rows:])
        other = jnp.where(is_first, side[edge_rows:], side[:edge_rows])
        return arrived, jnp.concatenate([near, move(other, "vel", 1)])

    send, keep = main_sums(own_ranks, 1, 1, maps, 0)
    arrived, side = lax.cond(taken, pass_own, lambda send, side: (send, side), send, side)

    shape = jax.ShapeDtypeStruct((block, tile, tile), F32)
    likelihood, flux = pl.pallas_call(
        functools.partial(finish_kernel, tile, block),
        out_shape=(shape, shape),
        in_specs=[vmem] * (3 + len(mains)),
        out_specs=(hbm, hbm),
        scratch_shapes=[
            pltpu.VMEM(shape.shape, F32),
            pltpu.VMEM(shape.shape, F32),
            pltpu.SemaphoreType.DMA((2 * block,)),
        ],
        compiler_params=params,
    )(keep, arrived, side, *mains)
    return likelihood[:, None], flux[:, None]


def solution(mesh):
    placed = (
        P(("epoch", "vel"), ("field", "sky"), None, None),
        P(("epoch", "vel"), ("field", "sky"), None, None),
        P(("epoch", "vel"), ("field", "sky")),
        P(("field", "epoch", "vel")),
        P(None, None, "epoch"),
    )
    return jax.shard_map(
        on_device,
        mesh=mesh,
        in_specs=placed,
        out_specs=(
            P(("epoch", "vel"), ("field", "sky"), None, None),
            P(("epoch", "vel"), ("field", "sky"), None, None),
        ),
        check_vma=False,
    )
```
